32 devices in a mesh: seq: 4 (over y, core), img: 8 (over z, x).
Axes of the slice: x: 2, y: 2, z: 4, core: 2. Of those that a mesh axis runs over, the one named last changes fastest.
Arguments:
- patches: bfloat16 [24, 512, 768], P('img', 'seq'), may hold values from -6 to 6
- widths: int32 [24], P('img'), may hold values from 8 to 32, as said below
- ln1_gain: float32 [768], replicated, may hold values from 0.5 to 1.5
- ln1_bias: float32 [768], replicated, may hold values from -4 to 4
- w_qkv: bfloat16 [768, 2304], replicated, may hold values from -0.21875 to 0.21875
- b_query: float32 [768], replicated, may hold values from -6 to 6
- b_value: float32 [768], replicated, may hold values from -6 to 6
- w_out: bfloat16 [768, 768], replicated, may hold values from -0.875 to 0.875
- b_out: float32 [768], replicated, may hold values from -4 to 4
- ln2_gain: float32 [768], replicated, may hold values from 0.5 to 1.5
- ln2_bias: float32 [768], replicated, may hold values from -4 to 4
- w_up: bfloat16 [768, 3072], replicated, may hold values from -0.21875 to 0.21875
- b_up: float32 [3072], replicated, may hold values from -4 to 4
- w_down: bfloat16 [3072, 768], replicated, may hold values from -0.109375 to 0.109375
- b_down: float32 [768], replicated, may hold values from -4 to 4
- codebook: bfloat16 [3584, 768], P(('seq', 'img')), may hold values from -6 to 6
- cotangent: bfloat16 [24, 512, 768], P('img', 'seq'), may hold values from -6 to 6
Outputs:
- quantized: bfloat16 [24, 512, 768], P('img', 'seq')
- token_loss: float32 [24, 512], P('img', 'seq')
- grad_input: float32 [24, 512, 768], P('img', 'seq')
- grad_ln1_gain: float32 [768], P('img')
- grad_ln1_bias: float32 [768], P('img')
- grad_w_qkv: float32 [768, 2304], P(None, 'img')
- grad_b_query: float32 [768], P('img')
- grad_b_value: float32 [768], P('img')
- grad_w_out: float32 [768, 768], P(None, 'img')
- grad_b_out: float32 [768], P('img')
- grad_ln2_gain: float32 [768], P('img')
- grad_ln2_bias: float32 [768], P('img')
- grad_w_up: float32 [768, 3072], P(None, 'img')
- grad_b_up: float32 [3072], P('img')
- grad_w_down: float32 [3072, 768], P(None, 'img')
- grad_b_down: float32 [768], P('img')
The draws below stay inside these ranges and needn't reach their ends.
Inputs may be any that keep to these rules, and one draw needn't show every extreme that they name: `widths`: in each aligned group of 3 images at least one has the full width 512 // 16; some image has the least width.
All inputs are finite; a program needn't handle non-finite values.
Results may differ from the reference program's by a relative error of at most 0.02.
Values may be sent and summed in bfloat16 or wider, within the bound.
No kernel may reach another device: no remote copies, remote signals or barrier semaphores. Data moves between devices by JAX's collectives and lax.ppermute only.
A program may use at most 320 MiB of HBM per device.

```python
import jax
import jax.numpy as jnp
from jax import lax

D = 768
HEADS = 12
HEAD_DIM = 64
FF = 3072
PATCHES = 512
GRID_H = 16
IMG_DEV = 3
VOCAB = 3584
IMAGES = 24


def draw_widths(key, part):
    key = jax.random.fold_in(key, 7)
    key_base, key_full, key_pick = jax.random.split(key, 3)
    widest = PATCHES // GRID_H
    narrowest = widest // 4
    groups = IMAGES // IMG_DEV
    chosen = jax.random.randint(key_base, (IMAGES,), narrowest, widest + 1)
    full_slot = jax.random.randint(key_full, (groups,), 0, IMG_DEV)
    full_index = jnp.arange(groups) * IMG_DEV + full_slot
    chosen = chosen.at[full_index].set(widest)
    group_pick = jax.random.randint(key_pick, (), 0, groups)
    narrow_index = group_pick * IMG_DEV + (full_slot[group_pick] + 1) % IMG_DEV
    chosen = chosen.at[narrow_index].set(narrowest)
    return chosen.astype(jnp.int32)


def raised(result, rng, source, target, parts, factor):
    def block_of(position):
        return (jnp.arange(result.shape[position]) // (result.shape[position] // parts)).reshape((-1,) + (1,) * (result.ndim - 1 - position))

    near = jax.random.permutation(rng, parts)[block_of(target)]
    other_side = (block_of(target) + parts // 2) % parts
    return jnp.where((block_of(source) == near) | (block_of(source) == other_side), factor * result, result)


def block_scale(own_key, extent, shards, low, largest):
    level = 1.0
    for axis_at, blocks in shards:
        steps = jax.random.uniform(jax.random.fold_in(jax.random.fold_in(own_key, 6), axis_at), (blocks,), jnp.float32, low / len(shards), largest / len(shards))
        level = level * jnp.repeat(jnp.exp(steps), extent[axis_at] // blocks).reshape((-1,) + (1,) * (len(extent) - 1 - axis_at))
    return level


def noise(rng, shape, scale, bound, pieces=(), kind=jnp.bfloat16):
    entries = scale * jax.random.normal(rng, shape, jnp.float32)
    if pieces:
        entries = entries * block_scale(rng, shape, pieces, -0.22, 0.18)
    return jnp.clip(entries, -bound, bound).astype(kind)


def heavy_noise(rng, shape, scale, limit, pieces, heavy, held_as=jnp.bfloat16):
    array = scale * jax.random.normal(rng, shape, jnp.float32)
    if pieces:
        array = array * block_scale(rng, shape, pieces, -0.22, 0.18)
    return jnp.clip(raised(array, jax.random.fold_in(rng, 3), *heavy), -limit, limit).astype(held_as)


def setup_inputs(seed: int = 0) -> dict:
    key_list = jax.random.split(jax.random.key(seed), 18)
    return {
        "patches": noise(key_list[0], (IMAGES, PATCHES, D), 1.0, 6.0, ((0, 8), (1, 4))),
        "widths": draw_widths(jax.random.fold_in(key_list[17], 71), 0),
        "ln1_gain": jnp.clip(1.0 + 0.1 * jax.random.normal(key_list[2], (D,), jnp.float32), 0.5, 1.5),
        "ln1_bias": noise(key_list[3], (D,), 0.3, 4.0, (), jnp.float32),
        "w_qkv": noise(key_list[4], (D, 3 * D), D ** -0.5, 0.21875),
        "b_query": noise(key_list[5], (D,), 0.5, 6.0, (), jnp.float32),
        "b_value": noise(key_list[6], (D,), 0.5, 6.0, (), jnp.float32),
        "w_out": noise(key_list[7], (D, D), (D // 16) ** -0.5, 0.875),
        "b_out": noise(key_list[8], (D,), 0.3, 4.0, (), jnp.float32),
        "ln2_gain": jnp.clip(1.0 + 0.1 * jax.random.normal(key_list[9], (D,), jnp.float32), 0.5, 1.5),
        "ln2_bias": noise(key_list[10], (D,), 0.3, 4.0, (), jnp.float32),
        "w_up": noise(key_list[11], (D, FF), D ** -0.5, 0.21875),
        "b_up": noise(key_list[12], (FF,), 0.3, 4.0, (), jnp.float32),
        "w_down": noise(key_list[13], (FF, D), FF ** -0.5, 0.109375),
        "b_down": noise(key_list[14], (D,), 0.3, 4.0, (), jnp.float32),
        "codebook": noise(key_list[15], (VOCAB, D), 1.0, 6.0, ((0, 32),)),
        "cotangent": heavy_noise(key_list[16], (IMAGES, PATCHES, D), 1.0, 6.0, ((0, 8), (1, 4)), (0, 2, 8, 2.0)),
    }


@jax.custom_vjp
def low(v):
    return lax.optimization_barrier(v.astype(jnp.bfloat16)).astype(jnp.float32)

@jax.custom_vjp
def low_back(v):
    return v

def low_keep(v):
    return (low(v), None)

def low_pass(kept, grad):
    return (grad,)

def back_keep(v):
    return (v, None)

def back_low(kept, grad):
    return (low(grad),)
low.defvjp(low_keep, low_pass)
low_back.defvjp(back_keep, back_low)
EPS_NORM = 1e-06
COMMIT = 16.0
HIGH = lax.Precision.HIGHEST

def layer_norm(values, gain, shift):
    center = values - lax.optimization_barrier(jnp.mean(values, axis=-1, keepdims=True))
    spread = lax.optimization_barrier(jnp.mean(center * center, axis=-1, keepdims=True))
    return center * lax.rsqrt(spread + EPS_NORM) * gain + shift

def image_forward(params, patch, width, book_full):
    ln1_gain, ln1_bias, w_qkv, b_query, b_value, w_out, b_out, ln2_gain, ln2_bias, w_up, b_up, w_down, b_down = params
    valid = jnp.arange(PATCHES) < GRID_H * width
    normed = low(layer_norm(patch, ln1_gain, ln1_bias))
    bias_all = jnp.concatenate([b_query, jnp.zeros_like(b_query), b_value])
    qkv = low(low_back(jnp.dot(normed, w_qkv, precision=HIGH) + bias_all))
    queries = qkv[:, :D].reshape(PATCHES, HEADS, HEAD_DIM)
    keys_all = qkv[:, D:2 * D].reshape(PATCHES, HEADS, HEAD_DIM)
    values_all = qkv[:, 2 * D:].reshape(PATCHES, HEADS, HEAD_DIM)
    raw_scores = low_back(jnp.einsum('qhd,khd->hqk', queries, keys_all, precision=HIGH))
    scores = jnp.where(valid[None, None, :], raw_scores * HEAD_DIM ** (-0.5), -1000000000.0)
    attn_probs = low(jax.nn.softmax(scores, axis=-1))
    attended = jnp.einsum('hqk,khd->qhd', attn_probs, values_all, precision=HIGH).reshape(PATCHES, D)
    attended = low(low_back(attended))
    branch = low_back(jnp.dot(attended, w_out, precision=HIGH) + b_out)
    middle = patch + branch
    normed_two = low(layer_norm(middle, ln2_gain, ln2_bias))
    hidden_pre = low_back(jnp.dot(normed_two, w_up, precision=HIGH) + b_up)
    hidden_act = low(jax.nn.gelu(hidden_pre, approximate=False))
    mlp_out = low_back(jnp.dot(hidden_act, w_down, precision=HIGH) + b_down)
    encoded = middle + mlp_out
    code_raw = low_back(jnp.dot(low(encoded), book_full.T, precision=HIGH))
    code_weights = low(jax.nn.softmax(code_raw * D ** (-0.5), axis=-1))
    mixture = low_back(jnp.dot(code_weights, book_full, precision=HIGH))
    difference = encoded - mixture
    token_loss = jnp.where(valid, lax.optimization_barrier(jnp.mean(difference * difference, axis=-1)), 0.0)
    return (mixture, token_loss)

def reference(patches, widths, ln1_gain, ln1_bias, w_qkv, b_query, b_value, w_out, b_out, ln2_gain, ln2_bias, w_up, b_up, w_down, b_down, codebook, cotangent):
    params = tuple((item.astype(jnp.float32) for item in (ln1_gain, ln1_bias, w_qkv, b_query, b_value, w_out, b_out, ln2_gain, ln2_bias, w_up, b_up, w_down, b_down)))
    book_full = codebook.astype(jnp.float32)

    def one_image(carry, item):
        patch, width, cotan = item

        def forward(params_in, patch_in):
            return image_forward(params_in, patch_in, width, book_full)
        outputs, pull_back = jax.vjp(forward, params, patch)
        grads, grad_patch = pull_back((cotan, jnp.full((PATCHES,), COMMIT, dtype=jnp.float32)))
        carry = jax.tree.map(lambda total, term: total + term, carry, grads)
        return (carry, (outputs[0].astype(jnp.bfloat16), outputs[1], grad_patch))
    initial = jax.tree.map(jnp.zeros_like, params)
    totals, (quantized, token_loss, grad_input) = lax.scan(one_image, initial, (patches.astype(jnp.float32), widths, cotangent.astype(jnp.float32)))
    return (quantized, token_loss, grad_input, totals[0], totals[1], totals[2], totals[3], totals[4], totals[5], totals[6], totals[7], totals[8], totals[9], totals[10], totals[11], totals[12])
```

```python
import jax
import jax.numpy as jnp
from jax import lax
from jax.sharding import PartitionSpec as P

HEAD_DIM = 64
GRID_H = 16
EPS_NORM = 1e-06
COMMIT = 16.0
BF = jnp.bfloat16
F32 = jnp.float32


def layer_norm(values, gain, shift):
    center = values - jnp.mean(values, axis=-1, keepdims=True)
    spread = jnp.mean(center * center, axis=-1, keepdims=True)
    return center * lax.rsqrt(spread + EPS_NORM) * gain + shift


def exact_gelu(values):
    return jax.nn.gelu(values, approximate=False)


def mm(a, b):
    return jnp.dot(a, b, preferred_element_type=F32)


def mm_nt(a, b):
    return lax.dot_general(a, b, (((1,), (1,)), ((), ())), preferred_element_type=F32)


def mm_tn(a, b):
    return lax.dot_general(a, b, (((0,), (0,)), ((), ())), preferred_element_type=F32)


def swap(value, axis, bit):
    count = lax.axis_size(axis)
    return lax.ppermute(value, axis, [(i, i ^ bit) for i in range(count)])


def pick(value, index, axis):
    return lax.dynamic_index_in_dim(value, index, axis, keepdims=False)


def img_bits():
    count, bits = lax.axis_size("img"), []
    bit = 1
    while bit < count:
        bits.append(bit)
        bit *= 2
    return bits


def reduce_shards(parts, order):
    count, rows, cols = parts.shape
    bits = img_bits()
    me, chip = lax.axis_index("img"), lax.axis_index("seq") // 2
    shape = [2] * len(bits)
    value = parts.reshape(shape + [2, rows // 2, cols])
    names = list(reversed(bits)) + ["y"]
    for step in order:
        axis = names.index(step)
        mine = chip if step == "y" else (me // step) % 2
        sent = pick(value, 1 - mine, axis)
        got = swap(sent, "seq", 2) if step == "y" else swap(sent, "img", step)
        value = (pick(value, mine, axis).astype(F32) + got.astype(F32)).astype(BF)
        names.pop(axis)
    other = swap(value, "seq", 2)
    first = jnp.where(chip == 0, value, other)
    second = jnp.where(chip == 0, other, value)
    return jnp.concatenate([first, second], axis=0)


def reduce_small(parts):
    value = parts
    me = lax.axis_index("img")
    value = value + swap(value, "seq", 1)
    value = value.reshape([2] * len(img_bits()) + [parts.shape[-1]])
    for step in reversed(img_bits()):
        mine = (me // step) % 2
        value = pick(value, mine, 0) + swap(pick(value, 1 - mine, 0), "img", step)
    return value + swap(value, "seq", 2)


def shards(
    patches,
    widths,
    ln1_gain,
    ln1_bias,
    w_qkv,
    b_query,
    b_value,
    w_out,
    b_out,
    ln2_gain,
    ln2_bias,
    w_up,
    b_up,
    w_down,
    b_down,
    codebook,
    cotangent,
):
    images, block, dim = patches.shape
    heads = dim // HEAD_DIM
    hidden = w_up.shape[1]
    n_img = lax.axis_size("img")
    me = lax.axis_index("seq")
    chip, core = me // 2, me % 2
    half = dim // 2
    rows = images * block
    main = 2 * block
    att_scale = HEAD_DIM ** (-0.5)
    code_scale = dim ** (-0.5)

    def gather_rows(value):
        own = pick(value, chip, 0)
        got = swap(pick(value, 1 - chip, 0), "seq", 2)
        return jnp.concatenate([own, got, value[2]], axis=0)

    def return_rows(value):
        own, back, last = value[:block], swap(value[block:main], "seq", 2), value[main:]
        first = jnp.where(chip == 0, own, back)
        second = jnp.where(chip == 0, back, own)
        return jnp.stack([first, second, last])

    spots = jnp.arange(block)
    order4 = [me, me ^ 2, me ^ 1, me ^ 3]
    key_spots = jnp.concatenate([place * block + spots for place in order4])
    limit_main = GRID_H * pick(widths, chip, 0)
    limit_last = GRID_H * widths[2]
    key_ok_main = key_spots < limit_main
    key_ok_last = key_spots < limit_last
    row_ok = jnp.concatenate([key_ok_main[:main], key_ok_last[:block]])

    source = gather_rows(patches).astype(F32)
    cot = gather_rows(cotangent)
    normed = layer_norm(source, ln1_gain, ln1_bias).astype(BF)
    bias_all = jnp.concatenate([b_query, jnp.zeros_like(b_query), b_value])
    qkv = (mm(normed, w_qkv) + bias_all).astype(BF)
    kv = qkv[:, dim:]
    kv_main = jnp.concatenate([kv[:main], swap(kv[:main], "seq", 1)])
    kv_last = jnp.concatenate([kv[main:], swap(kv[main:], "seq", 2)])
    kv_last = jnp.concatenate([kv_last, swap(kv_last, "seq", 1)])

    def attend(queries, keyvals, ok):
        count = queries.shape[0]
        q = queries.reshape(count, heads, HEAD_DIM)
        k = keyvals[:, :dim].reshape(-1, heads, HEAD_DIM)
        v = keyvals[:, dim:].reshape(-1, heads, HEAD_DIM)
        raw = jnp.einsum("bhd,khd->hbk", q, k, preferred_element_type=F32)
        scores = jnp.where(ok[None, None, :], raw * att_scale, -1000000000.0)
        peak = jnp.max(scores, axis=-1, keepdims=True)
        expo = jnp.exp(scores - peak)
        probs = expo / jnp.sum(expo, axis=-1, keepdims=True)
        low = probs.astype(BF)
        out = jnp.einsum("hbk,khd->bhd", low, v, preferred_element_type=F32)
        return probs, low, out.reshape(count, dim).astype(BF)

    probs_main, low_main, att_main = attend(qkv[:main, :dim], kv_main, key_ok_main)
    probs_last, low_last, att_last = attend(qkv[main:, :dim], kv_last, key_ok_last)
    attended = jnp.concatenate([att_main, att_last])
    middle = source + mm(attended, w_out) + b_out
    normed_two = layer_norm(middle, ln2_gain, ln2_bias).astype(BF)
    hidden_pre = mm(normed_two, w_up) + b_up
    act = exact_gelu(hidden_pre).astype(BF)
    encoded = middle + mm(act, w_down) + b_down

    book = lax.all_gather(codebook, ("seq", "img"), axis=0, tiled=True)
    code_scores = mm_nt(encoded.astype(BF), book) * code_scale
    peak_code = jnp.max(code_scores, axis=-1, keepdims=True)
    log_total = peak_code + jnp.log(jnp.sum(jnp.exp(code_scores - peak_code), axis=-1, keepdims=True))
    cweights = jnp.exp(code_scores - log_total)
    mixture = mm(cweights.astype(BF), book)
    difference = encoded - mixture
    token_loss = jnp.where(row_ok, jnp.mean(difference * difference, axis=-1), 0.0)
    pull = jnp.where(row_ok[:, None], 2.0 * COMMIT / dim * difference, 0.0)
    dmix = (cot.astype(F32) - pull).astype(BF)
    dweights = mm_nt(dmix, book)
    inner = jnp.sum(cweights * dweights, axis=-1, keepdims=True)
    dcode = (cweights * (dweights - inner) * code_scale).astype(BF)
    denc = mm(dcode, book) + pull
    dmlp = denc.astype(BF)

    def both(value):
        return jnp.concatenate([value, swap(value, "seq", 1)])

    def half_both(value, width):
        parts = value.reshape(rows, 2, width)
        return jnp.concatenate([pick(parts, core, 1), swap(pick(parts, 1 - core, 1), "seq", 1)])

    bits = img_bits()
    near = [bit for bit in bits if bit != 1]
    order_a = ["y"] + bits
    order_b = [1, "y"] + near
    order_c = near[:1] + ["y", 1] + near[1:]

    dmlp_both = both(dmlp)
    act_half = half_both(act, hidden // 2)
    part_down = mm_tn(dmlp_both, act_half).astype(BF).reshape(n_img, dim // n_img, hidden // 2)
    sum_down = reduce_shards(part_down, order_c)

    dhidden = mm_nt(dmlp, w_down)
    gelu_val, gelu_pull = jax.vjp(exact_gelu, hidden_pre)
    dpre = gelu_pull(dhidden)[0].astype(BF)
    part_up = mm_tn(both(dpre), half_both(normed_two, half)).astype(BF).reshape(n_img, hidden // n_img, half)
    sum_up = reduce_shards(part_up, order_b)

    dnormed_two = mm_nt(dpre, w_up)
    norm_val, norm_pull = jax.vjp(layer_norm, middle, ln2_gain, ln2_bias)
    dmid_norm, grad_gain_two, grad_shift_two = norm_pull(dnormed_two)
    dmiddle = denc + dmid_norm
    dbranch = dmiddle.astype(BF)
    part_out = mm_tn(both(dbranch), half_both(attended, half)).astype(BF).reshape(n_img, dim // n_img, half)
    datt = mm_nt(dbranch, w_out).astype(BF)

    def attend_back(queries, keyvals, probs, low, datt_rows):
        count = queries.shape[0]
        q = queries.reshape(count, heads, HEAD_DIM)
        k = keyvals[:, :dim].reshape(-1, heads, HEAD_DIM)
        v = keyvals[:, dim:].reshape(-1, heads, HEAD_DIM)
        da = datt_rows.reshape(count, heads, HEAD_DIM)
        dprobs = jnp.einsum("bhd,khd->hbk", da, v, preferred_element_type=F32)
        dv = jnp.einsum("hbk,bhd->khd", low, da, preferred_element_type=F32)
        att_inner = jnp.sum(probs * dprobs, axis=-1, keepdims=True)
        ds = (probs * (dprobs - att_inner) * att_scale).astype(BF)
        dq = jnp.einsum("hbk,khd->bhd", ds, k, preferred_element_type=F32)
        dk = jnp.einsum("hbk,bhd->khd", ds, q, preferred_element_type=F32)
        dkv = jnp.concatenate([dk.reshape(-1, dim), dv.reshape(-1, dim)], axis=1).astype(BF)
        return dq.reshape(count, dim).astype(BF), dkv

    dq_last, dkv_last = attend_back(qkv[main:, :dim], kv_last, probs_last, low_last, datt[main:])
    dkv_last = (dkv_last[:main].astype(F32) + swap(dkv_last[main:], "seq", 1).astype(F32)).astype(BF)
    dkv_last = (dkv_last[:block].astype(F32) + swap(dkv_last[block:], "seq", 2).astype(F32)).astype(BF)
    dq_main, dkv_main = attend_back(qkv[:main, :dim], kv_main, probs_main, low_main, datt[:main])
    dkv_main = (dkv_main[:main].astype(F32) + swap(dkv_main[main:], "seq", 1).astype(F32)).astype(BF)
    dqkv = jnp.concatenate(
        [jnp.concatenate([dq_main, dq_last]), jnp.concatenate([dkv_main, dkv_last])], axis=1
    )
    part_qkv = mm_tn(both(dqkv), half_both(normed, half)).astype(BF).reshape(n_img, 3 * dim // n_img, half)
    sum_qkv = reduce_shards(jnp.concatenate([part_qkv, part_out], axis=1), order_a)
    sum_qkv, sum_out = sum_qkv[: 3 * dim // n_img], sum_qkv[3 * dim // n_img :]

    dnormed = mm_nt(dqkv, w_qkv)
    first_val, first_pull = jax.vjp(layer_norm, source, ln1_gain, ln1_bias)
    dsource, grad_gain_one, grad_shift_one = first_pull(dnormed)
    grad_input = dmiddle + dsource

    def total(value):
        return jnp.sum(value.astype(F32), axis=0)

    dqkv_total = total(dqkv)
    vectors = [
        grad_gain_one,
        grad_shift_one,
        dqkv_total[:dim],
        dqkv_total[2 * dim :],
        total(dbranch),
        grad_gain_two,
        grad_shift_two,
        total(dpre),
        total(dmlp),
    ]
    small = reduce_small(jnp.concatenate([v.reshape(n_img, -1) for v in vectors], axis=1))
    sizes = [v.shape[0] // n_img for v in vectors]
    cuts = [sum(sizes[:k]) for k in range(len(sizes) + 1)]
    small = [small[cuts[k] : cuts[k + 1]] for k in range(len(sizes))]

    def finish(value):
        other = swap(value, "seq", 1)
        low = jnp.where(core == 0, value, other)
        high = jnp.where(core == 0, other, value)
        return jnp.concatenate([low, high], axis=1).T.astype(F32)

    return (
        return_rows(mixture.astype(BF)),
        return_rows(token_loss),
        return_rows(grad_input.astype(BF)).astype(F32),
        small[0],
        small[1],
        finish(sum_qkv),
        small[2],
        small[3],
        finish(sum_out),
        small[4],
        small[5],
        small[6],
        finish(sum_up),
        small[7],
        finish(sum_down),
        small[8],
    )


def solution(mesh):
    return jax.shard_map(
        shards,
        mesh=mesh,
        in_specs=(
            P("img", "seq", None),
            P("img"),
            P(),
            P(),
            P(),
            P(),
            P(),
            P(),
            P(),
            P(),
            P(),
            P(),
            P(),
            P(),
            P(),
            P(("seq", "img"), None),
            P("img", "seq", None),
        ),
        out_specs=(
            P("img", "seq", None),
            P("img", "seq"),
            P("img", "seq", None),
            P("img"),
            P("img"),
            P(None, "img"),
            P("img"),
            P("img"),
            P(None, "img"),
            P("img"),
            P("img"),
            P("img"),
            P(None, "img"),
            P("img"),
            P(None, "img"),
            P("img"),
        ),
        check_vma=False,
    )
```

```python
import functools

import jax
import jax.numpy as jnp
from jax import lax
from jax.experimental import pallas as pl
from jax.experimental.pallas import tpu as pltpu
from jax.sharding import PartitionSpec as P

HEAD_DIM = 64
GRID_H = 16
EPS_NORM = 1e-06
COMMIT = 16.0
BF = jnp.bfloat16
F32 = jnp.float32
VMEM_LIMIT = 56 * 1024 * 1024
MASKED = -1000000000.0


def mm(a, b):
    return jnp.dot(a, b, preferred_element_type=F32)


def mm_nt(a, b):
    return lax.dot_general(a, b, (((1,), (1,)), ((), ())), preferred_element_type=F32)


def mm_tn(a, b):
    return lax.dot_general(a, b, (((0,), (0,)), ((), ())), preferred_element_type=F32)


def swap(value, axis, bit):
    count = lax.axis_size(axis)
    return lax.ppermute(value, axis, [(i, i ^ bit) for i in range(count)])


def pick(value, index, axis):
    return lax.dynamic_index_in_dim(value, index, axis, keepdims=False)


def after(value, *others):
    return lax.optimization_barrier((value, *others))[0]


def img_bits():
    return [1 << k for k in range(lax.axis_size("img").bit_length() - 1)]


def cost(flops, size):
    return pl.CostEstimate(flops=int(flops), bytes_accessed=int(size), transcendentals=0)


def whole(shape):
    return pl.BlockSpec(tuple(shape), lambda *_: (0,) * len(shape))


def shaped(shape, dtype=BF):
    return jax.ShapeDtypeStruct(tuple(shape), dtype)


def call(kernel, name, grid, in_specs, out_specs, out_shape, scratch, estimate, *args):
    return pl.pallas_call(
        kernel,
        grid_spec=pltpu.PrefetchScalarGridSpec(
            num_scalar_prefetch=1, grid=grid, in_specs=in_specs, out_specs=out_specs, scratch_shapes=scratch
        ),
        out_shape=out_shape,
        compiler_params=pltpu.CompilerParams(
            dimension_semantics=("arbitrary",) * len(grid), vmem_limit_bytes=VMEM_LIMIT
        ),
        cost_estimate=estimate,
        name=name,
    )(*args)


ME, CORE, CHIP, LIMIT_MAIN, LIMIT_LAST, IMG = range(6)


def norm_stats(x):
    center = x - jnp.mean(x, axis=-1, keepdims=True)
    spread = jnp.mean(center * center, axis=-1, keepdims=True)
    inv = lax.rsqrt(spread + EPS_NORM)
    return center * inv, inv


def norm_back(xhat, inv, gain, dy):
    dxhat = dy * gain
    return inv * (
        dxhat - jnp.mean(dxhat, axis=-1, keepdims=True) - xhat * jnp.mean(dxhat * xhat, axis=-1, keepdims=True)
    )


def spots(index, block, me):
    place = index // block
    mask = (place % 2) * 2 + place // 2
    return (me ^ mask) * block + index % block


def qkv_kernel(s, *refs):
    parts, (gain, shift, w, b, q, kv, mine, send, h) = refs[:-9], refs[-9:]
    step = pl.program_id(0)
    half = mine.shape[1]

    @pl.when(step == 0)
    def _():
        for k, x in enumerate(parts):
            block = x.shape[-2]
            rows = x[...].reshape(block, -1).astype(F32)
            xhat, _ = norm_stats(rows)
            h[k * block : (k + 1) * block, :] = (xhat * gain[...] + shift[...]).astype(BF)
        mine[...] = h[:, pl.ds(s[CORE] * half, half)]
        send[...] = h[:, pl.ds((1 - s[CORE]) * half, half)]

    out = (mm(h[...], w[...]) + b[...]).astype(BF)

    @pl.when(step == 0)
    def _():
        q[...] = out

    @pl.when(step > 0)
    def _():
        kv[...] = out


def qkv_fwd(s, parts, specs, gain, shift, w, bias, block):
    dim = w.shape[0]
    n, half = block * len(parts), dim // 2
    vec = whole((1, dim))
    return call(
        qkv_kernel, "qkv_fwd", (3,),
        [*specs, vec, vec, pl.BlockSpec((dim, dim), lambda p, s: (0, p)), pl.BlockSpec((1, dim), lambda p, s: (0, p))],
        [
            whole((n, dim)),
            pl.BlockSpec((n, dim), lambda p, s: (0, jnp.maximum(p - 1, 0))),
            whole((n, half)),
            whole((n, half)),
        ],
        [shaped((n, dim)), shaped((n, 2 * dim)), shaped((n, half)), shaped((n, half))],
        [pltpu.VMEM((n, dim), BF)],
        cost(6 * n * dim * dim, 6 * dim * dim + 10 * n * dim),
        s, *parts, gain, shift, w, bias,
    )


def two_heads(value):
    left = lax.broadcasted_iota(jnp.int32, value.shape, 1) < HEAD_DIM
    zero = jnp.zeros_like(value)
    return jnp.concatenate([jnp.where(left, value, zero), jnp.where(left, zero, value)], axis=0)


def one_pair(value):
    n = value.shape[0] // 2
    left = lax.broadcasted_iota(jnp.int32, (n, value.shape[1]), 1) < HEAD_DIM
    return jnp.where(left, value[:n], value[n:])


def att_fwd_kernel(s, *refs, limit, block):
    q, o = refs[0], refs[-1]
    count = (len(refs) - 2) // 2
    k = jnp.concatenate([r[...] for r in refs[1 : 1 + count]], axis=0)
    v = jnp.concatenate([r[...] for r in refs[1 + count : -1]], axis=0)
    raw = mm_nt(two_heads(q[...]), k) * (HEAD_DIM**-0.5)
    index = lax.broadcasted_iota(jnp.int32, (1, k.shape[0]), 1)
    scores = jnp.where(spots(index, block, s[ME]) < s[limit], raw, MASKED)
    expo = jnp.exp(scores - jnp.max(scores, axis=1, keepdims=True))
    probs = expo * (1.0 / jnp.sum(expo, axis=1, keepdims=True))
    o[...] = one_pair(mm(probs.astype(BF), v)).astype(BF)


def attention_fwd(s, q, kvs, limit, block):
    n, dim = q.shape
    pairs = dim // 128
    row = pl.BlockSpec((n, 128), lambda p, s: (0, p))
    keys = [pl.BlockSpec((kv.shape[0], 128), lambda p, s: (0, p)) for kv in kvs]
    vals = [pl.BlockSpec((kv.shape[0], 128), lambda p, s: (0, p + pairs)) for kv in kvs]
    m = sum(kv.shape[0] for kv in kvs)
    return call(
        functools.partial(att_fwd_kernel, limit=limit, block=block), "attention_fwd", (pairs,),
        [row, *keys, *vals], row, shaped((n, dim)), [],
        cost(8 * n * m * dim, 4 * (n + m) * dim),
        s, q, *kvs, *kvs,
    )


def att_bwd_kernel(s, *refs, limit, block):
    q, do, out = refs[0], refs[-2], refs[-1]
    count = (len(refs) - 3) // 2
    q2, do2 = two_heads(q[...]), two_heads(do[...])
    k = jnp.concatenate([r[...] for r in refs[1 : 1 + count]], axis=0)
    v = jnp.concatenate([r[...] for r in refs[1 + count : -2]], axis=0)
    m = k.shape[0]
    raw = mm_nt(k, q2) * (HEAD_DIM**-0.5)
    index = lax.broadcasted_iota(jnp.int32, (m, 1), 0)
    scores = jnp.where(spots(index, block, s[ME]) < s[limit], raw, MASKED)
    expo = jnp.exp(scores - jnp.max(scores, axis=0, keepdims=True))
    probs = expo * (1.0 / jnp.sum(expo, axis=0, keepdims=True))
    out[m : 2 * m, :] = mm(probs.astype(BF), do2).astype(BF)
    dp = mm_nt(v, do2)
    inner = jnp.sum(probs * dp, axis=0, keepdims=True)
    ds = (probs * (dp - inner) * (HEAD_DIM**-0.5)).astype(BF)
    out[:m, :] = mm(ds, q2).astype(BF)
    out[2 * m :, :] = one_pair(mm_tn(ds, k)).astype(BF)


def attention_bwd(s, q, kvs, do, spec, limit, block):
    n, dim = q.shape
    pairs = dim // 128
    row = pl.BlockSpec((n, 128), lambda p, s: (0, p))
    keys = [pl.BlockSpec((kv.shape[0], 128), lambda p, s: (0, p)) for kv in kvs]
    vals = [pl.BlockSpec((kv.shape[0], 128), lambda p, s: (0, p + pairs)) for kv in kvs]
    m = sum(kv.shape[0] for kv in kvs)
    return call(
        functools.partial(att_bwd_kernel, limit=limit, block=block), "attention_bwd", (pairs,),
        [row, *keys, *vals, spec],
        pl.BlockSpec((2 * m + n, 128), lambda p, s: (0, p)),
        shaped((2 * m + n, dim)), [],
        cost(20 * n * m * dim, 2 * (3 * n + 4 * m) * dim),
        s, q, *kvs, *kvs, do,
    )


def gelu_pair(x):
    z = jnp.abs(x) * (0.5**0.5)
    t = 1.0 / (1.0 + 0.3275911 * z)
    expo = jnp.exp(-0.5 * x * x)
    poly = t * (0.254829592 + t * (-0.284496736 + t * (1.421413741 + t * (-1.453152027 + t * 1.061405429))))
    tail = 0.5 * poly * expo
    cdf = jnp.where(x < 0.0, tail, 1.0 - tail)
    return x * cdf, cdf + x * (expo * 0.3989422804014327)


def mlp_fwd_kernel(
    s, own, got, last, att_main, att_last, wout, bout, gain, shift, wup, bup, wdown, bdown,
    mid, slope, enc, mine, send, h2,
):
    step, steps = pl.program_id(0), pl.num_programs(0)
    block, dim = got.shape
    half = dim // 2
    hidden_half = mine.shape[1] - 2 * half
    tile = slope.shape[1]
    per = hidden_half // tile

    @pl.when(step == 0)
    def _():
        x = jnp.concatenate([own[0], got[...], last[0]], axis=0).astype(F32)
        att = jnp.concatenate([att_main[...], att_last[...]], axis=0)
        middle = x + mm(att, wout[...]) + bout[...]
        mid[...] = middle
        xhat, _ = norm_stats(middle)
        h2[...] = (xhat * gain[...] + shift[...]).astype(BF)
        enc[...] = middle + bdown[...]
        for out, side in ((mine, s[CORE]), (send, 1 - s[CORE])):
            cols = pl.ds(pl.multiple_of(side * half, half), half)
            out[:, hidden_half : hidden_half + half] = h2[:, cols]
            rows = att_main.shape[0]
            out[:rows, hidden_half + half :] = att_main[:, cols]
            out[rows:, hidden_half + half :] = att_last[:, cols]

    pre = mm(h2[...], wup[...]) + bup[...]
    act, rate = gelu_pair(pre)
    act = act.astype(BF)
    slope[...] = rate.astype(BF)
    enc[...] += mm(act, wdown[...])
    for k in range(2 * per):
        out = send if k < per else mine

        @pl.when(step == k)
        def _():
            out[:, (k % per) * tile : (k % per + 1) * tile] = act


def mlp_fwd(s, patches, got, att_main, att_last, wout, bout, gain, shift, wup, bup, wdown, bdown, tile):
    images, block, dim = patches.shape
    n, hidden = images * block, wup.shape[1]
    steps = hidden // tile
    per = steps // 2

    def at(p, s):
        return p % per + jnp.where(p < per, 1 - s[CORE], s[CORE]) * per

    full, vec = whole((n, dim)), whole((1, dim))
    wide = dim + hidden // 2
    return call(
        mlp_fwd_kernel, "mlp_fwd", (steps,),
        [
            pl.BlockSpec((1, block, dim), lambda p, s: (s[CHIP], 0, 0)),
            whole((block, dim)),
            pl.BlockSpec((1, block, dim), lambda p, s: (2, 0, 0)),
            whole(att_main.shape), whole(att_last.shape),
            whole((dim, dim)), vec, vec, vec,
            pl.BlockSpec((dim, tile), lambda p, s: (0, at(p, s))),
            pl.BlockSpec((1, tile), lambda p, s: (0, at(p, s))),
            pl.BlockSpec((tile, dim), lambda p, s: (at(p, s), 0)),
            vec,
        ],
        [full, pl.BlockSpec((n, tile), lambda p, s: (0, at(p, s))), full, whole((n, wide)), whole((n, wide))],
        [shaped((n, dim), F32), shaped((n, hidden)), shaped((n, dim), F32), shaped((n, wide)), shaped((n, wide))],
        [pltpu.VMEM((n, dim), BF)],
        cost(2 * n * dim * (dim + 2 * hidden), 2 * dim * (dim + 2 * hidden) + 4 * n * hidden + 14 * n * dim),
        s, patches, got, patches, att_main, att_last, wout, bout, gain, shift, wup, bup, wdown, bdown,
    )


def quant_kernel(s, enc, cot, cot_got, *refs, moves, tile, scale):
    pieces = refs[: -11]
    mix_own, mix_back, mix_last, loss, denc, dmlp, book, score, dweight, late, sems = refs[-11:]
    n, dim = enc.shape
    block = n // 3
    vocab = book.shape[0]
    steps = vocab // tile
    copies = []
    for k, (piece, source, target, rows, lane, width) in enumerate(moves):
        copies.append(
            pltpu.make_async_copy(
                pieces[piece].at[pl.ds(source, rows), :],
                book.at[pl.ds(target, rows), pl.ds(lane, width)],
                sems.at[k],
            )
        )
    for c in copies:
        c.start()
    low = enc[...].astype(BF)
    peak, waited = None, 0
    for t in range(steps):
        while waited < len(moves) and moves[waited][2] < (t + 1) * tile:
            copies[waited].wait()
            waited += 1
        cols = pl.ds(t * tile, tile)
        part = mm_nt(low, book[cols, :]) * scale
        score[:, cols] = part
        top = jnp.max(part, axis=1, keepdims=True)
        peak = top if peak is None else jnp.maximum(peak, top)
    total = jnp.zeros_like(peak)
    late[...] = jnp.zeros_like(late)
    for t in range(steps):
        cols = pl.ds(t * tile, tile)
        e = jnp.exp(score[:, cols] - peak)
        score[:, cols] = e
        total = total + jnp.sum(e, axis=1, keepdims=True)
        late[...] += mm(e.astype(BF), book[cols, :])
    inv = 1.0 / total
    mix = late[...] * inv
    low = mix.astype(BF)
    mix_own[...] = low[:block]
    mix_back[...] = low[block : 2 * block]
    mix_last[...] = low[2 * block :]
    index = lax.broadcasted_iota(jnp.int32, (n, 1), 0)
    spot = spots(index % (2 * block), block, s[ME])
    ok = spot < jnp.where(index < 2 * block, s[LIMIT_MAIN], s[LIMIT_LAST])
    diff = enc[...] - mix
    lost = jnp.where(ok, jnp.mean(diff * diff, axis=1, keepdims=True), 0.0)
    loss[...] = jnp.transpose(jnp.broadcast_to(lost, (n, 128)))[0:8, :]
    pull = jnp.where(ok, (2.0 * COMMIT / dim) * diff, 0.0)
    denc[...] = pull
    cots = jnp.concatenate([cot[s[CHIP]], cot_got[...], cot[2]], axis=0).astype(F32)
    dmix = (cots - pull).astype(BF)
    inner = jnp.zeros_like(peak)
    for t in range(steps):
        cols = pl.ds(t * tile, tile)
        d = mm_nt(dmix, book[cols, :])
        dweight[:, cols] = d
        inner = inner + jnp.sum(score[:, cols] * d, axis=1, keepdims=True)
    inner = inner * inv
    inv = inv * scale
    for t in range(steps):
        cols = pl.ds(t * tile, tile)
        dcode = (score[:, cols] * inv * (dweight[:, cols] - inner)).astype(BF)
        denc[...] += mm(dcode, book[cols, :])
    dmlp[...] = denc[...].astype(BF)


def quantizer(s, enc, cot, cot_got, pieces, moves, tile=512):
    n, dim = enc.shape
    block = n // 3
    vocab = sum(m[3] for m in moves if m[4] == 0)
    vm, hbm = pl.BlockSpec(memory_space=pltpu.VMEM), pl.BlockSpec(memory_space=pl.ANY)
    return call(
        functools.partial(quant_kernel, moves=moves, tile=tile, scale=dim**-0.5), "quantizer", (),
        [vm, vm, vm] + [hbm] * len(pieces),
        [vm] * 6,
        [shaped((block, dim))] * 3 + [shaped((8, n), F32), shaped((n, dim), F32), shaped((n, dim))],
        [
            pltpu.VMEM((vocab, dim), BF),
            pltpu.VMEM((n, vocab), F32),
            pltpu.VMEM((n, vocab), F32),
            pltpu.VMEM((n, dim), F32),
            pltpu.SemaphoreType.DMA((len(moves),)),
        ],
        cost(8 * n * dim * vocab, 2 * vocab * dim + 14 * n * dim),
        s, enc, cot, cot_got, *pieces,
    )


def quantizer_plain(s, enc, cots, book):
    n, dim = enc.shape
    block = n // 3
    index = jnp.arange(n)
    ok = spots(index % (2 * block), block, s[ME]) < jnp.where(index < 2 * block, s[LIMIT_MAIN], s[LIMIT_LAST])
    scale = dim**-0.5
    scores = mm_nt(enc.astype(BF), book) * scale
    peak = jnp.max(scores, axis=-1, keepdims=True)
    log_total = peak + jnp.log(jnp.sum(jnp.exp(scores - peak), axis=-1, keepdims=True))
    weights = jnp.exp(scores - log_total)
    mix = mm(weights.astype(BF), book)
    diff = enc - mix
    loss = jnp.where(ok, jnp.mean(diff * diff, axis=-1), 0.0)
    pull = jnp.where(ok[:, None], 2.0 * COMMIT / dim * diff, 0.0)
    dmix = (cots.astype(F32) - pull).astype(BF)
    dweights = mm_nt(dmix, book)
    inner = jnp.sum(weights * dweights, axis=-1, keepdims=True)
    dcode = (weights * (dweights - inner) * scale).astype(BF)
    denc = mm(dcode, book) + pull
    low = mix.astype(BF)
    return (
        low[:block], low[block : 2 * block], low[2 * block :],
        jnp.broadcast_to(loss[None, :], (8, n)), denc, denc.astype(BF),
    )


def mlp_bwd_kernel(
    s, dmlp, denc, mid, gain, slope, wdown, wup, wout, dpre_ref, dmid_ref, dbranch_ref, datt_ref, rows_ref, bup_ref, acc
):
    step = pl.program_id(0)
    dpre = (mm_nt(dmlp[...], wdown[...]) * slope[...].astype(F32)).astype(BF)
    dpre_ref[...] = dpre
    bup_ref[...] = jnp.sum(dpre.astype(F32), axis=0, keepdims=True)
    part = mm_nt(dpre, wup[...])

    @pl.when(step == 0)
    def _():
        acc[...] = part

    @pl.when(step > 0)
    def _():
        acc[...] += part

    @pl.when(step == pl.num_programs(0) - 1)
    def _():
        dy = acc[...]
        xhat, inv = norm_stats(mid[...])
        dmid = denc[...] + norm_back(xhat, inv, gain[...], dy)
        dmid_ref[...] = dmid
        low = dmid.astype(BF)
        dbranch_ref[...] = low
        datt_ref[...] = mm_nt(low, wout[...]).astype(BF)
        rows_ref[0:1, :] = jnp.sum(dy * xhat, axis=0, keepdims=True)
        rows_ref[1:2, :] = jnp.sum(dy, axis=0, keepdims=True)
        rows_ref[2:3, :] = jnp.sum(low.astype(F32), axis=0, keepdims=True)
        rows_ref[3:4, :] = jnp.sum(dmlp[...].astype(F32), axis=0, keepdims=True)


def mlp_bwd(s, dmlp, denc, mid, gain, slope, wdown, wup, wout, tile):
    n, dim = denc.shape
    hidden = wup.shape[1]
    full, vec = whole((n, dim)), whole((1, dim))
    col = pl.BlockSpec((n, tile), lambda p, s: (0, p))
    return call(
        mlp_bwd_kernel, "mlp_bwd", (hidden // tile,),
        [
            full, full, full, vec, col,
            pl.BlockSpec((tile, dim), lambda p, s: (p, 0)),
            pl.BlockSpec((dim, tile), lambda p, s: (0, p)),
            whole((dim, dim)),
        ],
        [col, full, full, full, whole((4, dim)), pl.BlockSpec((1, tile), lambda p, s: (0, p))],
        [
            shaped((n, hidden)), shaped((n, dim), F32), shaped((n, dim)), shaped((n, dim)),
            shaped((4, dim), F32), shaped((1, hidden), F32),
        ],
        [pltpu.VMEM((n, dim), F32)],
        cost(2 * n * dim * (dim + 2 * hidden), 2 * dim * (dim + 2 * hidden) + 4 * n * hidden + 18 * n * dim),
        s, dmlp, denc, mid, gain, slope, wdown, wup, wout,
    )


def place(keep, send, index, bit, mine, rows, value):
    slot = (index // (2 * bit)) * bit + index % bit
    here = (index // bit) % 2

    @pl.when(mine == here)
    def _():
        keep[slot, rows, :] = value

    @pl.when(mine != here)
    def _():
        send[slot, rows, :] = value


def grad_down_kernel(s, dm0, dm1, act0, act1, keep, send, *, shards, bit):
    rows = dm0.shape[1] // shards
    full = (mm_tn(dm0[...], act0[...]) + mm_tn(dm1[...], act1[...])).astype(BF)
    mine = (s[IMG] // bit) % 2
    for j in range(shards):
        place(keep, send, j, bit, mine, slice(None), full[j * rows : (j + 1) * rows])


def grad_down(s, dm0, dm1, act0, act1, shards, bit, tile=768):
    n, dim = dm0.shape
    width = act0.shape[1] - dim
    rows = dim // shards
    col = pl.BlockSpec((n, tile), lambda p, s: (0, p))
    out = pl.BlockSpec((shards // 2, rows, tile), lambda p, s: (0, 0, p))
    part = shaped((shards // 2, rows, width))
    return call(
        functools.partial(grad_down_kernel, shards=shards, bit=bit), "grad_down", (width // tile,),
        [whole((n, dim)), whole((n, dim)), col, col], [out, out], [part, part], [],
        cost(4 * n * dim * width, 4 * n * (dim + width) + 2 * dim * width),
        s, dm0, dm1, act0, act1,
    )


def grad_up_kernel(s, h0, h1, dp0, dp1, a0, a1, db0, db1, keep, send, *, shards, bit, per):
    step = pl.program_id(0)
    half = h0.shape[1]
    cols = dp0.shape[1] // per
    mine = (s[IMG] // bit) % 2
    full = (mm_tn(h0[...], dp0[...]) + mm_tn(h1[...], dp1[...])).astype(BF)
    for k in range(shards // per):

        @pl.when(step == k)
        def _():
            for j in range(per):
                place(keep, send, k * per + j, bit, mine, slice(0, half), full[:, j * cols : (j + 1) * cols])

    @pl.when(step == 0)
    def _():
        rows = db0.shape[1] // shards
        out = (mm_tn(db0[...], a0[...]) + mm_tn(db1[...], a1[...])).astype(BF)
        for j in range(shards):
            place(keep, send, j, bit, mine, slice(half, half + rows), out[j * rows : (j + 1) * rows])


def grad_up(s, mine, got, dp0, dp1, db0, db1, shards, bit, per=2):
    n, dim = db0.shape
    hidden = dp0.shape[1]
    half = dim // 2
    first = hidden // 2 // half
    cols = hidden // shards * per
    col = pl.BlockSpec((n, cols), lambda p, s: (0, p))
    h = pl.BlockSpec((n, half), lambda p, s: (0, first))
    att = pl.BlockSpec((n, half), lambda p, s: (0, first + 1))
    shape = (shards // 2, half + dim // shards, half)
    return call(
        functools.partial(grad_up_kernel, shards=shards, bit=bit, per=per), "grad_up", (shards // per,),
        [h, h, col, col, att, att, whole((n, dim)), whole((n, dim))],
        [whole(shape), whole(shape)], [shaped(shape), shaped(shape)], [],
        cost(4 * n * half * (hidden + dim), 4 * n * (hidden + dim) + 2 * half * (hidden + dim)),
        s, mine, got, dp0, dp1, mine, got, db0, db1,
    )


def grad_qkv_kernel(s, own, got, last_own, last_got, h_own, h_got, hl_own, hl_got, keep, send, *, shards):
    step = pl.program_id(0)
    n = h_own.shape[0]
    dim = own.shape[1]
    m = 2 * n

    def finish(d_own, d_got):
        full = mm_tn(d_own, h_own[...]) + mm_tn(d_got, h_got[...])
        full = full + mm_tn(last_own[...], hl_own[...]) + mm_tn(last_got[...], hl_got[...])
        return full.astype(BF)

    def emit(first, full):
        size = 3 * dim // shards // 2
        for k in range(first // size, (first + dim + size - 1) // size):
            lo, hi = max(first, k * size), min(first + dim, (k + 1) * size)
            rows, value = slice(lo - k * size, hi - k * size), full[lo - first : hi - first]

            @pl.when(s[CHIP] == k % 2)
            def _():
                keep[k // 2, rows, :] = value

            @pl.when(s[CHIP] != k % 2)
            def _():
                send[k // 2, rows, :] = value

    @pl.when(step == 0)
    def _():
        emit(0, finish(own[2 * m :, :], got[2 * m :, :]))

    for k in (1, 2):

        @pl.when(step == k)
        def _():
            base = (k - 1) * m
            d_own = own[base : base + n, :].astype(F32) + got[base + n : base + m, :].astype(F32)
            d_got = own[base + n : base + m, :].astype(F32) + got[base : base + n, :].astype(F32)
            emit(k * dim, finish(d_own.astype(BF), d_got.astype(BF)))


def grad_qkv(s, own, got, last_own, last_got, h_own, h_got, hl_own, hl_got, shards):
    dim, half = own.shape[1], h_own.shape[1]
    last = pl.BlockSpec((last_own.shape[0], dim), lambda p, s: (0, p))
    shape = (shards, 3 * dim // shards // 2, half)
    n = h_own.shape[0] + hl_own.shape[0]
    return call(
        functools.partial(grad_qkv_kernel, shards=shards), "grad_qkv", (3,),
        [whole(own.shape), whole(got.shape), last, last] + [whole(h.shape) for h in (h_own, h_got, hl_own, hl_got)],
        [whole(shape), whole(shape)], [shaped(shape), shaped(shape)], [],
        cost(12 * n * dim * half, 20 * n * dim),
        s, own, got, last_own, last_got, h_own, h_got, hl_own, hl_got,
    )


def qkv_bwd_kernel(s, own, got, last, w, x_own, x_got, x_last, gain, dmid, dx0, dx1, dx2, rows, sums, acc):
    step = pl.program_id(0)
    block, dim = x_got.shape
    n = 2 * block
    m = 2 * n

    def add(k, d_main):
        d = jnp.concatenate([d_main, last[...]], axis=0)
        sums[k : k + 1, :] = jnp.sum(d.astype(F32), axis=0, keepdims=True)
        part = mm_nt(d, w[...])
        if k == 0:
            acc[...] = part
        else:
            acc[...] += part

    @pl.when(step == 0)
    def _():
        add(0, own[2 * m :, :])

    for k in (1, 2):

        @pl.when(step == k)
        def _():
            base = (k - 1) * m
            add(k, (own[base : base + n, :].astype(F32) + got[base + n : base + m, :].astype(F32)).astype(BF))

    @pl.when(step == 2)
    def _():
        dy = acc[...]
        x = jnp.concatenate([x_own[0], x_got[...], x_last[0]], axis=0).astype(F32)
        xhat, inv = norm_stats(x)
        dx = dmid[...] + norm_back(xhat, inv, gain[...], dy)
        dx0[...] = dx[:block]
        dx1[...] = dx[block:n].astype(BF)
        dx2[...] = dx[n:]
        rows[0:1, :] = jnp.sum(dy * xhat, axis=0, keepdims=True)
        rows[1:2, :] = jnp.sum(dy, axis=0, keepdims=True)


def qkv_bwd(s, own, got, last, w, patches, x_got, gain, dmid):
    images, block, dim = patches.shape
    n = images * block
    part = whole((block, dim))
    return call(
        qkv_bwd_kernel, "qkv_bwd", (3,),
        [
            whole(own.shape), whole(got.shape),
            pl.BlockSpec((block, dim), lambda p, s: (0, p)),
            pl.BlockSpec((dim, dim), lambda p, s: (0, p)),
            pl.BlockSpec((1, block, dim), lambda p, s: (s[CHIP], 0, 0)),
            part,
            pl.BlockSpec((1, block, dim), lambda p, s: (2, 0, 0)),
            whole((1, dim)), whole((n, dim)),
        ],
        [part, part, part, whole((2, dim)), whole((3, dim))],
        [
            shaped((block, dim), F32), shaped((block, dim)), shaped((block, dim), F32),
            shaped((2, dim), F32), shaped((3, dim), F32),
        ],
        [pltpu.VMEM((n, dim), F32)],
        cost(6 * n * dim * dim, 6 * dim * dim + 26 * n * dim),
        s, own, got, last, w, patches, x_got, patches, gain, dmid,
    )


def gather_book(codebook):
    rows, dim = codebook.shape
    top, rest = img_bits()[-1], list(reversed(img_bits()[:-1]))
    pieces, moves, slots = [], [], None
    for k, order in enumerate(([top, *rest, "y"], [top, "y", *rest])):
        width = dim // 2
        value, masks = codebook[:, k * width : (k + 1) * width], [0]
        for step in order:
            got = swap(value, "seq", 2) if step == "y" else swap(value, "img", step)
            flip = lax.axis_size("img") if step == "y" else step
            more = [mask ^ flip for mask in masks]
            if step != order[-1]:
                value, masks = jnp.concatenate([value, got]), masks + more
        if slots is None:
            slots = {mask: at for at, mask in enumerate(masks + more)}
        half = len(slots) * rows
        for shift, arrays in ((0, (value, got)), (half, (swap(value, "seq", 1), swap(got, "seq", 1)))):
            for array, names in zip(arrays, (masks, more)):
                at = 0
                while at < len(names):
                    run = 1
                    while at + run < len(names) and slots[names[at + run]] == slots[names[at]] + run:
                        run += 1
                    moves.append(
                        (len(pieces), at * rows, shift + slots[names[at]] * rows, run * rows, k * width, width)
                    )
                    at += run
                pieces.append(array)
    moves.sort(key=lambda move: (move[2], move[4]))
    return pieces, tuple(moves)


def reduce_shards(parts, order):
    bits = img_bits()
    me, chip = lax.axis_index("img"), lax.axis_index("seq") // 2
    names = list(reversed(bits)) + ["y"]

    def add(kept, sent, step):
        got = swap(sent, "seq", 2) if step == "y" else swap(sent, "img", step)
        return (kept.astype(F32) + got.astype(F32)).astype(BF)

    if isinstance(parts, (tuple, list)):
        step, order = order[0], order[1:]
        names.remove(step)
        value = add(*parts, step)
    else:
        value = parts
    rows, cols = value.shape[-2:]
    shape = [2 for name in names if name != "y"]
    value = value.reshape(shape + ([2, rows // 2] if "y" in names else [rows]) + [cols])
    for step in order:
        axis = names.index(step)
        mine = chip if step == "y" else (me // step) % 2
        value = add(pick(value, mine, axis), pick(value, 1 - mine, axis), step)
        names.pop(axis)
    other = swap(value, "seq", 2)
    return jnp.concatenate([jnp.where(chip == 0, value, other), jnp.where(chip == 0, other, value)], axis=0)


def reduce_small(parts):
    me = lax.axis_index("img")
    value = parts + swap(parts, "seq", 1)
    value = value.reshape([2] * len(img_bits()) + [parts.shape[-1]])
    for step in reversed(img_bits()):
        mine = (me // step) % 2
        value = pick(value, mine, 0) + swap(pick(value, 1 - mine, 0), "img", step)
    return value + swap(value, "seq", 2)


def shards(
    patches,
    widths,
    ln1_gain,
    ln1_bias,
    w_qkv,
    b_query,
    b_value,
    w_out,
    b_out,
    ln2_gain,
    ln2_bias,
    w_up,
    b_up,
    w_down,
    b_down,
    codebook,
    cotangent,
):
    images, block, dim = patches.shape
    hidden = w_up.shape[1]
    n_img = lax.axis_size("img")
    me = lax.axis_index("seq")
    chip, core = me // 2, me % 2
    half, main = dim // 2, 2 * block
    fits = codebook.shape[0] * n_img * lax.axis_size("seq") <= 4096
    aligned = dim // n_img // 2 % 16 == 0 and 3 * dim // n_img // 2 % 16 == 0 and hidden // n_img % 128 == 0
    bits = img_bits()
    s = jnp.stack(
        [me, core, chip, GRID_H * pick(widths, chip, 0), GRID_H * widths[2], lax.axis_index("img")]
    ).astype(jnp.int32)

    def row(vector):
        return vector.reshape(1, -1)

    x_got = swap(pick(patches, 1 - chip, 0), "seq", 2)
    pieces, moves = gather_book(codebook)
    cot_got = swap(pick(cotangent, 1 - chip, 0), "seq", 2)
    bias_all = jnp.concatenate([b_query, jnp.zeros_like(b_query), b_value])
    own_spec = pl.BlockSpec((1, block, dim), lambda p, s: (s[CHIP], 0, 0))
    last_spec = pl.BlockSpec((1, block, dim), lambda p, s: (2, 0, 0))
    ln1 = (row(ln1_gain), row(ln1_bias), w_qkv, row(bias_all), block)
    q_last, kv_last, hl_mine, hl_send = qkv_fwd(s, [patches], [last_spec], *ln1)
    kv_y = swap(kv_last, "seq", 2)
    kv_c = swap(kv_last, "seq", 1)
    x_got = after(x_got, q_last)
    q_main, kv_main, h_mine, h_send = qkv_fwd(s, [patches, x_got], [own_spec, whole((block, dim))], *ln1)
    kv_other = swap(kv_main, "seq", 1)
    kvs_main = [kv_main, kv_other]
    att_main = attention_fwd(s, q_main, kvs_main, LIMIT_MAIN, block)
    kv_yc = swap(kv_y, "seq", 1)
    kvs_last = [kv_last, kv_y, kv_c, kv_yc]
    att_last = attention_fwd(s, after(q_last, att_main), kvs_last, LIMIT_LAST, block)
    mid, slope, enc, mine, send = mlp_fwd(
        s, patches, x_got, att_main, att_last, w_out, row(b_out), row(ln2_gain), row(ln2_bias), w_up, row(b_up),
        w_down, row(b_down), tile=768,
    )
    got = swap(send, "seq", 1)
    h_got, hl_got = swap(h_send, "seq", 1), swap(hl_send, "seq", 1)
    if fits:
        mix0, mix1, mix2, loss, denc, dmlp = quantizer(s, enc, cotangent, cot_got, pieces, moves)
    else:
        book = jnp.zeros((sum(m[3] for m in moves if m[4] == 0), dim), BF)
        for piece, at, target, rows, lane, width in moves:
            book = lax.dynamic_update_slice(book, pieces[piece][at : at + rows], (target, lane))
        cots = jnp.concatenate([pick(cotangent, chip, 0), cot_got, cotangent[2]])
        mix0, mix1, mix2, loss, denc, dmlp = quantizer_plain(s, enc, cots, book)

    near = bits[1:]
    order_down = [*near[:1], "y", bits[0], *near[1:]]
    order_up = [bits[0], "y", *near]
    order_qkv = ["y", *bits]
    dmlp_got = swap(dmlp, "seq", 1)
    if aligned:
        part_down = grad_down(s, dmlp, dmlp_got, mine, got, n_img, order_down[0])
    else:
        part_down = mm_tn(jnp.concatenate([dmlp, dmlp_got]), jnp.concatenate([mine, got])[:, : hidden // 2])
        part_down = part_down.astype(BF).reshape(n_img, dim // n_img, hidden // 2)
    sum_down = reduce_shards(part_down, order_down)
    dmlp = after(dmlp, part_down[0])
    dpre, dmid, dbranch, datt, rows_two, sum_bup = mlp_bwd(
        s, dmlp, denc, mid, row(ln2_gain), slope, w_down, w_up, w_out, tile=768
    )
    dpre_got, dbranch_got = swap(dpre, "seq", 1), swap(dbranch, "seq", 1)
    per_row = main // block
    d_last = attention_bwd(
        s, q_last, kvs_last, datt, pl.BlockSpec((block, 128), lambda p, s: (per_row, p)), LIMIT_LAST, block
    )
    dkv = d_last[: 4 * main].reshape(2, 2, main, dim)
    dkv = (dkv[:, 0].astype(F32) + swap(dkv[:, 1], "seq", 1).astype(F32)).astype(BF)
    dkv = dkv.reshape(2, 2, block, dim)
    dkv = (dkv[:, 0].astype(F32) + swap(dkv[:, 1], "seq", 2).astype(F32)).astype(BF)
    dqkv_last = jnp.concatenate([d_last[4 * main :], dkv[0], dkv[1]], axis=1)
    dqkv_last_got = swap(dqkv_last, "seq", 1)
    if aligned:
        part_up = grad_up(s, mine, got, after(dpre, d_last), dpre_got, dbranch, dbranch_got, n_img, order_up[0])
    else:
        both, a, b = jnp.concatenate([mine, got]), hidden // 2, hidden // 2 + half
        up = mm_tn(both[:, a:b], jnp.concatenate([dpre, dpre_got])).astype(BF)
        up = up.reshape(half, n_img, -1).transpose(1, 0, 2)
        out = mm_tn(jnp.concatenate([dbranch, dbranch_got]), both[:, b:]).astype(BF)
        part_up, sum_out = up, reduce_shards(out.reshape(n_img, -1, half), order_up)
    sum_up = reduce_shards(part_up, order_up)
    d_main = attention_bwd(
        s, after(q_main, part_up[0]), kvs_main, datt, pl.BlockSpec((main, 128), lambda p, s: (0, p)), LIMIT_MAIN, block
    )
    d_got = swap(d_main, "seq", 1)
    if aligned:
        sum_up, sum_out = sum_up[:half], sum_up[half:]
        part_qkv = grad_qkv(s, d_main, d_got, dqkv_last, dqkv_last_got, h_mine, h_got, hl_mine, hl_got, n_img)
    else:
        both = d_main[: 4 * main].reshape(2, 2, main, dim).astype(F32)
        both = both + d_got[: 4 * main].reshape(2, 2, main, dim)[:, ::-1].astype(F32)
        own = jnp.concatenate([d_main[4 * main :], both[0, 0].astype(BF), both[1, 0].astype(BF)], axis=1)
        other = jnp.concatenate([d_got[4 * main :], both[0, 1].astype(BF), both[1, 1].astype(BF)], axis=1)
        part_qkv = mm_tn(
            jnp.concatenate([own, other, dqkv_last, dqkv_last_got]), jnp.concatenate([h_mine, h_got, hl_mine, hl_got])
        )
        part_qkv = part_qkv.astype(BF).reshape(n_img, -1, half)
    sum_qkv = reduce_shards(part_qkv, order_qkv)
    dx0, dx1, dx2, rows_one, sums = qkv_bwd(
        s, d_main, after(d_got, part_qkv[0]), dqkv_last, w_qkv, patches, x_got, row(ln1_gain), dmid
    )

    vectors = [
        rows_one[0], rows_one[1], sums[0], sums[2], rows_two[2], rows_two[0], rows_two[1], sum_bup[0], rows_two[3],
    ]
    small = reduce_small(jnp.concatenate([v.reshape(n_img, -1) for v in vectors], axis=1))
    sizes = [v.shape[0] // n_img for v in vectors]
    cuts = [sum(sizes[:k]) for k in range(len(sizes) + 1)]
    small = [small[cuts[k] : cuts[k + 1]] for k in range(len(sizes))]

    def cores(value, axis):
        other = swap(value, "seq", 1)
        return jnp.concatenate(
            [jnp.where(core == 0, value, other), jnp.where(core == 0, other, value)], axis=axis
        ).astype(F32)

    def images_of(own, back, last):
        back = swap(back, "seq", 2).astype(own.dtype)
        return jnp.stack([jnp.where(chip == 0, own, back), jnp.where(chip == 0, back, own), last])

    return (
        images_of(mix0, mix1, mix2),
        images_of(loss[0, :block], loss[0, block:main], loss[0, main:]),
        images_of(dx0, dx1, dx2),
        small[0],
        small[1],
        cores(sum_qkv, 1).T,
        small[2],
        small[3],
        cores(sum_out, 1).T,
        small[4],
        small[5],
        small[6],
        cores(sum_up, 0),
        small[7],
        cores(sum_down, 1).T,
        small[8],
    )


def solution(mesh):
    return jax.shard_map(
        shards,
        mesh=mesh,
        in_specs=(
            P("img", "seq", None),
            P("img"),
            P(),
            P(),
            P(),
            P(),
            P(),
            P(),
            P(),
            P(),
            P(),
            P(),
            P(),
            P(),
            P(),
            P(("seq", "img"), None),
            P("img", "seq", None),
        ),
        out_specs=(
            P("img", "seq", None),
            P("img", "seq"),
            P("img", "seq", None),
            P("img"),
            P("img"),
            P(None, "img"),
            P("img"),
            P("img"),
            P(None, "img"),
            P("img"),
            P("img"),
            P("img"),
            P(None, "img"),
            P("img"),
            P(None, "img"),
            P("img"),
        ),
        check_vma=False,
    )
```

```python
import functools

import jax
import jax.numpy as jnp
from jax import lax
from jax.experimental import pallas as pl
from jax.experimental.pallas import tpu as pltpu
from jax.sharding import PartitionSpec as P

HEAD_DIM = 64
GRID_H = 16
EPS_NORM = 1e-06
COMMIT = 16.0
BF = jnp.bfloat16
F32 = jnp.float32
MIB = 1024 * 1024
MASKED = -1000000000.0


def mm(a, b):
    return jnp.dot(a, b, preferred_element_type=F32)


def mm_nt(a, b):
    return lax.dot_general(a, b, (((1,), (1,)), ((), ())), preferred_element_type=F32)


def mm_tn(a, b):
    return lax.dot_general(a, b, (((0,), (0,)), ((), ())), preferred_element_type=F32)


def swap(value, axis, bit):
    count = lax.axis_size(axis)
    return lax.ppermute(value, axis, [(i, i ^ bit) for i in range(count)])


def pick(value, index, axis):
    return lax.dynamic_index_in_dim(value, index, axis, keepdims=False)


def after(value, *others):
    return lax.optimization_barrier((value, *others))[0]


def parity(number):
    return bin(number).count("1") % 2


def shaped(shape, dtype=BF):
    return jax.ShapeDtypeStruct(tuple(shape), dtype)


def in_hbm(shape, dtype=BF):
    return pltpu.HBM(tuple(shape), dtype)


def call(kernel, name, mib, out_shape, scratch, s, *args, micros, streamed=0):
    vm, hbm = pl.BlockSpec(memory_space=pltpu.VMEM), pl.BlockSpec(memory_space=pltpu.HBM)
    direct = len(args) - streamed
    args = [
        pltpu.with_memory_space_constraint(arg, pltpu.HBM) if arg.ndim == 1 or k >= direct else arg
        for k, arg in enumerate(args)
    ]
    return pl.pallas_call(
        kernel,
        in_specs=[pl.BlockSpec(memory_space=pltpu.SMEM)] * 2 + [vm] * direct + [hbm] * streamed,
        out_specs=[vm] * len(out_shape),
        out_shape=out_shape,
        scratch_shapes=scratch,
        compiler_params=pltpu.CompilerParams(vmem_limit_bytes=mib * MIB),
        cost_estimate=pl.CostEstimate(flops=int(micros * 7e8), bytes_accessed=0, transcendentals=0),
        name=name,
    )(*s, *args)


class Stream:
    def __init__(self, sems, *pairs, ahead=3):
        self.copies = [pltpu.make_async_copy(a, b, sems.at[k]) for k, (a, b) in enumerate(pairs)]
        self.done, self.begun = 0, 0
        self.start(ahead)

    def start(self, count):
        while self.begun < min(count, len(self.copies)):
            self.copies[self.begun].start()
            self.begun += 1

    def wait(self, count):
        while self.done < count:
            self.copies[self.done].wait()
            self.done += 1
            self.start(self.begun + 1)


ME, CORE, CHIP, SIDES = range(4)


def line(ref, start=0, size=None):
    size = ref.shape[0] if size is None else size
    return ref[start : start + size].reshape(1, size)


def norm_stats(x):
    center = x - jnp.mean(x, axis=-1, keepdims=True)
    spread = jnp.mean(center * center, axis=-1, keepdims=True)
    inv = lax.rsqrt(spread + EPS_NORM)
    return center * inv, inv


def norm_back(xhat, inv, gain, dy):
    dxhat = dy * gain
    return inv * (
        dxhat - jnp.mean(dxhat, axis=-1, keepdims=True) - xhat * jnp.mean(dxhat * xhat, axis=-1, keepdims=True)
    )


def spots(index, block, me):
    place = index // block
    mask = (place % 2) * 2 + place // 2
    return (me ^ mask) * block + index % block


def limit_of(s, widths, last):
    return GRID_H * widths[2 if last else s[CHIP]]


def side_of(ref, side, width):
    return ref[:, pl.ds(pl.multiple_of(side * width, 128), width)]


def qkv_kernel(s, widths, *refs, last):
    refs = (None, *refs) if last else refs
    got, gain, shift, bq, bv, patches, w_hbm, q, kv, mine, send, h, x_own, w, sems = refs
    half, dim = mine.shape[1], w.shape[0]
    block = patches.shape[1]
    spans = [slice(k * dim, (k + 1) * dim) for k in (1, 2, 0)]
    pairs = [(patches.at[2 if last else s[CHIP]], x_own)] + [(w_hbm.at[:, span], w.at[:, span]) for span in spans]
    stream = Stream(sems, *pairs)
    stream.wait(1)
    parts = [x_own[...]] if last else [x_own[...], got[...]]
    for k, x in enumerate(parts):
        xhat, _ = norm_stats(x.astype(F32))
        h[k * block : (k + 1) * block, :] = (xhat * line(gain) + line(shift)).astype(BF)
    mine[...] = side_of(h, s[CORE], half)
    send[...] = side_of(h, 1 - s[CORE], half)
    stream.wait(2)
    kv[:, :dim] = mm(h[...], w[:, dim : 2 * dim]).astype(BF)
    stream.wait(3)
    kv[:, dim:] = (mm(h[...], w[:, 2 * dim :]) + line(bv)).astype(BF)
    stream.wait(4)
    q[...] = (mm(h[...], w[:, :dim]) + line(bq)).astype(BF)


def qkv_fwd(s, patches, got, gain, shift, bq, bv, w):
    dim, block = w.shape[0], patches.shape[1]
    last = got is None
    n, half = block * (1 if last else 2), dim // 2
    args = [] if last else [got]
    return call(
        functools.partial(qkv_kernel, last=last), "qkv_fwd", 9,
        [shaped((n, dim)), shaped((n, 2 * dim)), in_hbm((n, half)), shaped((n, half))],
        [pltpu.VMEM((n, dim), BF), pltpu.VMEM((block, dim), BF), pltpu.VMEM(w.shape, BF), pltpu.SemaphoreType.DMA((4,))],
        s, *args, gain, shift, bq, bv, patches, w, micros=2, streamed=2,
    )


def two_heads(value):
    left = lax.broadcasted_iota(jnp.int32, value.shape, 1) < HEAD_DIM
    zero = jnp.zeros_like(value)
    return jnp.concatenate([jnp.where(left, value, zero), jnp.where(left, zero, value)], axis=0)


def one_pair(value):
    n = value.shape[0] // 2
    left = lax.broadcasted_iota(jnp.int32, (n, value.shape[1]), 1) < HEAD_DIM
    return jnp.where(left, value[:n], value[n:])


def att_fwd_kernel(s, widths, q, *refs, last, block):
    kvs, o = refs[:-1], refs[-1]
    dim = q.shape[1]
    m = sum(kv.shape[0] for kv in kvs)
    index = lax.broadcasted_iota(jnp.int32, (1, m), 1)
    ok = spots(index, block, s[ME]) < limit_of(s, widths, last)
    for p in range(dim // 128):
        at, av = slice(p * 128, (p + 1) * 128), slice(dim + p * 128, dim + (p + 1) * 128)
        k = jnp.concatenate([kv[:, at] for kv in kvs], axis=0)
        v = jnp.concatenate([kv[:, av] for kv in kvs], axis=0)
        raw = mm_nt(two_heads(q[:, at]), k) * (HEAD_DIM**-0.5)
        scores = jnp.where(ok, raw, MASKED)
        expo = jnp.exp(scores - jnp.max(scores, axis=1, keepdims=True))
        probs = expo * (1.0 / jnp.sum(expo, axis=1, keepdims=True))
        o[:, at] = one_pair(mm(probs.astype(BF), v)).astype(BF)


def attention_fwd(s, q, kvs, last, block):
    return call(
        functools.partial(att_fwd_kernel, last=last, block=block), "attention_fwd", 10, [shaped(q.shape)], [],
        s, q, *kvs, micros=5,
    )[0]


def att_bwd_kernel(s, widths, q, do, *refs, last, block, first, pairs):
    n, dim = q.shape
    if pairs:
        kvs, out = refs[:-1], refs[-1]
        m = sum(kv.shape[0] for kv in kvs)
        parts = [out.at[k * m // 2 : (k + 1) * m // 2, :] for k in range(4)]
        dq = out.at[2 * m :, :]
    else:
        kvs, (keep, send, dq) = refs[:-3], refs[-3:]
        m = sum(kv.shape[0] for kv in kvs)
        parts = [keep.at[0], keep.at[1], send.at[0], send.at[1]]
    index = lax.broadcasted_iota(jnp.int32, (m, 1), 0)
    ok = spots(index, block, s[ME]) < limit_of(s, widths, last)
    for p in pairs or range(dim // 128):
        at, av = slice(p * 128, (p + 1) * 128), slice(dim + p * 128, dim + (p + 1) * 128)
        to = slice((p - pairs[0]) * 128, (p - pairs[0] + 1) * 128) if pairs else at
        k = jnp.concatenate([kv[:, at] for kv in kvs], axis=0)
        v = jnp.concatenate([kv[:, av] for kv in kvs], axis=0)
        q2, do2 = two_heads(q[:, at]), two_heads(do[first : first + n, at])
        raw = mm_nt(k, q2) * (HEAD_DIM**-0.5)
        scores = jnp.where(ok, raw, MASKED)
        expo = jnp.exp(scores - jnp.max(scores, axis=0, keepdims=True))
        probs = expo * (1.0 / jnp.sum(expo, axis=0, keepdims=True))
        dv = mm(probs.astype(BF), do2).astype(BF)
        dp = mm_nt(v, do2)
        inner = jnp.sum(probs * dp, axis=0, keepdims=True)
        ds = (probs * (dp - inner) * (HEAD_DIM**-0.5)).astype(BF)
        dk = mm(ds, q2).astype(BF)
        dq[:, to] = one_pair(mm_tn(ds, k)).astype(BF)
        for ref, part in zip(parts, (dk[: m // 2], dv[: m // 2], dk[m // 2 :], dv[m // 2 :])):
            ref[:, to] = part


def attention_bwd(s, q, kvs, do, first, last, block, pairs):
    n, dim = q.shape
    m = sum(kv.shape[0] for kv in kvs)
    return call(
        functools.partial(att_bwd_kernel, last=last, block=block, first=first, pairs=pairs), "attention_bwd", 12,
        [shaped((2 * m + n, 128 * len(pairs)))] if pairs else [shaped((2, m // 2, dim)), shaped((2, m // 2, dim)), shaped((n, dim))],
        [], s, q, do, *kvs, micros=3 if pairs else 4.5,
    )


def fold_kernel(s, widths, keep, got, keep_out, send_out):
    block = keep_out.shape[1]
    for k in range(2):
        total = (keep[k].astype(F32) + got[k].astype(F32)).astype(BF)
        keep_out[k] = total[:block]
        send_out[k] = total[block:]


def fold(s, keep, got):
    part = shaped((2, keep.shape[1] // 2, keep.shape[2]))
    return call(fold_kernel, "fold", 4, [part, part], [], s, keep, got, micros=0.5)


def join_kernel(s, widths, dq, keep, got, out):
    dim = dq.shape[1]
    out[:, :dim] = dq[...]
    for k in range(2):
        out[:, (k + 1) * dim : (k + 2) * dim] = (keep[k].astype(F32) + got[k].astype(F32)).astype(BF)


def join(s, dq, keep, got):
    return call(join_kernel, "join", 4, [shaped((dq.shape[0], 3 * dq.shape[1]))], [], s, dq, keep, got, micros=0.5)[0]


def halve_kernel(s, widths, keep, got, keep_out, send_out, *, at):
    mine = s[SIDES + at]
    keep_out[...] = (keep[mine].astype(F32) + got[mine].astype(F32)).astype(BF)
    send_out[...] = (keep[1 - mine].astype(F32) + got[1 - mine].astype(F32)).astype(BF)


def halve(s, keep, got, at):
    part = shaped(keep.shape[1:])
    return call(functools.partial(halve_kernel, at=at), "halve", 8, [part, part], [], s, keep, got, micros=0.7)


def gelu_pair(x):
    z = jnp.abs(x) * (0.5**0.5)
    t = 1.0 / (1.0 + 0.3275911 * z)
    expo = jnp.exp(-0.5 * x * x)
    poly = t * (0.254829592 + t * (-0.284496736 + t * (1.421413741 + t * (-1.453152027 + t * 1.061405429))))
    tail = 0.5 * poly * expo
    cdf = jnp.where(x < 0.0, tail, 1.0 - tail)
    return x * cdf, cdf + x * (expo * 0.3989422804014327)


def mlp_fwd_kernel(
    s, widths, got, att_main, att_last, h_main, h_last, bout, gain, shift, bup, bdown, patches, wout_hbm, wup_hbm,
    wdown_hbm, mid, slope, enc, mine, send, h2, x_own, wout, wup, wdown, sems, *, tile,
):
    block, dim = got.shape
    half = dim // 2
    hidden = wup.shape[1]
    wide = hidden // 2
    spans = [slice(t * tile, (t + 1) * tile) for t in range(hidden // tile)]
    pairs = [(wout_hbm, wout), (patches.at[s[CHIP]], x_own.at[0]), (patches.at[2], x_own.at[1])]
    for span in spans:
        pairs += [(wup_hbm.at[:, span], wup.at[:, span]), (wdown_hbm.at[span, :], wdown.at[span, :])]
    stream = Stream(sems, *pairs)
    stream.wait(3)
    x = jnp.concatenate([x_own[0], got[...], x_own[1]], axis=0).astype(F32)
    att = jnp.concatenate([att_main[...], att_last[...]], axis=0)
    middle = x + mm(att, wout[...]) + line(bout)
    mid[...] = middle
    xhat, _ = norm_stats(middle)
    h2[...] = (xhat * line(gain) + line(shift)).astype(BF)
    enc[...] = middle + line(bdown)
    rows = att_main.shape[0]
    for out, side in ((mine, s[CORE]), (send, 1 - s[CORE])):
        out[:, wide : wide + half] = side_of(h2, side, half)
        out[:rows, wide + half : wide + dim] = side_of(att_main, side, half)
        out[rows:, wide + half : wide + dim] = side_of(att_last, side, half)
    send[:rows, wide + dim :] = h_main[...]
    send[rows:, wide + dim :] = h_last[...]
    for t, cols in enumerate(spans):
        stream.wait(2 * t + 4)
        pre = mm(h2[...], wup[:, cols]) + line(bup, t * tile, tile)
        act, rate = gelu_pair(pre)
        act = act.astype(BF)
        slope[:, cols] = rate.astype(BF)
        stream.wait(2 * t + 5)
        enc[...] += mm(act, wdown[cols, :])
        side, local = t * tile // wide, slice(t * tile % wide, t * tile % wide + tile)

        @pl.when(s[CORE] == side)
        def _():
            mine[:, local] = act

        @pl.when(s[CORE] != side)
        def _():
            send[:, local] = act


def mlp_fwd(s, patches, got, att_main, att_last, h_main, h_last, bout, gain, shift, bup, bdown, wout, wup, wdown):
    images, block, dim = patches.shape
    n, hidden = images * block, wup.shape[1]
    wide, tile = dim + hidden // 2, 512
    return call(
        functools.partial(mlp_fwd_kernel, tile=tile), "mlp_fwd", 18,
        [
            shaped((n, dim), F32), shaped((n, hidden)), shaped((n, dim), F32), shaped((n, wide)),
            shaped((n, wide + dim // 2)),
        ],
        [
            pltpu.VMEM((n, dim), BF), pltpu.VMEM((2, block, dim), BF), pltpu.VMEM(wout.shape, BF),
            pltpu.VMEM(wup.shape, BF), pltpu.VMEM(wdown.shape, BF), pltpu.SemaphoreType.DMA((3 + 2 * (hidden // tile),)),
        ],
        s, got, att_main, att_last, h_main, h_last, bout, gain, shift, bup, bdown, patches, wout, wup, wdown,
        micros=10, streamed=4,
    )


def quant_kernel(s, widths, enc, cot_got, *refs, tile, scale):
    pieces, cot = refs[:-12], refs[-12]
    mix_own, mix_back, mix_last, loss, denc, dmlp, score, dweight, late, cot_own, sems = refs[-11:]
    n, dim = enc.shape
    block = n // 3
    chunks, place = [], 0
    for piece in pieces:
        for first in range(0, piece.shape[0], tile):
            size = min(tile, piece.shape[0] - first)
            chunks.append((piece, slice(first, first + size), slice(place, place + size)))
            place += size + -size % 128
    stream = Stream(sems, (cot.at[s[CHIP]], cot_own.at[0]), (cot.at[2], cot_own.at[1]))
    low = enc[...].astype(BF)
    peak = None
    for piece, rows, cols in chunks:
        part = mm_nt(low, piece[rows, :]) * scale
        score[:, cols] = part
        top = jnp.max(part, axis=1, keepdims=True)
        peak = top if peak is None else jnp.maximum(peak, top)
    total = jnp.zeros_like(peak)
    late[...] = jnp.zeros_like(late)
    for piece, rows, cols in chunks:
        e = jnp.exp(score[:, cols] - peak)
        score[:, cols] = e
        total = total + jnp.sum(e, axis=1, keepdims=True)
        late[...] += mm(e.astype(BF), piece[rows, :])
    inv = 1.0 / total
    mix = late[...] * inv
    low = mix.astype(BF)
    mix_own[...] = low[:block]
    mix_back[...] = low[block : 2 * block]
    mix_last[...] = low[2 * block :]
    index = lax.broadcasted_iota(jnp.int32, (n, 1), 0)
    spot = spots(index % (2 * block), block, s[ME])
    ok = spot < jnp.where(index < 2 * block, limit_of(s, widths, False), limit_of(s, widths, True))
    diff = enc[...] - mix
    lost = jnp.where(ok, jnp.mean(diff * diff, axis=1, keepdims=True), 0.0)
    loss[...] = jnp.transpose(jnp.broadcast_to(lost, (n, 128)))[0:8, :]
    pull = jnp.where(ok, (2.0 * COMMIT / dim) * diff, 0.0)
    denc[...] = pull
    stream.wait(2)
    cots = jnp.concatenate([cot_own[0], cot_got[...], cot_own[1]], axis=0).astype(F32)
    dmix = (cots - pull).astype(BF)
    inner = jnp.zeros_like(peak)
    for piece, rows, cols in chunks:
        d = mm_nt(dmix, piece[rows, :])
        dweight[:, cols] = d
        inner = inner + jnp.sum(score[:, cols] * d, axis=1, keepdims=True)
    inner = inner * inv
    inv = inv * scale
    for piece, rows, cols in chunks:
        dcode = (score[:, cols] * inv * (dweight[:, cols] - inner)).astype(BF)
        denc[...] += mm(dcode, piece[rows, :])
    dmlp[...] = denc[...].astype(BF)


def quantizer(s, enc, cot, cot_got, pieces, tile=512):
    n, dim = enc.shape
    block = n // 3
    count = sum(-(-piece.shape[0] // tile) for piece in pieces)
    wide = count * tile
    return call(
        functools.partial(quant_kernel, tile=tile, scale=dim**-0.5), "quantizer", 21,
        [in_hbm((block, dim))] * 3 + [in_hbm((8, n), F32), shaped((n, dim), F32), shaped((n, dim))],
        [
            pltpu.VMEM((n, wide), F32), pltpu.VMEM((n, wide), F32), pltpu.VMEM((n, dim), F32),
            pltpu.VMEM((2, block, dim), BF), pltpu.SemaphoreType.DMA((2,)),
        ],
        s, enc, cot_got, *pieces, cot, micros=14, streamed=1,
    )


def quantizer_plain(s, enc, cots, book):
    n, dim = enc.shape
    block = n // 3
    index = jnp.arange(n)
    s, widths = s
    ok = spots(index % (2 * block), block, s[ME])
    ok = ok < jnp.where(index < 2 * block, limit_of(s, widths, False), limit_of(s, widths, True))
    scale = dim**-0.5
    scores = mm_nt(enc.astype(BF), book) * scale
    peak = jnp.max(scores, axis=-1, keepdims=True)
    log_total = peak + jnp.log(jnp.sum(jnp.exp(scores - peak), axis=-1, keepdims=True))
    weights = jnp.exp(scores - log_total)
    mix = mm(weights.astype(BF), book)
    diff = enc - mix
    loss = jnp.where(ok, jnp.mean(diff * diff, axis=-1), 0.0)
    pull = jnp.where(ok[:, None], 2.0 * COMMIT / dim * diff, 0.0)
    dmix = (cots.astype(F32) - pull).astype(BF)
    dweights = mm_nt(dmix, book)
    inner = jnp.sum(weights * dweights, axis=-1, keepdims=True)
    dcode = (weights * (dweights - inner) * scale).astype(BF)
    denc = mm(dcode, book) + pull
    low = mix.astype(BF)
    return (
        low[:block], low[block : 2 * block], low[2 * block :],
        jnp.broadcast_to(loss[None, :], (8, n)), denc, denc.astype(BF),
    )


def mlp_bwd_kernel(
    s, widths, dmlp, denc, mid, gain, slope, wdown_hbm, wup_hbm, wout_hbm, dp, dmid_ref, datt, rows, bup, acc, wdown, wup, wout,
    sems, *, tile,
):
    hidden = wup.shape[1]
    spans = [slice(t * tile, (t + 1) * tile) for t in range(hidden // tile)]
    pairs = []
    for span in spans:
        pairs += [(wdown_hbm.at[span, :], wdown.at[span, :]), (wup_hbm.at[:, span], wup.at[:, span])]
    stream = Stream(sems, *pairs, (wout_hbm, wout))
    for t, cols in enumerate(spans):
        stream.wait(2 * t + 1)
        dpre = (mm_nt(dmlp[...], wdown[cols, :]) * slope[:, cols].astype(F32)).astype(BF)
        dp[:, cols] = dpre
        bup[:, cols] = jnp.sum(dpre.astype(F32), axis=0, keepdims=True)
        stream.wait(2 * t + 2)
        part = mm_nt(dpre, wup[:, cols])
        if t == 0:
            acc[...] = part
        else:
            acc[...] += part
    dy = acc[...]
    xhat, inv = norm_stats(mid[...])
    dmid = denc[...] + norm_back(xhat, inv, line(gain), dy)
    dmid_ref[...] = dmid
    low = dmid.astype(BF)
    dp[:, hidden:] = low
    stream.wait(2 * len(spans) + 1)
    datt[...] = mm_nt(low, wout[...]).astype(BF)
    rows[0:1, :] = jnp.sum(dy * xhat, axis=0, keepdims=True)
    rows[1:2, :] = jnp.sum(dy, axis=0, keepdims=True)
    rows[2:3, :] = jnp.sum(low.astype(F32), axis=0, keepdims=True)
    rows[3:4, :] = jnp.sum(dmlp[...].astype(F32), axis=0, keepdims=True)


def mlp_bwd(s, dmlp, denc, mid, gain, slope, wdown, wup, wout):
    n, dim = denc.shape
    hidden, tile = wup.shape[1], 512
    return call(
        functools.partial(mlp_bwd_kernel, tile=tile), "mlp_bwd", 18,
        [
            shaped((n, hidden + dim)), shaped((n, dim), F32), shaped((n, dim)), shaped((4, dim), F32),
            shaped((1, hidden), F32),
        ],
        [
            pltpu.VMEM((n, dim), F32), pltpu.VMEM(wdown.shape, BF), pltpu.VMEM(wup.shape, BF), pltpu.VMEM(wout.shape, BF),
            pltpu.SemaphoreType.DMA((1 + 2 * (hidden // tile),)),
        ],
        s, dmlp, denc, mid, gain, slope, wdown, wup, wout, micros=7, streamed=3,
    )


TINY_UP, TINY_QKV = 32, 16


def labels(steps, index, part):
    return [[part if step == "y" else parity(index & step[1]) for step in order] for order in steps]


def place(s, first, steps, keep, send, index, part, rows, value):
    sides = labels(steps, index, part)
    slots = [functools.reduce(lambda x, y: 2 * x + y, side[1:], 0) for side in sides]
    here = sides[0][0] + (sides[1][0] - sides[0][0]) * s[CORE]
    slot = slots[0] + (slots[1] - slots[0]) * s[CORE]

    @pl.when(s[first] == here)
    def _():
        keep[slot, rows, :] = value

    @pl.when(s[first] != here)
    def _():
        send[slot, rows, :] = value


def tiny_rows(rows, shards, half):
    dim = rows.shape[1]
    part = dim // shards
    shard = lax.broadcasted_iota(jnp.int32, (shards, dim), 0)
    of = lax.broadcasted_iota(jnp.int32, (shards, dim), 1) // part
    local = lax.broadcasted_iota(jnp.int32, (dim, 1), 0) % part
    lane = lax.broadcasted_iota(jnp.int32, (dim, half), 1)
    total = jnp.zeros((shards, half), F32)
    for k in range(4):
        spread = jnp.where(of == shard, jnp.broadcast_to(rows[k : k + 1, :], (shards, dim)), 0.0)
        total = total + mm(spread.astype(BF), (lane == local + k * part).astype(F32).astype(BF))
    return total


def grad_down_kernel(s, widths, dm0, dm1, act0, act1, keep, send, *, shards, steps):
    rows = dm0.shape[1] // shards // 2
    width = keep.shape[2]
    full = (mm_tn(dm0[...], act0[:, :width]) + mm_tn(dm1[...], act1[:, :width])).astype(BF)
    for j in range(2 * shards):
        place(s, SIDES, steps, keep, send, j // 2, j % 2, slice(None), full[j * rows : (j + 1) * rows])


def grad_down(s, dm0, dm1, act0, act1, shards, steps):
    dim = dm0.shape[1]
    part = shaped((shards, dim // shards // 2, act0.shape[1] - dim))
    return call(
        functools.partial(grad_down_kernel, shards=shards, steps=steps), "grad_down", 10, [part, part], [],
        s, dm0, dm1, act0, act1, micros=4,
    )


def grad_up_kernel(s, widths, a0, a1, d0, d1, four, bup, keep, send, *, shards, steps, hidden, per):
    size, half = keep.shape[1], keep.shape[2]
    first = hidden // 2
    cols = hidden // shards
    rows = (d0.shape[1] - hidden) // shards
    tiny = tiny_rows(four[...], shards, half)
    at = lax.broadcasted_iota(jnp.int32, (2 * size - half - rows, half), 0)

    def put(index, part, at, value):
        place(s, SIDES + 4, steps, keep, send, index, part, slice(at, at + value.shape[0]), value)

    h = slice(first + half, first + 2 * half)
    out = (mm_tn(d0[:, hidden:], a0[:, h]) + mm_tn(d1[:, hidden:], a1[:, h])).astype(BF)
    h = slice(first, first + half)
    for k in range(0, shards, per):
        span = slice(k * cols, (k + per) * cols)
        full = (mm_tn(a0[:, h], d0[:, span]) + mm_tn(a1[:, h], d1[:, span])).astype(BF)
        for j in range(per):
            put(k + j, 0, 0, full[:size, j * cols : (j + 1) * cols])
            put(k + j, 1, 0, full[size:, j * cols : (j + 1) * cols])
            put(k + j, 1, half - size, out[(k + j) * rows : (k + j + 1) * rows])
            both = jnp.where(at == 0, tiny[k + j : k + j + 1], 0.0)
            both = both + jnp.where(at == 1, bup[:, (k + j) * cols : (k + j + 1) * cols], 0.0)
            put(k + j, 1, half - size + rows, both.astype(BF))


def grad_up(s, mine, got, dp0, dp1, four, bup, hidden, shards, steps):
    dim = dp0.shape[1] - hidden
    half = dim // 2
    part = shaped((shards, (half + dim // shards + TINY_UP) // 2, half))
    return call(
        functools.partial(grad_up_kernel, shards=shards, steps=steps, hidden=hidden, per=2), "grad_up", 10,
        [part, part], [], s, mine, got, dp0, dp1, four, bup, micros=5,
    )


def d_of(owns, gots, step, n):
    if step == 0:
        return jnp.concatenate([own[4 * n :, :] for own in owns], axis=1)
    mine, theirs = slice((step - 1) * n, step * n), slice((step + 1) * n, (step + 2) * n)
    return jnp.concatenate(
        [(own[mine, :].astype(F32) + got[theirs, :].astype(F32)).astype(BF) for own, got in zip(owns, gots)], axis=1
    )


def grad_qkv_kernel(
    s, widths, *refs, shards, steps
):
    groups = (len(refs) - 9) // 2
    owns, gots = refs[:groups], refs[groups : 2 * groups]
    last_own, last_got, h_own, hl_own, other, norms, sums, keep, send = refs[-9:]
    n, half = h_own.shape
    dim = 2 * half
    h = slice(other.shape[1] - half, other.shape[1])
    size = 3 * dim // shards // 2

    def put(k, at, value):
        place(s, SIDES + 8, steps, keep, send, k // 2, k % 2, slice(at, at + value.shape[0]), value)

    for step in range(3):
        cols = slice(step * dim, (step + 1) * dim)
        d_own, d_got = d_of(owns, gots, step, n), d_of(gots, owns, step, n)
        full = mm_tn(d_own, h_own[...]) + mm_tn(d_got, other[:n, h])
        full = full + mm_tn(last_own[:, cols], hl_own[...]) + mm_tn(last_got[:, cols], other[n:, h])
        full = full.astype(BF)
        first = step * dim
        for k in range(first // size, (first + dim + size - 1) // size):
            lo, hi = max(first, k * size), min(first + dim, (k + 1) * size)
            put(k, lo - k * size, full[lo - first : hi - first])
    four = jnp.concatenate([norms[...], sums[0:1, :], sums[2:3, :]], axis=0)
    tiny = tiny_rows(four, shards, half)
    at = lax.broadcasted_iota(jnp.int32, (TINY_QKV, half), 0)
    for k in range(2 * shards):
        put(k, size, jnp.where(at == 0, tiny[k // 2 : k // 2 + 1], 0.0).astype(BF))


def grad_qkv(s, owns, gots, last_own, last_got, h_own, hl_own, other, norms, sums, shards, steps):
    half = h_own.shape[1]
    dim = 2 * half
    part = shaped((shards, 3 * dim // shards // 2 + TINY_QKV, half))
    return call(
        functools.partial(grad_qkv_kernel, shards=shards, steps=steps), "grad_qkv", 12, [part, part], [],
        s, *owns, *gots, last_own, last_got, h_own, hl_own, other, norms, sums, micros=4,
    )


def qkv_bwd_kernel(
    s, widths, *refs
):
    groups = (len(refs) - 15) // 2
    owns, gots = refs[:groups], refs[groups : 2 * groups]
    last, x_got, gain, dmid, patches, w_hbm, dx0, dx1, dx2, norms, sums, acc, x_own, w, sems = refs[-15:]
    block, dim = x_got.shape
    n = 2 * block
    spans = [slice(k * dim, (k + 1) * dim) for k in range(3)]
    pairs = [(w_hbm.at[:, span], w.at[:, span]) for span in spans]
    stream = Stream(sems, *pairs, (patches.at[s[CHIP]], x_own.at[0]), (patches.at[2], x_own.at[1]))
    for k, cols in enumerate(spans):
        d = jnp.concatenate([d_of(owns, gots, k, n), last[:, cols]], axis=0)
        sums[k : k + 1, :] = jnp.sum(d.astype(F32), axis=0, keepdims=True)
        stream.wait(k + 1)
        part = mm_nt(d, w[:, cols])
        if k == 0:
            acc[...] = part
        else:
            acc[...] += part
    dy = acc[...]
    stream.wait(5)
    x = jnp.concatenate([x_own[0], x_got[...], x_own[1]], axis=0).astype(F32)
    xhat, inv = norm_stats(x)
    dx = dmid[...] + norm_back(xhat, inv, line(gain), dy)
    dx0[...] = dx[:block]
    dx1[...] = dx[block:n].astype(BF)
    dx2[...] = dx[n:]
    norms[0:1, :] = jnp.sum(dy * xhat, axis=0, keepdims=True)
    norms[1:2, :] = jnp.sum(dy, axis=0, keepdims=True)


def qkv_bwd(s, owns, gots, last, patches, x_got, gain, dmid, w):
    images, block, dim = patches.shape
    return call(
        qkv_bwd_kernel, "qkv_bwd", 12,
        [
            in_hbm((block, dim), F32), in_hbm((block, dim)), in_hbm((block, dim), F32),
            shaped((2, dim), F32), shaped((3, dim), F32),
        ],
        [
            pltpu.VMEM((images * block, dim), F32), pltpu.VMEM((2, block, dim), BF), pltpu.VMEM(w.shape, BF),
            pltpu.SemaphoreType.DMA((5,)),
        ],
        s, *owns, *gots, last, x_got, gain, dmid, patches, w, micros=4, streamed=2,
    )


def finish_kernel(s, widths, both, both_got, down, down_got, up, out, qkv, wdown, *vectors, rows_up, size, parts):
    def sorted_of(value, other):
        cut = value.shape[0] // 2
        mine = [value[:cut].astype(F32), value[cut:].astype(F32)]
        theirs = [other[:cut].astype(F32), other[cut:].astype(F32)]
        second = s[CHIP] > 0
        pairs = [[jnp.where(second, v[1], v[0]), jnp.where(second, v[0], v[1])] for v in (mine, theirs)]
        swap_cores = s[CORE] > 0
        return [
            [jnp.where(swap_cores, b, a) for a, b in zip(*pairs)],
            [jnp.where(swap_cores, a, b) for a, b in zip(*pairs)],
        ]

    cores = sorted_of(both, both_got)
    rows = [jnp.concatenate([first[:rows_up], second[:rows_up]], axis=0) for first, second in cores]
    half = up.shape[0] // 2
    wide = out.shape[1]
    up[:half, :] = rows[0][:half]
    up[half:, :] = rows[1][:half]
    out[...] = jnp.concatenate([r[half : half + wide] for r in rows], axis=1).T
    pieces = [jnp.concatenate([f[rows_up : rows_up + size], g[rows_up : rows_up + size]], axis=0) for f, g in cores]
    qkv[...] = jnp.concatenate(pieces, axis=1).T
    two = rows[0][half + wide : half + wide + 8] + rows[1][half + wide : half + wide + 8]
    one = cores[0][0][rows_up + size : rows_up + size + 8] + cores[1][0][rows_up + size : rows_up + size + 8]
    for ref, (source, row, at) in zip(vectors, parts):
        ref[...] = (one, two)[source][row : row + 1, at : at + ref.shape[0]].reshape(ref.shape[0])
    cores = sorted_of(down, down_got)
    wdown[...] = jnp.concatenate([jnp.concatenate(pair, axis=0) for pair in cores], axis=1).T


def finish(s, both, both_got, down, down_got, rows_up, dim, hidden, shards):
    part, wide = dim // shards, hidden // shards
    size = 3 * dim // shards // 2
    parts = [(0, 0, k * part) for k in range(4)]
    parts += [(1, 0, 2 * part), (1, 0, 0), (1, 0, part), (1, 1, 0), (1, 0, 3 * part)]
    widths = [part] * 7 + [wide, part]
    return call(
        functools.partial(finish_kernel, rows_up=rows_up, size=size, parts=parts), "finish", 20,
        [shaped((dim, wide), F32), shaped((dim, part), F32), shaped((dim, 3 * part), F32), shaped((hidden, part), F32)]
        + [shaped((width,), F32) for width in widths],
        [], s, both, both_got, down, down_got, micros=3,
    )


X, NEAR, FAR = (1, 1), (2, 2), (4, 4)


def plans(n_img):
    if n_img == 8:
        return (
            ([NEAR, "y", X, FAR], [X, "y", NEAR, FAR]),
            ([X, NEAR, "y", FAR], [NEAR, X, "y", FAR]),
            ([X, NEAR, "y", FAR], [NEAR, X, "y", FAR]),
        )
    bits = [1 << k for k in reversed(range(n_img.bit_length() - 1))]
    order = [(bit, bit) for bit in bits] + ["y"]
    return ((order, order),) * 3


def hop(value, step0, step1):
    seq, img = lax.axis_size("seq"), lax.axis_size("img")
    pairs = []
    for s in range(seq):
        step = step1 if s % 2 else step0
        for i in range(img):
            to = (s ^ 2, i) if step == "y" else (s, i ^ (step if isinstance(step, int) else step[0]))
            pairs.append((s * img + i, to[0] * img + to[1]))
    return lax.ppermute(value, ("seq", "img"), pairs)


def side_here(step):
    if step == "y":
        return lax.axis_index("seq") // 2
    bits = lax.axis_index("img") & step[1]
    value = 0
    for k in range(step[1].bit_length()):
        value = value ^ ((bits >> k) & 1)
    return value


def sides_here(steps):
    core = lax.axis_index("seq") % 2
    return [jnp.where(core == 0, side_here(a), side_here(b)) for a, b in zip(*steps)]


def plus(kept, got):
    return (kept.astype(F32) + got.astype(F32)).astype(BF)


class Sum:
    def __init__(self, s, base, steps, keep, send):
        self.s, self.base, self.steps, self.sides, self.at = s, base, steps, sides_here(steps), 0
        self.keep = keep.reshape(-1, keep.shape[-1])
        self.got = self.go(send.reshape(self.keep.shape))

    def go(self, value):
        self.at += 1
        return hop(value, self.steps[0][self.at - 1], self.steps[1][self.at - 1])

    def step(self, *others):
        got = after(self.got, *others) if others else self.got
        shape = (2, got.shape[0] // 2, got.shape[1])
        keep, got = self.keep.reshape(shape), got.reshape(shape)
        if shape[1] % 16 == 0:
            self.keep, send = halve(self.s, keep, got, self.base + self.at)
        else:
            mine = self.sides[self.at]
            self.keep = plus(pick(keep, mine, 0), pick(got, mine, 0))
            send = plus(pick(keep, 1 - mine, 0), pick(got, 1 - mine, 0))
        self.got = self.go(send)
        return send

    def last(self, *others):
        return plus(self.keep, after(self.got, *others) if others else self.got)


def finish_plain(core, chip, both, both_got, down, down_got, rows_up, dim, hidden, shards):
    part, wide, half = dim // shards, hidden // shards, dim // 2
    size = 3 * dim // shards // 2

    def sorted_of(value, other):
        pairs = []
        for v in (value, other):
            a, b = jnp.split(v.astype(F32), 2)
            pairs.append([jnp.where(chip == 0, a, b), jnp.where(chip == 0, b, a)])
        mine, theirs = pairs
        first = [jnp.where(core == 0, a, b) for a, b in zip(mine, theirs)]
        return [first, [jnp.where(core == 0, b, a) for a, b in zip(mine, theirs)]]

    cores = sorted_of(both, both_got)
    rows = [jnp.concatenate([f[:rows_up], g[:rows_up]]) for f, g in cores]
    up = jnp.concatenate([r[:wide].T for r in rows])
    out = jnp.concatenate([r[wide : wide + part] for r in rows], axis=1).T
    pieces = [jnp.concatenate([f[rows_up : rows_up + size], g[rows_up : rows_up + size]]) for f, g in cores]
    two = sum(r[wide + part :] for r in rows).reshape(-1)
    one = sum(f[rows_up + size :] for f, _ in cores).reshape(-1)
    down = jnp.concatenate([jnp.concatenate(pair) for pair in sorted_of(down, down_got)], axis=1).T
    first = [one[k * part : (k + 1) * part] for k in range(4)]
    second = [two[k * part : (k + 1) * part] for k in (2, 0, 1)]
    last = [two[4 * part : 4 * part + wide], two[3 * part : 4 * part]]
    return [up, out, jnp.concatenate(pieces, axis=1).T, down, *first, *second, *last]


class Book:
    def __init__(self, codebook):
        n_img = lax.axis_size("img")
        bits = [1 << k for k in range(n_img.bit_length() - 1)]
        masks = [1, 2, 6] if n_img == 8 else bits
        self.orders = list(zip(masks[1:], [1, "y", *masks[3:]]))
        self.ends = ((1, masks[1]), ("y", masks[2]))
        self.value = codebook

    def start(self):
        self.got = hop(self.value, *self.orders.pop(0))

    def double(self, *others):
        self.value = jnp.concatenate([self.value, after(self.got, *others)])
        return self.value

    def spread(self):
        self.beside, self.across = hop(self.value, *self.ends[0]), hop(self.value, *self.ends[1])
        self.other = [swap(self.value, "seq", 1)]

    def corner(self, *others):
        beside, across = after(self.beside, *others), after(self.across, *others)
        cut = self.value.shape[0] // 2
        self.corners = hop(across[:cut], *self.ends[0]), hop(beside[cut:], *self.ends[1])
        self.sides = jnp.concatenate([beside, across])
        self.other.append(swap(self.sides, "seq", 1))
        return self.sides

    def finish(self, *others):
        rest = jnp.concatenate([after(corner, *others) for corner in self.corners])
        return [self.value, self.sides, rest, self.other[0], self.other[1], swap(rest, "seq", 1)]


def shards(
    patches,
    widths,
    ln1_gain,
    ln1_bias,
    w_qkv,
    b_query,
    b_value,
    w_out,
    b_out,
    ln2_gain,
    ln2_bias,
    w_up,
    b_up,
    w_down,
    b_down,
    codebook,
    cotangent,
):
    images, block, dim = patches.shape
    hidden = w_up.shape[1]
    n_img = lax.axis_size("img")
    me = lax.axis_index("seq")
    chip, core = me // 2, me % 2
    half, main = dim // 2, 2 * block
    fits = codebook.shape[0] * n_img * lax.axis_size("seq") <= 4096
    aligned = n_img == 8 and dim // n_img // 2 % 16 == 0
    steps_down, steps_up, steps_qkv = plans(n_img)
    sides = sides_here(steps_down) + sides_here(steps_up) + sides_here(steps_qkv)
    s = (jnp.stack([me, core, chip, *sides]).astype(jnp.int32), widths)

    book = Book(codebook)
    book.start()
    x_got = swap(pick(patches, 1 - chip, 0), "seq", 2)
    ln1 = (ln1_gain, ln1_bias, b_query, b_value, w_qkv)
    q_last, kv_last, hl_mine, hl_send = qkv_fwd(s, patches, None, *ln1)
    kv_y = swap(after(kv_last, x_got), "seq", 2)
    value = book.double(q_last)
    while book.orders[1:]:
        book.start()
        value = book.double()
    book.start()
    q_main, kv_main, h_mine, h_send = qkv_fwd(s, patches, after(x_got, value), *ln1)
    kv_other = swap(kv_main, "seq", 1)
    kv_y = after(kv_y, q_main)
    value = book.double(kv_y)
    book.spread()
    kv_c, kv_yc = swap(kv_last, "seq", 1), swap(kv_y, "seq", 1)
    kvs_main = [kv_main, kv_other]
    att_main = attention_fwd(s, after(q_main, value), kvs_main, False, block)
    kvs_last = [kv_last, kv_y, kv_c, kv_yc]
    att_last = attention_fwd(s, after(q_last, att_main), kvs_last, True, block)
    sides = book.corner(att_last)
    cot_got = swap(pick(after(cotangent, att_last), 1 - chip, 0), "seq", 2)
    mid, slope, enc, mine, send = mlp_fwd(
        s, patches, x_got, att_main, after(att_last, sides), h_send, hl_send, b_out, ln2_gain, ln2_bias, b_up, b_down,
        w_out, w_up, w_down,
    )
    cot_got = after(cot_got, enc)
    pieces = book.finish(enc)
    got = swap(after(send, pieces[-1]), "seq", 1)
    if fits:
        mix0, mix1, mix2, loss, denc, dmlp = quantizer(s, enc, cotangent, cot_got, pieces)
    else:
        cots = jnp.concatenate([pick(cotangent, chip, 0), cot_got, cotangent[2]])
        mix0, mix1, mix2, loss, denc, dmlp = quantizer_plain(s, enc, cots, jnp.concatenate(pieces))
    mix1 = swap(mix1, "seq", 2)
    loss1 = swap(loss[0, block:main], "seq", 2)

    def split(full, steps):
        rows, cols = full.shape[-2:]
        full = full.reshape([2] * len(steps[0]) + [rows // 2, cols])
        side = sides_here(steps)[0]
        return pick(full, side, 0), pick(full, 1 - side, 0)

    def lines_of(count, *vectors):
        rows = jnp.concatenate([v.reshape(n_img, -1) for v in vectors], axis=1).astype(BF)
        return jnp.pad(rows, ((0, 0), (0, count * half - rows.shape[1]))).reshape(n_img, count, half)

    dmlp_got = swap(dmlp, "seq", 1)
    dp, dmid, datt, rows_two, sum_bup = mlp_bwd(s, dmlp, denc, mid, ln2_gain, slope, w_down, w_up, w_out)
    dmlp_got = after(dmlp_got, dp)
    dp_got = swap(after(dp, dmlp_got), "seq", 1)
    keep_last, send_last, dq_last = attention_bwd(
        s, after(q_last, dmlp_got, mix1, loss1), kvs_last, datt, main, True, block, ()
    )
    got_last = swap(send_last, "seq", 1)
    mine = after(mine, dq_last)
    if aligned:
        keep, send = grad_down(s, dmlp, dmlp_got, mine, got, n_img, steps_down)
    else:
        both, dps = jnp.concatenate([mine, got[:, : mine.shape[1]]]), jnp.concatenate([dp, dp_got])
        full = mm_tn(jnp.concatenate([dmlp, dmlp_got]), both[:, : hidden // 2]).astype(BF)
        keep, send = split(full.reshape(n_img, -1, hidden // 2), steps_down)
    down = Sum(s, 0, steps_down, keep, send)
    keep_last, send_last = fold(s, keep_last, after(got_last, keep))
    got_last = swap(send_last, "seq", 2)
    if aligned:
        keep, send = grad_up(s, after(mine, keep_last), got, dp, dp_got, rows_two, sum_bup, hidden, n_img, steps_up)
    else:
        up = mm_tn(both[:, hidden // 2 : hidden // 2 + half], dps[:, :hidden]).astype(BF)
        up = up.reshape(half, n_img, -1).transpose(1, 2, 0)
        out = mm_tn(dps[:, hidden:], both[:, hidden // 2 + half :]).astype(BF).reshape(n_img, -1, half)
        tiny = lines_of(TINY_UP, rows_two[0], rows_two[1], rows_two[2], rows_two[3], sum_bup[0])
        keep, send = split(jnp.concatenate([up, out, tiny], axis=1), steps_up)
    up = Sum(s, len(steps_down[0]), steps_up, keep, send)
    dqkv_last = join(s, dq_last, keep_last, after(got_last, keep))
    dqkv_last_got = swap(dqkv_last, "seq", 1)
    d_main, d_got, sent = [], [], dqkv_last
    for pairs in ((0, 1), (2, 3), (4, 5)):
        d_main += attention_bwd(s, after(q_main, sent), kvs_main, datt, 0, False, block, pairs)
        sent = d_main[-1]
        d_got.append(swap(sent, "seq", 1))
    sent = down.step(sent)
    sent = up.step(sent)
    dx0, dx1, dx2, norms, sums = qkv_bwd(
        s, d_main, [*d_got[:-1], after(d_got[-1], sent)], dqkv_last, patches, x_got, ln1_gain, dmid, w_qkv
    )
    dx1 = swap(dx1, "seq", 2).astype(F32)
    if aligned:
        keep, send = grad_qkv(
            s, d_main, d_got, dqkv_last, dqkv_last_got, h_mine, hl_mine, got, norms, sums, n_img, steps_qkv
        )
    else:
        n = main
        d_main, d_got = jnp.concatenate(d_main, axis=1), jnp.concatenate(d_got, axis=1)

        def assembled(a, b, last):
            parts = [a[4 * n :]] + [plus(a[k * n : (k + 1) * n], b[(k + 2) * n : (k + 3) * n]) for k in (0, 1)]
            return [jnp.concatenate(parts, axis=1), last]

        d = jnp.concatenate(assembled(d_main, d_got, dqkv_last) + assembled(d_got, d_main, dqkv_last_got))
        h = jnp.concatenate([h_mine, hl_mine, got[:, -half:]])
        full = mm_tn(d, h).astype(BF).reshape(n_img, 2, -1, half)
        tiny = lines_of(TINY_QKV, norms[0], norms[1], sums[0], sums[2])
        full = jnp.concatenate([full, jnp.stack([tiny, tiny], axis=1)], axis=2)
        keep, send = split(full.reshape(n_img, -1, half), steps_qkv)
    qkv = Sum(s, 2 * len(steps_down[0]), steps_qkv, keep, send)

    count = len(steps_down[0])
    sent = down.step(keep, dx1)
    sent = up.step(sent)
    for _ in range(count - 4):
        sent = down.step(sent)
        sent = up.step(sent)
        sent = qkv.step(sent)
    sent = down.step(sent)
    sent = qkv.step(sent)
    sent = up.step(sent)
    sum_down = down.last(sent)
    down_both = jnp.concatenate([sum_down, swap(sum_down, "seq", 2)])
    down_got = swap(down_both, "seq", 1)
    sent = qkv.step(sent)
    sent = qkv.step(sent)
    sum_up = up.last()
    up_other = swap(sum_up, "seq", 2)
    sum_qkv = qkv.last()
    qkv_other = swap(sum_qkv, "seq", 2)
    both = jnp.concatenate([sum_up, sum_qkv, up_other, qkv_other])
    both_got = swap(both, "seq", 1)
    rows_up = sum_up.shape[0]
    if aligned:
        weights = finish(s, both, both_got, down_both, down_got, rows_up, dim, hidden, n_img)
    else:
        weights = finish_plain(core, chip, both, both_got, down_both, down_got, rows_up, dim, hidden, n_img)
    g_up, g_out, g_qkv, g_down, g_gain1, g_shift1, g_bq, g_bv, g_bout, g_gain2, g_shift2, g_bup, g_bdown = weights

    def images_of(own, back, last):
        return jnp.stack([jnp.where(chip == 0, own, back), jnp.where(chip == 0, back, own), last])

    return (
        images_of(mix0, mix1, mix2),
        images_of(loss[0, :block], loss1, loss[0, main:]),
        images_of(dx0, dx1, dx2),
        g_gain1,
        g_shift1,
        g_qkv,
        g_bq,
        g_bv,
        g_out,
        g_bout,
        g_gain2,
        g_shift2,
        g_up,
        g_bup,
        g_down,
        g_bdown,
    )


def solution(mesh):
    return jax.shard_map(
        shards,
        mesh=mesh,
        in_specs=(
            P("img", "seq", None),
            P("img"),
            P(),
            P(),
            P(),
            P(),
            P(),
            P(),
            P(),
            P(),
            P(),
            P(),
            P(),
            P(),
            P(),
            P(("seq", "img"), None),
            P("img", "seq", None),
        ),
        out_specs=(
            P("img", "seq", None),
            P("img", "seq"),
            P("img", "seq", None),
            P("img"),
            P("img"),
            P(None, "img"),
            P("img"),
            P("img"),
            P(None, "img"),
            P("img"),
            P("img"),
            P("img"),
            P(None, "img"),
            P("img"),
            P(None, "img"),
            P("img"),
        ),
        check_vma=False,
    )
```

```python
import functools

import jax
import jax.numpy as jnp
from jax import lax
from jax.experimental import pallas as pl
from jax.experimental.pallas import tpu as pltpu
from jax.sharding import PartitionSpec as P

HEAD_DIM = 64
GRID_H = 16
EPS_NORM = 1e-06
COMMIT = 16.0
BF = jnp.bfloat16
F32 = jnp.float32
MIB = 1024 * 1024
MASKED = -1000000000.0


def mm(a, b):
    return jnp.dot(a, b, preferred_element_type=F32)


def mm_nt(a, b):
    return lax.dot_general(a, b, (((1,), (1,)), ((), ())), preferred_element_type=F32)


def mm_tn(a, b):
    return lax.dot_general(a, b, (((0,), (0,)), ((), ())), preferred_element_type=F32)


def swap(value, axis, bit):
    count = lax.axis_size(axis)
    return lax.ppermute(value, axis, [(i, i ^ bit) for i in range(count)])


def pick(value, index, axis):
    return lax.dynamic_index_in_dim(value, index, axis, keepdims=False)


def after(value, *others):
    return lax.optimization_barrier((value, *others))[0]


def parity(number):
    return bin(number).count("1") % 2


def shaped(shape, dtype=BF):
    return jax.ShapeDtypeStruct(tuple(shape), dtype)


def in_hbm(shape, dtype=BF):
    return pltpu.HBM(tuple(shape), dtype)


class Order:
    token = None


def call(kernel, name, mib, out_shape, scratch, s, *args, micros, streamed=0):
    vm, hbm = pl.BlockSpec(memory_space=pltpu.VMEM), pl.BlockSpec(memory_space=pl.ANY)
    direct, count = len(args) - streamed, len(args) + len(out_shape)
    args = [
        pltpu.with_memory_space_constraint(arg, pltpu.HBM) if arg.ndim == 1 or (k >= direct and name != "stack") else arg
        for k, arg in enumerate(args)
    ]

    def body(scalars, widths, token, *refs):
        kernel(scalars, widths, *refs[:count], *refs[count + 1 :])
        refs[count][...] = token[...]

    out = pl.pallas_call(
        body,
        in_specs=[pl.BlockSpec(memory_space=pltpu.SMEM)] * 2 + [vm] * (direct + 1) + [hbm] * streamed,
        out_specs=[vm] * (len(out_shape) + 1),
        out_shape=[*out_shape, shaped((8, 128), F32)],
        scratch_shapes=scratch,
        compiler_params=pltpu.CompilerParams(vmem_limit_bytes=mib * MIB),
        cost_estimate=pl.CostEstimate(flops=int(micros * 2e8), bytes_accessed=0, transcendentals=0),
        name=name,
    )(*s, Order.token, *args)
    Order.token = out[-1]
    return out[:-1]


class Stream:
    def __init__(self, sems, *pairs, ahead=3):
        self.copies = [pltpu.make_async_copy(a, b, sems.at[k]) for k, (a, b) in enumerate(pairs)]
        self.done, self.begun = 0, 0
        self.start(ahead)

    def start(self, count):
        while self.begun < min(count, len(self.copies)):
            self.copies[self.begun].start()
            self.begun += 1

    def wait(self, count):
        while self.done < count:
            self.copies[self.done].wait()
            self.done += 1
            self.start(self.begun + 1)


ME, CORE, CHIP, SIDES = range(4)


def line(ref, start=0, size=None):
    size = ref.shape[0] if size is None else size
    return ref[start : start + size].reshape(1, size)


def norm_stats(x):
    center = x - jnp.mean(x, axis=-1, keepdims=True)
    spread = jnp.mean(center * center, axis=-1, keepdims=True)
    inv = lax.rsqrt(spread + EPS_NORM)
    return center * inv, inv


def norm_back(xhat, inv, gain, dy):
    dxhat = dy * gain
    return inv * (
        dxhat - jnp.mean(dxhat, axis=-1, keepdims=True) - xhat * jnp.mean(dxhat * xhat, axis=-1, keepdims=True)
    )


def spots(index, block, me):
    place = index // block
    mask = (place % 2) * 2 + place // 2
    return (me ^ mask) * block + index % block


def limit_of(s, widths, last):
    return GRID_H * widths[2 if last else s[CHIP]]


def side_of(ref, side, width):
    return ref[:, pl.ds(pl.multiple_of(side * width, 128), width)]


def qkv_kernel(
    s, widths, got, gain, shift, bq, bv, patches, w_hbm, q_main, q_last, kv0, kv1, kv2, mine, send, h, x_own, w, sems
):
    half, dim = mine.shape[1], w.shape[0]
    block = got.shape[0]
    spans = [slice(k * dim, (k + 1) * dim) for k in (1, 2, 0)]
    pairs = [(patches.at[s[CHIP]], x_own.at[0]), (patches.at[2], x_own.at[1])]
    stream = Stream(sems, *pairs, *((w_hbm.at[:, span], w.at[:, span]) for span in spans))
    stream.wait(2)
    for k, x in enumerate((x_own[0], got[...], x_own[1])):
        xhat, _ = norm_stats(x.astype(F32))
        h[k * block : (k + 1) * block, :] = (xhat * line(gain) + line(shift)).astype(BF)
    mine[...] = side_of(h, s[CORE], half)
    send[...] = side_of(h, 1 - s[CORE], half)
    stream.wait(3)
    keys = mm(h[...], w[:, dim : 2 * dim]).astype(BF)
    stream.wait(4)
    values = (mm(h[...], w[:, 2 * dim :]) + line(bv)).astype(BF)
    for k, out in enumerate((kv0, kv1, kv2)):
        out[:, :dim] = keys[k * block : (k + 1) * block]
        out[:, dim:] = values[k * block : (k + 1) * block]
    stream.wait(5)
    q = (mm(h[...], w[:, :dim]) + line(bq)).astype(BF)
    q_main[...] = q[: 2 * block]
    q_last[...] = q[2 * block :]


def qkv_fwd(s, patches, got, gain, shift, bq, bv, w):
    images, block, dim = patches.shape
    n, half = images * block, dim // 2
    return call(
        qkv_kernel, "qkv_fwd", 12,
        [
            shaped((2 * block, dim)), shaped((block, dim)), *[shaped((block, 2 * dim))] * 3,
            in_hbm((n, half)), shaped((n, half)),
        ],
        [
            pltpu.VMEM((n, dim), BF), pltpu.VMEM((2, block, dim), BF), pltpu.VMEM(w.shape, BF),
            pltpu.SemaphoreType.DMA((5,)),
        ],
        s, got, gain, shift, bq, bv, patches, w, micros=3, streamed=2,
    )


def two_heads(value):
    left = lax.broadcasted_iota(jnp.int32, value.shape, 1) < HEAD_DIM
    zero = jnp.zeros_like(value)
    return jnp.concatenate([jnp.where(left, value, zero), jnp.where(left, zero, value)], axis=0)


def one_pair(value):
    n = value.shape[0] // 2
    left = lax.broadcasted_iota(jnp.int32, (n, value.shape[1]), 1) < HEAD_DIM
    return jnp.where(left, value[:n], value[n:])


def rows_of(refs, lanes):
    return jnp.concatenate([ref[:, lanes] for ref in refs], axis=0)


def att_fwd_kernel(s, widths, q, *refs, last, block):
    kvs, o = refs[:-1], refs[-1]
    dim = q.shape[1]
    m = sum(kv.shape[0] for kv in kvs)
    index = lax.broadcasted_iota(jnp.int32, (1, m), 1)
    ok = spots(index, block, s[ME]) < limit_of(s, widths, last)
    for p in range(dim // 128):
        at, av = slice(p * 128, (p + 1) * 128), slice(dim + p * 128, dim + (p + 1) * 128)
        k, v = rows_of(kvs, at), rows_of(kvs, av)
        raw = mm_nt(two_heads(q[:, at]), k) * (HEAD_DIM**-0.5)
        scores = jnp.where(ok, raw, MASKED)
        expo = jnp.exp(scores - jnp.max(scores, axis=1, keepdims=True))
        probs = expo * (1.0 / jnp.sum(expo, axis=1, keepdims=True))
        o[:, at] = one_pair(mm(probs.astype(BF), v)).astype(BF)


def attention_fwd(s, q, kvs, last, block):
    return call(
        functools.partial(att_fwd_kernel, last=last, block=block), "attention_fwd", 10, [shaped(q.shape)], [],
        s, q, *kvs, micros=5,
    )[0]


def att_bwd_kernel(s, widths, q, do, *refs, last, block, first, pairs, more):
    n, dim = q.shape
    if pairs:
        kvs, out = refs[: len(refs) - 1 - more], refs[-1]
        m = sum(kv.shape[0] for kv in kvs)
        parts = [out.at[k * m // 2 : (k + 1) * m // 2, :] for k in range(4)]
        dq = out.at[2 * m : 2 * m + n, :]
        if more:
            dq_last, keep_last, got_last = refs[-4:-1]
            rows, wide = dq_last.shape[0], out.shape[1]
            parts_last = [dq_last[...]] + [
                (keep_last[k].astype(F32) + got_last[k].astype(F32)).astype(BF) for k in range(2)
            ]
            for k in range(3 * dim // wide):
                part, at = parts_last[k * wide // dim], k * wide % dim
                out[2 * m + n + k * rows : 2 * m + n + (k + 1) * rows, :] = part[:, at : at + wide]
    else:
        kvs, (keep, send, dq) = refs[:-3], refs[-3:]
        m = sum(kv.shape[0] for kv in kvs)
        parts = [keep.at[0], keep.at[1], send.at[0], send.at[1]]
    index = lax.broadcasted_iota(jnp.int32, (m, 1), 0)
    ok = spots(index, block, s[ME]) < limit_of(s, widths, last)
    for p in pairs or range(dim // 128):
        at, av = slice(p * 128, (p + 1) * 128), slice(dim + p * 128, dim + (p + 1) * 128)
        to = slice((p - pairs[0]) * 128, (p - pairs[0] + 1) * 128) if pairs else at
        k, v = rows_of(kvs, at), rows_of(kvs, av)
        q2, do2 = two_heads(q[:, at]), two_heads(do[first : first + n, at])
        raw = mm_nt(k, q2) * (HEAD_DIM**-0.5)
        scores = jnp.where(ok, raw, MASKED)
        expo = jnp.exp(scores - jnp.max(scores, axis=0, keepdims=True))
        probs = expo * (1.0 / jnp.sum(expo, axis=0, keepdims=True))
        dv = mm(probs.astype(BF), do2).astype(BF)
        dp = mm_nt(v, do2)
        inner = jnp.sum(probs * dp, axis=0, keepdims=True)
        ds = (probs * (dp - inner) * (HEAD_DIM**-0.5)).astype(BF)
        dk = mm(ds, q2).astype(BF)
        dq[:, to] = one_pair(mm_tn(ds, k)).astype(BF)
        for ref, part in zip(parts, (dk[: m // 2], dv[: m // 2], dk[m // 2 :], dv[m // 2 :])):
            ref[:, to] = part


def attention_bwd(s, q, kvs, do, first, last, block, pairs, more=()):
    n, dim = q.shape
    m = sum(kv.shape[0] for kv in kvs)
    return call(
        functools.partial(att_bwd_kernel, last=last, block=block, first=first, pairs=pairs, more=len(more)),
        "attention_bwd", 12,
        [shaped((2 * m + n + (len(more) and 3 * dim // len(pairs)), 128 * len(pairs)))] if pairs else [shaped((2, m // 2, dim)), shaped((2, m // 2, dim)), shaped((n, dim))],
        [], s, q, do, *kvs, *more, micros=4,
    )


def fold_kernel(s, widths, keep, got, keep_out, send_out):
    block = keep_out.shape[1]
    for k in range(2):
        total = (keep[k].astype(F32) + got[k].astype(F32)).astype(BF)
        keep_out[k] = total[:block]
        send_out[k] = total[block:]


def fold(s, keep, got):
    part = shaped((2, keep.shape[1] // 2, keep.shape[2]))
    return call(fold_kernel, "fold", 4, [part, part], [], s, keep, got, micros=0.5)


def stack_kernel(s, widths, *refs, count):
    at = 0
    for ref in refs[:count]:
        refs[-1][at : at + ref.shape[0], :] = ref[...]
        at += ref.shape[0]


def stack(s, *parts, there=()):
    shape = (sum(part.shape[0] for part in parts), parts[0].shape[1])
    kernel = functools.partial(stack_kernel, count=len(parts))
    return call(kernel, "stack", 8, [shaped(shape)], [], s, *parts, *there, micros=0.5, streamed=len(there))[0]


def cut_kernel(s, widths, a, b, first, second):
    rows = first.shape[0]
    first[...] = a[:rows, :]
    second[...] = b[rows:, :]


def cut(s, a, b):
    part = shaped((a.shape[0] // 2, a.shape[1]))
    return call(cut_kernel, "cut", 4, [part, part], [], s, a, b, micros=0.3)


def collect_kernel(s, widths, up, qkv, up_other, qkv_other, out):
    at = 0
    for ref in (up, qkv, up_other, qkv_other):
        rows = qkv.shape[0] if ref is qkv_other else ref.shape[0]
        rows = up.shape[0] if ref is up_other else rows
        out[at : at + rows, :] = ref[:rows, :]
        at += rows


def collect(s, up, qkv, up_other, qkv_other):
    shape = (2 * (up.shape[0] + qkv.shape[0]), up.shape[1])
    return call(collect_kernel, "collect", 6, [shaped(shape)], [], s, up, qkv, up_other, qkv_other, micros=0.5)[0]


def add_kernel(s, widths, keep, got, out):
    out[...] = (keep[...].astype(F32) + got[...].astype(F32)).astype(BF)


def add(s, keep, got):
    return call(add_kernel, "add", 4, [shaped(keep.shape)], [], s, keep, got, micros=0.5)[0]


def sorted_images(s, out, own, back, last):
    first = s[CHIP] == 0
    out[0] = jnp.where(first, own, back)
    out[1] = jnp.where(first, back, own)
    out[2] = last


def assemble_kernel(s, widths, mix0, mix1, mix2, loss, mix, losses):
    block = mix0.shape[0]
    sorted_images(s, mix, mix0[...], mix1[:block, :], mix2[...])
    first = s[CHIP] == 0
    own = loss[0:1, :block]
    back = sum(mix1[block : block + 8, k * block : (k + 1) * block].astype(F32) for k in range(3))[0:1]
    losses[0:1, :] = jnp.where(first, own, back)
    losses[1:2, :] = jnp.where(first, back, own)
    losses[2:3, :] = loss[0:1, 2 * block :]


def assemble(s, mix, loss):
    block, dim = mix[0].shape
    return call(
        assemble_kernel, "assemble", 8, [in_hbm((3, block, dim)), in_hbm((3, block), F32)], [],
        s, *mix, loss, micros=1,
    )


def assemble_dx_kernel(s, widths, dx0, pack, dx2, dx):
    block = dx0.shape[0]
    first = pack.shape[0] - 2 * block
    back = jnp.concatenate([pack[first : first + block, :], pack[first + block :, :]], axis=1)
    sorted_images(s, dx, dx0[...], back.astype(F32), dx2[...])


def assemble_dx(s, *dx):
    block, dim = dx[0].shape
    return call(assemble_dx_kernel, "assemble_dx", 8, [in_hbm((3, block, dim), F32)], [], s, *dx, micros=1)[0]


def halve_kernel(s, widths, keep, got, keep_out, send_out, *, at):
    mine = s[SIDES + at]
    keep_out[...] = (keep[mine].astype(F32) + got[mine].astype(F32)).astype(BF)
    send_out[...] = (keep[1 - mine].astype(F32) + got[1 - mine].astype(F32)).astype(BF)


def halve(s, keep, got, at):
    part = shaped(keep.shape[1:])
    return call(functools.partial(halve_kernel, at=at), "halve", 8, [part, part], [], s, keep, got, micros=0.7)


def gelu_pair(x):
    z = jnp.abs(x) * (0.5**0.5)
    t = 1.0 / (1.0 + 0.3275911 * z)
    expo = jnp.exp(-0.5 * x * x)
    poly = t * (0.254829592 + t * (-0.284496736 + t * (1.421413741 + t * (-1.453152027 + t * 1.061405429))))
    tail = 0.5 * poly * expo
    cdf = jnp.where(x < 0.0, tail, 1.0 - tail)
    return x * cdf, cdf + x * (expo * 0.3989422804014327)


def hidden_spans(side, wide, tile):
    return [
        (pl.ds(pl.multiple_of(side * wide + k * tile, 128), tile), slice(k * tile, (k + 1) * tile))
        for k in range(wide // tile)
    ]


def mlp_tiles(side, h2, bup, wup_hbm, wdown_hbm, wup, wdown, enc, act_ref, slope, sems, *more, tile, ready=None):
    wide = slope.shape[1]
    spans = hidden_spans(side, wide, tile)
    pairs = list(more)
    for there, here in spans:
        pairs += [(wup_hbm.at[:, there], wup.at[:, here]), (wdown_hbm.at[there, :], wdown.at[here, :])]
    stream = Stream(sems, *pairs)
    if ready is not None:
        stream.wait(len(more))
        ready()
    for k, (there, here) in enumerate(spans):
        stream.wait(len(more) + 2 * k + 1)
        act, rate = gelu_pair(mm(h2[...], wup[:, here]) + bup[there].reshape(1, tile))
        act = act.astype(BF)
        act_ref[:, here] = act
        slope[:, here] = rate.astype(BF)
        stream.wait(len(more) + 2 * k + 2)
        enc[...] += mm(act, wdown[here, :])


def mlp_first_kernel(
    s, widths, got, att_main, att_last, h1, bout, gain, shift, bup, bdown, patches, wout_hbm, wup_hbm,
    wdown_hbm, mid, h2, enc, slope, send, x_own, wout, wup, wdown, sems, *, tile,
):
    dim = got.shape[1]
    half, wide = dim // 2, slope.shape[1]
    rows = att_main.shape[0]
    side = 1 - s[CORE]

    def ready():
        x = jnp.concatenate([x_own[0], got[...], x_own[1]], axis=0).astype(F32)
        att = jnp.concatenate([att_main[...], att_last[...]], axis=0)
        middle = x + mm(att, wout[...]) + line(bout)
        mid[...] = middle
        xhat, _ = norm_stats(middle)
        h2[...] = (xhat * line(gain) + line(shift)).astype(BF)
        enc[...] = middle + line(bdown)
        send[:, wide : wide + half] = side_of(h2, side, half)
        send[:rows, wide + half : wide + dim] = side_of(att_main, side, half)
        send[rows:, wide + half : wide + dim] = side_of(att_last, side, half)
        send[:, wide + dim :] = h1[...]

    more = [(wout_hbm, wout), (patches.at[s[CHIP]], x_own.at[0]), (patches.at[2], x_own.at[1])]
    mlp_tiles(
        side, h2, bup, wup_hbm, wdown_hbm, wup, wdown, enc, send, slope, sems, *more, tile=tile, ready=ready
    )


def mlp_second_kernel(
    s, widths, h2, enc_in, att_main, att_last, bup, wup_hbm, wdown_hbm, enc, slope, mine, wup, wdown, sems, *, tile
):
    half, wide = h2.shape[1] // 2, slope.shape[1]
    rows = att_main.shape[0]
    enc[...] = enc_in[...]
    mine[:, wide : wide + half] = side_of(h2, s[CORE], half)
    mine[:rows, wide + half :] = side_of(att_main, s[CORE], half)
    mine[rows:, wide + half :] = side_of(att_last, s[CORE], half)
    mlp_tiles(s[CORE], h2, bup, wup_hbm, wdown_hbm, wup, wdown, enc, mine, slope, sems, tile=tile)


def mlp_first(s, patches, got, att_main, att_last, h1, bout, gain, shift, bup, bdown, wout, wup, wdown):
    images, block, dim = patches.shape
    n, wide, tile = images * block, wup.shape[1] // 2, 512
    return call(
        functools.partial(mlp_first_kernel, tile=tile), "mlp_first", 14,
        [
            shaped((n, dim), F32), shaped((n, dim)), shaped((n, dim), F32), shaped((n, wide)),
            shaped((n, wide + dim + dim // 2)),
        ],
        [
            pltpu.VMEM((2, block, dim), BF), pltpu.VMEM(wout.shape, BF), pltpu.VMEM((dim, wide), BF),
            pltpu.VMEM((wide, dim), BF), pltpu.SemaphoreType.DMA((3 + 2 * (wide // tile),)),
        ],
        s, got, att_main, att_last, h1, bout, gain, shift, bup, bdown, patches, wout, wup, wdown,
        micros=6, streamed=4,
    )


def mlp_second(s, h2, enc, att_main, att_last, bup, wup, wdown):
    n, dim = h2.shape
    wide, tile = wup.shape[1] // 2, 512
    return call(
        functools.partial(mlp_second_kernel, tile=tile), "mlp_second", 14,
        [shaped((n, dim), F32), shaped((n, wide)), shaped((n, wide + dim))],
        [pltpu.VMEM((dim, wide), BF), pltpu.VMEM((wide, dim), BF), pltpu.SemaphoreType.DMA((2 * (wide // tile),))],
        s, h2, enc, att_main, att_last, bup, wup, wdown, micros=5, streamed=2,
    )


def quant_kernel(s, widths, enc, cot_got, *refs, tile, scale):
    pieces, cot = refs[:-12], refs[-12]
    mix_own, mix_back, mix_last, loss, denc, dmlp, score, dweight, late, cot_own, sems = refs[-11:]
    n, dim = enc.shape
    block = n // 3
    chunks, place = [], 0
    for piece in pieces:
        for first in range(0, piece.shape[0], tile):
            size = min(tile, piece.shape[0] - first)
            chunks.append((piece, slice(first, first + size), slice(place, place + size)))
            place += size + -size % 128
    stream = Stream(sems, (cot.at[s[CHIP]], cot_own.at[0]), (cot.at[2], cot_own.at[1]))
    low = enc[...].astype(BF)
    peak = None
    for piece, rows, cols in chunks:
        part = mm_nt(low, piece[rows, :]) * scale
        score[:, cols] = part
        top = jnp.max(part, axis=1, keepdims=True)
        peak = top if peak is None else jnp.maximum(peak, top)
    total = jnp.zeros_like(peak)
    late[...] = jnp.zeros_like(late)
    for piece, rows, cols in chunks:
        e = jnp.exp(score[:, cols] - peak)
        score[:, cols] = e
        total = total + jnp.sum(e, axis=1, keepdims=True)
        late[...] += mm(e.astype(BF), piece[rows, :])
    inv = 1.0 / total
    mix = late[...] * inv
    low = mix.astype(BF)
    mix_own[...] = low[:block]
    mix_back[:block, :] = low[block : 2 * block]
    mix_last[...] = low[2 * block :]
    index = lax.broadcasted_iota(jnp.int32, (n, 1), 0)
    spot = spots(index % (2 * block), block, s[ME])
    ok = spot < jnp.where(index < 2 * block, limit_of(s, widths, False), limit_of(s, widths, True))
    diff = enc[...] - mix
    lost = jnp.where(ok, jnp.mean(diff * diff, axis=1, keepdims=True), 0.0)
    lost = jnp.transpose(jnp.broadcast_to(lost, (n, 128)))[0:8, :]
    loss[...] = lost
    back = lost[:, block : 2 * block]
    high = back.astype(BF)
    rest = back - high.astype(F32)
    mix_back[block:, :] = jnp.zeros((mix_back.shape[0] - block, dim), BF)
    mix_back[block : block + 8, :block] = high
    mix_back[block : block + 8, block : 2 * block] = rest.astype(BF)
    mix_back[block : block + 8, 2 * block : 3 * block] = (rest - rest.astype(BF).astype(F32)).astype(BF)
    pull = jnp.where(ok, (2.0 * COMMIT / dim) * diff, 0.0)
    denc[...] = pull
    stream.wait(2)
    cots = jnp.concatenate([cot_own[0], cot_got[...], cot_own[1]], axis=0).astype(F32)
    dmix = (cots - pull).astype(BF)
    inner = jnp.zeros_like(peak)
    for piece, rows, cols in chunks:
        d = mm_nt(dmix, piece[rows, :])
        dweight[:, cols] = d
        inner = inner + jnp.sum(score[:, cols] * d, axis=1, keepdims=True)
    inner = inner * inv
    inv = inv * scale
    for piece, rows, cols in chunks:
        dcode = (score[:, cols] * inv * (dweight[:, cols] - inner)).astype(BF)
        denc[...] += mm(dcode, piece[rows, :])
    dmlp[...] = denc[...].astype(BF)


def quantizer(s, enc, cot, cot_got, pieces, tile=512):
    n, dim = enc.shape
    block = n // 3
    count = sum(-(-piece.shape[0] // tile) for piece in pieces)
    wide = count * tile
    return call(
        functools.partial(quant_kernel, tile=tile, scale=dim**-0.5), "quantizer", 21,
        [in_hbm((block, dim)), in_hbm((block + 16, dim)), in_hbm((block, dim))]
        + [in_hbm((8, n), F32), shaped((n, dim), F32), shaped((n, dim))],
        [
            pltpu.VMEM((n, wide), F32), pltpu.VMEM((n, wide), F32), pltpu.VMEM((n, dim), F32),
            pltpu.VMEM((2, block, dim), BF), pltpu.SemaphoreType.DMA((2,)),
        ],
        s, enc, cot_got, *pieces, cot, micros=14, streamed=1,
    )


def quantizer_plain(s, enc, cots, book):
    n, dim = enc.shape
    block = n // 3
    index = jnp.arange(n)
    s, widths = s
    ok = spots(index % (2 * block), block, s[ME])
    ok = ok < jnp.where(index < 2 * block, limit_of(s, widths, False), limit_of(s, widths, True))
    scale = dim**-0.5
    scores = mm_nt(enc.astype(BF), book) * scale
    peak = jnp.max(scores, axis=-1, keepdims=True)
    log_total = peak + jnp.log(jnp.sum(jnp.exp(scores - peak), axis=-1, keepdims=True))
    weights = jnp.exp(scores - log_total)
    mix = mm(weights.astype(BF), book)
    diff = enc - mix
    loss = jnp.where(ok, jnp.mean(diff * diff, axis=-1), 0.0)
    pull = jnp.where(ok[:, None], 2.0 * COMMIT / dim * diff, 0.0)
    dmix = (cots.astype(F32) - pull).astype(BF)
    dweights = mm_nt(dmix, book)
    inner = jnp.sum(weights * dweights, axis=-1, keepdims=True)
    dcode = (weights * (dweights - inner) * scale).astype(BF)
    denc = mm(dcode, book) + pull
    low = mix.astype(BF)
    loss = jnp.broadcast_to(loss[None, :], (8, n))
    parts, rest = [], loss[:, block : 2 * block]
    for _ in range(3):
        parts.append(rest.astype(BF))
        rest = rest - parts[-1].astype(F32)
    parts = jnp.pad(jnp.concatenate(parts, axis=1), ((0, 8), (0, dim - 3 * block)))
    back = jnp.concatenate([low[block : 2 * block], parts])
    return low[:block], back, low[2 * block :], loss, denc, denc.astype(BF)


def mlp_bwd_kernel(
    s, widths, dmlp, denc, mid, gain, slope0, slope1, wdown_hbm, wup_hbm, wout_hbm, dp0, dp1, dbranch, dmid_ref, datt,
    rows, bup, acc, wdown, wup, wout, sems, *, tile,
):
    hidden, wide = wup.shape[1], slope0.shape[1]
    spans = [slice(k, k + tile) for k in range(0, hidden, tile)]
    pairs = []
    for span in spans:
        pairs += [(wdown_hbm.at[span, :], wdown.at[span, :]), (wup_hbm.at[:, span], wup.at[:, span])]
    stream = Stream(sems, *pairs, (wout_hbm, wout))
    for t, span in enumerate(spans):
        half, here = span.start // wide, slice(span.start % wide, span.start % wide + tile)
        stream.wait(2 * t + 1)
        slope = jnp.where(s[CORE] == half, slope1[:, here], slope0[:, here]).astype(F32)
        dpre = (mm_nt(dmlp[...], wdown[span, :]) * slope).astype(BF)
        (dp0, dp1)[half][:, here] = dpre
        bup[:, span] = jnp.sum(dpre.astype(F32), axis=0, keepdims=True)
        stream.wait(2 * t + 2)
        part = mm_nt(dpre, wup[:, span])
        if t == 0:
            acc[...] = part
        else:
            acc[...] += part
    dy = acc[...]
    xhat, inv = norm_stats(mid[...])
    dmid = denc[...] + norm_back(xhat, inv, line(gain), dy)
    dmid_ref[...] = dmid
    low = dmid.astype(BF)
    dbranch[...] = low
    stream.wait(2 * len(spans) + 1)
    datt[...] = mm_nt(low, wout[...]).astype(BF)
    rows[0:1, :] = jnp.sum(dy * xhat, axis=0, keepdims=True)
    rows[1:2, :] = jnp.sum(dy, axis=0, keepdims=True)
    rows[2:3, :] = jnp.sum(low.astype(F32), axis=0, keepdims=True)
    rows[3:4, :] = jnp.sum(dmlp[...].astype(F32), axis=0, keepdims=True)


def mlp_bwd(s, dmlp, denc, mid, gain, slopes, wdown, wup, wout):
    n, dim = denc.shape
    hidden, tile = wup.shape[1], 512
    return call(
        functools.partial(mlp_bwd_kernel, tile=tile), "mlp_bwd", 18,
        [
            shaped((n, hidden // 2)), shaped((n, hidden // 2)), shaped((n, dim)), shaped((n, dim), F32),
            shaped((n, dim)), shaped((4, dim), F32), shaped((1, hidden), F32),
        ],
        [
            pltpu.VMEM((n, dim), F32), pltpu.VMEM(wdown.shape, BF), pltpu.VMEM(wup.shape, BF), pltpu.VMEM(wout.shape, BF),
            pltpu.SemaphoreType.DMA((1 + 2 * (hidden // tile),)),
        ],
        s, dmlp, denc, mid, gain, *slopes, wdown, wup, wout, micros=9, streamed=3,
    )


TINY_UP, TINY_QKV = 32, 16


def labels(steps, index, part):
    return [[part if step == "y" else parity(index & step[1]) for step in order] for order in steps]


def place(s, first, steps, keep, send, index, part, rows, value):
    sides = labels(steps, index, part)
    slots = [functools.reduce(lambda x, y: 2 * x + y, side[1:], 0) for side in sides]
    here = sides[0][0] + (sides[1][0] - sides[0][0]) * s[CORE]
    slot = slots[0] + (slots[1] - slots[0]) * s[CORE]

    @pl.when(s[first] == here)
    def _():
        keep[slot, rows, :] = value

    @pl.when(s[first] != here)
    def _():
        send[slot, rows, :] = value


def tiny_rows(rows, shards, half):
    dim = rows.shape[1]
    part = dim // shards
    shard = lax.broadcasted_iota(jnp.int32, (shards, dim), 0)
    of = lax.broadcasted_iota(jnp.int32, (shards, dim), 1) // part
    local = lax.broadcasted_iota(jnp.int32, (dim, 1), 0) % part
    lane = lax.broadcasted_iota(jnp.int32, (dim, half), 1)
    total = jnp.zeros((shards, half), F32)
    for k in range(4):
        spread = jnp.where(of == shard, jnp.broadcast_to(rows[k : k + 1, :], (shards, dim)), 0.0)
        total = total + mm(spread.astype(BF), (lane == local + k * part).astype(F32).astype(BF))
    return total


def grad_down_kernel(s, widths, dm, act0, act1, keep, send, *, shards, steps):
    n, width = act0.shape[0], keep.shape[2]
    rows = dm.shape[1] // shards // 2
    full = (mm_tn(dm[:n, :], act0[:, :width]) + mm_tn(dm[n:, :], act1[:, :width])).astype(BF)
    for j in range(2 * shards):
        place(s, SIDES, steps, keep, send, j // 2, j % 2, slice(None), full[j * rows : (j + 1) * rows])


def grad_down(s, dm, act0, act1, shards, steps):
    dim = dm.shape[1]
    part = shaped((shards, dim // shards // 2, act0.shape[1] - dim))
    return call(
        functools.partial(grad_down_kernel, shards=shards, steps=steps), "grad_down", 10, [part, part], [],
        s, dm, act0, act1, micros=4,
    )


def grad_up_kernel(s, widths, a0, a1, *refs, shards, steps):
    d0, d1, (four, bup, keep, send) = refs[:3], refs[3:6], refs[6:]
    size, half = keep.shape[1], keep.shape[2]
    wide = d0[0].shape[1]
    hidden = 2 * wide
    first = hidden // 2
    cols = hidden // shards
    rows = 2 * half // shards
    per = shards // 4
    tiny = tiny_rows(four[...], shards, half)
    at = lax.broadcasted_iota(jnp.int32, (2 * size - half - rows, half), 0)

    def put(index, part, at, value):
        place(s, SIDES + 4, steps, keep, send, index, part, slice(at, at + value.shape[0]), value)

    h = slice(first + half, first + 2 * half)
    out = (mm_tn(d0[2][...], a0[:, h]) + mm_tn(d1[2][...], a1[:, h])).astype(BF)
    h = slice(first, first + half)
    for k in range(0, shards, per):
        side, first_col = k * cols // wide, k * cols % wide
        span = slice(first_col, first_col + per * cols)
        full = (mm_tn(a0[:, h], d0[side][:, span]) + mm_tn(a1[:, h], d1[side][:, span])).astype(BF)
        for j in range(per):
            put(k + j, 0, 0, full[:size, j * cols : (j + 1) * cols])
            put(k + j, 1, 0, full[size:, j * cols : (j + 1) * cols])
            put(k + j, 1, half - size, out[(k + j) * rows : (k + j + 1) * rows])
            both = jnp.where(at == 0, tiny[k + j : k + j + 1], 0.0)
            both = both + jnp.where(at == 1, bup[:, (k + j) * cols : (k + j + 1) * cols], 0.0)
            put(k + j, 1, half - size + rows, both.astype(BF))


def grad_up(s, mine, got, dp0, dp1, four, bup, shards, steps):
    half = got.shape[1] - mine.shape[1]
    dim = 2 * half
    part = shaped((shards, (half + dim // shards + TINY_UP) // 2, half))
    return call(
        functools.partial(grad_up_kernel, shards=shards, steps=steps), "grad_up", 10,
        [part, part], [], s, mine, got, *dp0, *dp1, four, bup, micros=5,
    )


def got_rows(owns):
    return owns[0].shape[0] // 5


def last_of(ref, step, n, block, dim):
    wide = ref.shape[1]
    blocks = [
        ref[5 * n + k * block : 5 * n + (k + 1) * block, :] for k in range(step * dim // wide, (step + 1) * dim // wide)
    ]
    return jnp.concatenate(blocks, axis=1)


def d_of(owns, gots, step, n):
    if step == 0:
        return jnp.concatenate([own[4 * n : 5 * n, :] for own in owns], axis=1)
    mine, theirs = slice((step - 1) * n, step * n), slice((step + 1) * n, (step + 2) * n)
    return jnp.concatenate(
        [(own[mine, :].astype(F32) + got[theirs, :].astype(F32)).astype(BF) for own, got in zip(owns, gots)], axis=1
    )


def grad_qkv_kernel(
    s, widths, *refs, shards, steps
):
    groups = (len(refs) - 6) // 2
    owns, gots = refs[:groups], refs[groups : 2 * groups]
    h_own, other, norms, sums, keep, send = refs[-6:]
    n, half = got_rows(owns), h_own.shape[1]
    block = n // 2
    dim = 2 * half
    h = slice(other.shape[1] - half, other.shape[1])
    size = 3 * dim // shards // 2

    def put(k, at, value):
        place(s, SIDES + 8, steps, keep, send, k // 2, k % 2, slice(at, at + value.shape[0]), value)

    for step in range(3):
        d_own, d_got = d_of(owns, gots, step, n), d_of(gots, owns, step, n)
        full = mm_tn(d_own, h_own[:n, :]) + mm_tn(d_got, other[:n, h])
        last_own, last_got = (last_of(refs[1], step, n, block, dim) for refs in (owns, gots))
        full = full + mm_tn(last_own, h_own[n:, :]) + mm_tn(last_got, other[n:, h])
        full = full.astype(BF)
        first = step * dim
        for k in range(first // size, (first + dim + size - 1) // size):
            lo, hi = max(first, k * size), min(first + dim, (k + 1) * size)
            put(k, lo - k * size, full[lo - first : hi - first])
    four = jnp.concatenate([norms[...], sums[0:1, :], sums[2:3, :]], axis=0)
    tiny = tiny_rows(four, shards, half)
    at = lax.broadcasted_iota(jnp.int32, (TINY_QKV, half), 0)
    for k in range(2 * shards):
        put(k, size, jnp.where(at == 0, tiny[k // 2 : k // 2 + 1], 0.0).astype(BF))


def grad_qkv(s, owns, gots, h_own, other, norms, sums, shards, steps):
    half = h_own.shape[1]
    dim = 2 * half
    part = shaped((shards, 3 * dim // shards // 2 + TINY_QKV, half))
    return call(
        functools.partial(grad_qkv_kernel, shards=shards, steps=steps), "grad_qkv", 12, [part, part], [],
        s, *owns, *gots, h_own, other, norms, sums, micros=4,
    )


def qkv_bwd_kernel(
    s, widths, *refs
):
    groups = (len(refs) - 14) // 2
    owns, gots = refs[:groups], refs[groups : 2 * groups]
    x_got, gain, dmid, patches, w_hbm, dx0, dx1, dx2, norms, sums, acc, x_own, w, sems = refs[-14:]
    block, dim = x_got.shape
    n = 2 * block
    spans = [slice(k * dim, (k + 1) * dim) for k in range(3)]
    pairs = [(w_hbm.at[:, span], w.at[:, span]) for span in spans]
    stream = Stream(sems, *pairs, (patches.at[s[CHIP]], x_own.at[0]), (patches.at[2], x_own.at[1]))
    for k, cols in enumerate(spans):
        d = jnp.concatenate([d_of(owns, gots, k, n), last_of(owns[1], k, n, block, dim)], axis=0)
        sums[k : k + 1, :] = jnp.sum(d.astype(F32), axis=0, keepdims=True)
        stream.wait(k + 1)
        part = mm_nt(d, w[:, cols])
        if k == 0:
            acc[...] = part
        else:
            acc[...] += part
    dy = acc[...]
    stream.wait(5)
    x = jnp.concatenate([x_own[0], x_got[...], x_own[1]], axis=0).astype(F32)
    xhat, inv = norm_stats(x)
    dx = dmid[...] + norm_back(xhat, inv, line(gain), dy)
    dx0[...] = dx[:block]
    for k in range(2):
        dx1[k * block : (k + 1) * block, :] = dx[block:n, k * dim // 2 : (k + 1) * dim // 2].astype(BF)
    dx2[...] = dx[n:]
    norms[0:1, :] = jnp.sum(dy * xhat, axis=0, keepdims=True)
    norms[1:2, :] = jnp.sum(dy, axis=0, keepdims=True)


def qkv_bwd(s, owns, gots, patches, x_got, gain, dmid, w):
    images, block, dim = patches.shape
    return call(
        qkv_bwd_kernel, "qkv_bwd", 12,
        [
            in_hbm((block, dim), F32), shaped((2 * block, dim // 2)), in_hbm((block, dim), F32),
            shaped((2, dim), F32), shaped((3, dim), F32),
        ],
        [
            pltpu.VMEM((images * block, dim), F32), pltpu.VMEM((2, block, dim), BF), pltpu.VMEM(w.shape, BF),
            pltpu.SemaphoreType.DMA((5,)),
        ],
        s, *owns, *gots, x_got, gain, dmid, patches, w, micros=4, streamed=2,
    )


def finish_kernel(s, widths, both, both_got, down, down_got, up, out, qkv, wdown, *vectors, rows_up, size, parts):
    def sorted_of(value, other):
        cut = value.shape[0] // 2
        mine = [value[:cut].astype(F32), value[cut:].astype(F32)]
        theirs = [other[:cut].astype(F32), other[cut:].astype(F32)]
        second = s[CHIP] > 0
        pairs = [[jnp.where(second, v[1], v[0]), jnp.where(second, v[0], v[1])] for v in (mine, theirs)]
        swap_cores = s[CORE] > 0
        return [
            [jnp.where(swap_cores, b, a) for a, b in zip(*pairs)],
            [jnp.where(swap_cores, a, b) for a, b in zip(*pairs)],
        ]

    cores = sorted_of(both, both_got)
    rows = [jnp.concatenate([first[:rows_up], second[:rows_up]], axis=0) for first, second in cores]
    half = up.shape[0] // 2
    wide = out.shape[0]
    up[:half, :] = rows[0][:half]
    up[half:, :] = rows[1][:half]
    out[...] = jnp.concatenate([r[half : half + wide] for r in rows], axis=1)
    pieces = [jnp.concatenate([f[rows_up : rows_up + size], g[rows_up : rows_up + size]], axis=0) for f, g in cores]
    qkv[...] = jnp.concatenate(pieces, axis=1)
    two = rows[0][half + wide : half + wide + 8] + rows[1][half + wide : half + wide + 8]
    one = cores[0][0][rows_up + size : rows_up + size + 8] + cores[1][0][rows_up + size : rows_up + size + 8]
    for ref, (source, row, at) in zip(vectors, parts):
        ref[...] = (one, two)[source][row : row + 1, at : at + ref.shape[0]].reshape(ref.shape[0])
    cores = sorted_of(down, down_got)
    wdown[...] = jnp.concatenate([jnp.concatenate(pair, axis=0) for pair in cores], axis=1)


def finish(s, both, both_got, down, down_got, rows_up, dim, hidden, shards):
    part, wide = dim // shards, hidden // shards
    size = 3 * dim // shards // 2
    parts = [(0, 0, k * part) for k in range(4)]
    parts += [(1, 0, 2 * part), (1, 0, 0), (1, 0, part), (1, 1, 0), (1, 0, 3 * part)]
    widths = [part] * 7 + [wide, part]
    return call(
        functools.partial(finish_kernel, rows_up=rows_up, size=size, parts=parts), "finish", 20,
        [in_hbm((dim, wide), F32), in_hbm((part, dim), F32), in_hbm((3 * part, dim), F32), in_hbm((part, hidden), F32)]
        + [in_hbm((width,), F32) for width in widths],
        [], s, both, both_got, down, down_got, micros=3,
    )


X, NEAR, FAR = (1, 1), (2, 2), (4, 4)


def plans(n_img):
    if n_img == 8:
        return (
            ([X, NEAR, "y", FAR], ["y", NEAR, X, FAR]),
            ([X, NEAR, "y", FAR], ["y", NEAR, X, FAR]),
            ([X, "y", NEAR, FAR], ["y", X, NEAR, FAR]),
        )
    bits = [1 << k for k in reversed(range(n_img.bit_length() - 1))]
    order = [(bit, bit) for bit in bits] + ["y"]
    return ((order, order),) * 3


def hop(value, step0, step1):
    seq, img = lax.axis_size("seq"), lax.axis_size("img")
    pairs = []
    for s in range(seq):
        step = step1 if s % 2 else step0
        for i in range(img):
            to = (s ^ 2, i) if step == "y" else (s, i ^ (step if isinstance(step, int) else step[0]))
            pairs.append((s * img + i, to[0] * img + to[1]))
    return lax.ppermute(value, ("seq", "img"), pairs)


def side_here(step):
    if step == "y":
        return lax.axis_index("seq") // 2
    bits = lax.axis_index("img") & step[1]
    value = 0
    for k in range(step[1].bit_length()):
        value = value ^ ((bits >> k) & 1)
    return value


def sides_here(steps):
    core = lax.axis_index("seq") % 2
    return [jnp.where(core == 0, side_here(a), side_here(b)) for a, b in zip(*steps)]


def plus(kept, got):
    return (kept.astype(F32) + got.astype(F32)).astype(BF)


class Sum:
    def __init__(self, s, base, steps, keep, send):
        self.s, self.base, self.steps, self.sides, self.at = s, base, steps, sides_here(steps), 0
        self.keep = keep.reshape(-1, keep.shape[-1])
        self.got = self.go(send.reshape(self.keep.shape))

    def go(self, value):
        self.at += 1
        return hop(value, self.steps[0][self.at - 1], self.steps[1][self.at - 1])

    def step(self):
        shape = (2, self.got.shape[0] // 2, self.got.shape[1])
        keep, got = self.keep.reshape(shape), self.got.reshape(shape)
        if shape[1] % 16 == 0:
            self.keep, send = halve(self.s, keep, got, self.base + self.at)
        else:
            mine = self.sides[self.at]
            self.keep = plus(pick(keep, mine, 0), pick(got, mine, 0))
            send = plus(pick(keep, 1 - mine, 0), pick(got, 1 - mine, 0))
        self.got = self.go(send)

    def steps_left(self, most):
        while len(self.steps[0]) - self.at > most:
            self.step()

    def last(self):
        return add(self.s, self.keep, self.got) if self.keep.shape[0] % 16 == 0 else plus(self.keep, self.got)


def finish_plain(core, chip, both, both_got, down, down_got, rows_up, dim, hidden, shards):
    part, wide, half = dim // shards, hidden // shards, dim // 2
    size = 3 * dim // shards // 2

    def sorted_of(value, other):
        pairs = []
        for v in (value, other):
            a, b = jnp.split(v.astype(F32), 2)
            pairs.append([jnp.where(chip == 0, a, b), jnp.where(chip == 0, b, a)])
        mine, theirs = pairs
        first = [jnp.where(core == 0, a, b) for a, b in zip(mine, theirs)]
        return [first, [jnp.where(core == 0, b, a) for a, b in zip(mine, theirs)]]

    cores = sorted_of(both, both_got)
    rows = [jnp.concatenate([f[:rows_up], g[:rows_up]]) for f, g in cores]
    up = jnp.concatenate([r[:wide].T for r in rows])
    out = jnp.concatenate([r[wide : wide + part] for r in rows], axis=1)
    pieces = [jnp.concatenate([f[rows_up : rows_up + size], g[rows_up : rows_up + size]]) for f, g in cores]
    two = sum(r[wide + part :] for r in rows).reshape(-1)
    one = sum(f[rows_up + size :] for f, _ in cores).reshape(-1)
    down = jnp.concatenate([jnp.concatenate(pair) for pair in sorted_of(down, down_got)], axis=1)
    first = [one[k * part : (k + 1) * part] for k in range(4)]
    second = [two[k * part : (k + 1) * part] for k in (2, 0, 1)]
    last = [two[4 * part : 4 * part + wide], two[3 * part : 4 * part]]
    return [up, out, jnp.concatenate(pieces, axis=1), down, *first, *second, *last]


class Book:
    def __init__(self, s, codebook):
        n_img = lax.axis_size("img")
        bits = [1 << k for k in range(n_img.bit_length() - 1)]
        masks = [1, 2, 6] if n_img == 8 else bits
        self.orders = list(zip(masks[1:], [1, "y", *masks[3:]]))
        self.ends = ((1, masks[1]), ("y", masks[2]))
        self.s, self.value = s, codebook

    def stack(self, *parts):
        return stack(self.s, *parts) if sum(part.size for part in parts) < 1 << 21 else jnp.concatenate(parts)

    def start(self):
        self.got = hop(self.value, *self.orders.pop(0))

    def double(self):
        self.value = self.stack(self.value, self.got)

    def spread(self):
        self.beside, self.across = hop(self.value, *self.ends[0]), hop(self.value, *self.ends[1])
        self.other = [swap(self.value, "seq", 1)]

    def corner(self):
        if self.value.size < 1 << 21:
            parts = cut(self.s, self.across, self.beside)
        else:
            half = self.value.shape[0] // 2
            parts = self.across[:half], self.beside[half:]
        self.corners = hop(parts[0], *self.ends[0]), hop(parts[1], *self.ends[1])

    def finish(self):
        rest = self.stack(self.beside, self.across, *self.corners)
        return [self.value, rest, *self.other, swap(rest, "seq", 1)]


def shards(
    patches,
    widths,
    ln1_gain,
    ln1_bias,
    w_qkv,
    b_query,
    b_value,
    w_out,
    b_out,
    ln2_gain,
    ln2_bias,
    w_up,
    b_up,
    w_down,
    b_down,
    codebook,
    cotangent,
):
    images, block, dim = patches.shape
    hidden = w_up.shape[1]
    n_img = lax.axis_size("img")
    me = lax.axis_index("seq")
    chip, core = me // 2, me % 2
    half, main = dim // 2, 2 * block
    fits = codebook.shape[0] * n_img * lax.axis_size("seq") <= 4096
    aligned = n_img == 8 and dim // n_img // 2 % 16 == 0
    steps_down, steps_up, steps_qkv = plans(n_img)
    sides = sides_here(steps_down) + sides_here(steps_up) + sides_here(steps_qkv)
    s = (jnp.stack([me, core, chip, *sides]).astype(jnp.int32), widths)

    Order.token = jnp.zeros((8, 128), F32)
    book = Book(s, codebook)
    book.start()
    x_got = swap(pick(patches, 1 - chip, 0), "seq", 2)
    ln1 = (ln1_gain, ln1_bias, b_query, b_value, w_qkv)
    while book.orders:
        book.double()
        book.start()
    q_main, q_last, *kvs, h_mine, h_send = qkv_fwd(s, patches, x_got, *ln1)
    kvs_other = [swap(kv, "seq", 1) for kv in kvs]
    kv_y = swap(kvs[2], "seq", 2)
    book.double()
    book.spread()
    kvs_main = kvs[:2] + kvs_other[:2]
    att_main = attention_fwd(s, q_main, kvs_main, False, block)
    cot_got = swap(pick(cotangent, 1 - chip, 0), "seq", 2)
    kvs_last = [kvs[2], kv_y, kvs_other[2], swap(kv_y, "seq", 1)]
    att_last = attention_fwd(s, q_last, kvs_last, True, block)
    book.corner()
    mid, h2, enc, slope0, send = mlp_first(
        s, patches, x_got, att_main, att_last, h_send, b_out, ln2_gain, ln2_bias, b_up, b_down, w_out, w_up,
        w_down,
    )
    got = swap(send, "seq", 1)
    pieces = book.finish()
    enc, slope1, mine = mlp_second(s, h2, enc, att_main, att_last, b_up, w_up, w_down)
    if fits:
        mix0, mix1, mix2, loss, denc, dmlp = quantizer(s, enc, cotangent, cot_got, pieces)
    else:
        cots = jnp.concatenate([pick(cotangent, chip, 0), cot_got, cotangent[2]])
        mix0, mix1, mix2, loss, denc, dmlp = quantizer_plain(s, enc, cots, jnp.concatenate(pieces))
    mix1 = swap(mix1, "seq", 2)

    def split(full, steps):
        rows, cols = full.shape[-2:]
        full = full.reshape([2] * len(steps[0]) + [rows // 2, cols])
        side = sides_here(steps)[0]
        return pick(full, side, 0), pick(full, 1 - side, 0)

    def lines_of(count, *vectors):
        rows = jnp.concatenate([v.reshape(n_img, -1) for v in vectors], axis=1).astype(BF)
        return jnp.pad(rows, ((0, 0), (0, count * half - rows.shape[1]))).reshape(n_img, count, half)

    dmlp_got = swap(dmlp, "seq", 1)
    both = jnp.concatenate([mine, got[:, : mine.shape[1]]])
    if aligned:
        dmlp_both = stack(s, dmlp, dmlp_got, there=(got,))
        keep, send = grad_down(s, dmlp_both, mine, got, n_img, steps_down)
    else:
        full = mm_tn(jnp.concatenate([dmlp, dmlp_got]), both[:, : hidden // 2]).astype(BF)
        keep, send = split(full.reshape(n_img, -1, hidden // 2), steps_down)
    down = Sum(s, 0, steps_down, keep, send)
    *dp, dmid, datt, rows_two, sum_bup = mlp_bwd(s, dmlp, denc, mid, ln2_gain, (slope0, slope1), w_down, w_up, w_out)
    dp_got = [swap(part, "seq", 1) for part in dp]
    quantized, token_loss = assemble(s, (mix0, mix1, mix2), loss)
    keep_last, send_last, dq_last = attention_bwd(s, q_last, kvs_last, datt, main, True, block, ())
    got_last = swap(send_last, "seq", 1)
    keep_last, send_last = fold(s, keep_last, got_last)
    got_last = swap(send_last, "seq", 2)
    if aligned:
        keep, send = grad_up(s, mine, got, dp, dp_got, rows_two, sum_bup, n_img, steps_up)
    else:
        dps = jnp.concatenate([jnp.concatenate(dp, axis=1), jnp.concatenate(dp_got, axis=1)])
        up = mm_tn(both[:, hidden // 2 : hidden // 2 + half], dps[:, :hidden]).astype(BF)
        up = up.reshape(half, n_img, -1).transpose(1, 2, 0)
        out = mm_tn(dps[:, hidden:], both[:, hidden // 2 + half :]).astype(BF).reshape(n_img, -1, half)
        tiny = lines_of(TINY_UP, rows_two[0], rows_two[1], rows_two[2], rows_two[3], sum_bup[0])
        keep, send = split(jnp.concatenate([up, out, tiny], axis=1), steps_up)
    up = Sum(s, len(steps_down[0]), steps_up, keep, send)
    down.step()
    d_main, d_got = [], []
    for pairs, more in (((0, 1), ()), ((2, 3), (dq_last, keep_last, got_last)), ((4, 5), ())):
        d_main += attention_bwd(s, q_main, kvs_main, datt, 0, False, block, pairs, more)
        d_got.append(swap(d_main[-1], "seq", 1))
    dx0, dx1, dx2, norms, sums = qkv_bwd(s, d_main, d_got, patches, x_got, ln1_gain, dmid, w_qkv)
    up.step()
    down.step()
    if aligned:
        keep, send = grad_qkv(
            s, d_main, d_got, h_mine, got, norms, sums, n_img, steps_qkv
        )
    else:
        n = main

        def assembled(owns, gots):
            rows = [jnp.concatenate([own[4 * n : 5 * n] for own in owns], axis=1)]
            for k in (0, 1):
                mine, theirs = slice(k * n, (k + 1) * n), slice((k + 2) * n, (k + 3) * n)
                rows.append(jnp.concatenate([plus(own[mine], got[theirs]) for own, got in zip(owns, gots)], axis=1))
            last = owns[1][5 * n :].reshape(-1, block, owns[1].shape[1])
            return [jnp.concatenate(rows, axis=1), jnp.concatenate(list(last), axis=1)]

        d = jnp.concatenate(assembled(d_main, d_got) + assembled(d_got, d_main))
        h = jnp.concatenate([h_mine, got[:, -half:]])
        full = mm_tn(d, h).astype(BF).reshape(n_img, 2, -1, half)
        tiny = lines_of(TINY_QKV, norms[0], norms[1], sums[0], sums[2])
        full = jnp.concatenate([full, jnp.stack([tiny, tiny], axis=1)], axis=2)
        keep, send = split(full.reshape(n_img, -1, half), steps_qkv)
    qkv = Sum(s, 2 * len(steps_down[0]), steps_qkv, keep, send)

    down.steps_left(0)
    qkv.step()
    up.step()
    sum_down = down.last()
    down_other = swap(sum_down, "seq", 2)
    qkv.step()
    up.steps_left(0)
    qkv.steps_left(0)
    sum_up = up.last()
    up_other = swap(stack(s, sum_up, dx1) if aligned else jnp.concatenate([sum_up, dx1]), "seq", 2)
    sum_qkv = qkv.last()
    qkv_other = swap(sum_qkv, "seq", 2)
    down_both = stack(s, sum_down, down_other) if aligned else jnp.concatenate([sum_down, down_other])
    down_got = swap(down_both, "seq", 1)
    grad_input = assemble_dx(s, dx0, up_other, dx2)
    if aligned:
        both = collect(s, sum_up, sum_qkv, up_other, qkv_other)
    else:
        both = jnp.concatenate([sum_up, sum_qkv, up_other[: sum_up.shape[0]], qkv_other])
    both_got = swap(both, "seq", 1)
    rows_up = sum_up.shape[0]
    if aligned:
        weights = finish(s, both, both_got, down_both, down_got, rows_up, dim, hidden, n_img)
    else:
        weights = finish_plain(core, chip, both, both_got, down_both, down_got, rows_up, dim, hidden, n_img)
    g_up, g_out, g_qkv, g_down, g_gain1, g_shift1, g_bq, g_bv, g_bout, g_gain2, g_shift2, g_bup, g_bdown = weights

    return (
        quantized,
        token_loss,
        grad_input,
        g_gain1,
        g_shift1,
        g_qkv.T,
        g_bq,
        g_bv,
        g_out.T,
        g_bout,
        g_gain2,
        g_shift2,
        g_up,
        g_bup,
        g_down.T,
        g_bdown,
    )


def solution(mesh):
    return jax.shard_map(
        shards,
        mesh=mesh,
        in_specs=(
            P("img", "seq", None),
            P("img"),
            P(),
            P(),
            P(),
            P(),
            P(),
            P(),
            P(),
            P(),
            P(),
            P(),
            P(),
            P(),
            P(),
            P(("seq", "img"), None),
            P("img", "seq", None),
        ),
        out_specs=(
            P("img", "seq", None),
            P("img", "seq"),
            P("img", "seq", None),
            P("img"),
            P("img"),
            P(None, "img"),
            P("img"),
            P("img"),
            P(None, "img"),
            P("img"),
            P("img"),
            P("img"),
            P(None, "img"),
            P("img"),
            P(None, "img"),
            P("img"),
        ),
        check_vma=False,
    )
```

```python
import functools

import jax
import jax.numpy as jnp
from jax import lax
from jax.experimental import pallas as pl
from jax.experimental.pallas import tpu as pltpu
from jax.sharding import PartitionSpec as P

HEAD_DIM = 64
GRID_H = 16
EPS_NORM = 1e-06
COMMIT = 16.0
BF = jnp.bfloat16
F32 = jnp.float32
MIB = 1024 * 1024
MASKED = -1000000000.0


def mm(a, b):
    return jnp.dot(a, b, preferred_element_type=F32)


def mm_nt(a, b):
    return lax.dot_general(a, b, (((1,), (1,)), ((), ())), preferred_element_type=F32)


def mm_tn(a, b):
    return lax.dot_general(a, b, (((0,), (0,)), ((), ())), preferred_element_type=F32)


def swap(value, axis, bit):
    count = lax.axis_size(axis)
    return lax.ppermute(value, axis, [(i, i ^ bit) for i in range(count)])


def pick(value, index, axis):
    return lax.dynamic_index_in_dim(value, index, axis, keepdims=False)


def after(value, *others):
    return lax.optimization_barrier((value, *others))[0]


def parity(number):
    return bin(number).count("1") % 2


def shaped(shape, dtype=BF):
    return jax.ShapeDtypeStruct(tuple(shape), dtype)


def in_hbm(shape, dtype=BF):
    return pltpu.HBM(tuple(shape), dtype)


class Order:
    token = None


def call(kernel, name, mib, out_shape, scratch, s, *args, micros, streamed=0, by_hand=()):
    vm, hbm = pl.BlockSpec(memory_space=pltpu.VMEM), pl.BlockSpec(memory_space=pl.ANY)
    direct, count = len(args) - streamed, len(args) + len(out_shape)
    args = [
        pltpu.with_memory_space_constraint(arg, pltpu.HBM) if arg.ndim == 1 or (k >= direct and name != "stack") else arg
        for k, arg in enumerate(args)
    ]

    def body(limits, token, *refs):
        kernel(Place(), limits, *refs[:count], *refs[count + 1 :])
        refs[count][...] = token[...]

    out = pl.pallas_call(
        body,
        in_specs=[vm] * (direct + 2) + [hbm] * streamed,
        out_specs=[hbm if out in by_hand else vm for out in range(len(out_shape))] + [vm],
        out_shape=[*out_shape, shaped((8, 128), F32)],
        scratch_shapes=scratch,
        compiler_params=pltpu.CompilerParams(vmem_limit_bytes=mib * MIB),
        cost_estimate=pl.CostEstimate(flops=int(micros * 2e8), bytes_accessed=0, transcendentals=0),
        name=name,
    )(s, Order.token, *args)
    Order.token = out[-1]
    return out[:-1]


class Stream:
    def __init__(self, sems, *pairs, ahead=3):
        self.copies = [pltpu.make_async_copy(a, b, sems.at[k]) for k, (a, b) in enumerate(pairs)]
        self.done, self.begun = 0, 0
        self.start(ahead)

    def start(self, count):
        while self.begun < min(count, len(self.copies)):
            self.copies[self.begun].start()
            self.begun += 1

    def wait(self, count):
        while self.done < count:
            self.copies[self.done].wait()
            self.done += 1
            self.start(self.begun + 1)


ME, CORE, CHIP, SIDES = range(4)
X, NEAR, FAR = (1, 1), (2, 2), (4, 4)


def plans(n_img):
    if n_img == 8:
        return (
            ([X, NEAR, "y", FAR], ["y", NEAR, X, FAR]),
            ([X, NEAR, "y", FAR], ["y", NEAR, X, FAR]),
            ([X, "y", NEAR, FAR], ["y", X, NEAR, FAR]),
        )
    bits = [1 << k for k in reversed(range(n_img.bit_length() - 1))]
    order = [(bit, bit) for bit in bits] + ["y"]
    return ((order, order),) * 3


def side_here(step):
    if step == "y":
        return lax.axis_index("seq") // 2
    bits = lax.axis_index("img") & step[1]
    value = 0
    for k in range(step[1].bit_length()):
        value = value ^ ((bits >> k) & 1)
    return value


def sides_here(steps):
    core = lax.axis_index("seq") % 2
    return [jnp.where(core == 0, side_here(a), side_here(b)) for a, b in zip(*steps)]


class Place:
    def __getitem__(self, what):
        me = lax.axis_index("seq")
        if what < SIDES:
            return (me, me % 2, me // 2)[what]
        steps = plans(lax.axis_size("img"))
        chain, step = divmod(what - SIDES, len(steps[0][0]))
        return sides_here([order[step : step + 1] for order in steps[chain]])[0]


def line(ref, start=0, size=None):
    size = ref.shape[0] if size is None else size
    return ref[start : start + size].reshape(1, size)


def norm_stats(x):
    center = x - jnp.mean(x, axis=-1, keepdims=True)
    spread = jnp.mean(center * center, axis=-1, keepdims=True)
    inv = lax.rsqrt(spread + EPS_NORM)
    return center * inv, inv


def norm_back(xhat, inv, gain, dy):
    dxhat = dy * gain
    return inv * (
        dxhat - jnp.mean(dxhat, axis=-1, keepdims=True) - xhat * jnp.mean(dxhat * xhat, axis=-1, keepdims=True)
    )


def spots(index, block, me):
    shift = block.bit_length() - 1
    assert block == 1 << shift
    place = index >> shift
    mask = ((place & 1) << 1) | (place >> 1)
    return ((me ^ mask) << shift) | (index & (block - 1))


def limit_of(s, widths, last):
    row = 1 if last else 0
    return widths[row : row + 1, 0:1]


def side_of(ref, side, width):
    return ref[:, pl.ds(pl.multiple_of(side * width, 128), width)]


def qkv_kernel(
    s, widths, got, gain, shift, bq, bv, w, patches, q_main, q_last, kv0, kv1, kv2, mine, send, h, x_own, sems
):
    half, dim = mine.shape[1], w.shape[0]
    block = got.shape[0]
    stream = Stream(sems, (patches.at[s[CHIP]], x_own.at[0]), (patches.at[2], x_own.at[1]))
    stream.wait(2)
    for k, x in enumerate((x_own[0], got[...], x_own[1])):
        xhat, _ = norm_stats(x.astype(F32))
        h[k * block : (k + 1) * block, :] = (xhat * line(gain) + line(shift)).astype(BF)
    mine[...] = side_of(h, s[CORE], half)
    send[...] = side_of(h, 1 - s[CORE], half)
    keys = mm(h[...], w[:, dim : 2 * dim]).astype(BF)
    values = (mm(h[...], w[:, 2 * dim :]) + line(bv)).astype(BF)
    for k, out in enumerate((kv0, kv1, kv2)):
        out[:, :dim] = keys[k * block : (k + 1) * block]
        out[:, dim:] = values[k * block : (k + 1) * block]
    q = (mm(h[...], w[:, :dim]) + line(bq)).astype(BF)
    q_main[...] = q[: 2 * block]
    q_last[...] = q[2 * block :]


def qkv_fwd(s, patches, got, gain, shift, bq, bv, w):
    images, block, dim = patches.shape
    n, half = images * block, dim // 2
    return call(
        qkv_kernel, "qkv_fwd", 8,
        [
            shaped((2 * block, dim)), shaped((block, dim)), *[shaped((block, 2 * dim))] * 3,
            in_hbm((n, half)), shaped((n, half)),
        ],
        [pltpu.VMEM((n, dim), BF), pltpu.VMEM((2, block, dim), BF), pltpu.SemaphoreType.DMA((2,))],
        s, got, gain, shift, bq, bv, w, patches, micros=3, streamed=1,
    )


def two_heads(value):
    left = lax.broadcasted_iota(jnp.int32, value.shape, 1) < HEAD_DIM
    zero = jnp.zeros_like(value)
    return jnp.concatenate([jnp.where(left, value, zero), jnp.where(left, zero, value)], axis=0)


def one_pair(value):
    n = value.shape[0] // 2
    left = lax.broadcasted_iota(jnp.int32, (n, value.shape[1]), 1) < HEAD_DIM
    return jnp.where(left, value[:n], value[n:])


def rows_of(refs, lanes):
    return jnp.concatenate([ref[:, lanes] for ref in refs], axis=0)


def att_fwd_kernel(s, widths, q, *refs, last, block):
    kvs, o = refs[:-1], refs[-1]
    dim = q.shape[1]
    m = sum(kv.shape[0] for kv in kvs)
    index = lax.broadcasted_iota(jnp.int32, (1, m), 1)
    ok = spots(index, block, s[ME]) < limit_of(s, widths, last)
    for p in range(dim // 128):
        at, av = slice(p * 128, (p + 1) * 128), slice(dim + p * 128, dim + (p + 1) * 128)
        k, v = rows_of(kvs, at), rows_of(kvs, av)
        raw = mm_nt(two_heads(q[:, at]), k) * (HEAD_DIM**-0.5)
        scores = jnp.where(ok, raw, MASKED)
        expo = jnp.exp(scores - jnp.max(scores, axis=1, keepdims=True))
        probs = expo * (1.0 / jnp.sum(expo, axis=1, keepdims=True))
        o[:, at] = one_pair(mm(probs.astype(BF), v)).astype(BF)


def attention_fwd(s, q, kvs, last, block):
    return call(
        functools.partial(att_fwd_kernel, last=last, block=block), "attention_fwd", 10, [shaped(q.shape)], [],
        s, q, *kvs, micros=5,
    )[0]


def att_bwd_kernel(s, widths, q, do, *refs, last, block, first, pairs, more):
    n, dim = q.shape
    if pairs:
        kvs, out = refs[: len(refs) - 1 - more], refs[-1]
        m = sum(kv.shape[0] for kv in kvs)
        parts = [out.at[k * m // 2 : (k + 1) * m // 2, :] for k in range(4)]
        dq = out.at[2 * m : 2 * m + n, :]
        if more:
            dq_last, keep_last, got_last = refs[-4:-1]
            rows, wide = dq_last.shape[0], out.shape[1]
            parts_last = [dq_last[...]] + [
                (keep_last[k].astype(F32) + got_last[k].astype(F32)).astype(BF) for k in range(2)
            ]
            for k in range(3 * dim // wide):
                part, at = parts_last[k * wide // dim], k * wide % dim
                out[2 * m + n + k * rows : 2 * m + n + (k + 1) * rows, :] = part[:, at : at + wide]
    else:
        kvs, (keep, send, dq) = refs[:-3], refs[-3:]
        m = sum(kv.shape[0] for kv in kvs)
        parts = [keep.at[0], keep.at[1], send.at[0], send.at[1]]
    index = lax.broadcasted_iota(jnp.int32, (m, 1), 0)
    ok = spots(index, block, s[ME]) < limit_of(s, widths, last)
    for p in pairs or range(dim // 128):
        at, av = slice(p * 128, (p + 1) * 128), slice(dim + p * 128, dim + (p + 1) * 128)
        to = slice((p - pairs[0]) * 128, (p - pairs[0] + 1) * 128) if pairs else at
        k, v = rows_of(kvs, at), rows_of(kvs, av)
        q2, do2 = two_heads(q[:, at]), two_heads(do[first : first + n, at])
        raw = mm_nt(k, q2) * (HEAD_DIM**-0.5)
        scores = jnp.where(ok, raw, MASKED)
        expo = jnp.exp(scores - jnp.max(scores, axis=0, keepdims=True))
        probs = expo * (1.0 / jnp.sum(expo, axis=0, keepdims=True))
        dv = mm(probs.astype(BF), do2).astype(BF)
        dp = mm_nt(v, do2)
        inner = jnp.sum(probs * dp, axis=0, keepdims=True)
        ds = (probs * (dp - inner) * (HEAD_DIM**-0.5)).astype(BF)
        dk = mm(ds, q2).astype(BF)
        dq[:, to] = one_pair(mm_tn(ds, k)).astype(BF)
        for ref, part in zip(parts, (dk[: m // 2], dv[: m // 2], dk[m // 2 :], dv[m // 2 :])):
            ref[:, to] = part


def attention_bwd(s, q, kvs, do, first, last, block, pairs, more=()):
    n, dim = q.shape
    m = sum(kv.shape[0] for kv in kvs)
    return call(
        functools.partial(att_bwd_kernel, last=last, block=block, first=first, pairs=pairs, more=len(more)),
        "attention_bwd", 12,
        [shaped((2 * m + n + (len(more) and 3 * dim // len(pairs)), 128 * len(pairs)))] if pairs else [shaped((2, m // 2, dim)), shaped((2, m // 2, dim)), shaped((n, dim))],
        [], s, q, do, *kvs, *more, micros=4,
    )


def fold_kernel(s, widths, keep, got, keep_out, send_out):
    block = keep_out.shape[1]
    for k in range(2):
        total = (keep[k].astype(F32) + got[k].astype(F32)).astype(BF)
        keep_out[k] = total[:block]
        send_out[k] = total[block:]


def fold(s, keep, got):
    part = shaped((2, keep.shape[1] // 2, keep.shape[2]))
    return call(fold_kernel, "fold", 4, [part, part], [], s, keep, got, micros=0.5)


def stack_kernel(s, widths, *refs, count):
    at = 0
    for ref in refs[:count]:
        refs[-1][at : at + ref.shape[0], :] = ref[...]
        at += ref.shape[0]


def stack(s, *parts, there=()):
    shape = (sum(part.shape[0] for part in parts), parts[0].shape[1])
    kernel = functools.partial(stack_kernel, count=len(parts))
    return call(kernel, "stack", 8, [shaped(shape)], [], s, *parts, *there, micros=0.5, streamed=len(there))[0]


def cut_kernel(s, widths, a, b, first, second):
    rows = first.shape[0]
    first[...] = a[:rows, :]
    second[...] = b[rows:, :]


def cut(s, a, b):
    part = shaped((a.shape[0] // 2, a.shape[1]))
    return call(cut_kernel, "cut", 4, [part, part], [], s, a, b, micros=0.3)


def collect_kernel(s, widths, up, qkv, up_other, qkv_other, out):
    at = 0
    for ref in (up, qkv, up_other, qkv_other):
        rows = qkv.shape[0] if ref is qkv_other else ref.shape[0]
        rows = up.shape[0] if ref is up_other else rows
        out[at : at + rows, :] = ref[:rows, :]
        at += rows


def collect(s, up, qkv, up_other, qkv_other):
    shape = (2 * (up.shape[0] + qkv.shape[0]), up.shape[1])
    return call(collect_kernel, "collect", 6, [shaped(shape)], [], s, up, qkv, up_other, qkv_other, micros=0.5)[0]


def add_kernel(s, widths, keep, got, out):
    out[...] = (keep[...].astype(F32) + got[...].astype(F32)).astype(BF)


def add(s, keep, got):
    return call(add_kernel, "add", 4, [shaped(keep.shape)], [], s, keep, got, micros=0.5)[0]


def sorted_images(s, out, own, back, last):
    first = s[CHIP] == 0
    out[0] = jnp.where(first, own, back)
    out[1] = jnp.where(first, back, own)
    out[2] = last


def assemble_kernel(s, widths, mix0, mix1, mix2, loss, mix, losses):
    block = mix0.shape[0]
    sorted_images(s, mix, mix0[...], mix1[:block, :], mix2[...])
    first = s[CHIP] == 0
    own = loss[0:1, :block]
    back = sum(mix1[block : block + 8, k * block : (k + 1) * block].astype(F32) for k in range(3))[0:1]
    losses[0:1, :] = jnp.where(first, own, back)
    losses[1:2, :] = jnp.where(first, back, own)
    losses[2:3, :] = loss[0:1, 2 * block :]


def assemble(s, mix, loss):
    block, dim = mix[0].shape
    return call(
        assemble_kernel, "assemble", 8, [in_hbm((3, block, dim)), in_hbm((3, block), F32)], [],
        s, *mix, loss, micros=1,
    )


def assemble_dx_kernel(s, widths, dx0, pack, dx2, dx):
    block = dx0.shape[0]
    first = pack.shape[0] - 2 * block
    back = jnp.concatenate([pack[first : first + block, :], pack[first + block :, :]], axis=1)
    sorted_images(s, dx, dx0[...], back.astype(F32), dx2[...])


def assemble_dx(s, *dx):
    block, dim = dx[0].shape
    return call(assemble_dx_kernel, "assemble_dx", 8, [in_hbm((3, block, dim), F32)], [], s, *dx, micros=1)[0]


def halve_kernel(s, widths, keep, got, keep_out, send_out, *, at):
    mine = s[SIDES + at]
    keep_out[...] = (keep[mine].astype(F32) + got[mine].astype(F32)).astype(BF)
    send_out[...] = (keep[1 - mine].astype(F32) + got[1 - mine].astype(F32)).astype(BF)


def halve(s, keep, got, at):
    part = shaped(keep.shape[1:])
    return call(functools.partial(halve_kernel, at=at), "halve", 8, [part, part], [], s, keep, got, micros=0.7)


def gelu_pair(x):
    z = jnp.abs(x) * (0.5**0.5)
    t = 1.0 / (1.0 + 0.3275911 * z)
    expo = jnp.exp(-0.5 * x * x)
    poly = t * (0.254829592 + t * (-0.284496736 + t * (1.421413741 + t * (-1.453152027 + t * 1.061405429))))
    tail = 0.5 * poly * expo
    cdf = jnp.where(x < 0.0, tail, 1.0 - tail)
    return x * cdf, cdf + x * (expo * 0.3989422804014327)


def mlp_tiles(side, h2, bup, wup, wdown, enc, act_ref, slope, tile):
    wide = slope.shape[1]
    for k in range(0, wide, tile):
        here, there = slice(k, k + tile), pl.ds(pl.multiple_of(side * wide + k, 128), tile)
        act, rate = gelu_pair(mm(h2[...], wup[:, there]) + bup[there].reshape(1, tile))
        act = act.astype(BF)
        act_ref[:, here] = act
        slope[:, here] = rate.astype(BF)
        enc[...] += mm(act, wdown[there, :])


def mlp_first_kernel(
    s, widths, got, att_main, att_last, h1, bout, gain, shift, bup, bdown, wout, wup, wdown, patches, mid, h2, enc, slope,
    send, x_own, sems, *, tile,
):
    dim = got.shape[1]
    half, wide = dim // 2, slope.shape[1]
    rows = att_main.shape[0]
    side = 1 - s[CORE]
    stream = Stream(sems, (patches.at[s[CHIP]], x_own.at[0]), (patches.at[2], x_own.at[1]))
    branch = mm(jnp.concatenate([att_main[...], att_last[...]], axis=0), wout[...])
    stream.wait(2)
    x = jnp.concatenate([x_own[0], got[...], x_own[1]], axis=0).astype(F32)
    middle = x + branch + line(bout)
    mid[...] = middle
    xhat, _ = norm_stats(middle)
    h2[...] = (xhat * line(gain) + line(shift)).astype(BF)
    enc[...] = middle + line(bdown)
    send[:, wide : wide + half] = side_of(h2, side, half)
    send[:rows, wide + half : wide + dim] = side_of(att_main, side, half)
    send[rows:, wide + half : wide + dim] = side_of(att_last, side, half)
    send[:, wide + dim :] = h1[...]
    mlp_tiles(side, h2, bup, wup, wdown, enc, send, slope, tile)


def mlp_second_kernel(s, widths, h2, enc_in, att_main, att_last, bup, wup, wdown, enc, slope, mine, *, tile):
    half, wide = h2.shape[1] // 2, slope.shape[1]
    rows = att_main.shape[0]
    enc[...] = enc_in[...]
    mine[:, wide : wide + half] = side_of(h2, s[CORE], half)
    mine[:rows, wide + half :] = side_of(att_main, s[CORE], half)
    mine[rows:, wide + half :] = side_of(att_last, s[CORE], half)
    mlp_tiles(s[CORE], h2, bup, wup, wdown, enc, mine, slope, tile)


def mlp_first(s, patches, got, att_main, att_last, h1, bout, gain, shift, bup, bdown, wout, wup, wdown):
    images, block, dim = patches.shape
    n, wide = images * block, wup.shape[1] // 2
    return call(
        functools.partial(mlp_first_kernel, tile=512), "mlp_first", 8,
        [
            shaped((n, dim), F32), shaped((n, dim)), shaped((n, dim), F32), shaped((n, wide)),
            shaped((n, wide + dim + dim // 2)),
        ],
        [pltpu.VMEM((2, block, dim), BF), pltpu.SemaphoreType.DMA((2,))],
        s, got, att_main, att_last, h1, bout, gain, shift, bup, bdown, wout, wup, wdown, patches, micros=6, streamed=1,
    )


def mlp_second(s, h2, enc, att_main, att_last, bup, wup, wdown):
    n, dim = h2.shape
    wide = wup.shape[1] // 2
    return call(
        functools.partial(mlp_second_kernel, tile=512), "mlp_second", 8,
        [shaped((n, dim), F32), shaped((n, wide)), shaped((n, wide + dim))], [],
        s, h2, enc, att_main, att_last, bup, wup, wdown, micros=5,
    )


def quant_kernel(s, widths, enc, cot_got, *refs, tile, scale):
    pieces, cot = refs[:-14], refs[-14]
    mix_own, mix_back, mix_last, loss, denc, dmlp, score, dweight, late, cot_own, mixes, losses, sems = refs[-13:]
    n, dim = enc.shape
    block = n // 3
    chunks, place = [], 0
    for piece in pieces:
        for first in range(0, piece.shape[0], tile):
            size = min(tile, piece.shape[0] - first)
            chunks.append((piece, slice(first, first + size), slice(place, place + size)))
            place += size + -size % 128
    stream = Stream(sems, (cot.at[s[CHIP]], cot_own.at[0]), (cot.at[2], cot_own.at[1]))
    low = enc[...].astype(BF)
    peak = None
    for piece, rows, cols in chunks:
        part = mm_nt(low, piece[rows, :]) * scale
        score[:, cols] = part
        top = jnp.max(part, axis=1, keepdims=True)
        peak = top if peak is None else jnp.maximum(peak, top)
    total = jnp.zeros_like(peak)
    late[...] = jnp.zeros_like(late)
    for piece, rows, cols in chunks:
        e = jnp.exp(score[:, cols] - peak)
        score[:, cols] = e
        total = total + jnp.sum(e, axis=1, keepdims=True)
        late[...] += mm(e.astype(BF), piece[rows, :])
    inv = 1.0 / total
    mix = late[...] * inv
    low = mix.astype(BF)
    mixes[: 2 * block, :] = low[: 2 * block]
    mixes[2 * block + 16 :, :] = low[2 * block :]
    index = lax.broadcasted_iota(jnp.int32, (n, 1), 0)
    spot = spots(index & (2 * block - 1), block, s[ME])
    ok = spot < jnp.where(index < 2 * block, limit_of(s, widths, False), limit_of(s, widths, True))
    diff = enc[...] - mix
    lost = jnp.where(ok, jnp.mean(diff * diff, axis=1, keepdims=True), 0.0)
    lost = jnp.transpose(jnp.broadcast_to(lost, (n, 128)))[0:8, :]
    losses[...] = lost
    back = lost[:, block : 2 * block]
    high = back.astype(BF)
    rest = back - high.astype(F32)
    below = 2 * block
    mixes[below : below + 16, :] = jnp.zeros((16, dim), BF)
    mixes[below : below + 8, :block] = high
    mixes[below : below + 8, block : 2 * block] = rest.astype(BF)
    mixes[below : below + 8, 2 * block : 3 * block] = (rest - rest.astype(BF).astype(F32)).astype(BF)
    spans = ((mix_own, 0, block), (mix_back, block, 2 * block + 16), (mix_last, 2 * block + 16, 3 * block + 16))
    outs = [pltpu.make_async_copy(mixes.at[a:b, :], out, sems.at[2 + k]) for k, (out, a, b) in enumerate(spans)]
    outs.append(pltpu.make_async_copy(losses, loss, sems.at[5]))
    for out in outs:
        out.start()
    pull = jnp.where(ok, (2.0 * COMMIT / dim) * diff, 0.0)
    denc[...] = pull
    stream.wait(2)
    cots = jnp.concatenate([cot_own[0], cot_got[...], cot_own[1]], axis=0).astype(F32)
    dmix = (cots - pull).astype(BF)
    inner = jnp.zeros_like(peak)
    for piece, rows, cols in chunks:
        d = mm_nt(dmix, piece[rows, :])
        dweight[:, cols] = d
        inner = inner + jnp.sum(score[:, cols] * d, axis=1, keepdims=True)
    inner = inner * inv
    inv = inv * scale
    for piece, rows, cols in chunks:
        dcode = (score[:, cols] * inv * (dweight[:, cols] - inner)).astype(BF)
        denc[...] += mm(dcode, piece[rows, :])
    dmlp[...] = denc[...].astype(BF)
    for out in outs:
        out.wait()


def quantizer(s, enc, cot, cot_got, pieces, tile=512):
    n, dim = enc.shape
    block = n // 3
    count = sum(-(-piece.shape[0] // tile) for piece in pieces)
    wide = count * tile
    return call(
        functools.partial(quant_kernel, tile=tile, scale=dim**-0.5), "quantizer", 21,
        [in_hbm((block, dim)), in_hbm((block + 16, dim)), in_hbm((block, dim))]
        + [in_hbm((8, n), F32), shaped((n, dim), F32), shaped((n, dim))],
        [
            pltpu.VMEM((n, wide), F32), pltpu.VMEM((n, wide), F32), pltpu.VMEM((n, dim), F32),
            pltpu.VMEM((2, block, dim), BF), pltpu.VMEM((n + 16, dim), BF), pltpu.VMEM((8, n), F32),
            pltpu.SemaphoreType.DMA((6,)),
        ],
        s, enc, cot_got, *pieces, cot, micros=14, streamed=1, by_hand=range(4),
    )


def quantizer_plain(s, enc, cots, book):
    n, dim = enc.shape
    block = n // 3
    index = jnp.arange(n)
    ok = spots(index & (2 * block - 1), block, lax.axis_index("seq")) < jnp.where(index < 2 * block, s[0, 0], s[1, 0])
    scale = dim**-0.5
    scores = mm_nt(enc.astype(BF), book) * scale
    peak = jnp.max(scores, axis=-1, keepdims=True)
    log_total = peak + jnp.log(jnp.sum(jnp.exp(scores - peak), axis=-1, keepdims=True))
    weights = jnp.exp(scores - log_total)
    mix = mm(weights.astype(BF), book)
    diff = enc - mix
    loss = jnp.where(ok, jnp.mean(diff * diff, axis=-1), 0.0)
    pull = jnp.where(ok[:, None], 2.0 * COMMIT / dim * diff, 0.0)
    dmix = (cots.astype(F32) - pull).astype(BF)
    dweights = mm_nt(dmix, book)
    inner = jnp.sum(weights * dweights, axis=-1, keepdims=True)
    dcode = (weights * (dweights - inner) * scale).astype(BF)
    denc = mm(dcode, book) + pull
    low = mix.astype(BF)
    loss = jnp.broadcast_to(loss[None, :], (8, n))
    parts, rest = [], loss[:, block : 2 * block]
    for _ in range(3):
        parts.append(rest.astype(BF))
        rest = rest - parts[-1].astype(F32)
    parts = jnp.pad(jnp.concatenate(parts, axis=1), ((0, 8), (0, dim - 3 * block)))
    back = jnp.concatenate([low[block : 2 * block], parts])
    return low[:block], back, low[2 * block :], loss, denc, denc.astype(BF)


def mlp_bwd_kernel(
    s, widths, dmlp, denc, mid, gain, slope0, slope1, wdown, wup, wout, dp0, dp1, dbranch, dmid_ref, datt, rows, bup, acc,
    *, tile,
):
    hidden, wide = wup.shape[1], slope0.shape[1]
    for t in range(0, hidden, tile):
        span, half, here = slice(t, t + tile), t // wide, slice(t % wide, t % wide + tile)
        slope = jnp.where(s[CORE] == half, slope1[:, here], slope0[:, here]).astype(F32)
        dpre = (mm_nt(dmlp[...], wdown[span, :]) * slope).astype(BF)
        (dp0, dp1)[half][:, here] = dpre
        bup[:, span] = jnp.sum(dpre.astype(F32), axis=0, keepdims=True)
        part = mm_nt(dpre, wup[:, span])
        if t == 0:
            acc[...] = part
        else:
            acc[...] += part
    dy = acc[...]
    xhat, inv = norm_stats(mid[...])
    dmid = denc[...] + norm_back(xhat, inv, line(gain), dy)
    dmid_ref[...] = dmid
    low = dmid.astype(BF)
    dbranch[...] = low
    datt[...] = mm_nt(low, wout[...]).astype(BF)
    rows[0:1, :] = jnp.sum(dy * xhat, axis=0, keepdims=True)
    rows[1:2, :] = jnp.sum(dy, axis=0, keepdims=True)
    rows[2:3, :] = jnp.sum(low.astype(F32), axis=0, keepdims=True)
    rows[3:4, :] = jnp.sum(dmlp[...].astype(F32), axis=0, keepdims=True)


def mlp_bwd(s, dmlp, denc, mid, gain, slopes, wdown, wup, wout):
    n, dim = denc.shape
    hidden, tile = wup.shape[1], 512
    return call(
        functools.partial(mlp_bwd_kernel, tile=tile), "mlp_bwd", 8,
        [
            shaped((n, hidden // 2)), shaped((n, hidden // 2)), shaped((n, dim)), shaped((n, dim), F32),
            shaped((n, dim)), shaped((4, dim), F32), shaped((1, hidden), F32),
        ],
        [pltpu.VMEM((n, dim), F32)],
        s, dmlp, denc, mid, gain, *slopes, wdown, wup, wout, micros=9,
    )


TINY_UP, TINY_QKV = 32, 16


def labels(steps, index, part):
    return [[part if step == "y" else parity(index & step[1]) for step in order] for order in steps]


def place(s, first, steps, keep, send, index, part, rows, value):
    sides = labels(steps, index, part)
    slots = [functools.reduce(lambda x, y: 2 * x + y, side[1:], 0) for side in sides]
    here = sides[0][0] + (sides[1][0] - sides[0][0]) * s[CORE]
    slot = slots[0] + (slots[1] - slots[0]) * s[CORE]

    @pl.when(s[first] == here)
    def _():
        keep[slot, rows, :] = value

    @pl.when(s[first] != here)
    def _():
        send[slot, rows, :] = value


def quotient(index, size):
    return ((index.astype(F32) + 0.5) * (1.0 / size)).astype(jnp.int32)


def tiny_rows(rows, shards, half):
    dim = rows.shape[1]
    part = dim // shards
    shard = lax.broadcasted_iota(jnp.int32, (shards, dim), 0)
    of = quotient(lax.broadcasted_iota(jnp.int32, (shards, dim), 1), part)
    local = lax.broadcasted_iota(jnp.int32, (dim, 1), 0)
    local = local - quotient(local, part) * part
    lane = lax.broadcasted_iota(jnp.int32, (dim, half), 1)
    total = jnp.zeros((shards, half), F32)
    for k in range(4):
        spread = jnp.where(of == shard, jnp.broadcast_to(rows[k : k + 1, :], (shards, dim)), 0.0)
        total = total + mm(spread.astype(BF), (lane == local + k * part).astype(F32).astype(BF))
    return total


def grad_down_kernel(s, widths, dm, act0, act1, keep, send, *, shards, steps):
    n, width = act0.shape[0], keep.shape[2]
    rows = dm.shape[1] // shards // 2
    full = (mm_tn(dm[:n, :], act0[:, :width]) + mm_tn(dm[n:, :], act1[:, :width])).astype(BF)
    for j in range(2 * shards):
        place(s, SIDES, steps, keep, send, j // 2, j % 2, slice(None), full[j * rows : (j + 1) * rows])


def grad_down(s, dm, act0, act1, shards, steps):
    dim = dm.shape[1]
    part = shaped((shards, dim // shards // 2, act0.shape[1] - dim))
    return call(
        functools.partial(grad_down_kernel, shards=shards, steps=steps), "grad_down", 10, [part, part], [],
        s, dm, act0, act1, micros=4,
    )


def grad_up_kernel(s, widths, a0, a1, *refs, shards, steps):
    d0, d1, (four, bup, keep, send) = refs[:3], refs[3:6], refs[6:]
    size, half = keep.shape[1], keep.shape[2]
    wide = d0[0].shape[1]
    hidden = 2 * wide
    first = hidden // 2
    cols = hidden // shards
    rows = 2 * half // shards
    per = shards // 4
    tiny = tiny_rows(four[...], shards, half)
    at = lax.broadcasted_iota(jnp.int32, (2 * size - half - rows, half), 0)

    def put(index, part, at, value):
        place(s, SIDES + 4, steps, keep, send, index, part, slice(at, at + value.shape[0]), value)

    h = slice(first + half, first + 2 * half)
    out = (mm_tn(d0[2][...], a0[:, h]) + mm_tn(d1[2][...], a1[:, h])).astype(BF)
    h = slice(first, first + half)
    for k in range(0, shards, per):
        side, first_col = k * cols // wide, k * cols % wide
        span = slice(first_col, first_col + per * cols)
        full = (mm_tn(a0[:, h], d0[side][:, span]) + mm_tn(a1[:, h], d1[side][:, span])).astype(BF)
        for j in range(per):
            put(k + j, 0, 0, full[:size, j * cols : (j + 1) * cols])
            put(k + j, 1, 0, full[size:, j * cols : (j + 1) * cols])
            put(k + j, 1, half - size, out[(k + j) * rows : (k + j + 1) * rows])
            both = jnp.where(at == 0, tiny[k + j : k + j + 1], 0.0)
            both = both + jnp.where(at == 1, bup[:, (k + j) * cols : (k + j + 1) * cols], 0.0)
            put(k + j, 1, half - size + rows, both.astype(BF))


def grad_up(s, mine, got, dp0, dp1, four, bup, shards, steps):
    half = got.shape[1] - mine.shape[1]
    dim = 2 * half
    part = shaped((shards, (half + dim // shards + TINY_UP) // 2, half))
    return call(
        functools.partial(grad_up_kernel, shards=shards, steps=steps), "grad_up", 10,
        [part, part], [], s, mine, got, *dp0, *dp1, four, bup, micros=5,
    )


def got_rows(owns):
    return owns[0].shape[0] // 5


def last_of(ref, step, n, block, dim):
    wide = ref.shape[1]
    blocks = [
        ref[5 * n + k * block : 5 * n + (k + 1) * block, :] for k in range(step * dim // wide, (step + 1) * dim // wide)
    ]
    return jnp.concatenate(blocks, axis=1)


def d_of(owns, gots, step, n):
    if step == 0:
        return jnp.concatenate([own[4 * n : 5 * n, :] for own in owns], axis=1)
    mine, theirs = slice((step - 1) * n, step * n), slice((step + 1) * n, (step + 2) * n)
    return jnp.concatenate(
        [(own[mine, :].astype(F32) + got[theirs, :].astype(F32)).astype(BF) for own, got in zip(owns, gots)], axis=1
    )


def grad_qkv_kernel(
    s, widths, *refs, shards, steps
):
    groups = (len(refs) - 6) // 2
    owns, gots = refs[:groups], refs[groups : 2 * groups]
    h_own, other, norms, sums, keep, send = refs[-6:]
    n, half = got_rows(owns), h_own.shape[1]
    block = n // 2
    dim = 2 * half
    h = slice(other.shape[1] - half, other.shape[1])
    size = 3 * dim // shards // 2

    def put(k, at, value):
        place(s, SIDES + 8, steps, keep, send, k // 2, k % 2, slice(at, at + value.shape[0]), value)

    for step in range(3):
        d_own, d_got = d_of(owns, gots, step, n), d_of(gots, owns, step, n)
        full = mm_tn(d_own, h_own[:n, :]) + mm_tn(d_got, other[:n, h])
        last_own, last_got = (last_of(refs[1], step, n, block, dim) for refs in (owns, gots))
        full = full + mm_tn(last_own, h_own[n:, :]) + mm_tn(last_got, other[n:, h])
        full = full.astype(BF)
        first = step * dim
        for k in range(first // size, (first + dim + size - 1) // size):
            lo, hi = max(first, k * size), min(first + dim, (k + 1) * size)
            put(k, lo - k * size, full[lo - first : hi - first])
    four = jnp.concatenate([norms[...], sums[0:1, :], sums[2:3, :]], axis=0)
    tiny = tiny_rows(four, shards, half)
    at = lax.broadcasted_iota(jnp.int32, (TINY_QKV, half), 0)
    for k in range(2 * shards):
        put(k, size, jnp.where(at == 0, tiny[k // 2 : k // 2 + 1], 0.0).astype(BF))


def grad_qkv(s, owns, gots, h_own, other, norms, sums, shards, steps):
    half = h_own.shape[1]
    dim = 2 * half
    part = shaped((shards, 3 * dim // shards // 2 + TINY_QKV, half))
    return call(
        functools.partial(grad_qkv_kernel, shards=shards, steps=steps), "grad_qkv", 12, [part, part], [],
        s, *owns, *gots, h_own, other, norms, sums, micros=4,
    )


def qkv_bwd_kernel(
    s, widths, *refs
):
    groups = (len(refs) - 13) // 2
    owns, gots = refs[:groups], refs[groups : 2 * groups]
    x_got, gain, dmid, w, patches, dx0, dx1, dx2, norms, sums, acc, x_own, sems = refs[-13:]
    block, dim = x_got.shape
    n = 2 * block
    spans = [slice(k * dim, (k + 1) * dim) for k in range(3)]
    stream = Stream(sems, (patches.at[s[CHIP]], x_own.at[0]), (patches.at[2], x_own.at[1]))
    for k, cols in enumerate(spans):
        d = jnp.concatenate([d_of(owns, gots, k, n), last_of(owns[1], k, n, block, dim)], axis=0)
        sums[k : k + 1, :] = jnp.sum(d.astype(F32), axis=0, keepdims=True)
        part = mm_nt(d, w[:, cols])
        if k == 0:
            acc[...] = part
        else:
            acc[...] += part
    dy = acc[...]
    stream.wait(2)
    x = jnp.concatenate([x_own[0], x_got[...], x_own[1]], axis=0).astype(F32)
    xhat, inv = norm_stats(x)
    dx = dmid[...] + norm_back(xhat, inv, line(gain), dy)
    dx0[...] = dx[:block]
    for k in range(2):
        dx1[k * block : (k + 1) * block, :] = dx[block:n, k * dim // 2 : (k + 1) * dim // 2].astype(BF)
    dx2[...] = dx[n:]
    norms[0:1, :] = jnp.sum(dy * xhat, axis=0, keepdims=True)
    norms[1:2, :] = jnp.sum(dy, axis=0, keepdims=True)


def qkv_bwd(s, owns, gots, patches, x_got, gain, dmid, w):
    images, block, dim = patches.shape
    return call(
        qkv_bwd_kernel, "qkv_bwd", 9,
        [
            in_hbm((block, dim), F32), shaped((2 * block, dim // 2)), in_hbm((block, dim), F32),
            shaped((2, dim), F32), shaped((3, dim), F32),
        ],
        [
            pltpu.VMEM((images * block, dim), F32), pltpu.VMEM((2, block, dim), BF),
            pltpu.SemaphoreType.DMA((2,)),
        ],
        s, *owns, *gots, x_got, gain, dmid, w, patches, micros=4, streamed=1,
    )


def finish_kernel(s, widths, both, both_got, down, down_got, up, out, qkv, wdown, *vectors, rows_up, size, parts):
    def sorted_of(value, other):
        cut = value.shape[0] // 2
        mine = [value[:cut].astype(F32), value[cut:].astype(F32)]
        theirs = [other[:cut].astype(F32), other[cut:].astype(F32)]
        second = s[CHIP] > 0
        pairs = [[jnp.where(second, v[1], v[0]), jnp.where(second, v[0], v[1])] for v in (mine, theirs)]
        swap_cores = s[CORE] > 0
        return [
            [jnp.where(swap_cores, b, a) for a, b in zip(*pairs)],
            [jnp.where(swap_cores, a, b) for a, b in zip(*pairs)],
        ]

    cores = sorted_of(both, both_got)
    rows = [jnp.concatenate([first[:rows_up], second[:rows_up]], axis=0) for first, second in cores]
    half = up.shape[0] // 2
    wide = out.shape[0]
    up[:half, :] = rows[0][:half]
    up[half:, :] = rows[1][:half]
    out[...] = jnp.concatenate([r[half : half + wide] for r in rows], axis=1)
    pieces = [jnp.concatenate([f[rows_up : rows_up + size], g[rows_up : rows_up + size]], axis=0) for f, g in cores]
    qkv[...] = jnp.concatenate(pieces, axis=1)
    two = rows[0][half + wide : half + wide + 8] + rows[1][half + wide : half + wide + 8]
    one = cores[0][0][rows_up + size : rows_up + size + 8] + cores[1][0][rows_up + size : rows_up + size + 8]
    for ref, (source, row, at) in zip(vectors, parts):
        ref[...] = (one, two)[source][row : row + 1, at : at + ref.shape[0]].reshape(ref.shape[0])
    cores = sorted_of(down, down_got)
    wdown[...] = jnp.concatenate([jnp.concatenate(pair, axis=0) for pair in cores], axis=1)


def finish(s, both, both_got, down, down_got, rows_up, dim, hidden, shards):
    part, wide = dim // shards, hidden // shards
    size = 3 * dim // shards // 2
    parts = [(0, 0, k * part) for k in range(4)]
    parts += [(1, 0, 2 * part), (1, 0, 0), (1, 0, part), (1, 1, 0), (1, 0, 3 * part)]
    widths = [part] * 7 + [wide, part]
    return call(
        functools.partial(finish_kernel, rows_up=rows_up, size=size, parts=parts), "finish", 20,
        [in_hbm((dim, wide), F32), in_hbm((part, dim), F32), in_hbm((3 * part, dim), F32), in_hbm((part, hidden), F32)]
        + [in_hbm((width,), F32) for width in widths],
        [], s, both, both_got, down, down_got, micros=3,
    )


def hop(value, step0, step1):
    seq, img = lax.axis_size("seq"), lax.axis_size("img")
    pairs = []
    for s in range(seq):
        step = step1 if s % 2 else step0
        for i in range(img):
            to = (s ^ 2, i) if step == "y" else (s, i ^ (step if isinstance(step, int) else step[0]))
            pairs.append((s * img + i, to[0] * img + to[1]))
    return lax.ppermute(value, ("seq", "img"), pairs)


def plus(kept, got):
    return (kept.astype(F32) + got.astype(F32)).astype(BF)


class Sum:
    def __init__(self, s, base, steps, keep, send):
        self.s, self.base, self.steps, self.sides, self.at = s, base, steps, sides_here(steps), 0
        self.keep = keep.reshape(-1, keep.shape[-1])
        self.got = self.go(send.reshape(self.keep.shape))

    def go(self, value):
        self.at += 1
        return hop(value, self.steps[0][self.at - 1], self.steps[1][self.at - 1])

    def step(self):
        shape = (2, self.got.shape[0] // 2, self.got.shape[1])
        keep, got = self.keep.reshape(shape), self.got.reshape(shape)
        if shape[1] % 16 == 0:
            self.keep, send = halve(self.s, keep, got, self.base + self.at)
        else:
            mine = self.sides[self.at]
            self.keep = plus(pick(keep, mine, 0), pick(got, mine, 0))
            send = plus(pick(keep, 1 - mine, 0), pick(got, 1 - mine, 0))
        self.got = self.go(send)

    def steps_left(self, most):
        while len(self.steps[0]) - self.at > most:
            self.step()

    def last(self):
        return add(self.s, self.keep, self.got) if self.keep.shape[0] % 16 == 0 else plus(self.keep, self.got)


def finish_plain(core, chip, both, both_got, down, down_got, rows_up, dim, hidden, shards):
    part, wide, half = dim // shards, hidden // shards, dim // 2
    size = 3 * dim // shards // 2

    def sorted_of(value, other):
        pairs = []
        for v in (value, other):
            a, b = jnp.split(v.astype(F32), 2)
            pairs.append([jnp.where(chip == 0, a, b), jnp.where(chip == 0, b, a)])
        mine, theirs = pairs
        first = [jnp.where(core == 0, a, b) for a, b in zip(mine, theirs)]
        return [first, [jnp.where(core == 0, b, a) for a, b in zip(mine, theirs)]]

    cores = sorted_of(both, both_got)
    rows = [jnp.concatenate([f[:rows_up], g[:rows_up]]) for f, g in cores]
    up = jnp.concatenate([r[:wide].T for r in rows])
    out = jnp.concatenate([r[wide : wide + part] for r in rows], axis=1)
    pieces = [jnp.concatenate([f[rows_up : rows_up + size], g[rows_up : rows_up + size]]) for f, g in cores]
    two = sum(r[wide + part :] for r in rows).reshape(-1)
    one = sum(f[rows_up + size :] for f, _ in cores).reshape(-1)
    down = jnp.concatenate([jnp.concatenate(pair) for pair in sorted_of(down, down_got)], axis=1)
    first = [one[k * part : (k + 1) * part] for k in range(4)]
    second = [two[k * part : (k + 1) * part] for k in (2, 0, 1)]
    last = [two[4 * part : 4 * part + wide], two[3 * part : 4 * part]]
    return [up, out, jnp.concatenate(pieces, axis=1), down, *first, *second, *last]


class Book:
    def __init__(self, s, codebook):
        n_img = lax.axis_size("img")
        bits = [1 << k for k in range(n_img.bit_length() - 1)]
        masks = [1, 2, 6] if n_img == 8 else bits
        self.orders = list(zip(masks[1:], [1, "y", *masks[3:]]))
        self.ends = ((1, masks[1]), ("y", masks[2]))
        self.s, self.value = s, codebook

    def stack(self, *parts):
        return stack(self.s, *parts) if sum(part.size for part in parts) < 1 << 21 else jnp.concatenate(parts)

    def start(self):
        self.got = hop(self.value, *self.orders.pop(0))

    def double(self):
        self.value = self.stack(self.value, self.got)

    def spread(self):
        self.beside, self.across = hop(self.value, *self.ends[0]), hop(self.value, *self.ends[1])
        self.other = [swap(self.value, "seq", 1)]

    def corner(self):
        if self.value.size < 1 << 21:
            parts = cut(self.s, self.across, self.beside)
        else:
            half = self.value.shape[0] // 2
            parts = self.across[:half], self.beside[half:]
        self.corners = hop(parts[0], *self.ends[0]), hop(parts[1], *self.ends[1])

    def finish(self):
        rest = self.stack(self.beside, self.across, *self.corners)
        return [self.value, rest, *self.other, swap(rest, "seq", 1)]


def shards(
    patches,
    widths,
    ln1_gain,
    ln1_bias,
    w_qkv,
    b_query,
    b_value,
    w_out,
    b_out,
    ln2_gain,
    ln2_bias,
    w_up,
    b_up,
    w_down,
    b_down,
    codebook,
    cotangent,
):
    images, block, dim = patches.shape
    hidden = w_up.shape[1]
    n_img = lax.axis_size("img")
    me = lax.axis_index("seq")
    chip, core = me // 2, me % 2
    half, main = dim // 2, 2 * block
    fits = codebook.shape[0] * n_img * lax.axis_size("seq") <= 4096
    aligned = n_img == 8 and dim // n_img // 2 % 16 == 0
    steps_down, steps_up, steps_qkv = plans(n_img)
    limits = jnp.stack([widths[0] + (widths[1] - widths[0]) * chip, widths[2]])
    s = jnp.broadcast_to(jnp.pad(GRID_H * limits, (0, 6))[:, None], (8, 128))

    Order.token = jnp.zeros((8, 128), F32)
    book = Book(s, codebook)
    book.start()
    x_got = swap(pick(patches, 1 - chip, 0), "seq", 2)
    ln1 = (ln1_gain, ln1_bias, b_query, b_value, w_qkv)
    while book.orders:
        book.double()
        book.start()
    q_main, q_last, *kvs, h_mine, h_send = qkv_fwd(s, patches, x_got, *ln1)
    kvs_other = [swap(kv, "seq", 1) for kv in kvs]
    kv_y = swap(kvs[2], "seq", 2)
    book.double()
    book.spread()
    kvs_main = kvs[:2] + kvs_other[:2]
    att_main = attention_fwd(s, q_main, kvs_main, False, block)
    cot_got = swap(pick(cotangent, 1 - chip, 0), "seq", 2)
    kvs_last = [kvs[2], kv_y, kvs_other[2], swap(kv_y, "seq", 1)]
    att_last = attention_fwd(s, q_last, kvs_last, True, block)
    book.corner()
    mid, h2, enc, slope0, send = mlp_first(
        s, patches, x_got, att_main, att_last, h_send, b_out, ln2_gain, ln2_bias, b_up, b_down, w_out, w_up,
        w_down,
    )
    got = swap(send, "seq", 1)
    pieces = book.finish()
    enc, slope1, mine = mlp_second(s, h2, enc, att_main, att_last, b_up, w_up, w_down)
    if fits:
        mix0, mix1, mix2, loss, denc, dmlp = quantizer(s, enc, cotangent, cot_got, pieces)
    else:
        cots = jnp.concatenate([pick(cotangent, chip, 0), cot_got, cotangent[2]])
        mix0, mix1, mix2, loss, denc, dmlp = quantizer_plain(s, enc, cots, jnp.concatenate(pieces))
    mix1 = swap(mix1, "seq", 2)

    def split(full, steps):
        rows, cols = full.shape[-2:]
        full = full.reshape([2] * len(steps[0]) + [rows // 2, cols])
        side = sides_here(steps)[0]
        return pick(full, side, 0), pick(full, 1 - side, 0)

    def lines_of(count, *vectors):
        rows = jnp.concatenate([v.reshape(n_img, -1) for v in vectors], axis=1).astype(BF)
        return jnp.pad(rows, ((0, 0), (0, count * half - rows.shape[1]))).reshape(n_img, count, half)

    dmlp_got = swap(dmlp, "seq", 1)
    both = jnp.concatenate([mine, got[:, : mine.shape[1]]])
    if aligned:
        dmlp_both = stack(s, dmlp, dmlp_got, there=(got,))
        keep, send = grad_down(s, dmlp_both, mine, got, n_img, steps_down)
    else:
        full = mm_tn(jnp.concatenate([dmlp, dmlp_got]), both[:, : hidden // 2]).astype(BF)
        keep, send = split(full.reshape(n_img, -1, hidden // 2), steps_down)
    down = Sum(s, 0, steps_down, keep, send)
    *dp, dmid, datt, rows_two, sum_bup = mlp_bwd(s, dmlp, denc, mid, ln2_gain, (slope0, slope1), w_down, w_up, w_out)
    dp_got = [swap(part, "seq", 1) for part in dp]
    quantized, token_loss = assemble(s, (mix0, mix1, mix2), loss)
    keep_last, send_last, dq_last = attention_bwd(s, q_last, kvs_last, datt, main, True, block, ())
    got_last = swap(send_last, "seq", 1)
    keep_last, send_last = fold(s, keep_last, got_last)
    got_last = swap(send_last, "seq", 2)
    if aligned:
        keep, send = grad_up(s, mine, got, dp, dp_got, rows_two, sum_bup, n_img, steps_up)
    else:
        dps = jnp.concatenate([jnp.concatenate(dp, axis=1), jnp.concatenate(dp_got, axis=1)])
        up = mm_tn(both[:, hidden // 2 : hidden // 2 + half], dps[:, :hidden]).astype(BF)
        up = up.reshape(half, n_img, -1).transpose(1, 2, 0)
        out = mm_tn(dps[:, hidden:], both[:, hidden // 2 + half :]).astype(BF).reshape(n_img, -1, half)
        tiny = lines_of(TINY_UP, rows_two[0], rows_two[1], rows_two[2], rows_two[3], sum_bup[0])
        keep, send = split(jnp.concatenate([up, out, tiny], axis=1), steps_up)
    up = Sum(s, len(steps_down[0]), steps_up, keep, send)
    down.step()
    d_main, d_got = [], []
    for pairs, more in (((0, 1), ()), ((2, 3), (dq_last, keep_last, got_last)), ((4, 5), ())):
        d_main += attention_bwd(s, q_main, kvs_main, datt, 0, False, block, pairs, more)
        d_got.append(swap(d_main[-1], "seq", 1))
    dx0, dx1, dx2, norms, sums = qkv_bwd(s, d_main, d_got, patches, x_got, ln1_gain, dmid, w_qkv)
    up.step()
    down.step()
    if aligned:
        keep, send = grad_qkv(
            s, d_main, d_got, h_mine, got, norms, sums, n_img, steps_qkv
        )
    else:
        n = main

        def assembled(owns, gots):
            rows = [jnp.concatenate([own[4 * n : 5 * n] for own in owns], axis=1)]
            for k in (0, 1):
                mine, theirs = slice(k * n, (k + 1) * n), slice((k + 2) * n, (k + 3) * n)
                rows.append(jnp.concatenate([plus(own[mine], got[theirs]) for own, got in zip(owns, gots)], axis=1))
            last = owns[1][5 * n :].reshape(-1, block, owns[1].shape[1])
            return [jnp.concatenate(rows, axis=1), jnp.concatenate(list(last), axis=1)]

        d = jnp.concatenate(assembled(d_main, d_got) + assembled(d_got, d_main))
        h = jnp.concatenate([h_mine, got[:, -half:]])
        full = mm_tn(d, h).astype(BF).reshape(n_img, 2, -1, half)
        tiny = lines_of(TINY_QKV, norms[0], norms[1], sums[0], sums[2])
        full = jnp.concatenate([full, jnp.stack([tiny, tiny], axis=1)], axis=2)
        keep, send = split(full.reshape(n_img, -1, half), steps_qkv)
    qkv = Sum(s, 2 * len(steps_down[0]), steps_qkv, keep, send)

    down.steps_left(0)
    qkv.step()
    up.step()
    sum_down = down.last()
    down_other = swap(sum_down, "seq", 2)
    qkv.step()
    up.steps_left(0)
    qkv.steps_left(0)
    sum_up = up.last()
    up_other = swap(stack(s, sum_up, dx1) if aligned else jnp.concatenate([sum_up, dx1]), "seq", 2)
    sum_qkv = qkv.last()
    qkv_other = swap(sum_qkv, "seq", 2)
    down_both = stack(s, sum_down, down_other) if aligned else jnp.concatenate([sum_down, down_other])
    down_got = swap(down_both, "seq", 1)
    grad_input = assemble_dx(s, dx0, up_other, dx2)
    if aligned:
        both = collect(s, sum_up, sum_qkv, up_other, qkv_other)
    else:
        both = jnp.concatenate([sum_up, sum_qkv, up_other[: sum_up.shape[0]], qkv_other])
    both_got = swap(both, "seq", 1)
    rows_up = sum_up.shape[0]
    if aligned:
        weights = finish(s, both, both_got, down_both, down_got, rows_up, dim, hidden, n_img)
    else:
        weights = finish_plain(core, chip, both, both_got, down_both, down_got, rows_up, dim, hidden, n_img)
    g_up, g_out, g_qkv, g_down, g_gain1, g_shift1, g_bq, g_bv, g_bout, g_gain2, g_shift2, g_bup, g_bdown = weights

    return (
        quantized,
        token_loss,
        grad_input,
        g_gain1,
        g_shift1,
        g_qkv.T,
        g_bq,
        g_bv,
        g_out.T,
        g_bout,
        g_gain2,
        g_shift2,
        g_up,
        g_bup,
        g_down.T,
        g_bdown,
    )


def solution(mesh):
    return jax.shard_map(
        shards,
        mesh=mesh,
        in_specs=(
            P("img", "seq", None),
            P("img"),
            P(),
            P(),
            P(),
            P(),
            P(),
            P(),
            P(),
            P(),
            P(),
            P(),
            P(),
            P(),
            P(),
            P(("seq", "img"), None),
            P("img", "seq", None),
        ),
        out_specs=(
            P("img", "seq", None),
            P("img", "seq"),
            P("img", "seq", None),
            P("img"),
            P("img"),
            P(None, "img"),
            P("img"),
            P("img"),
            P(None, "img"),
            P("img"),
            P("img"),
            P("img"),
            P(None, "img"),
            P("img"),
            P(None, "img"),
            P("img"),
        ),
        check_vma=False,
    )
```

```python
import functools

import jax
import jax.numpy as jnp
from jax import lax
from jax.experimental import pallas as pl
from jax.experimental.pallas import tpu as pltpu
from jax.sharding import PartitionSpec as P

HEAD_DIM = 64
GRID_H = 16
EPS_NORM = 1e-06
COMMIT = 16.0
BF = jnp.bfloat16
F32 = jnp.float32
MIB = 1024 * 1024
MASKED = -1000000000.0


def mm(a, b):
    return jnp.dot(a, b, preferred_element_type=F32)


def mm_nt(a, b):
    return lax.dot_general(a, b, (((1,), (1,)), ((), ())), preferred_element_type=F32)


def mm_tn(a, b):
    return lax.dot_general(a, b, (((0,), (0,)), ((), ())), preferred_element_type=F32)


def swap(value, axis, bit):
    count = lax.axis_size(axis)
    return lax.ppermute(value, axis, [(i, i ^ bit) for i in range(count)])


def pick(value, index, axis):
    return lax.dynamic_index_in_dim(value, index, axis, keepdims=False)


def after(value, *others):
    return lax.optimization_barrier((value, *others))[0]


def parity(number):
    return bin(number).count("1") % 2


def shaped(shape, dtype=BF):
    return jax.ShapeDtypeStruct(tuple(shape), dtype)


def in_hbm(shape, dtype=BF):
    return pltpu.HBM(tuple(shape), dtype)


class Order:
    token = None


def call(kernel, name, mib, out_shape, scratch, s, *args, micros, streamed=0, by_hand=(), bounds=False):
    vm, hbm = pl.BlockSpec(memory_space=pltpu.VMEM), pl.BlockSpec(memory_space=pl.ANY)
    direct, count = len(args) - streamed, len(args) + len(out_shape)
    args = [
        pltpu.with_memory_space_constraint(arg, pltpu.HBM) if arg.ndim == 1 or (k >= direct and name not in ("stack", "cut")) else arg
        for k, arg in enumerate(args)
    ]

    def body(*refs):
        limits, token, refs = refs[0], refs[bounds], refs[bounds + 1 :]
        kernel(Place(), limits, *refs[:count], *refs[count + 1 :])
        refs[count][...] = token[...]

    out = pl.pallas_call(
        body,
        in_specs=[vm] * (direct + 1 + bounds) + [hbm] * streamed,
        out_specs=[hbm if out in by_hand else vm for out in range(len(out_shape))] + [vm],
        out_shape=[*out_shape, shaped((8, 128), F32)],
        scratch_shapes=scratch,
        compiler_params=pltpu.CompilerParams(vmem_limit_bytes=mib * MIB),
        cost_estimate=pl.CostEstimate(flops=int(micros * 2e8), bytes_accessed=0, transcendentals=0),
        name=name,
    )(*([s] if bounds else []), Order.token, *args)
    Order.token = out[-1]
    return out[:-1]


class Stream:
    def __init__(self, sems, *pairs, ahead=3):
        self.copies = [pltpu.make_async_copy(a, b, sems.at[k]) for k, (a, b) in enumerate(pairs)]
        self.done, self.begun = 0, 0
        self.start(ahead)

    def start(self, count):
        while self.begun < min(count, len(self.copies)):
            self.copies[self.begun].start()
            self.begun += 1

    def wait(self, count):
        while self.done < count:
            self.copies[self.done].wait()
            self.done += 1
            self.start(self.begun + 1)


ME, CORE, CHIP, SIDES = range(4)
X, NEAR, FAR = (1, 1), (2, 2), (4, 4)


def plans(n_img):
    if n_img == 8:
        return (
            ([X, NEAR, "y", FAR], ["y", NEAR, X, FAR]),
            ([X, NEAR, "y", FAR], ["y", NEAR, X, FAR]),
            ([X, "y", NEAR, FAR], ["y", X, NEAR, FAR]),
        )
    bits = [1 << k for k in reversed(range(n_img.bit_length() - 1))]
    order = [(bit, bit) for bit in bits] + ["y"]
    return ((order, order),) * 3


def side_here(step):
    if step == "y":
        return lax.axis_index("seq") // 2
    bits = lax.axis_index("img") & step[1]
    value = 0
    for k in range(step[1].bit_length()):
        value = value ^ ((bits >> k) & 1)
    return value


def sides_here(steps):
    core = lax.axis_index("seq") % 2
    return [jnp.where(core == 0, side_here(a), side_here(b)) for a, b in zip(*steps)]


class Place:
    def __getitem__(self, what):
        me = lax.axis_index("seq")
        if what < SIDES:
            return (me, me % 2, me // 2)[what]
        steps = plans(lax.axis_size("img"))
        chain, step = divmod(what - SIDES, len(steps[0][0]))
        return sides_here([order[step : step + 1] for order in steps[chain]])[0]


def line(ref, start=0, size=None):
    size = ref.shape[0] if size is None else size
    return ref[start : start + size].reshape(1, size)


def norm_stats(x):
    center = x - jnp.mean(x, axis=-1, keepdims=True)
    spread = jnp.mean(center * center, axis=-1, keepdims=True)
    inv = lax.rsqrt(spread + EPS_NORM)
    return center * inv, inv


def norm_back(xhat, inv, gain, dy):
    dxhat = dy * gain
    return inv * (
        dxhat - jnp.mean(dxhat, axis=-1, keepdims=True) - xhat * jnp.mean(dxhat * xhat, axis=-1, keepdims=True)
    )


def spots(index, block, me):
    shift = block.bit_length() - 1
    assert block == 1 << shift
    place = index >> shift
    mask = ((place & 1) << 1) | (place >> 1)
    return ((me ^ mask) << shift) | (index & (block - 1))


def limit_of(s, widths, last):
    row = widths[...].reshape(1, widths.shape[0])
    return GRID_H * (row[:, 2:3] if last else jnp.where(s[CHIP] == 0, row[:, 0:1], row[:, 1:2]))


def side_of(ref, side, width):
    return ref[:, pl.ds(pl.multiple_of(side * width, 128), width)]


def kv_last_kernel(s, widths, gain, shift, bv, patches, w_hbm, kv, h, x, w, sems):
    dim = h.shape[1]
    stream = Stream(sems, (patches.at[2], x), *((w_hbm.at[:, k * dim : (k + 1) * dim], w.at[k - 1]) for k in (1, 2)))
    stream.wait(1)
    xhat, _ = norm_stats(x[...].astype(F32))
    h[...] = (xhat * line(gain) + line(shift)).astype(BF)
    stream.wait(2)
    kv[:, :dim] = mm(h[...], w[0]).astype(BF)
    stream.wait(3)
    kv[:, dim:] = (mm(h[...], w[1]) + line(bv)).astype(BF)


def kv_last_fwd(s, patches, gain, shift, bv, w):
    _, block, dim = patches.shape
    return call(
        kv_last_kernel, "kv_last_fwd", 8, [shaped((block, 2 * dim)), shaped((block, dim))],
        [pltpu.VMEM((block, dim), BF), pltpu.VMEM((2, dim, dim), BF), pltpu.SemaphoreType.DMA((3,))],
        s, gain, shift, bv, patches, w, micros=2, streamed=2,
    )


def qkv_kernel(
    s, widths, got, h_last, gain, shift, bq, bv, w, patches, q_main, q_last, kv0, kv1, mine, send, h, x_own, sems
):
    half, dim = mine.shape[1], w.shape[0]
    block = got.shape[0]
    stream = Stream(sems, (patches.at[s[CHIP]], x_own))
    h[2 * block :, :] = h_last[...]
    xhat, _ = norm_stats(got[...].astype(F32))
    h[block : 2 * block, :] = (xhat * line(gain) + line(shift)).astype(BF)
    stream.wait(1)
    xhat, _ = norm_stats(x_own[...].astype(F32))
    h[:block, :] = (xhat * line(gain) + line(shift)).astype(BF)
    mine[...] = side_of(h, s[CORE], half)
    send[...] = side_of(h, 1 - s[CORE], half)
    keys = mm(h[: 2 * block, :], w[:, dim : 2 * dim]).astype(BF)
    values = (mm(h[: 2 * block, :], w[:, 2 * dim :]) + line(bv)).astype(BF)
    for k, out in enumerate((kv0, kv1)):
        out[:, :dim] = keys[k * block : (k + 1) * block]
        out[:, dim:] = values[k * block : (k + 1) * block]
    q = (mm(h[...], w[:, :dim]) + line(bq)).astype(BF)
    q_main[...] = q[: 2 * block]
    q_last[...] = q[2 * block :]


def qkv_fwd(s, patches, got, h_last, gain, shift, bq, bv, w):
    images, block, dim = patches.shape
    n, half = images * block, dim // 2
    return call(
        qkv_kernel, "qkv_fwd", 8,
        [
            shaped((2 * block, dim)), shaped((block, dim)), *[shaped((block, 2 * dim))] * 2, in_hbm((n, half)),
            shaped((n, half)),
        ],
        [pltpu.VMEM((n, dim), BF), pltpu.VMEM((block, dim), BF), pltpu.SemaphoreType.DMA((1,))],
        s, got, h_last, gain, shift, bq, bv, w, patches, micros=3, streamed=1,
    )


def two_heads(value):
    left = lax.broadcasted_iota(jnp.int32, value.shape, 1) < HEAD_DIM
    zero = jnp.zeros_like(value)
    return jnp.concatenate([jnp.where(left, value, zero), jnp.where(left, zero, value)], axis=0)


def one_pair(value):
    n = value.shape[0] // 2
    left = lax.broadcasted_iota(jnp.int32, (n, value.shape[1]), 1) < HEAD_DIM
    return jnp.where(left, value[:n], value[n:])


def rows_of(refs, lanes):
    return jnp.concatenate([ref[:, lanes] for ref in refs], axis=0)


def att_fwd_kernel(s, widths, q, *refs, last, block):
    kvs, o = refs[:-1], refs[-1]
    dim = q.shape[1]
    m = sum(kv.shape[0] for kv in kvs)
    index = lax.broadcasted_iota(jnp.int32, (1, m), 1)
    ok = spots(index, block, s[ME]) < limit_of(s, widths, last)
    for p in range(dim // 128):
        at, av = slice(p * 128, (p + 1) * 128), slice(dim + p * 128, dim + (p + 1) * 128)
        k, v = rows_of(kvs, at), rows_of(kvs, av)
        raw = mm_nt(two_heads(q[:, at]), k) * (HEAD_DIM**-0.5)
        scores = jnp.where(ok, raw, MASKED)
        expo = jnp.exp(scores - jnp.max(scores, axis=1, keepdims=True))
        probs = expo * (1.0 / jnp.sum(expo, axis=1, keepdims=True))
        o[:, at] = one_pair(mm(probs.astype(BF), v)).astype(BF)


def attention_fwd(s, q, kvs, last, block):
    return call(
        functools.partial(att_fwd_kernel, last=last, block=block), "attention_fwd", 10, [shaped(q.shape)], [],
        s, q, *kvs, micros=5, bounds=True,
    )[0]


def att_bwd_kernel(s, widths, q, do, *refs, last, block, first, pairs, more):
    n, dim = q.shape
    if pairs:
        kvs, out = refs[: len(refs) - 1 - more], refs[-1]
        m = sum(kv.shape[0] for kv in kvs)
        parts = [out.at[k * m // 2 : (k + 1) * m // 2, :] for k in range(4)]
        dq = out.at[2 * m : 2 * m + n, :]
        if more:
            dq_last, keep_last, got_last = refs[-4:-1]
            rows, wide = dq_last.shape[0], out.shape[1]
            parts_last = [dq_last[...]] + [
                (keep_last[k].astype(F32) + got_last[k].astype(F32)).astype(BF) for k in range(2)
            ]
            for k in range(3 * dim // wide):
                part, at = parts_last[k * wide // dim], k * wide % dim
                out[2 * m + n + k * rows : 2 * m + n + (k + 1) * rows, :] = part[:, at : at + wide]
    else:
        kvs, (keep, send, dq) = refs[:-3], refs[-3:]
        m = sum(kv.shape[0] for kv in kvs)
        parts = [keep.at[0], keep.at[1], send.at[0], send.at[1]]
    index = lax.broadcasted_iota(jnp.int32, (m, 1), 0)
    ok = spots(index, block, s[ME]) < limit_of(s, widths, last)
    for p in pairs or range(dim // 128):
        at, av = slice(p * 128, (p + 1) * 128), slice(dim + p * 128, dim + (p + 1) * 128)
        to = slice((p - pairs[0]) * 128, (p - pairs[0] + 1) * 128) if pairs else at
        k, v = rows_of(kvs, at), rows_of(kvs, av)
        q2, do2 = two_heads(q[:, at]), two_heads(do[first : first + n, at])
        raw = mm_nt(k, q2) * (HEAD_DIM**-0.5)
        scores = jnp.where(ok, raw, MASKED)
        expo = jnp.exp(scores - jnp.max(scores, axis=0, keepdims=True))
        probs = expo * (1.0 / jnp.sum(expo, axis=0, keepdims=True))
        dv = mm(probs.astype(BF), do2).astype(BF)
        dp = mm_nt(v, do2)
        inner = jnp.sum(probs * dp, axis=0, keepdims=True)
        ds = (probs * (dp - inner) * (HEAD_DIM**-0.5)).astype(BF)
        dk = mm(ds, q2).astype(BF)
        dq[:, to] = one_pair(mm_tn(ds, k)).astype(BF)
        for ref, part in zip(parts, (dk[: m // 2], dv[: m // 2], dk[m // 2 :], dv[m // 2 :])):
            ref[:, to] = part


def attention_bwd(s, q, kvs, do, first, last, block, pairs, more=()):
    n, dim = q.shape
    m = sum(kv.shape[0] for kv in kvs)
    return call(
        functools.partial(att_bwd_kernel, last=last, block=block, first=first, pairs=pairs, more=len(more)),
        "attention_bwd", 12,
        [shaped((2 * m + n + (len(more) and 3 * dim // len(pairs)), 128 * len(pairs)))] if pairs else [shaped((2, m // 2, dim)), shaped((2, m // 2, dim)), shaped((n, dim))],
        [], s, q, do, *kvs, *more, micros=4, bounds=True,
    )


def fold_kernel(s, widths, keep, got, keep_out, send_out):
    block = keep_out.shape[1]
    for k in range(2):
        total = (keep[k].astype(F32) + got[k].astype(F32)).astype(BF)
        keep_out[k] = total[:block]
        send_out[k] = total[block:]


def fold(s, keep, got):
    part = shaped((2, keep.shape[1] // 2, keep.shape[2]))
    return call(fold_kernel, "fold", 4, [part, part], [], s, keep, got, micros=0.5)


def stack_kernel(s, widths, *refs, count):
    at = 0
    for ref in refs[:count]:
        refs[-1][at : at + ref.shape[0], :] = ref[...]
        at += ref.shape[0]


def stack(s, *parts, there=()):
    shape = (sum(part.shape[0] for part in parts), parts[0].shape[1])
    kernel = functools.partial(stack_kernel, count=len(parts))
    return call(kernel, "stack", 8, [shaped(shape)], [], s, *parts, *there, micros=0.5, streamed=len(there))[0]


def cut_kernel(s, widths, a, b, *refs):
    first, second, both = refs[-3:]
    rows = first.shape[0]
    first[...] = a[:rows, :]
    second[...] = b[rows:, :]
    both[: 2 * rows, :] = b[...]
    both[2 * rows :, :] = a[...]


def cut(s, a, b, there):
    rows, dim = a.shape
    part = shaped((rows // 2, dim))
    return call(
        cut_kernel, "cut", 6, [part, part, shaped((2 * rows, dim))], [], s, a, b, *there, micros=0.3, streamed=len(there)
    )


def collect_kernel(s, widths, up, qkv, up_other, qkv_other, out):
    at = 0
    for ref in (up, qkv, up_other, qkv_other):
        rows = qkv.shape[0] if ref is qkv_other else ref.shape[0]
        rows = up.shape[0] if ref is up_other else rows
        out[at : at + rows, :] = ref[:rows, :]
        at += rows


def collect(s, up, qkv, up_other, qkv_other):
    shape = (2 * (up.shape[0] + qkv.shape[0]), up.shape[1])
    return call(collect_kernel, "collect", 6, [shaped(shape)], [], s, up, qkv, up_other, qkv_other, micros=0.5)[0]


def add_kernel(s, widths, keep, got, out):
    out[...] = (keep[...].astype(F32) + got[...].astype(F32)).astype(BF)


def add(s, keep, got):
    return call(add_kernel, "add", 4, [shaped(keep.shape)], [], s, keep, got, micros=0.5)[0]


def sorted_images(s, out, own, back, last):
    first = s[CHIP] == 0
    out[0] = jnp.where(first, own, back)
    out[1] = jnp.where(first, back, own)
    out[2] = last


def assemble_kernel(s, widths, mix0, mix1, mix2, loss, mix, losses):
    block = mix0.shape[0]
    sorted_images(s, mix, mix0[...], mix1[:block, :], mix2[...])
    first = s[CHIP] == 0
    own = loss[0:1, :block]
    back = sum(mix1[block : block + 8, k * block : (k + 1) * block].astype(F32) for k in range(3))[0:1]
    losses[0:1, :] = jnp.where(first, own, back)
    losses[1:2, :] = jnp.where(first, back, own)
    losses[2:3, :] = loss[0:1, 2 * block :]


def assemble(s, mix, loss):
    block, dim = mix[0].shape
    return call(
        assemble_kernel, "assemble", 8, [in_hbm((3, block, dim)), in_hbm((3, block), F32)], [],
        s, *mix, loss, micros=1,
    )


def assemble_dx_kernel(s, widths, dx0, pack, dx2, dx):
    block = dx0.shape[0]
    first = pack.shape[0] - 2 * block
    back = jnp.concatenate([pack[first : first + block, :], pack[first + block :, :]], axis=1)
    sorted_images(s, dx, dx0[...], back.astype(F32), dx2[...])


def assemble_dx(s, *dx):
    block, dim = dx[0].shape
    return call(assemble_dx_kernel, "assemble_dx", 8, [in_hbm((3, block, dim), F32)], [], s, *dx, micros=1)[0]


def halve_kernel(s, widths, keep, got, keep_out, send_out, *, at):
    mine = s[SIDES + at]
    keep_out[...] = (keep[mine].astype(F32) + got[mine].astype(F32)).astype(BF)
    send_out[...] = (keep[1 - mine].astype(F32) + got[1 - mine].astype(F32)).astype(BF)


def halve(s, keep, got, at):
    part = shaped(keep.shape[1:])
    return call(functools.partial(halve_kernel, at=at), "halve", 8, [part, part], [], s, keep, got, micros=0.7)


def gelu_pair(x):
    z = jnp.abs(x) * (0.5**0.5)
    t = 1.0 / (1.0 + 0.3275911 * z)
    expo = jnp.exp(-0.5 * x * x)
    poly = t * (0.254829592 + t * (-0.284496736 + t * (1.421413741 + t * (-1.453152027 + t * 1.061405429))))
    tail = 0.5 * poly * expo
    cdf = jnp.where(x < 0.0, tail, 1.0 - tail)
    return x * cdf, cdf + x * (expo * 0.3989422804014327)


def mlp_tiles(side, h2, bup, wup, wdown, enc, act_ref, slope, tile):
    wide = slope.shape[1]
    for k in range(0, wide, tile):
        here, there = slice(k, k + tile), pl.ds(pl.multiple_of(side * wide + k, 128), tile)
        act, rate = gelu_pair(mm(h2[...], wup[:, there]) + bup[there].reshape(1, tile))
        act = act.astype(BF)
        act_ref[:, here] = act
        slope[:, here] = rate.astype(BF)
        enc[...] += mm(act, wdown[there, :])


def mlp_first_kernel(
    s, widths, got, att_main, att_last, h1, bout, gain, shift, bup, bdown, wout, wup, wdown, patches, mid, h2, enc, slope,
    send, x_own, sems, *, tile,
):
    dim = got.shape[1]
    half, wide = dim // 2, slope.shape[1]
    rows = att_main.shape[0]
    side = 1 - s[CORE]
    stream = Stream(sems, (patches.at[s[CHIP]], x_own.at[0]), (patches.at[2], x_own.at[1]))
    branch = mm(jnp.concatenate([att_main[...], att_last[...]], axis=0), wout[...])
    stream.wait(2)
    x = jnp.concatenate([x_own[0], got[...], x_own[1]], axis=0).astype(F32)
    middle = x + branch + line(bout)
    mid[...] = middle
    xhat, _ = norm_stats(middle)
    h2[...] = (xhat * line(gain) + line(shift)).astype(BF)
    enc[...] = middle + line(bdown)
    send[:, wide : wide + half] = side_of(h2, side, half)
    send[:rows, wide + half : wide + dim] = side_of(att_main, side, half)
    send[rows:, wide + half : wide + dim] = side_of(att_last, side, half)
    send[:, wide + dim :] = h1[...]
    mlp_tiles(side, h2, bup, wup, wdown, enc, send, slope, tile)


def mlp_second_kernel(s, widths, h2, enc_in, att_main, att_last, bup, wup, wdown, enc, slope, mine, *, tile):
    half, wide = h2.shape[1] // 2, slope.shape[1]
    rows = att_main.shape[0]
    enc[...] = enc_in[...]
    mine[:, wide : wide + half] = side_of(h2, s[CORE], half)
    mine[:rows, wide + half :] = side_of(att_main, s[CORE], half)
    mine[rows:, wide + half :] = side_of(att_last, s[CORE], half)
    mlp_tiles(s[CORE], h2, bup, wup, wdown, enc, mine, slope, tile)


def mlp_first(s, patches, got, att_main, att_last, h1, bout, gain, shift, bup, bdown, wout, wup, wdown):
    images, block, dim = patches.shape
    n, wide = images * block, wup.shape[1] // 2
    return call(
        functools.partial(mlp_first_kernel, tile=512), "mlp_first", 8,
        [
            shaped((n, dim), F32), shaped((n, dim)), shaped((n, dim), F32), shaped((n, wide)),
            shaped((n, wide + dim + dim // 2)),
        ],
        [pltpu.VMEM((2, block, dim), BF), pltpu.SemaphoreType.DMA((2,))],
        s, got, att_main, att_last, h1, bout, gain, shift, bup, bdown, wout, wup, wdown, patches, micros=6, streamed=1,
    )


def mlp_second(s, h2, enc, att_main, att_last, bup, wup, wdown):
    n, dim = h2.shape
    wide = wup.shape[1] // 2
    return call(
        functools.partial(mlp_second_kernel, tile=512), "mlp_second", 8,
        [shaped((n, dim), F32), shaped((n, wide)), shaped((n, wide + dim))], [],
        s, h2, enc, att_main, att_last, bup, wup, wdown, micros=5,
    )


def quant_kernel(s, widths, enc, cot_got, *refs, tile, scale):
    pieces, cot = refs[:-14], refs[-14]
    mix_own, mix_back, mix_last, loss, denc, dmlp, score, dweight, late, cot_own, mixes, losses, sems = refs[-13:]
    n, dim = enc.shape
    block = n // 3
    chunks, place = [], 0
    for piece in pieces:
        for first in range(0, piece.shape[0], tile):
            size = min(tile, piece.shape[0] - first)
            chunks.append((piece, slice(first, first + size), slice(place, place + size)))
            place += size + -size % 128
    stream = Stream(sems, (cot.at[s[CHIP]], cot_own.at[0]), (cot.at[2], cot_own.at[1]))
    low = enc[...].astype(BF)
    peak = None
    for piece, rows, cols in chunks:
        part = mm_nt(low, piece[rows, :]) * scale
        score[:, cols] = part
        top = jnp.max(part, axis=1, keepdims=True)
        peak = top if peak is None else jnp.maximum(peak, top)
    total = jnp.zeros_like(peak)
    late[...] = jnp.zeros_like(late)
    for piece, rows, cols in chunks:
        e = jnp.exp(score[:, cols] - peak)
        score[:, cols] = e
        total = total + jnp.sum(e, axis=1, keepdims=True)
        late[...] += mm(e.astype(BF), piece[rows, :])
    inv = 1.0 / total
    mix = late[...] * inv
    low = mix.astype(BF)
    mixes[: 2 * block, :] = low[: 2 * block]
    mixes[2 * block + 16 :, :] = low[2 * block :]
    index = lax.broadcasted_iota(jnp.int32, (n, 1), 0)
    spot = spots(index & (2 * block - 1), block, s[ME])
    ok = spot < jnp.where(index < 2 * block, limit_of(s, widths, False), limit_of(s, widths, True))
    diff = enc[...] - mix
    lost = jnp.where(ok, jnp.mean(diff * diff, axis=1, keepdims=True), 0.0)
    lost = jnp.transpose(jnp.broadcast_to(lost, (n, 128)))[0:8, :]
    losses[...] = lost
    back = lost[:, block : 2 * block]
    high = back.astype(BF)
    rest = back - high.astype(F32)
    below = 2 * block
    mixes[below : below + 16, :] = jnp.zeros((16, dim), BF)
    mixes[below : below + 8, :block] = high
    mixes[below : below + 8, block : 2 * block] = rest.astype(BF)
    mixes[below : below + 8, 2 * block : 3 * block] = (rest - rest.astype(BF).astype(F32)).astype(BF)
    spans = ((mix_own, 0, block), (mix_back, block, 2 * block + 16), (mix_last, 2 * block + 16, 3 * block + 16))
    outs = [pltpu.make_async_copy(mixes.at[a:b, :], out, sems.at[2 + k]) for k, (out, a, b) in enumerate(spans)]
    outs.append(pltpu.make_async_copy(losses, loss, sems.at[5]))
    for out in outs:
        out.start()
    pull = jnp.where(ok, (2.0 * COMMIT / dim) * diff, 0.0)
    denc[...] = pull
    stream.wait(2)
    cots = jnp.concatenate([cot_own[0], cot_got[...], cot_own[1]], axis=0).astype(F32)
    dmix = (cots - pull).astype(BF)
    inner = jnp.zeros_like(peak)
    for piece, rows, cols in chunks:
        d = mm_nt(dmix, piece[rows, :])
        dweight[:, cols] = d
        inner = inner + jnp.sum(score[:, cols] * d, axis=1, keepdims=True)
    inner = inner * inv
    inv = inv * scale
    for piece, rows, cols in chunks:
        dcode = (score[:, cols] * inv * (dweight[:, cols] - inner)).astype(BF)
        denc[...] += mm(dcode, piece[rows, :])
    dmlp[...] = denc[...].astype(BF)
    for out in outs:
        out.wait()


def quantizer(s, enc, cot, cot_got, pieces, tile=512):
    n, dim = enc.shape
    block = n // 3
    count = sum(-(-piece.shape[0] // tile) for piece in pieces)
    wide = count * tile
    return call(
        functools.partial(quant_kernel, tile=tile, scale=dim**-0.5), "quantizer", 21,
        [in_hbm((block, dim)), in_hbm((block + 16, dim)), in_hbm((block, dim))]
        + [in_hbm((8, n), F32), shaped((n, dim), F32), shaped((n, dim))],
        [
            pltpu.VMEM((n, wide), F32), pltpu.VMEM((n, wide), F32), pltpu.VMEM((n, dim), F32),
            pltpu.VMEM((2, block, dim), BF), pltpu.VMEM((n + 16, dim), BF), pltpu.VMEM((8, n), F32),
            pltpu.SemaphoreType.DMA((6,)),
        ],
        s, enc, cot_got, *pieces, cot, micros=14, streamed=1, by_hand=range(4), bounds=True,
    )


def quantizer_plain(s, enc, cots, book):
    n, dim = enc.shape
    block = n // 3
    index = jnp.arange(n)
    ok = spots(index & (2 * block - 1), block, lax.axis_index("seq")) < jnp.where(index < 2 * block, GRID_H * pick(s, lax.axis_index("seq") // 2, 0), GRID_H * s[2])
    scale = dim**-0.5
    scores = mm_nt(enc.astype(BF), book) * scale
    peak = jnp.max(scores, axis=-1, keepdims=True)
    log_total = peak + jnp.log(jnp.sum(jnp.exp(scores - peak), axis=-1, keepdims=True))
    weights = jnp.exp(scores - log_total)
    mix = mm(weights.astype(BF), book)
    diff = enc - mix
    loss = jnp.where(ok, jnp.mean(diff * diff, axis=-1), 0.0)
    pull = jnp.where(ok[:, None], 2.0 * COMMIT / dim * diff, 0.0)
    dmix = (cots.astype(F32) - pull).astype(BF)
    dweights = mm_nt(dmix, book)
    inner = jnp.sum(weights * dweights, axis=-1, keepdims=True)
    dcode = (weights * (dweights - inner) * scale).astype(BF)
    denc = mm(dcode, book) + pull
    low = mix.astype(BF)
    loss = jnp.broadcast_to(loss[None, :], (8, n))
    parts, rest = [], loss[:, block : 2 * block]
    for _ in range(3):
        parts.append(rest.astype(BF))
        rest = rest - parts[-1].astype(F32)
    parts = jnp.pad(jnp.concatenate(parts, axis=1), ((0, 8), (0, dim - 3 * block)))
    back = jnp.concatenate([low[block : 2 * block], parts])
    return low[:block], back, low[2 * block :], loss, denc, denc.astype(BF)


def mlp_bwd_kernel(
    s, widths, dmlp, denc, mid, gain, slope0, slope1, wdown, wup, wout, dp0, dp1, dbranch, dmid_ref, datt, rows, bup, acc,
    *, tile,
):
    hidden, wide = wup.shape[1], slope0.shape[1]
    for t in range(0, hidden, tile):
        span, half, here = slice(t, t + tile), t // wide, slice(t % wide, t % wide + tile)
        slope = jnp.where(s[CORE] == half, slope1[:, here], slope0[:, here]).astype(F32)
        dpre = (mm_nt(dmlp[...], wdown[span, :]) * slope).astype(BF)
        (dp0, dp1)[half][:, here] = dpre
        bup[:, span] = jnp.sum(dpre.astype(F32), axis=0, keepdims=True)
        part = mm_nt(dpre, wup[:, span])
        if t == 0:
            acc[...] = part
        else:
            acc[...] += part
    dy = acc[...]
    xhat, inv = norm_stats(mid[...])
    dmid = denc[...] + norm_back(xhat, inv, line(gain), dy)
    dmid_ref[...] = dmid
    low = dmid.astype(BF)
    dbranch[...] = low
    datt[...] = mm_nt(low, wout[...]).astype(BF)
    rows[0:1, :] = jnp.sum(dy * xhat, axis=0, keepdims=True)
    rows[1:2, :] = jnp.sum(dy, axis=0, keepdims=True)
    rows[2:3, :] = jnp.sum(low.astype(F32), axis=0, keepdims=True)
    rows[3:4, :] = jnp.sum(dmlp[...].astype(F32), axis=0, keepdims=True)


def mlp_bwd(s, dmlp, denc, mid, gain, slopes, wdown, wup, wout):
    n, dim = denc.shape
    hidden, tile = wup.shape[1], 512
    return call(
        functools.partial(mlp_bwd_kernel, tile=tile), "mlp_bwd", 8,
        [
            shaped((n, hidden // 2)), shaped((n, hidden // 2)), shaped((n, dim)), shaped((n, dim), F32),
            shaped((n, dim)), shaped((4, dim), F32), shaped((1, hidden), F32),
        ],
        [pltpu.VMEM((n, dim), F32)],
        s, dmlp, denc, mid, gain, *slopes, wdown, wup, wout, micros=9,
    )


TINY_UP, TINY_QKV = 32, 16


def labels(steps, index, part):
    return [[part if step == "y" else parity(index & step[1]) for step in order] for order in steps]


def place(s, first, steps, keep, send, index, part, rows, value):
    sides = labels(steps, index, part)
    slots = [functools.reduce(lambda x, y: 2 * x + y, side[1:], 0) for side in sides]
    here = sides[0][0] + (sides[1][0] - sides[0][0]) * s[CORE]
    slot = slots[0] + (slots[1] - slots[0]) * s[CORE]

    @pl.when(s[first] == here)
    def _():
        keep[slot, rows, :] = value

    @pl.when(s[first] != here)
    def _():
        send[slot, rows, :] = value


def quotient(index, size):
    return ((index.astype(F32) + 0.5) * (1.0 / size)).astype(jnp.int32)


def tiny_rows(rows, shards, half):
    dim = rows.shape[1]
    part = dim // shards
    shard = lax.broadcasted_iota(jnp.int32, (shards, dim), 0)
    of = quotient(lax.broadcasted_iota(jnp.int32, (shards, dim), 1), part)
    local = lax.broadcasted_iota(jnp.int32, (dim, 1), 0)
    local = local - quotient(local, part) * part
    lane = lax.broadcasted_iota(jnp.int32, (dim, half), 1)
    total = jnp.zeros((shards, half), F32)
    for k in range(4):
        spread = jnp.where(of == shard, jnp.broadcast_to(rows[k : k + 1, :], (shards, dim)), 0.0)
        total = total + mm(spread.astype(BF), (lane == local + k * part).astype(F32).astype(BF))
    return total


def grad_down_kernel(s, widths, dm, act0, act1, keep, send, *, shards, steps):
    n, width = act0.shape[0], keep.shape[2]
    rows = dm.shape[1] // shards // 2
    full = (mm_tn(dm[:n, :], act0[:, :width]) + mm_tn(dm[n:, :], act1[:, :width])).astype(BF)
    for j in range(2 * shards):
        place(s, SIDES, steps, keep, send, j // 2, j % 2, slice(None), full[j * rows : (j + 1) * rows])


def grad_down(s, dm, act0, act1, shards, steps):
    dim = dm.shape[1]
    part = shaped((shards, dim // shards // 2, act0.shape[1] - dim))
    return call(
        functools.partial(grad_down_kernel, shards=shards, steps=steps), "grad_down", 10, [part, part], [],
        s, dm, act0, act1, micros=4,
    )


def grad_up_kernel(s, widths, a0, a1, *refs, shards, steps):
    d0, d1, (four, bup, keep, send) = refs[:3], refs[3:6], refs[6:]
    size, half = keep.shape[1], keep.shape[2]
    wide = d0[0].shape[1]
    hidden = 2 * wide
    first = hidden // 2
    cols = hidden // shards
    rows = 2 * half // shards
    per = shards // 4
    tiny = tiny_rows(four[...], shards, half)
    at = lax.broadcasted_iota(jnp.int32, (2 * size - half - rows, half), 0)

    def put(index, part, at, value):
        place(s, SIDES + 4, steps, keep, send, index, part, slice(at, at + value.shape[0]), value)

    h = slice(first + half, first + 2 * half)
    out = (mm_tn(d0[2][...], a0[:, h]) + mm_tn(d1[2][...], a1[:, h])).astype(BF)
    h = slice(first, first + half)
    for k in range(0, shards, per):
        side, first_col = k * cols // wide, k * cols % wide
        span = slice(first_col, first_col + per * cols)
        full = (mm_tn(a0[:, h], d0[side][:, span]) + mm_tn(a1[:, h], d1[side][:, span])).astype(BF)
        for j in range(per):
            put(k + j, 0, 0, full[:size, j * cols : (j + 1) * cols])
            put(k + j, 1, 0, full[size:, j * cols : (j + 1) * cols])
            put(k + j, 1, half - size, out[(k + j) * rows : (k + j + 1) * rows])
            both = jnp.where(at == 0, tiny[k + j : k + j + 1], 0.0)
            both = both + jnp.where(at == 1, bup[:, (k + j) * cols : (k + j + 1) * cols], 0.0)
            put(k + j, 1, half - size + rows, both.astype(BF))


def grad_up(s, mine, got, dp0, dp1, four, bup, shards, steps):
    half = got.shape[1] - mine.shape[1]
    dim = 2 * half
    part = shaped((shards, (half + dim // shards + TINY_UP) // 2, half))
    return call(
        functools.partial(grad_up_kernel, shards=shards, steps=steps), "grad_up", 10,
        [part, part], [], s, mine, got, *dp0, *dp1, four, bup, micros=5,
    )


def got_rows(owns):
    return owns[0].shape[0] // 5


def last_of(ref, step, n, block, dim):
    wide = ref.shape[1]
    blocks = [
        ref[5 * n + k * block : 5 * n + (k + 1) * block, :] for k in range(step * dim // wide, (step + 1) * dim // wide)
    ]
    return jnp.concatenate(blocks, axis=1)


def d_of(owns, gots, step, n):
    if step == 0:
        return jnp.concatenate([own[4 * n : 5 * n, :] for own in owns], axis=1)
    mine, theirs = slice((step - 1) * n, step * n), slice((step + 1) * n, (step + 2) * n)
    return jnp.concatenate(
        [(own[mine, :].astype(F32) + got[theirs, :].astype(F32)).astype(BF) for own, got in zip(owns, gots)], axis=1
    )


def grad_qkv_kernel(
    s, widths, *refs, shards, steps
):
    groups = (len(refs) - 6) // 2
    owns, gots = refs[:groups], refs[groups : 2 * groups]
    h_own, other, norms, sums, keep, send = refs[-6:]
    n, half = got_rows(owns), h_own.shape[1]
    block = n // 2
    dim = 2 * half
    h = slice(other.shape[1] - half, other.shape[1])
    size = 3 * dim // shards // 2

    def put(k, at, value):
        place(s, SIDES + 8, steps, keep, send, k // 2, k % 2, slice(at, at + value.shape[0]), value)

    for step in range(3):
        d_own, d_got = d_of(owns, gots, step, n), d_of(gots, owns, step, n)
        full = mm_tn(d_own, h_own[:n, :]) + mm_tn(d_got, other[:n, h])
        last_own, last_got = (last_of(refs[1], step, n, block, dim) for refs in (owns, gots))
        full = full + mm_tn(last_own, h_own[n:, :]) + mm_tn(last_got, other[n:, h])
        full = full.astype(BF)
        first = step * dim
        for k in range(first // size, (first + dim + size - 1) // size):
            lo, hi = max(first, k * size), min(first + dim, (k + 1) * size)
            put(k, lo - k * size, full[lo - first : hi - first])
    four = jnp.concatenate([norms[...], sums[0:1, :], sums[2:3, :]], axis=0)
    tiny = tiny_rows(four, shards, half)
    at = lax.broadcasted_iota(jnp.int32, (TINY_QKV, half), 0)
    for k in range(2 * shards):
        put(k, size, jnp.where(at == 0, tiny[k // 2 : k // 2 + 1], 0.0).astype(BF))


def grad_qkv(s, owns, gots, h_own, other, norms, sums, shards, steps):
    half = h_own.shape[1]
    dim = 2 * half
    part = shaped((shards, 3 * dim // shards // 2 + TINY_QKV, half))
    return call(
        functools.partial(grad_qkv_kernel, shards=shards, steps=steps), "grad_qkv", 12, [part, part], [],
        s, *owns, *gots, h_own, other, norms, sums, micros=4,
    )


def qkv_bwd_kernel(
    s, widths, *refs
):
    groups = (len(refs) - 13) // 2
    owns, gots = refs[:groups], refs[groups : 2 * groups]
    x_got, gain, dmid, w, patches, dx0, dx1, dx2, norms, sums, acc, x_own, sems = refs[-13:]
    block, dim = x_got.shape
    n = 2 * block
    spans = [slice(k * dim, (k + 1) * dim) for k in range(3)]
    stream = Stream(sems, (patches.at[s[CHIP]], x_own.at[0]), (patches.at[2], x_own.at[1]))
    for k, cols in enumerate(spans):
        d = jnp.concatenate([d_of(owns, gots, k, n), last_of(owns[1], k, n, block, dim)], axis=0)
        sums[k : k + 1, :] = jnp.sum(d.astype(F32), axis=0, keepdims=True)
        part = mm_nt(d, w[:, cols])
        if k == 0:
            acc[...] = part
        else:
            acc[...] += part
    dy = acc[...]
    stream.wait(2)
    x = jnp.concatenate([x_own[0], x_got[...], x_own[1]], axis=0).astype(F32)
    xhat, inv = norm_stats(x)
    dx = dmid[...] + norm_back(xhat, inv, line(gain), dy)
    dx0[...] = dx[:block]
    for k in range(2):
        dx1[k * block : (k + 1) * block, :] = dx[block:n, k * dim // 2 : (k + 1) * dim // 2].astype(BF)
    dx2[...] = dx[n:]
    norms[0:1, :] = jnp.sum(dy * xhat, axis=0, keepdims=True)
    norms[1:2, :] = jnp.sum(dy, axis=0, keepdims=True)


def qkv_bwd(s, owns, gots, patches, x_got, gain, dmid, w):
    images, block, dim = patches.shape
    return call(
        qkv_bwd_kernel, "qkv_bwd", 9,
        [
            in_hbm((block, dim), F32), shaped((2 * block, dim // 2)), in_hbm((block, dim), F32),
            shaped((2, dim), F32), shaped((3, dim), F32),
        ],
        [
            pltpu.VMEM((images * block, dim), F32), pltpu.VMEM((2, block, dim), BF),
            pltpu.SemaphoreType.DMA((2,)),
        ],
        s, *owns, *gots, x_got, gain, dmid, w, patches, micros=4, streamed=1,
    )


def finish_kernel(s, widths, both, both_got, down, down_got, up, out, qkv, wdown, *vectors, rows_up, size, parts):
    def sorted_of(value, other):
        cut = value.shape[0] // 2
        mine = [value[:cut].astype(F32), value[cut:].astype(F32)]
        theirs = [other[:cut].astype(F32), other[cut:].astype(F32)]
        second = s[CHIP] > 0
        pairs = [[jnp.where(second, v[1], v[0]), jnp.where(second, v[0], v[1])] for v in (mine, theirs)]
        swap_cores = s[CORE] > 0
        return [
            [jnp.where(swap_cores, b, a) for a, b in zip(*pairs)],
            [jnp.where(swap_cores, a, b) for a, b in zip(*pairs)],
        ]

    cores = sorted_of(both, both_got)
    rows = [jnp.concatenate([first[:rows_up], second[:rows_up]], axis=0) for first, second in cores]
    half = up.shape[0] // 2
    wide = out.shape[0]
    up[:half, :] = rows[0][:half]
    up[half:, :] = rows[1][:half]
    out[...] = jnp.concatenate([r[half : half + wide] for r in rows], axis=1)
    pieces = [jnp.concatenate([f[rows_up : rows_up + size], g[rows_up : rows_up + size]], axis=0) for f, g in cores]
    qkv[...] = jnp.concatenate(pieces, axis=1)
    two = rows[0][half + wide : half + wide + 8] + rows[1][half + wide : half + wide + 8]
    one = cores[0][0][rows_up + size : rows_up + size + 8] + cores[1][0][rows_up + size : rows_up + size + 8]
    for ref, (source, row, at) in zip(vectors, parts):
        ref[...] = (one, two)[source][row : row + 1, at : at + ref.shape[0]].reshape(ref.shape[0])
    cores = sorted_of(down, down_got)
    wdown[...] = jnp.concatenate([jnp.concatenate(pair, axis=0) for pair in cores], axis=1)


def finish(s, both, both_got, down, down_got, rows_up, dim, hidden, shards):
    part, wide = dim // shards, hidden // shards
    size = 3 * dim // shards // 2
    parts = [(0, 0, k * part) for k in range(4)]
    parts += [(1, 0, 2 * part), (1, 0, 0), (1, 0, part), (1, 1, 0), (1, 0, 3 * part)]
    widths = [part] * 7 + [wide, part]
    return call(
        functools.partial(finish_kernel, rows_up=rows_up, size=size, parts=parts), "finish", 20,
        [in_hbm((dim, wide), F32), in_hbm((part, dim), F32), in_hbm((3 * part, dim), F32), in_hbm((part, hidden), F32)]
        + [in_hbm((width,), F32) for width in widths],
        [], s, both, both_got, down, down_got, micros=3,
    )


def hop(value, step0, step1):
    seq, img = lax.axis_size("seq"), lax.axis_size("img")
    pairs = []
    for s in range(seq):
        step = step1 if s % 2 else step0
        for i in range(img):
            to = (s ^ 2, i) if step == "y" else (s, i ^ (step if isinstance(step, int) else step[0]))
            pairs.append((s * img + i, to[0] * img + to[1]))
    return lax.ppermute(value, ("seq", "img"), pairs)


def plus(kept, got):
    return (kept.astype(F32) + got.astype(F32)).astype(BF)


class Sum:
    def __init__(self, s, base, steps, keep, send):
        self.s, self.base, self.steps, self.sides, self.at = s, base, steps, sides_here(steps), 0
        self.keep = keep.reshape(-1, keep.shape[-1])
        self.got = self.go(send.reshape(self.keep.shape))

    def go(self, value):
        self.at += 1
        return hop(value, self.steps[0][self.at - 1], self.steps[1][self.at - 1])

    def step(self):
        shape = (2, self.got.shape[0] // 2, self.got.shape[1])
        keep, got = self.keep.reshape(shape), self.got.reshape(shape)
        if shape[1] % 16 == 0:
            self.keep, send = halve(self.s, keep, got, self.base + self.at)
        else:
            mine = self.sides[self.at]
            self.keep = plus(pick(keep, mine, 0), pick(got, mine, 0))
            send = plus(pick(keep, 1 - mine, 0), pick(got, 1 - mine, 0))
        self.got = self.go(send)

    def steps_left(self, most):
        while len(self.steps[0]) - self.at > most:
            self.step()

    def last(self):
        return add(self.s, self.keep, self.got) if self.keep.shape[0] % 16 == 0 else plus(self.keep, self.got)


def finish_plain(core, chip, both, both_got, down, down_got, rows_up, dim, hidden, shards):
    part, wide, half = dim // shards, hidden // shards, dim // 2
    size = 3 * dim // shards // 2

    def sorted_of(value, other):
        pairs = []
        for v in (value, other):
            a, b = jnp.split(v.astype(F32), 2)
            pairs.append([jnp.where(chip == 0, a, b), jnp.where(chip == 0, b, a)])
        mine, theirs = pairs
        first = [jnp.where(core == 0, a, b) for a, b in zip(mine, theirs)]
        return [first, [jnp.where(core == 0, b, a) for a, b in zip(mine, theirs)]]

    cores = sorted_of(both, both_got)
    rows = [jnp.concatenate([f[:rows_up], g[:rows_up]]) for f, g in cores]
    up = jnp.concatenate([r[:wide].T for r in rows])
    out = jnp.concatenate([r[wide : wide + part] for r in rows], axis=1)
    pieces = [jnp.concatenate([f[rows_up : rows_up + size], g[rows_up : rows_up + size]]) for f, g in cores]
    two = sum(r[wide + part :] for r in rows).reshape(-1)
    one = sum(f[rows_up + size :] for f, _ in cores).reshape(-1)
    down = jnp.concatenate([jnp.concatenate(pair) for pair in sorted_of(down, down_got)], axis=1)
    first = [one[k * part : (k + 1) * part] for k in range(4)]
    second = [two[k * part : (k + 1) * part] for k in (2, 0, 1)]
    last = [two[4 * part : 4 * part + wide], two[3 * part : 4 * part]]
    return [up, out, jnp.concatenate(pieces, axis=1), down, *first, *second, *last]


class Book:
    def __init__(self, s, codebook):
        n_img = lax.axis_size("img")
        bits = [1 << k for k in range(n_img.bit_length() - 1)]
        masks = [1, 2, 6] if n_img == 8 else bits
        self.orders = list(zip(masks[1:], [1, "y", *masks[3:]]))
        self.ends = ((1, masks[1]), ("y", masks[2]))
        self.s, self.value = s, codebook

    def stack(self, *parts, there=()):
        return stack(self.s, *parts, there=there) if sum(part.size for part in parts) < 1 << 21 else jnp.concatenate(parts)

    def start(self):
        self.got = hop(self.value, *self.orders.pop(0))

    def double(self):
        self.value = self.stack(self.value, self.got)

    def spread(self):
        self.beside, self.across = hop(self.value, *self.ends[0]), hop(self.value, *self.ends[1])
        self.other = [swap(self.value, "seq", 1)]

    def corner(self, there):
        if self.value.size < 1 << 21:
            *parts, self.sides = cut(self.s, self.across, self.beside, (there, self.other[0]))
        else:
            half = self.value.shape[0] // 2
            parts = self.across[:half], self.beside[half:]
            self.sides = jnp.concatenate([self.beside, self.across])
        self.corners = hop(parts[0], *self.ends[0]), hop(parts[1], *self.ends[1])
        self.other.append(swap(self.sides, "seq", 1))

    def finish(self):
        rest = self.stack(*self.corners, there=(self.other[1],))
        return [self.value, self.sides, rest, *self.other, swap(rest, "seq", 1)]


def shards(
    patches,
    widths,
    ln1_gain,
    ln1_bias,
    w_qkv,
    b_query,
    b_value,
    w_out,
    b_out,
    ln2_gain,
    ln2_bias,
    w_up,
    b_up,
    w_down,
    b_down,
    codebook,
    cotangent,
):
    images, block, dim = patches.shape
    hidden = w_up.shape[1]
    n_img = lax.axis_size("img")
    me = lax.axis_index("seq")
    chip, core = me // 2, me % 2
    half, main = dim // 2, 2 * block
    fits = codebook.shape[0] * n_img * lax.axis_size("seq") <= 4096
    aligned = n_img == 8 and dim // n_img // 2 % 16 == 0
    steps_down, steps_up, steps_qkv = plans(n_img)
    s = widths

    Order.token = jnp.zeros((8, 128), F32)
    book = Book(s, codebook)
    book.start()
    x_got = swap(pick(patches, 1 - chip, 0), "seq", 2)
    kv_last, h_last = kv_last_fwd(s, patches, ln1_gain, ln1_bias, b_value, w_qkv)
    kv_y = swap(kv_last, "seq", 2)
    while book.orders:
        book.double()
        book.start()
    q_main, q_last, *kvs, h_mine, h_send = qkv_fwd(s, patches, x_got, h_last, ln1_gain, ln1_bias, b_query, b_value, w_qkv)
    kvs.append(kv_last)
    kvs_other = [swap(kv, "seq", 1) for kv in kvs]
    book.double()
    book.spread()
    kvs_main = kvs[:2] + kvs_other[:2]
    att_main = attention_fwd(s, q_main, kvs_main, False, block)
    cot_got = swap(pick(cotangent, 1 - chip, 0), "seq", 2)
    kvs_last = [kvs[2], kv_y, kvs_other[2], swap(kv_y, "seq", 1)]
    att_last = attention_fwd(s, q_last, kvs_last, True, block)
    mid, h2, enc, slope0, send = mlp_first(
        s, patches, x_got, att_main, att_last, h_send, b_out, ln2_gain, ln2_bias, b_up, b_down, w_out, w_up,
        w_down,
    )
    got = swap(send, "seq", 1)
    book.corner(cot_got)
    enc, slope1, mine = mlp_second(s, h2, enc, att_main, att_last, b_up, w_up, w_down)
    pieces = book.finish()
    if fits:
        mix0, mix1, mix2, loss, denc, dmlp = quantizer(s, enc, cotangent, cot_got, pieces)
    else:
        cots = jnp.concatenate([pick(cotangent, chip, 0), cot_got, cotangent[2]])
        mix0, mix1, mix2, loss, denc, dmlp = quantizer_plain(s, enc, cots, jnp.concatenate(pieces))
    mix1 = swap(mix1, "seq", 2)

    def split(full, steps):
        rows, cols = full.shape[-2:]
        full = full.reshape([2] * len(steps[0]) + [rows // 2, cols])
        side = sides_here(steps)[0]
        return pick(full, side, 0), pick(full, 1 - side, 0)

    def lines_of(count, *vectors):
        rows = jnp.concatenate([v.reshape(n_img, -1) for v in vectors], axis=1).astype(BF)
        return jnp.pad(rows, ((0, 0), (0, count * half - rows.shape[1]))).reshape(n_img, count, half)

    dmlp_got = swap(dmlp, "seq", 1)
    both = jnp.concatenate([mine, got[:, : mine.shape[1]]])
    if aligned:
        dmlp_both = stack(s, dmlp, dmlp_got, there=(got,))
        keep, send = grad_down(s, dmlp_both, mine, got, n_img, steps_down)
    else:
        full = mm_tn(jnp.concatenate([dmlp, dmlp_got]), both[:, : hidden // 2]).astype(BF)
        keep, send = split(full.reshape(n_img, -1, hidden // 2), steps_down)
    down = Sum(s, 0, steps_down, keep, send)
    *dp, dmid, datt, rows_two, sum_bup = mlp_bwd(s, dmlp, denc, mid, ln2_gain, (slope0, slope1), w_down, w_up, w_out)
    dp_got = [swap(part, "seq", 1) for part in dp]
    quantized, token_loss = assemble(s, (mix0, mix1, mix2), loss)
    keep_last, send_last, dq_last = attention_bwd(s, q_last, kvs_last, datt, main, True, block, ())
    got_last = swap(send_last, "seq", 1)
    keep_last, send_last = fold(s, keep_last, got_last)
    down.step()
    got_last = swap(send_last, "seq", 2)
    if aligned:
        keep, send = grad_up(s, mine, got, dp, dp_got, rows_two, sum_bup, n_img, steps_up)
    else:
        dps = jnp.concatenate([jnp.concatenate(dp, axis=1), jnp.concatenate(dp_got, axis=1)])
        up = mm_tn(both[:, hidden // 2 : hidden // 2 + half], dps[:, :hidden]).astype(BF)
        up = up.reshape(half, n_img, -1).transpose(1, 2, 0)
        out = mm_tn(dps[:, hidden:], both[:, hidden // 2 + half :]).astype(BF).reshape(n_img, -1, half)
        tiny = lines_of(TINY_UP, rows_two[0], rows_two[1], rows_two[2], rows_two[3], sum_bup[0])
        keep, send = split(jnp.concatenate([up, out, tiny], axis=1), steps_up)
    up = Sum(s, len(steps_down[0]), steps_up, keep, send)
    d_main, d_got = [], []
    for pairs, more in (((0, 1), ()), ((2, 3), (dq_last, keep_last, got_last)), ((4, 5), ())):
        d_main += attention_bwd(s, q_main, kvs_main, datt, 0, False, block, pairs, more)
        d_got.append(swap(d_main[-1], "seq", 1))
        if len(d_main) == 2:
            down.step()
    dx0, dx1, dx2, norms, sums = qkv_bwd(s, d_main, d_got, patches, x_got, ln1_gain, dmid, w_qkv)
    up.step()
    down.step()
    if aligned:
        keep, send = grad_qkv(
            s, d_main, d_got, h_mine, got, norms, sums, n_img, steps_qkv
        )
    else:
        n = main

        def assembled(owns, gots):
            rows = [jnp.concatenate([own[4 * n : 5 * n] for own in owns], axis=1)]
            for k in (0, 1):
                mine, theirs = slice(k * n, (k + 1) * n), slice((k + 2) * n, (k + 3) * n)
                rows.append(jnp.concatenate([plus(own[mine], got[theirs]) for own, got in zip(owns, gots)], axis=1))
            last = owns[1][5 * n :].reshape(-1, block, owns[1].shape[1])
            return [jnp.concatenate(rows, axis=1), jnp.concatenate(list(last), axis=1)]

        d = jnp.concatenate(assembled(d_main, d_got) + assembled(d_got, d_main))
        h = jnp.concatenate([h_mine, got[:, -half:]])
        full = mm_tn(d, h).astype(BF).reshape(n_img, 2, -1, half)
        tiny = lines_of(TINY_QKV, norms[0], norms[1], sums[0], sums[2])
        full = jnp.concatenate([full, jnp.stack([tiny, tiny], axis=1)], axis=2)
        keep, send = split(full.reshape(n_img, -1, half), steps_qkv)
    qkv = Sum(s, 2 * len(steps_down[0]), steps_qkv, keep, send)

    down.steps_left(0)
    qkv.step()
    up.step()
    sum_down = down.last()
    down_other = swap(sum_down, "seq", 2)
    qkv.step()
    up.steps_left(0)
    qkv.steps_left(0)
    sum_up = up.last()
    up_other = swap(stack(s, sum_up, dx1) if aligned else jnp.concatenate([sum_up, dx1]), "seq", 2)
    sum_qkv = qkv.last()
    qkv_other = swap(sum_qkv, "seq", 2)
    down_both = stack(s, sum_down, down_other) if aligned else jnp.concatenate([sum_down, down_other])
    down_got = swap(down_both, "seq", 1)
    grad_input = assemble_dx(s, dx0, up_other, dx2)
    if aligned:
        both = collect(s, sum_up, sum_qkv, up_other, qkv_other)
    else:
        both = jnp.concatenate([sum_up, sum_qkv, up_other[: sum_up.shape[0]], qkv_other])
    both_got = swap(both, "seq", 1)
    rows_up = sum_up.shape[0]
    if aligned:
        weights = finish(s, both, both_got, down_both, down_got, rows_up, dim, hidden, n_img)
    else:
        weights = finish_plain(core, chip, both, both_got, down_both, down_got, rows_up, dim, hidden, n_img)
    g_up, g_out, g_qkv, g_down, g_gain1, g_shift1, g_bq, g_bv, g_bout, g_gain2, g_shift2, g_bup, g_bdown = weights

    return (
        quantized,
        token_loss,
        grad_input,
        g_gain1,
        g_shift1,
        g_qkv.T,
        g_bq,
        g_bv,
        g_out.T,
        g_bout,
        g_gain2,
        g_shift2,
        g_up,
        g_bup,
        g_down.T,
        g_bdown,
    )


def solution(mesh):
    return jax.shard_map(
        shards,
        mesh=mesh,
        in_specs=(
            P("img", "seq", None),
            P("img"),
            P(),
            P(),
            P(),
            P(),
            P(),
            P(),
            P(),
            P(),
            P(),
            P(),
            P(),
            P(),
            P(),
            P(("seq", "img"), None),
            P("img", "seq", None),
        ),
        out_specs=(
            P("img", "seq", None),
            P("img", "seq"),
            P("img", "seq", None),
            P("img"),
            P("img"),
            P(None, "img"),
            P("img"),
            P("img"),
            P(None, "img"),
            P("img"),
            P("img"),
            P("img"),
            P(None, "img"),
            P("img"),
            P(None, "img"),
            P("img"),
        ),
        check_vma=False,
    )
```

```python
import functools

import jax
import jax.numpy as jnp
from jax import lax
from jax.experimental import pallas as pl
from jax.experimental.pallas import tpu as pltpu
from jax.sharding import PartitionSpec as P

HEAD_DIM = 64
GRID_H = 16
EPS_NORM = 1e-06
COMMIT = 16.0
BF = jnp.bfloat16
F32 = jnp.float32
MIB = 1024 * 1024
MASKED = -1000000000.0


def mm(a, b):
    return jnp.dot(a, b, preferred_element_type=F32)


def mm_nt(a, b):
    return lax.dot_general(a, b, (((1,), (1,)), ((), ())), preferred_element_type=F32)


def mm_tn(a, b):
    return lax.dot_general(a, b, (((0,), (0,)), ((), ())), preferred_element_type=F32)


def swap(value, axis, bit):
    count = lax.axis_size(axis)
    return lax.ppermute(value, axis, [(i, i ^ bit) for i in range(count)])


def pick(value, index, axis):
    return lax.dynamic_index_in_dim(value, index, axis, keepdims=False)


def after(value, *others):
    return lax.optimization_barrier((value, *others))[0]


def parity(number):
    return bin(number).count("1") % 2


def shaped(shape, dtype=BF):
    return jax.ShapeDtypeStruct(tuple(shape), dtype)


def in_hbm(shape, dtype=BF):
    return pltpu.HBM(tuple(shape), dtype)


class Order:
    token = None


def call(kernel, name, mib, out_shape, scratch, s, *args, micros, streamed=0, by_hand=(), bounds=False):
    vm, hbm = pl.BlockSpec(memory_space=pltpu.VMEM), pl.BlockSpec(memory_space=pl.ANY)
    direct, count = len(args) - streamed, len(args) + len(out_shape)
    args = [
        pltpu.with_memory_space_constraint(arg, pltpu.HBM) if arg.ndim == 1 or (k >= direct and name not in ("stack", "cut")) else arg
        for k, arg in enumerate(args)
    ]

    def body(*refs):
        limits, token, refs = refs[0], refs[bounds], refs[bounds + 1 :]
        kernel(Place(), limits, *refs[:count], *refs[count + 1 :])
        refs[count][...] = token[...]

    out = pl.pallas_call(
        body,
        in_specs=[vm] * (direct + 1 + bounds) + [hbm] * streamed,
        out_specs=[hbm if out in by_hand else vm for out in range(len(out_shape))] + [vm],
        out_shape=[*out_shape, shaped((8, 128), F32)],
        scratch_shapes=scratch,
        compiler_params=pltpu.CompilerParams(vmem_limit_bytes=mib * MIB),
        cost_estimate=pl.CostEstimate(flops=int(micros * 2e8), bytes_accessed=0, transcendentals=0),
        name=name,
    )(*([s] if bounds else []), Order.token, *args)
    Order.token = out[-1]
    return out[:-1]


class Stream:
    def __init__(self, sems, *pairs, ahead=3):
        self.copies = [pltpu.make_async_copy(a, b, sems.at[k]) for k, (a, b) in enumerate(pairs)]
        self.done, self.begun = 0, 0
        self.start(ahead)

    def start(self, count):
        while self.begun < min(count, len(self.copies)):
            self.copies[self.begun].start()
            self.begun += 1

    def wait(self, count):
        while self.done < count:
            self.copies[self.done].wait()
            self.done += 1
            self.start(self.begun + 1)


ME, CORE, CHIP, SIDES = range(4)
X, NEAR, FAR = (1, 1), (2, 2), (4, 4)


def plans(n_img):
    if n_img == 8:
        return (
            ([X, NEAR, "y", FAR], ["y", NEAR, X, FAR]),
            ([X, "y", NEAR, FAR], ["y", X, NEAR, FAR]),
            ([NEAR, X, "y", FAR], [NEAR, "y", X, FAR]),
        )
    bits = [1 << k for k in reversed(range(n_img.bit_length() - 1))]
    order = [(bit, bit) for bit in bits] + ["y"]
    return ((order, order),) * 3


def side_here(step):
    if step == "y":
        return lax.axis_index("seq") // 2
    bits = lax.axis_index("img") & step[1]
    value = 0
    for k in range(step[1].bit_length()):
        value = value ^ ((bits >> k) & 1)
    return value


def sides_here(steps):
    core = lax.axis_index("seq") % 2
    return [jnp.where(core == 0, side_here(a), side_here(b)) for a, b in zip(*steps)]


class Place:
    def __getitem__(self, what):
        me = lax.axis_index("seq")
        if what < SIDES:
            return (me, me % 2, me // 2)[what]
        steps = plans(lax.axis_size("img"))
        chain, step = divmod(what - SIDES, len(steps[0][0]))
        return sides_here([order[step : step + 1] for order in steps[chain]])[0]


def line(ref, start=0, size=None):
    size = ref.shape[0] if size is None else size
    return ref[start : start + size].reshape(1, size)


def norm_stats(x):
    center = x - jnp.mean(x, axis=-1, keepdims=True)
    spread = jnp.mean(center * center, axis=-1, keepdims=True)
    inv = lax.rsqrt(spread + EPS_NORM)
    return center * inv, inv


def norm_back(xhat, inv, gain, dy):
    dxhat = dy * gain
    return inv * (
        dxhat - jnp.mean(dxhat, axis=-1, keepdims=True) - xhat * jnp.mean(dxhat * xhat, axis=-1, keepdims=True)
    )


def spots(index, block, me):
    shift = block.bit_length() - 1
    assert block == 1 << shift
    place = index >> shift
    mask = ((place & 1) << 1) | (place >> 1)
    return ((me ^ mask) << shift) | (index & (block - 1))


def limit_of(s, widths, last):
    row = widths[...].reshape(1, widths.shape[0])
    return GRID_H * (row[:, 2:3] if last else jnp.where(s[CHIP] == 0, row[:, 0:1], row[:, 1:2]))


def side_of(ref, side, width):
    return ref[:, pl.ds(pl.multiple_of(side * width, 128), width)]


def kv_last_kernel(s, widths, gain, shift, bv, patches, w_hbm, kv, h, x, w, sems):
    dim = h.shape[1]
    stream = Stream(sems, (patches.at[2], x), *((w_hbm.at[:, k * dim : (k + 1) * dim], w.at[k - 1]) for k in (1, 2)))
    stream.wait(1)
    xhat, _ = norm_stats(x[...].astype(F32))
    h[...] = (xhat * line(gain) + line(shift)).astype(BF)
    stream.wait(2)
    kv[:, :dim] = mm(h[...], w[0]).astype(BF)
    stream.wait(3)
    kv[:, dim:] = (mm(h[...], w[1]) + line(bv)).astype(BF)


def kv_last_fwd(s, patches, gain, shift, bv, w):
    _, block, dim = patches.shape
    return call(
        kv_last_kernel, "kv_last_fwd", 8, [shaped((block, 2 * dim)), shaped((block, dim))],
        [pltpu.VMEM((block, dim), BF), pltpu.VMEM((2, dim, dim), BF), pltpu.SemaphoreType.DMA((3,))],
        s, gain, shift, bv, patches, w, micros=2, streamed=2,
    )


def qkv_kernel(
    s, widths, got, h_last, gain, shift, bq, bv, w, patches, q_main, q_last, kv0, kv1, mine, send, h, x_own, sems
):
    half, dim = mine.shape[1], w.shape[0]
    block = got.shape[0]
    stream = Stream(sems, (patches.at[s[CHIP]], x_own))
    h[2 * block :, :] = h_last[...]
    xhat, _ = norm_stats(got[...].astype(F32))
    h[block : 2 * block, :] = (xhat * line(gain) + line(shift)).astype(BF)
    stream.wait(1)
    xhat, _ = norm_stats(x_own[...].astype(F32))
    h[:block, :] = (xhat * line(gain) + line(shift)).astype(BF)
    mine[...] = side_of(h, s[CORE], half)
    send[...] = side_of(h, 1 - s[CORE], half)
    keys = mm(h[: 2 * block, :], w[:, dim : 2 * dim]).astype(BF)
    values = (mm(h[: 2 * block, :], w[:, 2 * dim :]) + line(bv)).astype(BF)
    for k, out in enumerate((kv0, kv1)):
        out[:, :dim] = keys[k * block : (k + 1) * block]
        out[:, dim:] = values[k * block : (k + 1) * block]
    q = (mm(h[...], w[:, :dim]) + line(bq)).astype(BF)
    q_main[...] = q[: 2 * block]
    q_last[...] = q[2 * block :]


def qkv_fwd(s, patches, got, h_last, gain, shift, bq, bv, w):
    images, block, dim = patches.shape
    n, half = images * block, dim // 2
    return call(
        qkv_kernel, "qkv_fwd", 8,
        [
            shaped((2 * block, dim)), shaped((block, dim)), *[shaped((block, 2 * dim))] * 2, in_hbm((n, half)),
            shaped((n, half)),
        ],
        [pltpu.VMEM((n, dim), BF), pltpu.VMEM((block, dim), BF), pltpu.SemaphoreType.DMA((1,))],
        s, got, h_last, gain, shift, bq, bv, w, patches, micros=3, streamed=1,
    )


def two_heads(value):
    left = lax.broadcasted_iota(jnp.int32, value.shape, 1) < HEAD_DIM
    zero = jnp.zeros_like(value)
    return jnp.concatenate([jnp.where(left, value, zero), jnp.where(left, zero, value)], axis=0)


def one_pair(value):
    n = value.shape[0] // 2
    left = lax.broadcasted_iota(jnp.int32, (n, value.shape[1]), 1) < HEAD_DIM
    return jnp.where(left, value[:n], value[n:])


def rows_of(refs, lanes):
    return jnp.concatenate([ref[:, lanes] for ref in refs], axis=0)


def att_fwd_kernel(s, widths, q, *refs, last, block):
    kvs, o = refs[:-1], refs[-1]
    dim = q.shape[1]
    m = sum(kv.shape[0] for kv in kvs)
    index = lax.broadcasted_iota(jnp.int32, (1, m), 1)
    ok = spots(index, block, s[ME]) < limit_of(s, widths, last)
    for p in range(dim // 128):
        at, av = slice(p * 128, (p + 1) * 128), slice(dim + p * 128, dim + (p + 1) * 128)
        k, v = rows_of(kvs, at), rows_of(kvs, av)
        raw = mm_nt(two_heads(q[:, at]), k) * (HEAD_DIM**-0.5)
        scores = jnp.where(ok, raw, MASKED)
        expo = jnp.exp(scores - jnp.max(scores, axis=1, keepdims=True))
        probs = expo * (1.0 / jnp.sum(expo, axis=1, keepdims=True))
        o[:, at] = one_pair(mm(probs.astype(BF), v)).astype(BF)


def attention_fwd(s, q, kvs, last, block):
    return call(
        functools.partial(att_fwd_kernel, last=last, block=block), "attention_fwd", 10, [shaped(q.shape)], [],
        s, q, *kvs, micros=5, bounds=True,
    )[0]


def att_bwd_kernel(s, widths, q, do, *refs, last, block, first, pairs, more):
    n, dim = q.shape
    if pairs:
        kvs, out = refs[: len(refs) - 1 - more], refs[-1]
        m = sum(kv.shape[0] for kv in kvs)
        parts = [out.at[k * m // 2 : (k + 1) * m // 2, :] for k in range(4)]
        dq = out.at[2 * m : 2 * m + n, :]
        if more:
            dq_last, keep_last, got_last = refs[-4:-1]
            rows, wide = dq_last.shape[0], out.shape[1]
            parts_last = [dq_last[...]] + [
                (keep_last[k].astype(F32) + got_last[k].astype(F32)).astype(BF) for k in range(2)
            ]
            for k in range(3 * dim // wide):
                part, at = parts_last[k * wide // dim], k * wide % dim
                out[2 * m + n + k * rows : 2 * m + n + (k + 1) * rows, :] = part[:, at : at + wide]
    else:
        kvs, (keep, send, dq) = refs[:-3], refs[-3:]
        m = sum(kv.shape[0] for kv in kvs)
        parts = [keep.at[0], keep.at[1], send.at[0], send.at[1]]
    index = lax.broadcasted_iota(jnp.int32, (m, 1), 0)
    ok = spots(index, block, s[ME]) < limit_of(s, widths, last)
    for p in pairs or range(dim // 128):
        at, av = slice(p * 128, (p + 1) * 128), slice(dim + p * 128, dim + (p + 1) * 128)
        to = slice((p - pairs[0]) * 128, (p - pairs[0] + 1) * 128) if pairs else at
        k, v = rows_of(kvs, at), rows_of(kvs, av)
        q2, do2 = two_heads(q[:, at]), two_heads(do[first : first + n, at])
        raw = mm_nt(k, q2) * (HEAD_DIM**-0.5)
        scores = jnp.where(ok, raw, MASKED)
        expo = jnp.exp(scores - jnp.max(scores, axis=0, keepdims=True))
        probs = expo * (1.0 / jnp.sum(expo, axis=0, keepdims=True))
        dv = mm(probs.astype(BF), do2).astype(BF)
        dp = mm_nt(v, do2)
        inner = jnp.sum(probs * dp, axis=0, keepdims=True)
        ds = (probs * (dp - inner) * (HEAD_DIM**-0.5)).astype(BF)
        dk = mm(ds, q2).astype(BF)
        dq[:, to] = one_pair(mm_tn(ds, k)).astype(BF)
        for ref, part in zip(parts, (dk[: m // 2], dv[: m // 2], dk[m // 2 :], dv[m // 2 :])):
            ref[:, to] = part


def attention_bwd(s, q, kvs, do, first, last, block, pairs, more=()):
    n, dim = q.shape
    m = sum(kv.shape[0] for kv in kvs)
    return call(
        functools.partial(att_bwd_kernel, last=last, block=block, first=first, pairs=pairs, more=len(more)),
        "attention_bwd", 12,
        [shaped((2 * m + n + (len(more) and 3 * dim // len(pairs)), 128 * len(pairs)))] if pairs else [shaped((2, m // 2, dim)), shaped((2, m // 2, dim)), shaped((n, dim))],
        [], s, q, do, *kvs, *more, micros=4, bounds=True,
    )


def fold_kernel(s, widths, keep, got, keep_out, send_out):
    block = keep_out.shape[1]
    for k in range(2):
        total = (keep[k].astype(F32) + got[k].astype(F32)).astype(BF)
        keep_out[k] = total[:block]
        send_out[k] = total[block:]


def fold(s, keep, got):
    part = shaped((2, keep.shape[1] // 2, keep.shape[2]))
    return call(fold_kernel, "fold", 4, [part, part], [], s, keep, got, micros=0.5)


def stack_kernel(s, widths, *refs, count):
    at = 0
    for ref in refs[:count]:
        refs[-1][at : at + ref.shape[0], :] = ref[...]
        at += ref.shape[0]


def stack(s, *parts, there=()):
    shape = (sum(part.shape[0] for part in parts), parts[0].shape[1])
    kernel = functools.partial(stack_kernel, count=len(parts))
    return call(kernel, "stack", 8, [shaped(shape)], [], s, *parts, *there, micros=0.5, streamed=len(there))[0]


def cut_kernel(s, widths, a, b, *refs):
    first, second, both = refs[-3:]
    rows = first.shape[0]
    first[...] = a[:rows, :]
    second[...] = b[rows:, :]
    both[: 2 * rows, :] = b[...]
    both[2 * rows :, :] = a[...]


def cut(s, a, b, there):
    rows, dim = a.shape
    part = shaped((rows // 2, dim))
    return call(
        cut_kernel, "cut", 6, [part, part, shaped((2 * rows, dim))], [], s, a, b, *there, micros=0.3, streamed=len(there)
    )


def collect_kernel(s, widths, *refs):
    count = (len(refs) - 1) // 2
    at = 0
    for k, ref in enumerate(refs[:-1]):
        rows = refs[k % count].shape[0]
        refs[-1][at : at + rows, :] = ref[:rows, :]
        at += rows


def collect(s, own, others):
    shape = (2 * sum(part.shape[0] for part in own), own[0].shape[1])
    return call(collect_kernel, "collect", 6, [shaped(shape)], [], s, *own, *others, micros=0.5)[0]


def add_kernel(s, widths, keep, got, out, *, first):
    out[...] = (keep[...].astype(F32) + got[first : first + keep.shape[0], :].astype(F32)).astype(BF)


def add(s, keep, got, first):
    kernel = functools.partial(add_kernel, first=first)
    return call(kernel, "add", 4, [shaped(keep.shape)], [], s, keep, got, micros=0.5)[0]


def sorted_images(s, out, own, back, last):
    first = s[CHIP] == 0
    out[0] = jnp.where(first, own, back)
    out[1] = jnp.where(first, back, own)
    out[2] = last


def assemble_kernel(s, widths, mix0, mix1, mix2, loss, mix, losses):
    block = mix0.shape[0]
    sorted_images(s, mix, mix0[...], mix1[:block, :], mix2[...])
    first = s[CHIP] == 0
    own = loss[0:1, :block]
    back = sum(mix1[block : block + 8, k * block : (k + 1) * block].astype(F32) for k in range(3))[0:1]
    losses[0:1, :] = jnp.where(first, own, back)
    losses[1:2, :] = jnp.where(first, back, own)
    losses[2:3, :] = loss[0:1, 2 * block :]


def assemble(s, mix, loss):
    block, dim = mix[0].shape
    return call(
        assemble_kernel, "assemble", 8, [in_hbm((3, block, dim)), in_hbm((3, block), F32)], [],
        s, *mix, loss, micros=1,
    )


def assemble_dx_kernel(s, widths, dx0, pack, dx2, dx):
    block = dx0.shape[0]
    first = pack.shape[0] - 2 * block
    back = jnp.concatenate([pack[first : first + block, :], pack[first + block :, :]], axis=1)
    sorted_images(s, dx, dx0[...], back.astype(F32), dx2[...])


def assemble_dx(s, *dx):
    block, dim = dx[0].shape
    return call(assemble_dx_kernel, "assemble_dx", 8, [in_hbm((3, block, dim), F32)], [], s, *dx, micros=1)[0]


def halve_kernel(s, widths, keep, got, keep_out, send_out, *, at, first):
    rows = keep_out.shape[0]
    for out, side in ((keep_out, s[SIDES + at]), (send_out, 1 - s[SIDES + at])):
        here = keep[pl.ds(pl.multiple_of(side * rows, 16), rows), :].astype(F32)
        out[...] = (here + got[pl.ds(pl.multiple_of(first + side * rows, 16), rows), :].astype(F32)).astype(BF)


def halve(s, keep, got, at, first):
    part = shaped((keep.shape[0] // 2, keep.shape[1]))
    return call(functools.partial(halve_kernel, at=at, first=first), "halve", 8, [part, part], [], s, keep, got, micros=0.7)


def gelu_pair(x):
    z = jnp.abs(x) * (0.5**0.5)
    t = 1.0 / (1.0 + 0.3275911 * z)
    expo = jnp.exp(-0.5 * x * x)
    poly = t * (0.254829592 + t * (-0.284496736 + t * (1.421413741 + t * (-1.453152027 + t * 1.061405429))))
    tail = 0.5 * poly * expo
    cdf = jnp.where(x < 0.0, tail, 1.0 - tail)
    return x * cdf, cdf + x * (expo * 0.3989422804014327)


def mlp_tiles(side, h2, bup, wup, wdown, enc, act_ref, slope, tile):
    wide = slope.shape[1]
    for k in range(0, wide, tile):
        here, there = slice(k, k + tile), pl.ds(pl.multiple_of(side * wide + k, 128), tile)
        act, rate = gelu_pair(mm(h2[...], wup[:, there]) + bup[there].reshape(1, tile))
        act = act.astype(BF)
        act_ref[:, here] = act
        slope[:, here] = rate.astype(BF)
        enc[...] += mm(act, wdown[there, :])


def mlp_first_kernel(
    s, widths, got, att_main, att_last, h1, bout, gain, shift, bup, bdown, wout, wup, wdown, patches, mid, h2, enc, slope,
    send, x_own, sems, *, tile,
):
    dim = got.shape[1]
    half, wide = dim // 2, slope.shape[1]
    rows = att_main.shape[0]
    side = 1 - s[CORE]
    stream = Stream(sems, (patches.at[s[CHIP]], x_own.at[0]), (patches.at[2], x_own.at[1]))
    branch = mm(jnp.concatenate([att_main[...], att_last[...]], axis=0), wout[...])
    stream.wait(2)
    x = jnp.concatenate([x_own[0], got[...], x_own[1]], axis=0).astype(F32)
    middle = x + branch + line(bout)
    mid[...] = middle
    xhat, _ = norm_stats(middle)
    h2[...] = (xhat * line(gain) + line(shift)).astype(BF)
    enc[...] = middle + line(bdown)
    send[:, wide : wide + half] = side_of(h2, side, half)
    send[:rows, wide + half : wide + dim] = side_of(att_main, side, half)
    send[rows:, wide + half : wide + dim] = side_of(att_last, side, half)
    send[:, wide + dim :] = h1[...]
    mlp_tiles(side, h2, bup, wup, wdown, enc, send, slope, tile)


def mlp_second_kernel(s, widths, h2, enc_in, att_main, att_last, bup, wup, wdown, enc, slope, mine, *, tile):
    half, wide = h2.shape[1] // 2, slope.shape[1]
    rows = att_main.shape[0]
    enc[...] = enc_in[...]
    mine[:, wide : wide + half] = side_of(h2, s[CORE], half)
    mine[:rows, wide + half :] = side_of(att_main, s[CORE], half)
    mine[rows:, wide + half :] = side_of(att_last, s[CORE], half)
    mlp_tiles(s[CORE], h2, bup, wup, wdown, enc, mine, slope, tile)


def mlp_first(s, patches, got, att_main, att_last, h1, bout, gain, shift, bup, bdown, wout, wup, wdown):
    images, block, dim = patches.shape
    n, wide = images * block, wup.shape[1] // 2
    return call(
        functools.partial(mlp_first_kernel, tile=512), "mlp_first", 8,
        [
            shaped((n, dim), F32), shaped((n, dim)), shaped((n, dim), F32), shaped((n, wide)),
            shaped((n, wide + dim + dim // 2)),
        ],
        [pltpu.VMEM((2, block, dim), BF), pltpu.SemaphoreType.DMA((2,))],
        s, got, att_main, att_last, h1, bout, gain, shift, bup, bdown, wout, wup, wdown, patches, micros=6, streamed=1,
    )


def mlp_second(s, h2, enc, att_main, att_last, bup, wup, wdown):
    n, dim = h2.shape
    wide = wup.shape[1] // 2
    return call(
        functools.partial(mlp_second_kernel, tile=512), "mlp_second", 8,
        [shaped((n, dim), F32), shaped((n, wide)), shaped((n, wide + dim))], [],
        s, h2, enc, att_main, att_last, bup, wup, wdown, micros=5,
    )


def quant_kernel(s, widths, enc, cot_got, *refs, tile, scale):
    pieces, cot = refs[:-14], refs[-14]
    mix_own, mix_back, mix_last, loss, denc, dmlp, score, dweight, late, cot_own, mixes, losses, sems = refs[-13:]
    n, dim = enc.shape
    block = n // 3
    chunks, place = [], 0
    for piece in pieces:
        for first in range(0, piece.shape[0], tile):
            size = min(tile, piece.shape[0] - first)
            chunks.append((piece, slice(first, first + size), slice(place, place + size)))
            place += size + -size % 128
    stream = Stream(sems, (cot.at[s[CHIP]], cot_own.at[0]), (cot.at[2], cot_own.at[1]))
    low = enc[...].astype(BF)
    peak = None
    for piece, rows, cols in chunks:
        part = mm_nt(low, piece[rows, :]) * scale
        score[:, cols] = part
        top = jnp.max(part, axis=1, keepdims=True)
        peak = top if peak is None else jnp.maximum(peak, top)
    total = jnp.zeros_like(peak)
    late[...] = jnp.zeros_like(late)
    for piece, rows, cols in chunks:
        e = jnp.exp(score[:, cols] - peak)
        score[:, cols] = e
        total = total + jnp.sum(e, axis=1, keepdims=True)
        late[...] += mm(e.astype(BF), piece[rows, :])
    inv = 1.0 / total
    mix = late[...] * inv
    low = mix.astype(BF)
    mixes[: 2 * block, :] = low[: 2 * block]
    mixes[2 * block + 16 :, :] = low[2 * block :]
    index = lax.broadcasted_iota(jnp.int32, (n, 1), 0)
    spot = spots(index & (2 * block - 1), block, s[ME])
    ok = spot < jnp.where(index < 2 * block, limit_of(s, widths, False), limit_of(s, widths, True))
    diff = enc[...] - mix
    lost = jnp.where(ok, jnp.mean(diff * diff, axis=1, keepdims=True), 0.0)
    lost = jnp.transpose(jnp.broadcast_to(lost, (n, 128)))[0:8, :]
    losses[...] = lost
    back = lost[:, block : 2 * block]
    high = back.astype(BF)
    rest = back - high.astype(F32)
    below = 2 * block
    mixes[below : below + 16, :] = jnp.zeros((16, dim), BF)
    mixes[below : below + 8, :block] = high
    mixes[below : below + 8, block : 2 * block] = rest.astype(BF)
    mixes[below : below + 8, 2 * block : 3 * block] = (rest - rest.astype(BF).astype(F32)).astype(BF)
    spans = ((mix_own, 0, block), (mix_back, block, 2 * block + 16), (mix_last, 2 * block + 16, 3 * block + 16))
    outs = [pltpu.make_async_copy(mixes.at[a:b, :], out, sems.at[2 + k]) for k, (out, a, b) in enumerate(spans)]
    outs.append(pltpu.make_async_copy(losses, loss, sems.at[5]))
    for out in outs:
        out.start()
    pull = jnp.where(ok, (2.0 * COMMIT / dim) * diff, 0.0)
    denc[...] = pull
    stream.wait(2)
    cots = jnp.concatenate([cot_own[0], cot_got[...], cot_own[1]], axis=0).astype(F32)
    dmix = (cots - pull).astype(BF)
    inner = jnp.zeros_like(peak)
    for piece, rows, cols in chunks:
        d = mm_nt(dmix, piece[rows, :])
        dweight[:, cols] = d
        inner = inner + jnp.sum(score[:, cols] * d, axis=1, keepdims=True)
    inner = inner * inv
    inv = inv * scale
    for piece, rows, cols in chunks:
        dcode = (score[:, cols] * inv * (dweight[:, cols] - inner)).astype(BF)
        denc[...] += mm(dcode, piece[rows, :])
    dmlp[...] = denc[...].astype(BF)
    for out in outs:
        out.wait()


def quantizer(s, enc, cot, cot_got, pieces, tile=512):
    n, dim = enc.shape
    block = n // 3
    count = sum(-(-piece.shape[0] // tile) for piece in pieces)
    wide = count * tile
    return call(
        functools.partial(quant_kernel, tile=tile, scale=dim**-0.5), "quantizer", 21,
        [in_hbm((block, dim)), in_hbm((block + 16, dim)), in_hbm((block, dim))]
        + [in_hbm((8, n), F32), shaped((n, dim), F32), shaped((n, dim))],
        [
            pltpu.VMEM((n, wide), F32), pltpu.VMEM((n, wide), F32), pltpu.VMEM((n, dim), F32),
            pltpu.VMEM((2, block, dim), BF), pltpu.VMEM((n + 16, dim), BF), pltpu.VMEM((8, n), F32),
            pltpu.SemaphoreType.DMA((6,)),
        ],
        s, enc, cot_got, *pieces, cot, micros=14, streamed=1, by_hand=range(4), bounds=True,
    )


def quantizer_plain(s, enc, cots, book):
    n, dim = enc.shape
    block = n // 3
    index = jnp.arange(n)
    ok = spots(index & (2 * block - 1), block, lax.axis_index("seq")) < jnp.where(index < 2 * block, GRID_H * pick(s, lax.axis_index("seq") // 2, 0), GRID_H * s[2])
    scale = dim**-0.5
    scores = mm_nt(enc.astype(BF), book) * scale
    peak = jnp.max(scores, axis=-1, keepdims=True)
    log_total = peak + jnp.log(jnp.sum(jnp.exp(scores - peak), axis=-1, keepdims=True))
    weights = jnp.exp(scores - log_total)
    mix = mm(weights.astype(BF), book)
    diff = enc - mix
    loss = jnp.where(ok, jnp.mean(diff * diff, axis=-1), 0.0)
    pull = jnp.where(ok[:, None], 2.0 * COMMIT / dim * diff, 0.0)
    dmix = (cots.astype(F32) - pull).astype(BF)
    dweights = mm_nt(dmix, book)
    inner = jnp.sum(weights * dweights, axis=-1, keepdims=True)
    dcode = (weights * (dweights - inner) * scale).astype(BF)
    denc = mm(dcode, book) + pull
    low = mix.astype(BF)
    loss = jnp.broadcast_to(loss[None, :], (8, n))
    parts, rest = [], loss[:, block : 2 * block]
    for _ in range(3):
        parts.append(rest.astype(BF))
        rest = rest - parts[-1].astype(F32)
    parts = jnp.pad(jnp.concatenate(parts, axis=1), ((0, 8), (0, dim - 3 * block)))
    back = jnp.concatenate([low[block : 2 * block], parts])
    return low[:block], back, low[2 * block :], loss, denc, denc.astype(BF)


def mlp_bwd_kernel(
    s, widths, dmlp, denc, mid, gain, slope0, slope1, wdown, wup, wout, dp0, dp1, dbranch, dmid_ref, datt, rows, bup, acc,
    *, tile,
):
    hidden, wide = wup.shape[1], slope0.shape[1]
    for t in range(0, hidden, tile):
        span, half, here = slice(t, t + tile), t // wide, slice(t % wide, t % wide + tile)
        slope = jnp.where(s[CORE] == half, slope1[:, here], slope0[:, here]).astype(F32)
        dpre = (mm_nt(dmlp[...], wdown[span, :]) * slope).astype(BF)
        (dp0, dp1)[half][:, here] = dpre
        bup[:, span] = jnp.sum(dpre.astype(F32), axis=0, keepdims=True)
        part = mm_nt(dpre, wup[:, span])
        if t == 0:
            acc[...] = part
        else:
            acc[...] += part
    dy = acc[...]
    xhat, inv = norm_stats(mid[...])
    dmid = denc[...] + norm_back(xhat, inv, line(gain), dy)
    dmid_ref[...] = dmid
    low = dmid.astype(BF)
    dbranch[...] = low
    datt[...] = mm_nt(low, wout[...]).astype(BF)
    rows[0:1, :] = jnp.sum(dy * xhat, axis=0, keepdims=True)
    rows[1:2, :] = jnp.sum(dy, axis=0, keepdims=True)
    rows[2:3, :] = jnp.sum(low.astype(F32), axis=0, keepdims=True)
    rows[3:4, :] = jnp.sum(dmlp[...].astype(F32), axis=0, keepdims=True)


def mlp_bwd(s, dmlp, denc, mid, gain, slopes, wdown, wup, wout):
    n, dim = denc.shape
    hidden, tile = wup.shape[1], 512
    return call(
        functools.partial(mlp_bwd_kernel, tile=tile), "mlp_bwd", 8,
        [
            shaped((n, hidden // 2)), shaped((n, hidden // 2)), shaped((n, dim)), shaped((n, dim), F32),
            shaped((n, dim)), shaped((4, dim), F32), shaped((1, hidden), F32),
        ],
        [pltpu.VMEM((n, dim), F32)],
        s, dmlp, denc, mid, gain, *slopes, wdown, wup, wout, micros=9,
    )


TINY_UP, TINY_QKV = 32, 16


def labels(steps, index, part):
    return [[part if step == "y" else parity(index & step[1]) for step in order] for order in steps]


def place(s, first, steps, keep, send, index, part, rows, value):
    sides = labels(steps, index, part)
    slots = [functools.reduce(lambda x, y: 2 * x + y, side[1:], 0) for side in sides]
    here = sides[0][0] + (sides[1][0] - sides[0][0]) * s[CORE]
    slot = slots[0] + (slots[1] - slots[0]) * s[CORE]

    @pl.when(s[first] == here)
    def _():
        keep[slot, rows, :] = value

    @pl.when(s[first] != here)
    def _():
        send[slot, rows, :] = value


def quotient(index, size):
    return ((index.astype(F32) + 0.5) * (1.0 / size)).astype(jnp.int32)


def tiny_rows(rows, shards, half):
    dim = rows.shape[1]
    part = dim // shards
    shard = lax.broadcasted_iota(jnp.int32, (shards, dim), 0)
    of = quotient(lax.broadcasted_iota(jnp.int32, (shards, dim), 1), part)
    local = lax.broadcasted_iota(jnp.int32, (dim, 1), 0)
    local = local - quotient(local, part) * part
    lane = lax.broadcasted_iota(jnp.int32, (dim, half), 1)
    total = jnp.zeros((shards, half), F32)
    for k in range(4):
        spread = jnp.where(of == shard, jnp.broadcast_to(rows[k : k + 1, :], (shards, dim)), 0.0)
        total = total + mm(spread.astype(BF), (lane == local + k * part).astype(F32).astype(BF))
    return total


def grad_down_kernel(s, widths, dm, act0, act1, keep, send, *, shards, steps):
    n, half = act0.shape[0], keep.shape[2]
    rows = dm.shape[1] // shards // 2
    width = keep.shape[1] // rows * half
    full = (mm_tn(dm[:n, :], act0[:, :width]) + mm_tn(dm[n:, :], act1[:, :width])).astype(BF)
    for j in range(2 * shards):
        for k in range(width // half):
            value = full[j * rows : (j + 1) * rows, k * half : (k + 1) * half]
            place(s, SIDES, steps, keep, send, j // 2, j % 2, slice(k * rows, (k + 1) * rows), value)


def grad_down(s, dm, act0, act1, shards, steps):
    dim = dm.shape[1]
    half = dim // 2
    part = shaped((shards, dim // shards // 2 * ((act0.shape[1] - dim) // half), half))
    return call(
        functools.partial(grad_down_kernel, shards=shards, steps=steps), "grad_down", 10, [part, part], [],
        s, dm, act0, act1, micros=4,
    )


def grad_up_kernel(s, widths, a0, a1, *refs, shards, steps):
    d0, d1, (four, bup, keep, send) = refs[:3], refs[3:6], refs[6:]
    size, half = keep.shape[1], keep.shape[2]
    wide = d0[0].shape[1]
    hidden = 2 * wide
    first = hidden // 2
    cols = hidden // shards
    rows = 2 * half // shards
    per = shards // 4
    tiny = tiny_rows(four[...], shards, half)
    at = lax.broadcasted_iota(jnp.int32, (2 * size - half - rows, half), 0)

    def put(index, part, at, value):
        place(s, SIDES + 4, steps, keep, send, index, part, slice(at, at + value.shape[0]), value)

    h = slice(first + half, first + 2 * half)
    out = (mm_tn(d0[2][...], a0[:, h]) + mm_tn(d1[2][...], a1[:, h])).astype(BF)
    h = slice(first, first + half)
    for k in range(0, shards, per):
        side, first_col = k * cols // wide, k * cols % wide
        span = slice(first_col, first_col + per * cols)
        full = (mm_tn(a0[:, h], d0[side][:, span]) + mm_tn(a1[:, h], d1[side][:, span])).astype(BF)
        for j in range(per):
            put(k + j, 0, 0, full[:size, j * cols : (j + 1) * cols])
            put(k + j, 1, 0, full[size:, j * cols : (j + 1) * cols])
            put(k + j, 1, half - size, out[(k + j) * rows : (k + j + 1) * rows])
            both = jnp.where(at == 0, tiny[k + j : k + j + 1], 0.0)
            both = both + jnp.where(at == 1, bup[:, (k + j) * cols : (k + j + 1) * cols], 0.0)
            put(k + j, 1, half - size + rows, both.astype(BF))


def grad_up(s, mine, got, dp0, dp1, four, bup, shards, steps):
    half = got.shape[1] - mine.shape[1]
    dim = 2 * half
    part = shaped((shards, (half + dim // shards + TINY_UP) // 2, half))
    return call(
        functools.partial(grad_up_kernel, shards=shards, steps=steps), "grad_up", 10,
        [part, part], [], s, mine, got, *dp0, *dp1, four, bup, micros=5,
    )


def got_rows(owns):
    return owns[0].shape[0] // 5


def last_of(ref, step, n, block, dim):
    wide = ref.shape[1]
    blocks = [
        ref[5 * n + k * block : 5 * n + (k + 1) * block, :] for k in range(step * dim // wide, (step + 1) * dim // wide)
    ]
    return jnp.concatenate(blocks, axis=1)


def d_of(owns, gots, step, n):
    if step == 0:
        return jnp.concatenate([own[4 * n : 5 * n, :] for own in owns], axis=1)
    mine, theirs = slice((step - 1) * n, step * n), slice((step + 1) * n, (step + 2) * n)
    return jnp.concatenate(
        [(own[mine, :].astype(F32) + got[theirs, :].astype(F32)).astype(BF) for own, got in zip(owns, gots)], axis=1
    )


def grad_qkv_kernel(
    s, widths, *refs, shards, steps
):
    groups = (len(refs) - 4) // 2
    owns, gots = refs[:groups], refs[groups : 2 * groups]
    h_own, other, keep, send = refs[-4:]
    n, half = got_rows(owns), h_own.shape[1]
    block = n // 2
    dim = 2 * half
    h = slice(other.shape[1] - half, other.shape[1])
    size = 3 * dim // shards // 2

    def put(k, at, value):
        place(s, SIDES + 8, steps, keep, send, k // 2, k % 2, slice(at, at + value.shape[0]), value)

    for step in range(3):
        d_own, d_got = d_of(owns, gots, step, n), d_of(gots, owns, step, n)
        full = mm_tn(d_own, h_own[:n, :]) + mm_tn(d_got, other[:n, h])
        last_own, last_got = (last_of(refs[1], step, n, block, dim) for refs in (owns, gots))
        full = full + mm_tn(last_own, h_own[n:, :]) + mm_tn(last_got, other[n:, h])
        full = full.astype(BF)
        first = step * dim
        for k in range(first // size, (first + dim + size - 1) // size):
            lo, hi = max(first, k * size), min(first + dim, (k + 1) * size)
            put(k, lo - k * size, full[lo - first : hi - first])


def grad_qkv(s, owns, gots, h_own, other, shards, steps):
    half = h_own.shape[1]
    part = shaped((shards, 3 * half // shards, half))
    return call(
        functools.partial(grad_qkv_kernel, shards=shards, steps=steps), "grad_qkv", 12, [part, part], [],
        s, *owns, *gots, h_own, other, micros=4,
    )


def grad_vec_kernel(s, widths, norms, sums, keep, send, *, shards, steps):
    half = keep.shape[2]
    tiny = tiny_rows(jnp.concatenate([norms[...], sums[0:1, :], sums[2:3, :]], axis=0), shards, half)
    at = lax.broadcasted_iota(jnp.int32, (TINY_QKV, half), 0)
    for k in range(2 * shards):
        value = jnp.where(at == 0, tiny[k // 2 : k // 2 + 1], 0.0).astype(BF)
        place(s, SIDES + 8, steps, keep, send, k // 2, k % 2, slice(None), value)


def grad_vec(s, norms, sums, shards, steps):
    part = shaped((shards, TINY_QKV, norms.shape[1] // 2))
    return call(
        functools.partial(grad_vec_kernel, shards=shards, steps=steps), "grad_vec", 8, [part, part], [],
        s, norms, sums, micros=1,
    )


def qkv_bwd_kernel(
    s, widths, *refs
):
    groups = (len(refs) - 13) // 2
    owns, gots = refs[:groups], refs[groups : 2 * groups]
    x_got, gain, dmid, w, patches, dx0, dx1, dx2, norms, sums, acc, x_own, sems = refs[-13:]
    block, dim = x_got.shape
    n = 2 * block
    spans = [slice(k * dim, (k + 1) * dim) for k in range(3)]
    stream = Stream(sems, (patches.at[s[CHIP]], x_own.at[0]), (patches.at[2], x_own.at[1]))
    for k, cols in enumerate(spans):
        d = jnp.concatenate([d_of(owns, gots, k, n), last_of(owns[1], k, n, block, dim)], axis=0)
        sums[k : k + 1, :] = jnp.sum(d.astype(F32), axis=0, keepdims=True)
        part = mm_nt(d, w[:, cols])
        if k == 0:
            acc[...] = part
        else:
            acc[...] += part
    dy = acc[...]
    stream.wait(2)
    x = jnp.concatenate([x_own[0], x_got[...], x_own[1]], axis=0).astype(F32)
    xhat, inv = norm_stats(x)
    dx = dmid[...] + norm_back(xhat, inv, line(gain), dy)
    dx0[...] = dx[:block]
    for k in range(2):
        dx1[k * block : (k + 1) * block, :] = dx[block:n, k * dim // 2 : (k + 1) * dim // 2].astype(BF)
    dx2[...] = dx[n:]
    norms[0:1, :] = jnp.sum(dy * xhat, axis=0, keepdims=True)
    norms[1:2, :] = jnp.sum(dy, axis=0, keepdims=True)


def qkv_bwd(s, owns, gots, patches, x_got, gain, dmid, w):
    images, block, dim = patches.shape
    return call(
        qkv_bwd_kernel, "qkv_bwd", 9,
        [
            in_hbm((block, dim), F32), shaped((2 * block, dim // 2)), in_hbm((block, dim), F32),
            shaped((2, dim), F32), shaped((3, dim), F32),
        ],
        [
            pltpu.VMEM((images * block, dim), F32), pltpu.VMEM((2, block, dim), BF),
            pltpu.SemaphoreType.DMA((2,)),
        ],
        s, *owns, *gots, x_got, gain, dmid, w, patches, micros=4, streamed=1,
    )


def finish_kernel(s, widths, both, both_got, up, out, qkv, wdown, *vectors, rows_up, rows_qkv, size, parts):
    def sorted_of(value, other):
        cut = value.shape[0] // 2
        mine = [value[:cut].astype(F32), value[cut:].astype(F32)]
        theirs = [other[:cut].astype(F32), other[cut:].astype(F32)]
        second = s[CHIP] > 0
        pairs = [[jnp.where(second, v[1], v[0]), jnp.where(second, v[0], v[1])] for v in (mine, theirs)]
        swap_cores = s[CORE] > 0
        return [
            [jnp.where(swap_cores, b, a) for a, b in zip(*pairs)],
            [jnp.where(swap_cores, a, b) for a, b in zip(*pairs)],
        ]

    cores = sorted_of(both, both_got)
    rows = [jnp.concatenate([first[:rows_up], second[:rows_up]], axis=0) for first, second in cores]
    half = up.shape[0] // 2
    wide = out.shape[0]
    up[:half, :] = rows[0][:half]
    up[half:, :] = rows[1][:half]
    out[...] = jnp.concatenate([r[half : half + wide] for r in rows], axis=1)
    pieces = [jnp.concatenate([f[rows_up : rows_up + size], g[rows_up : rows_up + size]], axis=0) for f, g in cores]
    qkv[...] = jnp.concatenate(pieces, axis=1)
    two = rows[0][half + wide : half + wide + 8] + rows[1][half + wide : half + wide + 8]
    one = cores[0][0][rows_up + size : rows_up + size + 8] + cores[1][0][rows_up + size : rows_up + size + 8]
    for ref, (source, row, at) in zip(vectors, parts):
        ref[...] = (one, two)[source][row : row + 1, at : at + ref.shape[0]].reshape(ref.shape[0])
    first = rows_up + rows_qkv
    blocks = out.shape[0] // 2
    count = (both.shape[0] // 2 - first) // blocks
    for c, pair in enumerate(cores):
        for y, part in enumerate(pair):
            for k in range(count):
                at = (c * count + k) * half
                wdown[y * blocks : (y + 1) * blocks, at : at + half] = part[first + k * blocks : first + (k + 1) * blocks]


def finish(s, both, both_got, rows_up, rows_qkv, dim, hidden, shards):
    part, wide = dim // shards, hidden // shards
    size = 3 * dim // shards // 2
    parts = [(0, 0, k * part) for k in range(4)]
    parts += [(1, 0, 2 * part), (1, 0, 0), (1, 0, part), (1, 1, 0), (1, 0, 3 * part)]
    widths = [part] * 7 + [wide, part]
    return call(
        functools.partial(finish_kernel, rows_up=rows_up, rows_qkv=rows_qkv, size=size, parts=parts), "finish", 20,
        [in_hbm((dim, wide), F32), in_hbm((part, dim), F32), in_hbm((3 * part, dim), F32), in_hbm((part, hidden), F32)]
        + [in_hbm((width,), F32) for width in widths],
        [], s, both, both_got, micros=3,
    )


def hop(value, step0, step1):
    seq, img = lax.axis_size("seq"), lax.axis_size("img")
    pairs = []
    for s in range(seq):
        step = step1 if s % 2 else step0
        for i in range(img):
            to = (s ^ 2, i) if step == "y" else (s, i ^ (step if isinstance(step, int) else step[0]))
            pairs.append((s * img + i, to[0] * img + to[1]))
    return lax.ppermute(value, ("seq", "img"), pairs)


def plus(kept, got):
    return (kept.astype(F32) + got.astype(F32)).astype(BF)


class Sum:
    def __init__(self, s, chain, steps, keep, send):
        self.s, self.base, self.steps, self.at = s, chain * len(steps[0]), steps, 0
        self.keep, self.send = (part.reshape(-1, part.shape[-1]) for part in (keep, send))

    def go(self):
        self.got, self.first = hop(self.send, self.steps[0][self.at], self.steps[1][self.at]), 0
        self.at += 1

    def halve(self):
        if self.keep.shape[0] % 32 == 0:
            self.keep, self.send = halve(self.s, self.keep, self.got, self.base + self.at, self.first)
            return
        total = plus(self.keep, self.got[self.first : self.first + self.keep.shape[0]]).reshape(2, -1, self.keep.shape[1])
        side = sides_here(self.steps)[self.at]
        self.keep, self.send = pick(total, side, 0), pick(total, 1 - side, 0)

    def step(self):
        self.halve()
        self.go()

    def steps_left(self, most):
        while len(self.steps[0]) - self.at > most:
            self.step()

    def last(self):
        if self.keep.shape[0] % 16 == 0:
            return add(self.s, self.keep, self.got, self.first)
        return plus(self.keep, self.got[self.first : self.first + self.keep.shape[0]])


def go_together(s, a, b):
    if [order[a.at] for order in a.steps] != [order[b.at] for order in b.steps]:
        a.go()
        b.go()
        return
    rows = a.send.shape[0]
    both = stack(s, a.send, b.send) if rows % 16 == 0 else jnp.concatenate([a.send, b.send])
    got = hop(both, a.steps[0][a.at], a.steps[1][a.at])
    for chain, first in ((a, 0), (b, rows)):
        chain.got, chain.first = got, first
        chain.at += 1


def finish_plain(core, chip, both, both_got, rows_up, rows_qkv, dim, hidden, shards):
    part, wide, half = dim // shards, hidden // shards, dim // 2
    size = 3 * dim // shards // 2

    def sorted_of(value, other):
        pairs = []
        for v in (value, other):
            a, b = jnp.split(v.astype(F32), 2)
            pairs.append([jnp.where(chip == 0, a, b), jnp.where(chip == 0, b, a)])
        mine, theirs = pairs
        first = [jnp.where(core == 0, a, b) for a, b in zip(mine, theirs)]
        return [first, [jnp.where(core == 0, b, a) for a, b in zip(mine, theirs)]]

    cores = sorted_of(both, both_got)
    rows = [jnp.concatenate([f[:rows_up], g[:rows_up]]) for f, g in cores]
    up = jnp.concatenate([r[:wide].T for r in rows])
    out = jnp.concatenate([r[wide : wide + part] for r in rows], axis=1)
    pieces = [jnp.concatenate([f[rows_up : rows_up + size], g[rows_up : rows_up + size]]) for f, g in cores]
    two = sum(r[wide + part :] for r in rows).reshape(-1)
    one = sum(f[rows_up + size : rows_up + rows_qkv] for f, _ in cores).reshape(-1)
    downs = [[f[rows_up + rows_qkv :].reshape(-1, part // 2, half) for f in pair] for pair in cores]
    downs = [jnp.concatenate([f.transpose(1, 0, 2).reshape(part // 2, -1) for f in pair]) for pair in downs]
    down = jnp.concatenate(downs, axis=1)
    first = [one[k * part : (k + 1) * part] for k in range(4)]
    second = [two[k * part : (k + 1) * part] for k in (2, 0, 1)]
    last = [two[4 * part : 4 * part + wide], two[3 * part : 4 * part]]
    return [up, out, jnp.concatenate(pieces, axis=1), down, *first, *second, *last]


class Book:
    def __init__(self, s, codebook):
        n_img = lax.axis_size("img")
        bits = [1 << k for k in range(n_img.bit_length() - 1)]
        masks = [1, 2, 6] if n_img == 8 else bits
        self.orders = list(zip(masks[1:], [1, "y", *masks[3:]]))
        self.ends = ((1, masks[1]), ("y", masks[2]))
        self.s, self.value = s, codebook

    def stack(self, *parts, there=()):
        return stack(self.s, *parts, there=there) if sum(part.size for part in parts) < 1 << 21 else jnp.concatenate(parts)

    def start(self):
        self.got = hop(self.value, *self.orders.pop(0))

    def double(self):
        self.value = self.stack(self.value, self.got)

    def spread(self):
        self.beside, self.across = hop(self.value, *self.ends[0]), hop(self.value, *self.ends[1])
        self.other = [swap(self.value, "seq", 1)]

    def corner(self, there):
        if self.value.size < 1 << 21:
            *parts, self.sides = cut(self.s, self.across, self.beside, (there, self.other[0]))
        else:
            half = self.value.shape[0] // 2
            parts = self.across[:half], self.beside[half:]
            self.sides = jnp.concatenate([self.beside, self.across])
        self.corners = hop(parts[0], *self.ends[0]), hop(parts[1], *self.ends[1])
        self.other.append(swap(self.sides, "seq", 1))

    def finish(self):
        rest = self.stack(*self.corners, there=(self.other[1],))
        return [self.value, self.sides, rest, *self.other, swap(rest, "seq", 1)]


def shards(
    patches,
    widths,
    ln1_gain,
    ln1_bias,
    w_qkv,
    b_query,
    b_value,
    w_out,
    b_out,
    ln2_gain,
    ln2_bias,
    w_up,
    b_up,
    w_down,
    b_down,
    codebook,
    cotangent,
):
    images, block, dim = patches.shape
    hidden = w_up.shape[1]
    n_img = lax.axis_size("img")
    me = lax.axis_index("seq")
    chip, core = me // 2, me % 2
    half, main = dim // 2, 2 * block
    fits = codebook.shape[0] * n_img * lax.axis_size("seq") <= 4096
    aligned = n_img == 8 and dim // n_img // 2 % 16 == 0
    steps_down, steps_up, steps_qkv = plans(n_img)
    s = widths

    Order.token = jnp.zeros((8, 128), F32)
    book = Book(s, codebook)
    book.start()
    x_got = swap(pick(patches, 1 - chip, 0), "seq", 2)
    kv_last, h_last = kv_last_fwd(s, patches, ln1_gain, ln1_bias, b_value, w_qkv)
    kv_y = swap(kv_last, "seq", 2)
    while book.orders:
        book.double()
        book.start()
    q_main, q_last, *kvs, h_mine, h_send = qkv_fwd(s, patches, x_got, h_last, ln1_gain, ln1_bias, b_query, b_value, w_qkv)
    kvs.append(kv_last)
    kvs_other = [swap(kv, "seq", 1) for kv in kvs]
    book.double()
    book.spread()
    kvs_main = kvs[:2] + kvs_other[:2]
    att_main = attention_fwd(s, q_main, kvs_main, False, block)
    cot_got = swap(pick(cotangent, 1 - chip, 0), "seq", 2)
    kvs_last = [kvs[2], kv_y, kvs_other[2], swap(kv_y, "seq", 1)]
    att_last = attention_fwd(s, q_last, kvs_last, True, block)
    mid, h2, enc, slope0, send = mlp_first(
        s, patches, x_got, att_main, att_last, h_send, b_out, ln2_gain, ln2_bias, b_up, b_down, w_out, w_up,
        w_down,
    )
    got = swap(send, "seq", 1)
    book.corner(cot_got)
    enc, slope1, mine = mlp_second(s, h2, enc, att_main, att_last, b_up, w_up, w_down)
    pieces = book.finish()
    if fits:
        mix0, mix1, mix2, loss, denc, dmlp = quantizer(s, enc, cotangent, cot_got, pieces)
    else:
        cots = jnp.concatenate([pick(cotangent, chip, 0), cot_got, cotangent[2]])
        mix0, mix1, mix2, loss, denc, dmlp = quantizer_plain(s, enc, cots, jnp.concatenate(pieces))
    mix1 = swap(mix1, "seq", 2)

    def split(full, steps):
        rows, cols = full.shape[-2:]
        full = full.reshape([2] * len(steps[0]) + [rows // 2, cols])
        side = sides_here(steps)[0]
        return pick(full, side, 0), pick(full, 1 - side, 0)

    def lines_of(count, *vectors):
        rows = jnp.concatenate([v.reshape(n_img, -1) for v in vectors], axis=1).astype(BF)
        return jnp.pad(rows, ((0, 0), (0, count * half - rows.shape[1]))).reshape(n_img, count, half)

    dmlp_got = swap(dmlp, "seq", 1)
    both = jnp.concatenate([mine, got[:, : mine.shape[1]]])
    if aligned:
        dmlp_both = stack(s, dmlp, dmlp_got, there=(got,))
        keep, send = grad_down(s, dmlp_both, mine, got, n_img, steps_down)
    else:
        full = mm_tn(jnp.concatenate([dmlp, dmlp_got]), both[:, : hidden // 2]).astype(BF)
        full = full.reshape(n_img, 2, dim // n_img // 2, -1, half).transpose(0, 1, 3, 2, 4)
        keep, send = split(full.reshape(n_img, -1, half), steps_down)
    down = Sum(s, 0, steps_down, keep, send)
    down.go()
    *dp, dmid, datt, rows_two, sum_bup = mlp_bwd(s, dmlp, denc, mid, ln2_gain, (slope0, slope1), w_down, w_up, w_out)
    dp_got = [swap(part, "seq", 1) for part in dp]
    quantized, token_loss = assemble(s, (mix0, mix1, mix2), loss)
    keep_last, send_last, dq_last = attention_bwd(s, q_last, kvs_last, datt, main, True, block, ())
    got_last = swap(send_last, "seq", 1)
    keep_last, send_last = fold(s, keep_last, got_last)
    down.step()
    got_last = swap(send_last, "seq", 2)
    if aligned:
        keep, send = grad_up(s, mine, got, dp, dp_got, rows_two, sum_bup, n_img, steps_up)
    else:
        dps = jnp.concatenate([jnp.concatenate(dp, axis=1), jnp.concatenate(dp_got, axis=1)])
        up = mm_tn(both[:, hidden // 2 : hidden // 2 + half], dps[:, :hidden]).astype(BF)
        up = up.reshape(half, n_img, -1).transpose(1, 2, 0)
        out = mm_tn(dps[:, hidden:], both[:, hidden // 2 + half :]).astype(BF).reshape(n_img, -1, half)
        tiny = lines_of(TINY_UP, rows_two[0], rows_two[1], rows_two[2], rows_two[3], sum_bup[0])
        keep, send = split(jnp.concatenate([up, out, tiny], axis=1), steps_up)
    up = Sum(s, 1, steps_up, keep, send)
    up.go()
    d_main, d_got = [], []
    for pairs, more in (((0, 1), ()), ((2, 3), (dq_last, keep_last, got_last)), ((4, 5), ())):
        d_main += attention_bwd(s, q_main, kvs_main, datt, 0, False, block, pairs, more)
        d_got.append(swap(d_main[-1], "seq", 1))
        if len(d_main) == 2:
            down.step()
    if aligned:
        keep, send = grad_qkv(s, d_main, d_got, h_mine, got, n_img, steps_qkv)
    else:
        n = main

        def assembled(owns, gots):
            rows = [jnp.concatenate([own[4 * n : 5 * n] for own in owns], axis=1)]
            for k in (0, 1):
                mine, theirs = slice(k * n, (k + 1) * n), slice((k + 2) * n, (k + 3) * n)
                rows.append(jnp.concatenate([plus(own[mine], got[theirs]) for own, got in zip(owns, gots)], axis=1))
            last = owns[1][5 * n :].reshape(-1, block, owns[1].shape[1])
            return [jnp.concatenate(rows, axis=1), jnp.concatenate(list(last), axis=1)]

        d = jnp.concatenate(assembled(d_main, d_got) + assembled(d_got, d_main))
        h = jnp.concatenate([h_mine, got[:, -half:]])
        keep, send = split(mm_tn(d, h).astype(BF).reshape(n_img, -1, half), steps_qkv)
    qkv = Sum(s, 2, steps_qkv, keep, send)
    qkv.go()
    dx0, dx1, dx2, norms, sums = qkv_bwd(s, d_main, d_got, patches, x_got, ln1_gain, dmid, w_qkv)
    if aligned:
        keep, send = grad_vec(s, norms, sums, n_img, steps_qkv)
    else:
        tiny = lines_of(TINY_QKV, norms[0], norms[1], sums[0], sums[2])
        keep, send = split(jnp.concatenate([tiny, tiny], axis=1), steps_qkv)
    vec = Sum(s, 2, steps_qkv, keep, send)
    vec.go()
    up.step()
    down.step()
    def step_qkv():
        qkv.halve()
        vec.halve()
        go_together(s, qkv, vec)

    for _ in range(len(steps_qkv[0]) - 4):
        down.step()
        up.step()
        step_qkv()
    step_qkv()
    up.step()
    sum_down = down.last()
    down_other = swap(sum_down, "seq", 2)
    step_qkv()
    step_qkv()
    up.steps_left(0)
    parts = (qkv.last(), vec.last())
    sum_qkv = stack(s, *parts, there=(down_other,)) if aligned else jnp.concatenate(parts)
    qkv_other = swap(stack(s, sum_qkv, dx1) if aligned else jnp.concatenate([sum_qkv, dx1]), "seq", 2)
    sum_up = up.last()
    up_other = swap(sum_up, "seq", 2)
    grad_input = assemble_dx(s, dx0, qkv_other, dx2)
    own, others = (sum_up, sum_qkv, sum_down), (up_other, qkv_other, down_other)
    if aligned:
        both = collect(s, own, others)
    else:
        both = jnp.concatenate([*own, *[b[: a.shape[0]] for a, b in zip(own, others)]])
    both_got = swap(both, "seq", 1)
    done = (both, both_got, sum_up.shape[0], sum_qkv.shape[0], dim, hidden, n_img)
    weights = finish(s, *done) if aligned else finish_plain(core, chip, *done)
    g_up, g_out, g_qkv, g_down, g_gain1, g_shift1, g_bq, g_bv, g_bout, g_gain2, g_shift2, g_bup, g_bdown = weights

    return (
        quantized,
        token_loss,
        grad_input,
        g_gain1,
        g_shift1,
        g_qkv.T,
        g_bq,
        g_bv,
        g_out.T,
        g_bout,
        g_gain2,
        g_shift2,
        g_up,
        g_bup,
        g_down.T,
        g_bdown,
    )


def solution(mesh):
    return jax.shard_map(
        shards,
        mesh=mesh,
        in_specs=(
            P("img", "seq", None),
            P("img"),
            P(),
            P(),
            P(),
            P(),
            P(),
            P(),
            P(),
            P(),
            P(),
            P(),
            P(),
            P(),
            P(),
            P(("seq", "img"), None),
            P("img", "seq", None),
        ),
        out_specs=(
            P("img", "seq", None),
            P("img", "seq"),
            P("img", "seq", None),
            P("img"),
            P("img"),
            P(None, "img"),
            P("img"),
            P("img"),
            P(None, "img"),
            P("img"),
            P("img"),
            P("img"),
            P(None, "img"),
            P("img"),
            P(None, "img"),
            P("img"),
        ),
        check_vma=False,
    )
```

```python
import functools

import jax
import jax.numpy as jnp
from jax import lax
from jax.experimental import pallas as pl
from jax.experimental.pallas import tpu as pltpu
from jax.sharding import PartitionSpec as P

HEAD_DIM = 64
GRID_H = 16
EPS_NORM = 1e-06
COMMIT = 16.0
BF = jnp.bfloat16
F32 = jnp.float32
MIB = 1024 * 1024
MASKED = -1000000000.0


def mm(a, b):
    return jnp.dot(a, b, preferred_element_type=F32)


def mm_nt(a, b):
    return lax.dot_general(a, b, (((1,), (1,)), ((), ())), preferred_element_type=F32)


def mm_tn(a, b):
    return lax.dot_general(a, b, (((0,), (0,)), ((), ())), preferred_element_type=F32)


def swap(value, axis, bit):
    count = lax.axis_size(axis)
    return lax.ppermute(value, axis, [(i, i ^ bit) for i in range(count)])


def pick(value, index, axis):
    return lax.dynamic_index_in_dim(value, index, axis, keepdims=False)


def after(value, *others):
    return lax.optimization_barrier((value, *others))[0]


def parity(number):
    return bin(number).count("1") % 2


def shaped(shape, dtype=BF):
    return jax.ShapeDtypeStruct(tuple(shape), dtype)


def in_hbm(shape, dtype=BF):
    return pltpu.HBM(tuple(shape), dtype)


class Order:
    token = None


def call(kernel, name, mib, out_shape, scratch, s, *args, micros, streamed=0, by_hand=(), bounds=False):
    vm, hbm = pl.BlockSpec(memory_space=pltpu.VMEM), pl.BlockSpec(memory_space=pl.ANY)
    direct, count = len(args) - streamed, len(args) + len(out_shape)
    args = [
        pltpu.with_memory_space_constraint(arg, pltpu.HBM) if arg.ndim == 1 or (k >= direct and name not in ("stack", "cut")) else arg
        for k, arg in enumerate(args)
    ]

    def body(*refs):
        limits, token, refs = refs[0], refs[bounds], refs[bounds + 1 :]
        kernel(Place(), limits, *refs[:count], *refs[count + 1 :])
        refs[count][...] = token[...]

    out = pl.pallas_call(
        body,
        in_specs=[vm] * (direct + 1 + bounds) + [hbm] * streamed,
        out_specs=[hbm if out in by_hand else vm for out in range(len(out_shape))] + [vm],
        out_shape=[*out_shape, shaped((8, 128), F32)],
        scratch_shapes=scratch,
        compiler_params=pltpu.CompilerParams(vmem_limit_bytes=mib * MIB),
        cost_estimate=pl.CostEstimate(flops=int(micros * 2e8), bytes_accessed=0, transcendentals=0),
        name=name,
    )(*([s] if bounds else []), Order.token, *args)
    Order.token = out[-1]
    return out[:-1]


class Stream:
    def __init__(self, sems, *pairs, ahead=3):
        self.copies = [pltpu.make_async_copy(a, b, sems.at[k]) for k, (a, b) in enumerate(pairs)]
        self.done, self.begun = 0, 0
        self.start(ahead)

    def start(self, count):
        while self.begun < min(count, len(self.copies)):
            self.copies[self.begun].start()
            self.begun += 1

    def wait(self, count):
        while self.done < count:
            self.copies[self.done].wait()
            self.done += 1
            self.start(self.begun + 1)


ME, CORE, CHIP, SIDES = range(4)
X, NEAR, FAR = (1, 1), (2, 2), (4, 4)


def plans(n_img):
    if n_img == 8:
        return (
            ([X, NEAR, "y", FAR], ["y", NEAR, X, FAR]),
            ([X, "y", NEAR, FAR], ["y", X, NEAR, FAR]),
            ([NEAR, X, "y", FAR], [NEAR, "y", X, FAR]),
        )
    bits = [1 << k for k in reversed(range(n_img.bit_length() - 1))]
    order = [(bit, bit) for bit in bits] + ["y"]
    return ((order, order),) * 3


def side_here(step):
    if step == "y":
        return lax.axis_index("seq") // 2
    bits = lax.axis_index("img") & step[1]
    value = 0
    for k in range(step[1].bit_length()):
        value = value ^ ((bits >> k) & 1)
    return value


def sides_here(steps):
    core = lax.axis_index("seq") % 2
    return [jnp.where(core == 0, side_here(a), side_here(b)) for a, b in zip(*steps)]


class Place:
    def __getitem__(self, what):
        me = lax.axis_index("seq")
        if what < SIDES:
            return (me, me % 2, me // 2)[what]
        steps = plans(lax.axis_size("img"))
        chain, step = divmod(what - SIDES, len(steps[0][0]))
        return sides_here([order[step : step + 1] for order in steps[chain]])[0]


def line(ref, start=0, size=None):
    size = ref.shape[0] if size is None else size
    return ref[start : start + size].reshape(1, size)


def norm_stats(x):
    center = x - jnp.mean(x, axis=-1, keepdims=True)
    spread = jnp.mean(center * center, axis=-1, keepdims=True)
    inv = lax.rsqrt(spread + EPS_NORM)
    return center * inv, inv


def norm_back(xhat, inv, gain, dy):
    dxhat = dy * gain
    return inv * (
        dxhat - jnp.mean(dxhat, axis=-1, keepdims=True) - xhat * jnp.mean(dxhat * xhat, axis=-1, keepdims=True)
    )


def spots(index, block, me):
    shift = block.bit_length() - 1
    assert block == 1 << shift
    place = index >> shift
    mask = ((place & 1) << 1) | (place >> 1)
    return ((me ^ mask) << shift) | (index & (block - 1))


def limit_of(s, widths, last):
    row = widths[...].reshape(1, widths.shape[0])
    return GRID_H * (row[:, 2:3] if last else jnp.where(s[CHIP] == 0, row[:, 0:1], row[:, 1:2]))


def side_of(ref, side, width):
    return ref[:, pl.ds(pl.multiple_of(side * width, 128), width)]


def kv_last_kernel(s, widths, gain, shift, bv, patches, w_hbm, kv, h, x, w, sems):
    dim = h.shape[1]
    stream = Stream(sems, (patches.at[2], x), *((w_hbm.at[:, k * dim : (k + 1) * dim], w.at[k - 1]) for k in (1, 2)))
    stream.wait(1)
    xhat, _ = norm_stats(x[...].astype(F32))
    h[...] = (xhat * line(gain) + line(shift)).astype(BF)
    stream.wait(2)
    kv[:, :dim] = mm(h[...], w[0]).astype(BF)
    stream.wait(3)
    kv[:, dim:] = (mm(h[...], w[1]) + line(bv)).astype(BF)


def kv_last_fwd(s, patches, gain, shift, bv, w):
    _, block, dim = patches.shape
    return call(
        kv_last_kernel, "kv_last_fwd", 8, [shaped((block, 2 * dim)), shaped((block, dim))],
        [pltpu.VMEM((block, dim), BF), pltpu.VMEM((2, dim, dim), BF), pltpu.SemaphoreType.DMA((3,))],
        s, gain, shift, bv, patches, w, micros=2, streamed=2,
    )


def qkv_kernel(
    s, widths, got, h_last, gain, shift, bq, bv, w, patches, q_main, q_last, kv0, kv1, mine, send, h, x_own, sems
):
    half, dim = mine.shape[1], w.shape[0]
    block = got.shape[0]
    stream = Stream(sems, (patches.at[s[CHIP]], x_own))
    h[2 * block :, :] = h_last[...]
    xhat, _ = norm_stats(got[...].astype(F32))
    h[block : 2 * block, :] = (xhat * line(gain) + line(shift)).astype(BF)
    stream.wait(1)
    xhat, _ = norm_stats(x_own[...].astype(F32))
    h[:block, :] = (xhat * line(gain) + line(shift)).astype(BF)
    mine[...] = side_of(h, s[CORE], half)
    send[...] = side_of(h, 1 - s[CORE], half)
    keys = mm(h[: 2 * block, :], w[:, dim : 2 * dim]).astype(BF)
    values = (mm(h[: 2 * block, :], w[:, 2 * dim :]) + line(bv)).astype(BF)
    for k, out in enumerate((kv0, kv1)):
        out[:, :dim] = keys[k * block : (k + 1) * block]
        out[:, dim:] = values[k * block : (k + 1) * block]
    q = (mm(h[...], w[:, :dim]) + line(bq)).astype(BF)
    q_main[...] = q[: 2 * block]
    q_last[...] = q[2 * block :]


def qkv_fwd(s, patches, got, h_last, gain, shift, bq, bv, w):
    images, block, dim = patches.shape
    n, half = images * block, dim // 2
    return call(
        qkv_kernel, "qkv_fwd", 8,
        [
            shaped((2 * block, dim)), shaped((block, dim)), *[shaped((block, 2 * dim))] * 2, in_hbm((n, half)),
            shaped((n, half)),
        ],
        [pltpu.VMEM((n, dim), BF), pltpu.VMEM((block, dim), BF), pltpu.SemaphoreType.DMA((1,))],
        s, got, h_last, gain, shift, bq, bv, w, patches, micros=3, streamed=1,
    )


def two_heads(value):
    left = lax.broadcasted_iota(jnp.int32, value.shape, 1) < HEAD_DIM
    zero = jnp.zeros_like(value)
    return jnp.concatenate([jnp.where(left, value, zero), jnp.where(left, zero, value)], axis=0)


def one_pair(value):
    n = value.shape[0] // 2
    left = lax.broadcasted_iota(jnp.int32, (n, value.shape[1]), 1) < HEAD_DIM
    return jnp.where(left, value[:n], value[n:])


def rows_of(refs, lanes):
    return jnp.concatenate([ref[:, lanes] for ref in refs], axis=0)


def att_fwd_kernel(s, widths, q, *refs, last, block):
    kvs, o = refs[:-1], refs[-1]
    dim = q.shape[1]
    m = sum(kv.shape[0] for kv in kvs)
    index = lax.broadcasted_iota(jnp.int32, (1, m), 1)
    ok = spots(index, block, s[ME]) < limit_of(s, widths, last)
    for p in range(dim // 128):
        at, av = slice(p * 128, (p + 1) * 128), slice(dim + p * 128, dim + (p + 1) * 128)
        k, v = rows_of(kvs, at), rows_of(kvs, av)
        raw = mm_nt(two_heads(q[:, at]), k) * (HEAD_DIM**-0.5)
        scores = jnp.where(ok, raw, MASKED)
        expo = jnp.exp(scores - jnp.max(scores, axis=1, keepdims=True))
        probs = expo * (1.0 / jnp.sum(expo, axis=1, keepdims=True))
        o[:, at] = one_pair(mm(probs.astype(BF), v)).astype(BF)


def attention_fwd(s, q, kvs, last, block):
    return call(
        functools.partial(att_fwd_kernel, last=last, block=block), "attention_fwd", 10, [shaped(q.shape)], [],
        s, q, *kvs, micros=5, bounds=True,
    )[0]


def att_bwd_kernel(s, widths, q, do, *refs, last, block, first, pairs, more):
    n, dim = q.shape
    if pairs:
        kvs, out = refs[: len(refs) - 1 - more], refs[-1]
        m = sum(kv.shape[0] for kv in kvs)
        parts = [out.at[k * m // 2 : (k + 1) * m // 2, :] for k in range(4)]
        dq = out.at[2 * m : 2 * m + n, :]
        if more:
            dq_last, keep_last, got_last = refs[-4:-1]
            rows, wide = dq_last.shape[0], out.shape[1]
            parts_last = [dq_last[...]] + [
                (keep_last[k].astype(F32) + got_last[k].astype(F32)).astype(BF) for k in range(2)
            ]
            for k in range(3 * dim // wide):
                part, at = parts_last[k * wide // dim], k * wide % dim
                out[2 * m + n + k * rows : 2 * m + n + (k + 1) * rows, :] = part[:, at : at + wide]
    else:
        kvs, (keep, send, dq) = refs[:-3], refs[-3:]
        m = sum(kv.shape[0] for kv in kvs)
        parts = [keep.at[0], keep.at[1], send.at[0], send.at[1]]
    index = lax.broadcasted_iota(jnp.int32, (m, 1), 0)
    ok = spots(index, block, s[ME]) < limit_of(s, widths, last)
    for p in pairs or range(dim // 128):
        at, av = slice(p * 128, (p + 1) * 128), slice(dim + p * 128, dim + (p + 1) * 128)
        to = slice((p - pairs[0]) * 128, (p - pairs[0] + 1) * 128) if pairs else at
        k, v = rows_of(kvs, at), rows_of(kvs, av)
        q2, do2 = two_heads(q[:, at]), two_heads(do[first : first + n, at])
        raw = mm_nt(k, q2) * (HEAD_DIM**-0.5)
        scores = jnp.where(ok, raw, MASKED)
        expo = jnp.exp(scores - jnp.max(scores, axis=0, keepdims=True))
        probs = expo * (1.0 / jnp.sum(expo, axis=0, keepdims=True))
        dv = mm(probs.astype(BF), do2).astype(BF)
        dp = mm_nt(v, do2)
        inner = jnp.sum(probs * dp, axis=0, keepdims=True)
        ds = (probs * (dp - inner) * (HEAD_DIM**-0.5)).astype(BF)
        dk = mm(ds, q2).astype(BF)
        dq[:, to] = one_pair(mm_tn(ds, k)).astype(BF)
        for ref, part in zip(parts, (dk[: m // 2], dv[: m // 2], dk[m // 2 :], dv[m // 2 :])):
            ref[:, to] = part


def attention_bwd(s, q, kvs, do, first, last, block, pairs, more=()):
    n, dim = q.shape
    m = sum(kv.shape[0] for kv in kvs)
    return call(
        functools.partial(att_bwd_kernel, last=last, block=block, first=first, pairs=pairs, more=len(more)),
        "attention_bwd", 12,
        [shaped((2 * m + n + (len(more) and 3 * dim // len(pairs)), 128 * len(pairs)))] if pairs else [shaped((2, m // 2, dim)), shaped((2, m // 2, dim)), shaped((n, dim))],
        [], s, q, do, *kvs, *more, micros=4, bounds=True,
    )


def fold_kernel(s, widths, keep, got, keep_out, send_out):
    block = keep_out.shape[1]
    for k in range(2):
        total = (keep[k].astype(F32) + got[k].astype(F32)).astype(BF)
        keep_out[k] = total[:block]
        send_out[k] = total[block:]


def fold(s, keep, got):
    part = shaped((2, keep.shape[1] // 2, keep.shape[2]))
    return call(fold_kernel, "fold", 4, [part, part], [], s, keep, got, micros=0.5)


def stack_kernel(s, widths, *refs, count):
    at = 0
    for ref in refs[:count]:
        refs[-1][at : at + ref.shape[0], :] = ref[...]
        at += ref.shape[0]


def stack(s, *parts, there=()):
    shape = (sum(part.shape[0] for part in parts), parts[0].shape[1])
    kernel = functools.partial(stack_kernel, count=len(parts))
    return call(kernel, "stack", 8, [shaped(shape)], [], s, *parts, *there, micros=0.5, streamed=len(there))[0]


def cut_kernel(s, widths, a, b, *refs):
    first, second, both = refs[-3:]
    rows = first.shape[0]
    first[...] = a[:rows, :]
    second[...] = b[rows:, :]
    both[: 2 * rows, :] = b[...]
    both[2 * rows :, :] = a[...]


def cut(s, a, b, there):
    rows, dim = a.shape
    part = shaped((rows // 2, dim))
    return call(
        cut_kernel, "cut", 6, [part, part, shaped((2 * rows, dim))], [], s, a, b, *there, micros=0.3, streamed=len(there)
    )


def collect_kernel(s, widths, *refs):
    count = (len(refs) - 1) // 2
    at = 0
    for k, ref in enumerate(refs[:-1]):
        rows = refs[k % count].shape[0]
        refs[-1][at : at + rows, :] = ref[:rows, :]
        at += rows


def collect(s, own, others):
    shape = (2 * sum(part.shape[0] for part in own), own[0].shape[1])
    return call(collect_kernel, "collect", 6, [shaped(shape)], [], s, *own, *others, micros=0.5)[0]


def add_kernel(s, widths, keep, got, out, *, first):
    out[...] = (keep[...].astype(F32) + got[first : first + keep.shape[0], :].astype(F32)).astype(BF)


def add(s, keep, got, first):
    kernel = functools.partial(add_kernel, first=first)
    return call(kernel, "add", 4, [shaped(keep.shape)], [], s, keep, got, micros=0.5)[0]


def sorted_images(s, out, own, back, last):
    first = s[CHIP] == 0
    out[0] = jnp.where(first, own, back)
    out[1] = jnp.where(first, back, own)
    out[2] = last


def assemble_kernel(s, widths, mix0, mix1, mix2, loss, mix, losses):
    block = mix0.shape[0]
    sorted_images(s, mix, mix0[...], mix1[:block, :], mix2[...])
    first = s[CHIP] == 0
    own = loss[0:1, :block]
    back = sum(mix1[block : block + 8, k * block : (k + 1) * block].astype(F32) for k in range(3))[0:1]
    losses[0:1, :] = jnp.where(first, own, back)
    losses[1:2, :] = jnp.where(first, back, own)
    losses[2:3, :] = loss[0:1, 2 * block :]


def assemble(s, mix, loss):
    block, dim = mix[0].shape
    return call(
        assemble_kernel, "assemble", 8, [in_hbm((3, block, dim)), in_hbm((3, block), F32)], [],
        s, *mix, loss, micros=1,
    )


def assemble_dx_kernel(s, widths, dx0, pack, dx2, dx):
    block = dx0.shape[0]
    first = pack.shape[0] - 2 * block
    back = jnp.concatenate([pack[first : first + block, :], pack[first + block :, :]], axis=1)
    sorted_images(s, dx, dx0[...], back.astype(F32), dx2[...])


def assemble_dx(s, *dx):
    block, dim = dx[0].shape
    return call(assemble_dx_kernel, "assemble_dx", 8, [in_hbm((3, block, dim), F32)], [], s, *dx, micros=1)[0]


def halve_kernel(s, widths, keep, got, keep_out, send_out, *, at, first):
    rows = keep_out.shape[0]
    for out, side in ((keep_out, s[SIDES + at]), (send_out, 1 - s[SIDES + at])):
        here = keep[pl.ds(pl.multiple_of(side * rows, 16), rows), :].astype(F32)
        out[...] = (here + got[pl.ds(pl.multiple_of(first + side * rows, 16), rows), :].astype(F32)).astype(BF)


def halve(s, keep, got, at, first):
    part = shaped((keep.shape[0] // 2, keep.shape[1]))
    return call(functools.partial(halve_kernel, at=at, first=first), "halve", 8, [part, part], [], s, keep, got, micros=0.7)


def gelu_pair(x):
    z = jnp.abs(x) * (0.5**0.5)
    t = 1.0 / (1.0 + 0.3275911 * z)
    expo = jnp.exp(-0.5 * x * x)
    poly = t * (0.254829592 + t * (-0.284496736 + t * (1.421413741 + t * (-1.453152027 + t * 1.061405429))))
    tail = 0.5 * poly * expo
    cdf = jnp.where(x < 0.0, tail, 1.0 - tail)
    return x * cdf, cdf + x * (expo * 0.3989422804014327)


def mlp_tiles(side, h2, bup, wup, wdown, enc, act_ref, slope, tile):
    wide = slope.shape[1]
    for k in range(0, wide, tile):
        here, there = slice(k, k + tile), pl.ds(pl.multiple_of(side * wide + k, 128), tile)
        act, rate = gelu_pair(mm(h2[...], wup[:, there]) + bup[there].reshape(1, tile))
        act = act.astype(BF)
        act_ref[:, here] = act
        slope[:, here] = rate.astype(BF)
        enc[...] += mm(act, wdown[there, :])


def mlp_first_kernel(
    s, widths, got, att_main, att_last, h1, bout, gain, shift, bup, bdown, wout, wup, wdown, patches, mid, h2, enc, slope,
    send, x_own, sems, *, tile,
):
    dim = got.shape[1]
    half, wide = dim // 2, slope.shape[1]
    rows = att_main.shape[0]
    side = 1 - s[CORE]
    stream = Stream(sems, (patches.at[s[CHIP]], x_own.at[0]), (patches.at[2], x_own.at[1]))
    branch = mm(jnp.concatenate([att_main[...], att_last[...]], axis=0), wout[...])
    stream.wait(2)
    x = jnp.concatenate([x_own[0], got[...], x_own[1]], axis=0).astype(F32)
    middle = x + branch + line(bout)
    mid[...] = middle
    xhat, _ = norm_stats(middle)
    h2[...] = (xhat * line(gain) + line(shift)).astype(BF)
    enc[...] = middle + line(bdown)
    send[:, wide : wide + half] = side_of(h2, side, half)
    send[:rows, wide + half : wide + dim] = side_of(att_main, side, half)
    send[rows:, wide + half : wide + dim] = side_of(att_last, side, half)
    send[:, wide + dim :] = h1[...]
    mlp_tiles(side, h2, bup, wup, wdown, enc, send, slope, tile)


def mlp_second_kernel(s, widths, h2, enc_in, att_main, att_last, bup, wup, wdown, enc, slope, mine, *, tile):
    half, wide = h2.shape[1] // 2, slope.shape[1]
    rows = att_main.shape[0]
    enc[...] = enc_in[...]
    mine[:, wide : wide + half] = side_of(h2, s[CORE], half)
    mine[:rows, wide + half :] = side_of(att_main, s[CORE], half)
    mine[rows:, wide + half :] = side_of(att_last, s[CORE], half)
    mlp_tiles(s[CORE], h2, bup, wup, wdown, enc, mine, slope, tile)


def mlp_first(s, patches, got, att_main, att_last, h1, bout, gain, shift, bup, bdown, wout, wup, wdown):
    images, block, dim = patches.shape
    n, wide = images * block, wup.shape[1] // 2
    return call(
        functools.partial(mlp_first_kernel, tile=512), "mlp_first", 8,
        [
            shaped((n, dim), F32), shaped((n, dim)), shaped((n, dim), F32), shaped((n, wide)),
            shaped((n, wide + dim + dim // 2)),
        ],
        [pltpu.VMEM((2, block, dim), BF), pltpu.SemaphoreType.DMA((2,))],
        s, got, att_main, att_last, h1, bout, gain, shift, bup, bdown, wout, wup, wdown, patches, micros=6, streamed=1,
    )


def mlp_second(s, h2, enc, att_main, att_last, bup, wup, wdown):
    n, dim = h2.shape
    wide = wup.shape[1] // 2
    return call(
        functools.partial(mlp_second_kernel, tile=512), "mlp_second", 8,
        [shaped((n, dim), F32), shaped((n, wide)), shaped((n, wide + dim))], [],
        s, h2, enc, att_main, att_last, bup, wup, wdown, micros=5,
    )


def quant_kernel(s, widths, enc, cot_got, *refs, tile, scale):
    pieces, cot = refs[:-14], refs[-14]
    mix_own, mix_back, mix_last, loss, denc, dmlp, score, dweight, late, cot_own, mixes, losses, sems = refs[-13:]
    n, dim = enc.shape
    block = n // 3
    chunks, place = [], 0
    for piece in pieces:
        for first in range(0, piece.shape[0], tile):
            size = min(tile, piece.shape[0] - first)
            chunks.append((piece, slice(first, first + size), slice(place, place + size)))
            place += size + -size % 128
    stream = Stream(sems, (cot.at[s[CHIP]], cot_own.at[0]), (cot.at[2], cot_own.at[1]))
    low = enc[...].astype(BF)
    peak = None
    for piece, rows, cols in chunks:
        part = mm_nt(low, piece[rows, :]) * scale
        score[:, cols] = part
        top = jnp.max(part, axis=1, keepdims=True)
        peak = top if peak is None else jnp.maximum(peak, top)
    total = jnp.zeros_like(peak)
    late[...] = jnp.zeros_like(late)
    for piece, rows, cols in chunks:
        e = jnp.exp(score[:, cols] - peak)
        score[:, cols] = e
        total = total + jnp.sum(e, axis=1, keepdims=True)
        late[...] += mm(e.astype(BF), piece[rows, :])
    inv = 1.0 / total
    mix = late[...] * inv
    low = mix.astype(BF)
    mixes[: 2 * block, :] = low[: 2 * block]
    mixes[2 * block + 16 :, :] = low[2 * block :]
    index = lax.broadcasted_iota(jnp.int32, (n, 1), 0)
    spot = spots(index & (2 * block - 1), block, s[ME])
    ok = spot < jnp.where(index < 2 * block, limit_of(s, widths, False), limit_of(s, widths, True))
    diff = enc[...] - mix
    lost = jnp.where(ok, jnp.mean(diff * diff, axis=1, keepdims=True), 0.0)
    lost = jnp.transpose(jnp.broadcast_to(lost, (n, 128)))[0:8, :]
    losses[...] = lost
    back = lost[:, block : 2 * block]
    high = back.astype(BF)
    rest = back - high.astype(F32)
    below = 2 * block
    mixes[below : below + 16, :] = jnp.zeros((16, dim), BF)
    mixes[below : below + 8, :block] = high
    mixes[below : below + 8, block : 2 * block] = rest.astype(BF)
    mixes[below : below + 8, 2 * block : 3 * block] = (rest - rest.astype(BF).astype(F32)).astype(BF)
    spans = ((mix_own, 0, block), (mix_back, block, 2 * block + 16), (mix_last, 2 * block + 16, 3 * block + 16))
    outs = [pltpu.make_async_copy(mixes.at[a:b, :], out, sems.at[2 + k]) for k, (out, a, b) in enumerate(spans)]
    outs.append(pltpu.make_async_copy(losses, loss, sems.at[5]))
    for out in outs:
        out.start()
    pull = jnp.where(ok, (2.0 * COMMIT / dim) * diff, 0.0)
    denc[...] = pull
    stream.wait(2)
    cots = jnp.concatenate([cot_own[0], cot_got[...], cot_own[1]], axis=0).astype(F32)
    dmix = (cots - pull).astype(BF)
    inner = jnp.zeros_like(peak)
    for piece, rows, cols in chunks:
        d = mm_nt(dmix, piece[rows, :])
        dweight[:, cols] = d
        inner = inner + jnp.sum(score[:, cols] * d, axis=1, keepdims=True)
    inner = inner * inv
    inv = inv * scale
    for piece, rows, cols in chunks:
        dcode = (score[:, cols] * inv * (dweight[:, cols] - inner)).astype(BF)
        denc[...] += mm(dcode, piece[rows, :])
    dmlp[...] = denc[...].astype(BF)
    for out in outs:
        out.wait()


def quantizer(s, enc, cot, cot_got, pieces, tile=512):
    n, dim = enc.shape
    block = n // 3
    count = sum(-(-piece.shape[0] // tile) for piece in pieces)
    wide = count * tile
    return call(
        functools.partial(quant_kernel, tile=tile, scale=dim**-0.5), "quantizer", 21,
        [in_hbm((block, dim)), in_hbm((block + 16, dim)), in_hbm((block, dim))]
        + [in_hbm((8, n), F32), shaped((n, dim), F32), shaped((n, dim))],
        [
            pltpu.VMEM((n, wide), F32), pltpu.VMEM((n, wide), F32), pltpu.VMEM((n, dim), F32),
            pltpu.VMEM((2, block, dim), BF), pltpu.VMEM((n + 16, dim), BF), pltpu.VMEM((8, n), F32),
            pltpu.SemaphoreType.DMA((6,)),
        ],
        s, enc, cot_got, *pieces, cot, micros=14, streamed=1, by_hand=range(4), bounds=True,
    )


def quantizer_plain(s, enc, cots, book):
    n, dim = enc.shape
    block = n // 3
    index = jnp.arange(n)
    ok = spots(index & (2 * block - 1), block, lax.axis_index("seq")) < jnp.where(index < 2 * block, GRID_H * pick(s, lax.axis_index("seq") // 2, 0), GRID_H * s[2])
    scale = dim**-0.5
    scores = mm_nt(enc.astype(BF), book) * scale
    peak = jnp.max(scores, axis=-1, keepdims=True)
    log_total = peak + jnp.log(jnp.sum(jnp.exp(scores - peak), axis=-1, keepdims=True))
    weights = jnp.exp(scores - log_total)
    mix = mm(weights.astype(BF), book)
    diff = enc - mix
    loss = jnp.where(ok, jnp.mean(diff * diff, axis=-1), 0.0)
    pull = jnp.where(ok[:, None], 2.0 * COMMIT / dim * diff, 0.0)
    dmix = (cots.astype(F32) - pull).astype(BF)
    dweights = mm_nt(dmix, book)
    inner = jnp.sum(weights * dweights, axis=-1, keepdims=True)
    dcode = (weights * (dweights - inner) * scale).astype(BF)
    denc = mm(dcode, book) + pull
    low = mix.astype(BF)
    loss = jnp.broadcast_to(loss[None, :], (8, n))
    parts, rest = [], loss[:, block : 2 * block]
    for _ in range(3):
        parts.append(rest.astype(BF))
        rest = rest - parts[-1].astype(F32)
    parts = jnp.pad(jnp.concatenate(parts, axis=1), ((0, 8), (0, dim - 3 * block)))
    back = jnp.concatenate([low[block : 2 * block], parts])
    return low[:block], back, low[2 * block :], loss, denc, denc.astype(BF)


def mlp_bwd_kernel(
    s, widths, dmlp, denc, mid, gain, slope0, slope1, wdown, wup, wout, dp0, dp1, dbranch, dmid_ref, datt, rows, bup, acc,
    *, tile,
):
    hidden, wide = wup.shape[1], slope0.shape[1]
    for t in range(0, hidden, tile):
        span, half, here = slice(t, t + tile), t // wide, slice(t % wide, t % wide + tile)
        slope = jnp.where(s[CORE] == half, slope1[:, here], slope0[:, here]).astype(F32)
        dpre = (mm_nt(dmlp[...], wdown[span, :]) * slope).astype(BF)
        (dp0, dp1)[half][:, here] = dpre
        bup[:, span] = jnp.sum(dpre.astype(F32), axis=0, keepdims=True)
        part = mm_nt(dpre, wup[:, span])
        if t == 0:
            acc[...] = part
        else:
            acc[...] += part
    dy = acc[...]
    xhat, inv = norm_stats(mid[...])
    dmid = denc[...] + norm_back(xhat, inv, line(gain), dy)
    dmid_ref[...] = dmid
    low = dmid.astype(BF)
    dbranch[...] = low
    datt[...] = mm_nt(low, wout[...]).astype(BF)
    rows[0:1, :] = jnp.sum(dy * xhat, axis=0, keepdims=True)
    rows[1:2, :] = jnp.sum(dy, axis=0, keepdims=True)
    rows[2:3, :] = jnp.sum(low.astype(F32), axis=0, keepdims=True)
    rows[3:4, :] = jnp.sum(dmlp[...].astype(F32), axis=0, keepdims=True)


def mlp_bwd(s, dmlp, denc, mid, gain, slopes, wdown, wup, wout):
    n, dim = denc.shape
    hidden, tile = wup.shape[1], 512
    return call(
        functools.partial(mlp_bwd_kernel, tile=tile), "mlp_bwd", 8,
        [
            shaped((n, hidden // 2)), shaped((n, hidden // 2)), shaped((n, dim)), shaped((n, dim), F32),
            shaped((n, dim)), shaped((4, dim), F32), shaped((1, hidden), F32),
        ],
        [pltpu.VMEM((n, dim), F32)],
        s, dmlp, denc, mid, gain, *slopes, wdown, wup, wout, micros=9,
    )


TINY_UP, TINY_QKV = 32, 16


def labels(steps, index, part):
    return [[part if step == "y" else parity(index & step[1]) for step in order] for order in steps]


def place(s, first, steps, keep, send, index, part, rows, value):
    sides = labels(steps, index, part)
    slots = [functools.reduce(lambda x, y: 2 * x + y, side[1:], 0) for side in sides]
    here = sides[0][0] + (sides[1][0] - sides[0][0]) * s[CORE]
    slot = slots[0] + (slots[1] - slots[0]) * s[CORE]

    @pl.when(s[first] == here)
    def _():
        keep[slot, rows, :] = value

    @pl.when(s[first] != here)
    def _():
        send[slot, rows, :] = value


def quotient(index, size):
    return ((index.astype(F32) + 0.5) * (1.0 / size)).astype(jnp.int32)


def tiny_rows(rows, shards, half):
    dim = rows.shape[1]
    part = dim // shards
    shard = lax.broadcasted_iota(jnp.int32, (shards, dim), 0)
    of = quotient(lax.broadcasted_iota(jnp.int32, (shards, dim), 1), part)
    local = lax.broadcasted_iota(jnp.int32, (dim, 1), 0)
    local = local - quotient(local, part) * part
    lane = lax.broadcasted_iota(jnp.int32, (dim, half), 1)
    total = jnp.zeros((shards, half), F32)
    for k in range(4):
        spread = jnp.where(of == shard, jnp.broadcast_to(rows[k : k + 1, :], (shards, dim)), 0.0)
        total = total + mm(spread.astype(BF), (lane == local + k * part).astype(F32).astype(BF))
    return total


def grad_down_kernel(s, widths, dm, act0, act1, keep, send, *, shards, steps):
    n, half = act0.shape[0], keep.shape[2]
    rows = dm.shape[1] // shards // 2
    width = keep.shape[1] // rows * half
    full = (mm_tn(dm[:n, :], act0[:, :width]) + mm_tn(dm[n:, :], act1[:, :width])).astype(BF)
    for j in range(2 * shards):
        for k in range(width // half):
            value = full[j * rows : (j + 1) * rows, k * half : (k + 1) * half]
            place(s, SIDES, steps, keep, send, j // 2, j % 2, slice(k * rows, (k + 1) * rows), value)


def grad_down(s, dm, act0, act1, shards, steps):
    dim = dm.shape[1]
    half = dim // 2
    part = shaped((shards, dim // shards // 2 * ((act0.shape[1] - dim) // half), half))
    return call(
        functools.partial(grad_down_kernel, shards=shards, steps=steps), "grad_down", 10, [part, part], [],
        s, dm, act0, act1, micros=4,
    )


def grad_up_kernel(s, widths, a0, a1, *refs, shards, steps):
    d0, d1, (four, bup, keep, send) = refs[:3], refs[3:6], refs[6:]
    size, half = keep.shape[1], keep.shape[2]
    wide = d0[0].shape[1]
    hidden = 2 * wide
    first = hidden // 2
    cols = hidden // shards
    rows = 2 * half // shards
    per = shards // 4
    tiny = tiny_rows(four[...], shards, half)
    at = lax.broadcasted_iota(jnp.int32, (2 * size - half - rows, half), 0)

    def put(index, part, at, value):
        place(s, SIDES + 4, steps, keep, send, index, part, slice(at, at + value.shape[0]), value)

    h = slice(first + half, first + 2 * half)
    out = (mm_tn(d0[2][...], a0[:, h]) + mm_tn(d1[2][...], a1[:, h])).astype(BF)
    h = slice(first, first + half)
    for k in range(0, shards, per):
        side, first_col = k * cols // wide, k * cols % wide
        span = slice(first_col, first_col + per * cols)
        full = (mm_tn(a0[:, h], d0[side][:, span]) + mm_tn(a1[:, h], d1[side][:, span])).astype(BF)
        for j in range(per):
            put(k + j, 0, 0, full[:size, j * cols : (j + 1) * cols])
            put(k + j, 1, 0, full[size:, j * cols : (j + 1) * cols])
            put(k + j, 1, half - size, out[(k + j) * rows : (k + j + 1) * rows])
            both = jnp.where(at == 0, tiny[k + j : k + j + 1], 0.0)
            both = both + jnp.where(at == 1, bup[:, (k + j) * cols : (k + j + 1) * cols], 0.0)
            put(k + j, 1, half - size + rows, both.astype(BF))


def grad_up(s, mine, got, dp0, dp1, four, bup, shards, steps):
    half = got.shape[1] - mine.shape[1]
    dim = 2 * half
    part = shaped((shards, (half + dim // shards + TINY_UP) // 2, half))
    return call(
        functools.partial(grad_up_kernel, shards=shards, steps=steps), "grad_up", 10,
        [part, part], [], s, mine, got, *dp0, *dp1, four, bup, micros=5,
    )


def got_rows(owns):
    return owns[0].shape[0] // 5


def last_of(ref, step, n, block, dim):
    wide = ref.shape[1]
    blocks = [
        ref[5 * n + k * block : 5 * n + (k + 1) * block, :] for k in range(step * dim // wide, (step + 1) * dim // wide)
    ]
    return jnp.concatenate(blocks, axis=1)


def d_of(owns, gots, step, n):
    if step == 0:
        return jnp.concatenate([own[4 * n : 5 * n, :] for own in owns], axis=1)
    mine, theirs = slice((step - 1) * n, step * n), slice((step + 1) * n, (step + 2) * n)
    return jnp.concatenate(
        [(own[mine, :].astype(F32) + got[theirs, :].astype(F32)).astype(BF) for own, got in zip(owns, gots)], axis=1
    )


def grad_qkv_kernel(
    s, widths, *refs, shards, steps
):
    groups = (len(refs) - 4) // 2
    owns, gots = refs[:groups], refs[groups : 2 * groups]
    h_own, other, keep, send = refs[-4:]
    n, half = got_rows(owns), h_own.shape[1]
    block = n // 2
    dim = 2 * half
    h = slice(other.shape[1] - half, other.shape[1])
    size = 3 * dim // shards // 2

    def put(k, at, value):
        place(s, SIDES + 8, steps, keep, send, k // 2, k % 2, slice(at, at + value.shape[0]), value)

    for step in range(3):
        d_own, d_got = d_of(owns, gots, step, n), d_of(gots, owns, step, n)
        full = mm_tn(d_own, h_own[:n, :]) + mm_tn(d_got, other[:n, h])
        last_own, last_got = (last_of(refs[1], step, n, block, dim) for refs in (owns, gots))
        full = full + mm_tn(last_own, h_own[n:, :]) + mm_tn(last_got, other[n:, h])
        full = full.astype(BF)
        first = step * dim
        for k in range(first // size, (first + dim + size - 1) // size):
            lo, hi = max(first, k * size), min(first + dim, (k + 1) * size)
            put(k, lo - k * size, full[lo - first : hi - first])


def grad_qkv(s, owns, gots, h_own, other, shards, steps):
    half = h_own.shape[1]
    part = shaped((shards, 3 * half // shards, half))
    return call(
        functools.partial(grad_qkv_kernel, shards=shards, steps=steps), "grad_qkv", 12, [part, part], [],
        s, *owns, *gots, h_own, other, micros=4,
    )


def grad_vec_kernel(s, widths, norms, sums, keep, send, *, shards, steps):
    half = keep.shape[2]
    tiny = tiny_rows(jnp.concatenate([norms[...], sums[0:1, :], sums[2:3, :]], axis=0), shards, half)
    at = lax.broadcasted_iota(jnp.int32, (TINY_QKV, half), 0)
    for k in range(2 * shards):
        value = jnp.where(at == 0, tiny[k // 2 : k // 2 + 1], 0.0).astype(BF)
        place(s, SIDES + 8, steps, keep, send, k // 2, k % 2, slice(None), value)


def grad_vec(s, norms, sums, shards, steps):
    part = shaped((shards, TINY_QKV, norms.shape[1] // 2))
    return call(
        functools.partial(grad_vec_kernel, shards=shards, steps=steps), "grad_vec", 8, [part, part], [],
        s, norms, sums, micros=1,
    )


def qkv_bwd_kernel(
    s, widths, *refs
):
    groups = (len(refs) - 13) // 2
    owns, gots = refs[:groups], refs[groups : 2 * groups]
    x_got, gain, dmid, w, patches, dx0, dx1, dx2, norms, sums, acc, x_own, sems = refs[-13:]
    block, dim = x_got.shape
    n = 2 * block
    spans = [slice(k * dim, (k + 1) * dim) for k in range(3)]
    stream = Stream(sems, (patches.at[s[CHIP]], x_own.at[0]), (patches.at[2], x_own.at[1]))
    for k, cols in enumerate(spans):
        d = jnp.concatenate([d_of(owns, gots, k, n), last_of(owns[1], k, n, block, dim)], axis=0)
        sums[k : k + 1, :] = jnp.sum(d.astype(F32), axis=0, keepdims=True)
        part = mm_nt(d, w[:, cols])
        if k == 0:
            acc[...] = part
        else:
            acc[...] += part
    dy = acc[...]
    stream.wait(2)
    x = jnp.concatenate([x_own[0], x_got[...], x_own[1]], axis=0).astype(F32)
    xhat, inv = norm_stats(x)
    dx = dmid[...] + norm_back(xhat, inv, line(gain), dy)
    dx0[...] = dx[:block]
    for k in range(2):
        dx1[k * block : (k + 1) * block, :] = dx[block:n, k * dim // 2 : (k + 1) * dim // 2].astype(BF)
    dx2[...] = dx[n:]
    norms[0:1, :] = jnp.sum(dy * xhat, axis=0, keepdims=True)
    norms[1:2, :] = jnp.sum(dy, axis=0, keepdims=True)


def qkv_bwd(s, owns, gots, patches, x_got, gain, dmid, w):
    images, block, dim = patches.shape
    return call(
        qkv_bwd_kernel, "qkv_bwd", 9,
        [
            in_hbm((block, dim), F32), shaped((2 * block, dim // 2)), in_hbm((block, dim), F32),
            shaped((2, dim), F32), shaped((3, dim), F32),
        ],
        [
            pltpu.VMEM((images * block, dim), F32), pltpu.VMEM((2, block, dim), BF),
            pltpu.SemaphoreType.DMA((2,)),
        ],
        s, *owns, *gots, x_got, gain, dmid, w, patches, micros=4, streamed=1,
    )


def finish_kernel(s, widths, both, both_got, up, out, qkv, wdown, *vectors, rows_up, rows_qkv, size, parts):
    def sorted_of(value, other):
        cut = value.shape[0] // 2
        mine = [value[:cut].astype(F32), value[cut:].astype(F32)]
        theirs = [other[:cut].astype(F32), other[cut:].astype(F32)]
        second = s[CHIP] > 0
        pairs = [[jnp.where(second, v[1], v[0]), jnp.where(second, v[0], v[1])] for v in (mine, theirs)]
        swap_cores = s[CORE] > 0
        return [
            [jnp.where(swap_cores, b, a) for a, b in zip(*pairs)],
            [jnp.where(swap_cores, a, b) for a, b in zip(*pairs)],
        ]

    cores = sorted_of(both, both_got)
    rows = [jnp.concatenate([first[:rows_up], second[:rows_up]], axis=0) for first, second in cores]
    half = up.shape[0] // 2
    wide = out.shape[0]
    up[:half, :] = rows[0][:half]
    up[half:, :] = rows[1][:half]
    out[...] = jnp.concatenate([r[half : half + wide] for r in rows], axis=1)
    pieces = [jnp.concatenate([f[rows_up : rows_up + size], g[rows_up : rows_up + size]], axis=0) for f, g in cores]
    qkv[...] = jnp.concatenate(pieces, axis=1)
    two = rows[0][half + wide : half + wide + 8] + rows[1][half + wide : half + wide + 8]
    one = cores[0][0][rows_up + size : rows_up + size + 8] + cores[1][0][rows_up + size : rows_up + size + 8]
    for ref, (source, row, at) in zip(vectors, parts):
        ref[...] = (one, two)[source][row : row + 1, at : at + ref.shape[0]].reshape(ref.shape[0])
    first = rows_up + rows_qkv
    blocks = out.shape[0] // 2
    count = (both.shape[0] // 2 - first) // blocks
    for c, pair in enumerate(cores):
        for y, part in enumerate(pair):
            for k in range(count):
                at = (c * count + k) * half
                wdown[y * blocks : (y + 1) * blocks, at : at + half] = part[first + k * blocks : first + (k + 1) * blocks]


def finish(s, both, both_got, rows_up, rows_qkv, dim, hidden, shards):
    part, wide = dim // shards, hidden // shards
    size = 3 * dim // shards // 2
    parts = [(0, 0, k * part) for k in range(4)]
    parts += [(1, 0, 2 * part), (1, 0, 0), (1, 0, part), (1, 1, 0), (1, 0, 3 * part)]
    widths = [part] * 7 + [wide, part]
    return call(
        functools.partial(finish_kernel, rows_up=rows_up, rows_qkv=rows_qkv, size=size, parts=parts), "finish", 20,
        [in_hbm((dim, wide), F32), in_hbm((part, dim), F32), in_hbm((3 * part, dim), F32), in_hbm((part, hidden), F32)]
        + [in_hbm((width,), F32) for width in widths],
        [], s, both, both_got, micros=3,
    )


def hop(value, step0, step1):
    seq, img = lax.axis_size("seq"), lax.axis_size("img")
    pairs = []
    for s in range(seq):
        step = step1 if s % 2 else step0
        for i in range(img):
            to = (s ^ 2, i) if step == "y" else (s, i ^ (step if isinstance(step, int) else step[0]))
            pairs.append((s * img + i, to[0] * img + to[1]))
    return lax.ppermute(value, ("seq", "img"), pairs)


def plus(kept, got):
    return (kept.astype(F32) + got.astype(F32)).astype(BF)


class Sum:
    def __init__(self, s, chain, steps, keep, send):
        self.s, self.base, self.steps, self.at = s, chain * len(steps[0]), steps, 0
        self.keep, self.send = (part.reshape(-1, part.shape[-1]) for part in (keep, send))

    def go(self):
        self.got, self.first = hop(self.send, self.steps[0][self.at], self.steps[1][self.at]), 0
        self.at += 1

    def halve(self):
        if self.keep.shape[0] % 32 == 0:
            self.keep, self.send = halve(self.s, self.keep, self.got, self.base + self.at, self.first)
            return
        total = plus(self.keep, self.got[self.first : self.first + self.keep.shape[0]]).reshape(2, -1, self.keep.shape[1])
        side = sides_here(self.steps)[self.at]
        self.keep, self.send = pick(total, side, 0), pick(total, 1 - side, 0)

    def step(self):
        self.halve()
        self.go()

    def steps_left(self, most):
        while len(self.steps[0]) - self.at > most:
            self.step()

    def last(self):
        if self.keep.shape[0] % 16 == 0:
            return add(self.s, self.keep, self.got, self.first)
        return plus(self.keep, self.got[self.first : self.first + self.keep.shape[0]])


def go_together(s, a, b):
    if [order[a.at] for order in a.steps] != [order[b.at] for order in b.steps]:
        a.go()
        b.go()
        return
    rows = a.send.shape[0]
    both = stack(s, a.send, b.send) if rows % 16 == 0 else jnp.concatenate([a.send, b.send])
    got = hop(both, a.steps[0][a.at], a.steps[1][a.at])
    for chain, first in ((a, 0), (b, rows)):
        chain.got, chain.first = got, first
        chain.at += 1


def finish_plain(core, chip, both, both_got, rows_up, rows_qkv, dim, hidden, shards):
    part, wide, half = dim // shards, hidden // shards, dim // 2
    size = 3 * dim // shards // 2

    def sorted_of(value, other):
        pairs = []
        for v in (value, other):
            a, b = jnp.split(v.astype(F32), 2)
            pairs.append([jnp.where(chip == 0, a, b), jnp.where(chip == 0, b, a)])
        mine, theirs = pairs
        first = [jnp.where(core == 0, a, b) for a, b in zip(mine, theirs)]
        return [first, [jnp.where(core == 0, b, a) for a, b in zip(mine, theirs)]]

    cores = sorted_of(both, both_got)
    rows = [jnp.concatenate([f[:rows_up], g[:rows_up]]) for f, g in cores]
    up = jnp.concatenate([r[:wide].T for r in rows])
    out = jnp.concatenate([r[wide : wide + part] for r in rows], axis=1)
    pieces = [jnp.concatenate([f[rows_up : rows_up + size], g[rows_up : rows_up + size]]) for f, g in cores]
    two = sum(r[wide + part :] for r in rows).reshape(-1)
    one = sum(f[rows_up + size : rows_up + rows_qkv] for f, _ in cores).reshape(-1)
    downs = [[f[rows_up + rows_qkv :].reshape(-1, part // 2, half) for f in pair] for pair in cores]
    downs = [jnp.concatenate([f.transpose(1, 0, 2).reshape(part // 2, -1) for f in pair]) for pair in downs]
    down = jnp.concatenate(downs, axis=1)
    first = [one[k * part : (k + 1) * part] for k in range(4)]
    second = [two[k * part : (k + 1) * part] for k in (2, 0, 1)]
    last = [two[4 * part : 4 * part + wide], two[3 * part : 4 * part]]
    return [up, out, jnp.concatenate(pieces, axis=1), down, *first, *second, *last]


class Book:
    def __init__(self, s, codebook):
        n_img = lax.axis_size("img")
        bits = [1 << k for k in range(n_img.bit_length() - 1)]
        masks = [1, 2, 6] if n_img == 8 else bits
        self.orders = list(zip(masks[1:], [1, "y", *masks[3:]]))
        self.ends = ((1, masks[1]), ("y", masks[2]))
        self.s, self.value = s, codebook

    def stack(self, *parts, there=()):
        return stack(self.s, *parts, there=there) if sum(part.size for part in parts) < 1 << 21 else jnp.concatenate(parts)

    def start(self):
        self.got = hop(self.value, *self.orders.pop(0))

    def double(self):
        self.value = self.stack(self.value, self.got)

    def spread(self):
        self.beside, self.across = hop(self.value, *self.ends[0]), hop(self.value, *self.ends[1])
        self.other = [swap(self.value, "seq", 1)]

    def corner(self, there):
        if self.value.size < 1 << 21:
            *parts, self.sides = cut(self.s, self.across, self.beside, (there, self.other[0]))
        else:
            half = self.value.shape[0] // 2
            parts = self.across[:half], self.beside[half:]
            self.sides = jnp.concatenate([self.beside, self.across])
        self.corners = hop(parts[0], *self.ends[0]), hop(parts[1], *self.ends[1])
        self.other.append(swap(self.sides, "seq", 1))

    def finish(self):
        rest = self.stack(*self.corners, there=(self.other[1],))
        return [self.value, self.sides, rest, *self.other, swap(rest, "seq", 1)]


def shards(
    patches,
    widths,
    ln1_gain,
    ln1_bias,
    w_qkv,
    b_query,
    b_value,
    w_out,
    b_out,
    ln2_gain,
    ln2_bias,
    w_up,
    b_up,
    w_down,
    b_down,
    codebook,
    cotangent,
):
    images, block, dim = patches.shape
    hidden = w_up.shape[1]
    n_img = lax.axis_size("img")
    me = lax.axis_index("seq")
    chip, core = me // 2, me % 2
    half, main = dim // 2, 2 * block
    fits = codebook.shape[0] * n_img * lax.axis_size("seq") <= 4096
    aligned = n_img == 8 and dim // n_img // 2 % 16 == 0
    steps_down, steps_up, steps_qkv = plans(n_img)
    s = widths

    Order.token = jnp.zeros((8, 128), F32)
    book = Book(s, codebook)
    book.start()
    x_got = swap(pick(patches, 1 - chip, 0), "seq", 2)
    kv_last, h_last = kv_last_fwd(s, patches, ln1_gain, ln1_bias, b_value, w_qkv)
    kv_y = swap(kv_last, "seq", 2)
    while book.orders:
        book.double()
        book.start()
    q_main, q_last, *kvs, h_mine, h_send = qkv_fwd(s, patches, x_got, h_last, ln1_gain, ln1_bias, b_query, b_value, w_qkv)
    kvs.append(kv_last)
    kvs_other = [swap(kv, "seq", 1) for kv in kvs]
    book.double()
    book.spread()
    kvs_main = kvs[:2] + kvs_other[:2]
    att_main = attention_fwd(s, q_main, kvs_main, False, block)
    cot_got = swap(pick(cotangent, 1 - chip, 0), "seq", 2)
    kvs_last = [kvs[2], kv_y, kvs_other[2], swap(kv_y, "seq", 1)]
    att_last = attention_fwd(s, q_last, kvs_last, True, block)
    mid, h2, enc, slope0, send = mlp_first(
        s, patches, x_got, att_main, att_last, h_send, b_out, ln2_gain, ln2_bias, b_up, b_down, w_out, w_up,
        w_down,
    )
    got = swap(send, "seq", 1)
    book.corner(cot_got)
    enc, slope1, mine = mlp_second(s, h2, enc, att_main, att_last, b_up, w_up, w_down)
    pieces = book.finish()
    if fits:
        mix0, mix1, mix2, loss, denc, dmlp = quantizer(s, enc, cotangent, cot_got, pieces)
    else:
        cots = jnp.concatenate([pick(cotangent, chip, 0), cot_got, cotangent[2]])
        mix0, mix1, mix2, loss, denc, dmlp = quantizer_plain(s, enc, cots, jnp.concatenate(pieces))
    mix1 = swap(mix1, "seq", 2)

    def split(full, steps):
        rows, cols = full.shape[-2:]
        full = full.reshape([2] * len(steps[0]) + [rows // 2, cols])
        side = sides_here(steps)[0]
        return pick(full, side, 0), pick(full, 1 - side, 0)

    def lines_of(count, *vectors):
        rows = jnp.concatenate([v.reshape(n_img, -1) for v in vectors], axis=1).astype(BF)
        return jnp.pad(rows, ((0, 0), (0, count * half - rows.shape[1]))).reshape(n_img, count, half)

    dmlp_got = swap(dmlp, "seq", 1)
    both = jnp.concatenate([mine, got[:, : mine.shape[1]]])
    if aligned:
        dmlp_both = stack(s, dmlp, dmlp_got, there=(got,))
        keep, send = grad_down(s, dmlp_both, mine, got, n_img, steps_down)
    else:
        full = mm_tn(jnp.concatenate([dmlp, dmlp_got]), both[:, : hidden // 2]).astype(BF)
        full = full.reshape(n_img, 2, dim // n_img // 2, -1, half).transpose(0, 1, 3, 2, 4)
        keep, send = split(full.reshape(n_img, -1, half), steps_down)
    down = Sum(s, 0, steps_down, keep, send)
    down.go()
    *dp, dmid, datt, rows_two, sum_bup = mlp_bwd(s, dmlp, denc, mid, ln2_gain, (slope0, slope1), w_down, w_up, w_out)
    dp_got = [swap(part, "seq", 1) for part in dp]
    quantized, token_loss = assemble(s, (mix0, mix1, mix2), loss)
    keep_last, send_last, dq_last = attention_bwd(s, q_last, kvs_last, datt, main, True, block, ())
    got_last = swap(send_last, "seq", 1)
    keep_last, send_last = fold(s, keep_last, got_last)
    down.step()
    got_last = swap(send_last, "seq", 2)
    if aligned:
        keep, send = grad_up(s, mine, got, dp, dp_got, rows_two, sum_bup, n_img, steps_up)
    else:
        dps = jnp.concatenate([jnp.concatenate(dp, axis=1), jnp.concatenate(dp_got, axis=1)])
        up = mm_tn(both[:, hidden // 2 : hidden // 2 + half], dps[:, :hidden]).astype(BF)
        up = up.reshape(half, n_img, -1).transpose(1, 2, 0)
        out = mm_tn(dps[:, hidden:], both[:, hidden // 2 + half :]).astype(BF).reshape(n_img, -1, half)
        tiny = lines_of(TINY_UP, rows_two[0], rows_two[1], rows_two[2], rows_two[3], sum_bup[0])
        keep, send = split(jnp.concatenate([up, out, tiny], axis=1), steps_up)
    up = Sum(s, 1, steps_up, keep, send)
    up.go()
    d_main, d_got = [], []
    for pairs, more in (((0, 1), ()), ((2, 3), (dq_last, keep_last, got_last)), ((4, 5), ())):
        d_main += attention_bwd(s, q_main, kvs_main, datt, 0, False, block, pairs, more)
        d_got.append(swap(d_main[-1], "seq", 1))
        if len(d_main) == 2:
            down.step()
    if aligned:
        keep, send = grad_qkv(s, d_main, d_got, h_mine, got, n_img, steps_qkv)
    else:
        n = main

        def assembled(owns, gots):
            rows = [jnp.concatenate([own[4 * n : 5 * n] for own in owns], axis=1)]
            for k in (0, 1):
                mine, theirs = slice(k * n, (k + 1) * n), slice((k + 2) * n, (k + 3) * n)
                rows.append(jnp.concatenate([plus(own[mine], got[theirs]) for own, got in zip(owns, gots)], axis=1))
            last = owns[1][5 * n :].reshape(-1, block, owns[1].shape[1])
            return [jnp.concatenate(rows, axis=1), jnp.concatenate(list(last), axis=1)]

        d = jnp.concatenate(assembled(d_main, d_got) + assembled(d_got, d_main))
        h = jnp.concatenate([h_mine, got[:, -half:]])
        keep, send = split(mm_tn(d, h).astype(BF).reshape(n_img, -1, half), steps_qkv)
    qkv = Sum(s, 2, steps_qkv, keep, send)
    qkv.go()
    dx0, dx1, dx2, norms, sums = qkv_bwd(s, d_main, d_got, patches, x_got, ln1_gain, dmid, w_qkv)
    if aligned:
        keep, send = grad_vec(s, norms, sums, n_img, steps_qkv)
    else:
        tiny = lines_of(TINY_QKV, norms[0], norms[1], sums[0], sums[2])
        keep, send = split(jnp.concatenate([tiny, tiny], axis=1), steps_qkv)
    vec = Sum(s, 2, steps_qkv, keep, send)
    vec.go()
    up.step()
    down.step()
    def step_qkv():
        qkv.halve()
        vec.halve()
        go_together(s, qkv, vec)

    for _ in range(len(steps_qkv[0]) - 4):
        down.step()
        up.step()
        step_qkv()
    step_qkv()
    up.step()
    sum_down = down.last()
    down_other = swap(sum_down, "seq", 2)
    step_qkv()
    step_qkv()
    up.steps_left(0)
    parts = (qkv.last(), vec.last())
    sum_qkv = stack(s, *parts, there=(down_other,)) if aligned else jnp.concatenate(parts)
    qkv_other = swap(stack(s, sum_qkv, dx1) if aligned else jnp.concatenate([sum_qkv, dx1]), "seq", 2)
    sum_up = up.last()
    up_other = swap(sum_up, "seq", 2)
    own, others = (sum_up, sum_qkv, sum_down), (up_other, qkv_other, down_other)
    if aligned:
        both = collect(s, own, others)
    else:
        both = jnp.concatenate([*own, *[b[: a.shape[0]] for a, b in zip(own, others)]])
    both_got = swap(both, "seq", 1)
    grad_input = assemble_dx(s, dx0, qkv_other, dx2)
    done = (both, both_got, sum_up.shape[0], sum_qkv.shape[0], dim, hidden, n_img)
    weights = finish(s, *done) if aligned else finish_plain(core, chip, *done)
    g_up, g_out, g_qkv, g_down, g_gain1, g_shift1, g_bq, g_bv, g_bout, g_gain2, g_shift2, g_bup, g_bdown = weights

    return (
        quantized,
        token_loss,
        grad_input,
        g_gain1,
        g_shift1,
        g_qkv.T,
        g_bq,
        g_bv,
        g_out.T,
        g_bout,
        g_gain2,
        g_shift2,
        g_up,
        g_bup,
        g_down.T,
        g_bdown,
    )


def solution(mesh):
    return jax.shard_map(
        shards,
        mesh=mesh,
        in_specs=(
            P("img", "seq", None),
            P("img"),
            P(),
            P(),
            P(),
            P(),
            P(),
            P(),
            P(),
            P(),
            P(),
            P(),
            P(),
            P(),
            P(),
            P(("seq", "img"), None),
            P("img", "seq", None),
        ),
        out_specs=(
            P("img", "seq", None),
            P("img", "seq"),
            P("img", "seq", None),
            P("img"),
            P("img"),
            P(None, "img"),
            P("img"),
            P("img"),
            P(None, "img"),
            P("img"),
            P("img"),
            P("img"),
            P(None, "img"),
            P("img"),
            P(None, "img"),
            P("img"),
        ),
        check_vma=False,
    )
```

```python
import functools

import jax
import jax.numpy as jnp
from jax import lax
from jax.experimental import pallas as pl
from jax.experimental.pallas import tpu as pltpu
from jax.sharding import PartitionSpec as P

HEAD_DIM = 64
GRID_H = 16
EPS_NORM = 1e-06
COMMIT = 16.0
BF = jnp.bfloat16
F32 = jnp.float32
MIB = 1024 * 1024
MASKED = -1000000000.0


def mm(a, b):
    return jnp.dot(a, b, preferred_element_type=F32)


def mm_nt(a, b):
    return lax.dot_general(a, b, (((1,), (1,)), ((), ())), preferred_element_type=F32)


def mm_tn(a, b):
    return lax.dot_general(a, b, (((0,), (0,)), ((), ())), preferred_element_type=F32)


def swap(value, axis, bit):
    count = lax.axis_size(axis)
    return lax.ppermute(value, axis, [(i, i ^ bit) for i in range(count)])


def pick(value, index, axis):
    return lax.dynamic_index_in_dim(value, index, axis, keepdims=False)


def after(value, *others):
    return lax.optimization_barrier((value, *others))[0]


def parity(number):
    return bin(number).count("1") % 2


def shaped(shape, dtype=BF):
    return jax.ShapeDtypeStruct(tuple(shape), dtype)


def in_hbm(shape, dtype=BF):
    return pltpu.HBM(tuple(shape), dtype)


class Order:
    token = None


def call(kernel, name, mib, out_shape, scratch, s, *args, micros, streamed=0, by_hand=(), bounds=False):
    vm, hbm = pl.BlockSpec(memory_space=pltpu.VMEM), pl.BlockSpec(memory_space=pl.ANY)
    direct, count = len(args) - streamed, len(args) + len(out_shape)
    args = [
        pltpu.with_memory_space_constraint(arg, pltpu.HBM) if arg.ndim == 1 or (k >= direct and name not in ("stack", "cut")) else arg
        for k, arg in enumerate(args)
    ]

    def body(*refs):
        limits, token, refs = refs[0], refs[bounds], refs[bounds + 1 :]
        kernel(Place(), limits, *refs[:count], *refs[count + 1 :])
        refs[count][...] = token[...]

    out = pl.pallas_call(
        body,
        in_specs=[vm] * (direct + 1 + bounds) + [hbm] * streamed,
        out_specs=[hbm if out in by_hand else vm for out in range(len(out_shape))] + [vm],
        out_shape=[*out_shape, shaped((8, 128), F32)],
        scratch_shapes=scratch,
        compiler_params=pltpu.CompilerParams(vmem_limit_bytes=mib * MIB),
        cost_estimate=pl.CostEstimate(flops=int(micros * 2e8), bytes_accessed=0, transcendentals=0),
        name=name,
    )(*([s] if bounds else []), Order.token, *args)
    Order.token = out[-1]
    return out[:-1]


class Stream:
    def __init__(self, sems, *pairs, ahead=3):
        self.copies = [pltpu.make_async_copy(a, b, sems.at[k]) for k, (a, b) in enumerate(pairs)]
        self.done, self.begun = 0, 0
        self.start(ahead)

    def start(self, count):
        while self.begun < min(count, len(self.copies)):
            self.copies[self.begun].start()
            self.begun += 1

    def wait(self, count):
        while self.done < count:
            self.copies[self.done].wait()
            self.done += 1
            self.start(self.begun + 1)


ME, CORE, CHIP, SIDES = range(4)
X, NEAR, FAR = (1, 1), (2, 2), (4, 4)


def plans(n_img):
    if n_img == 8:
        return (
            ([X, NEAR, "y", FAR], ["y", NEAR, X, FAR]),
            ([X, "y", NEAR, FAR], ["y", X, NEAR, FAR]),
            ([NEAR, X, "y", FAR], [NEAR, "y", X, FAR]),
        )
    bits = [1 << k for k in reversed(range(n_img.bit_length() - 1))]
    order = [(bit, bit) for bit in bits] + ["y"]
    return ((order, order),) * 3


def side_here(step):
    if step == "y":
        return lax.axis_index("seq") // 2
    bits = lax.axis_index("img") & step[1]
    value = 0
    for k in range(step[1].bit_length()):
        value = value ^ ((bits >> k) & 1)
    return value


def sides_here(steps):
    core = lax.axis_index("seq") % 2
    return [jnp.where(core == 0, side_here(a), side_here(b)) for a, b in zip(*steps)]


class Place:
    def __getitem__(self, what):
        me = lax.axis_index("seq")
        if what < SIDES:
            return (me, me % 2, me // 2)[what]
        steps = plans(lax.axis_size("img"))
        chain, step = divmod(what - SIDES, len(steps[0][0]))
        return sides_here([order[step : step + 1] for order in steps[chain]])[0]


def line(ref, start=0, size=None):
    size = ref.shape[0] if size is None else size
    return ref[start : start + size].reshape(1, size)


def norm_stats(x):
    center = x - jnp.mean(x, axis=-1, keepdims=True)
    spread = jnp.mean(center * center, axis=-1, keepdims=True)
    inv = lax.rsqrt(spread + EPS_NORM)
    return center * inv, inv


def norm_back(xhat, inv, gain, dy):
    dxhat = dy * gain
    return inv * (
        dxhat - jnp.mean(dxhat, axis=-1, keepdims=True) - xhat * jnp.mean(dxhat * xhat, axis=-1, keepdims=True)
    )


def spots(index, block, me):
    shift = block.bit_length() - 1
    assert block == 1 << shift
    place = index >> shift
    mask = ((place & 1) << 1) | (place >> 1)
    return ((me ^ mask) << shift) | (index & (block - 1))


def limit_of(s, widths, last):
    row = widths[...].reshape(1, widths.shape[0])
    return GRID_H * (row[:, 2:3] if last else jnp.where(s[CHIP] == 0, row[:, 0:1], row[:, 1:2]))


def side_of(ref, side, width):
    return ref[:, pl.ds(pl.multiple_of(side * width, 128), width)]


def kv_last_kernel(s, widths, gain, shift, bv, patches, w_hbm, kv, h, x, w, sems):
    dim = h.shape[1]
    stream = Stream(sems, (patches.at[2], x), *((w_hbm.at[:, k * dim : (k + 1) * dim], w.at[k - 1]) for k in (1, 2)))
    stream.wait(1)
    xhat, _ = norm_stats(x[...].astype(F32))
    h[...] = (xhat * line(gain) + line(shift)).astype(BF)
    stream.wait(2)
    kv[:, :dim] = mm(h[...], w[0]).astype(BF)
    stream.wait(3)
    kv[:, dim:] = (mm(h[...], w[1]) + line(bv)).astype(BF)


def kv_last_fwd(s, patches, gain, shift, bv, w):
    _, block, dim = patches.shape
    return call(
        kv_last_kernel, "kv_last_fwd", 8, [shaped((block, 2 * dim)), shaped((block, dim))],
        [pltpu.VMEM((block, dim), BF), pltpu.VMEM((2, dim, dim), BF), pltpu.SemaphoreType.DMA((3,))],
        s, gain, shift, bv, patches, w, micros=2, streamed=2,
    )


def qkv_kernel(
    s, widths, got, h_last, gain, shift, bq, bv, w, patches, q_main, q_last, kv0, kv1, mine, send, h, x_own, sems
):
    half, dim = mine.shape[1], w.shape[0]
    block = got.shape[0]
    stream = Stream(sems, (patches.at[s[CHIP]], x_own))
    h[2 * block :, :] = h_last[...]
    xhat, _ = norm_stats(got[...].astype(F32))
    h[block : 2 * block, :] = (xhat * line(gain) + line(shift)).astype(BF)
    stream.wait(1)
    xhat, _ = norm_stats(x_own[...].astype(F32))
    h[:block, :] = (xhat * line(gain) + line(shift)).astype(BF)
    mine[...] = side_of(h, s[CORE], half)
    send[...] = side_of(h, 1 - s[CORE], half)
    keys = mm(h[: 2 * block, :], w[:, dim : 2 * dim]).astype(BF)
    values = (mm(h[: 2 * block, :], w[:, 2 * dim :]) + line(bv)).astype(BF)
    for k, out in enumerate((kv0, kv1)):
        out[:, :dim] = keys[k * block : (k + 1) * block]
        out[:, dim:] = values[k * block : (k + 1) * block]
    q = (mm(h[...], w[:, :dim]) + line(bq)).astype(BF)
    q_main[...] = q[: 2 * block]
    q_last[...] = q[2 * block :]


def qkv_fwd(s, patches, got, h_last, gain, shift, bq, bv, w):
    images, block, dim = patches.shape
    n, half = images * block, dim // 2
    return call(
        qkv_kernel, "qkv_fwd", 8,
        [
            shaped((2 * block, dim)), shaped((block, dim)), *[shaped((block, 2 * dim))] * 2, in_hbm((n, half)),
            shaped((n, half)),
        ],
        [pltpu.VMEM((n, dim), BF), pltpu.VMEM((block, dim), BF), pltpu.SemaphoreType.DMA((1,))],
        s, got, h_last, gain, shift, bq, bv, w, patches, micros=3, streamed=1,
    )


def two_heads(value):
    left = lax.broadcasted_iota(jnp.int32, value.shape, 1) < HEAD_DIM
    zero = jnp.zeros_like(value)
    return jnp.concatenate([jnp.where(left, value, zero), jnp.where(left, zero, value)], axis=0)


def one_pair(value):
    n = value.shape[0] // 2
    left = lax.broadcasted_iota(jnp.int32, (n, value.shape[1]), 1) < HEAD_DIM
    return jnp.where(left, value[:n], value[n:])


def rows_of(refs, lanes):
    return jnp.concatenate([ref[:, lanes] for ref in refs], axis=0)


def att_fwd_kernel(s, widths, q, *refs, last, block):
    kvs, o = refs[:-1], refs[-1]
    dim = q.shape[1]
    m = sum(kv.shape[0] for kv in kvs)
    index = lax.broadcasted_iota(jnp.int32, (1, m), 1)
    ok = spots(index, block, s[ME]) < limit_of(s, widths, last)
    for p in range(dim // 128):
        at, av = slice(p * 128, (p + 1) * 128), slice(dim + p * 128, dim + (p + 1) * 128)
        k, v = rows_of(kvs, at), rows_of(kvs, av)
        raw = mm_nt(two_heads(q[:, at]), k) * (HEAD_DIM**-0.5)
        scores = jnp.where(ok, raw, MASKED)
        expo = jnp.exp(scores - jnp.max(scores, axis=1, keepdims=True))
        probs = expo * (1.0 / jnp.sum(expo, axis=1, keepdims=True))
        o[:, at] = one_pair(mm(probs.astype(BF), v)).astype(BF)


def attention_fwd(s, q, kvs, last, block):
    return call(
        functools.partial(att_fwd_kernel, last=last, block=block), "attention_fwd", 10, [shaped(q.shape)], [],
        s, q, *kvs, micros=5, bounds=True,
    )[0]


def att_bwd_kernel(s, widths, q, do, *refs, last, block, first, pairs, more):
    n, dim = q.shape
    if pairs:
        kvs, out = refs[: len(refs) - 1 - more], refs[-1]
        m = sum(kv.shape[0] for kv in kvs)
        parts = [out.at[k * m // 2 : (k + 1) * m // 2, :] for k in range(4)]
        dq = out.at[2 * m : 2 * m + n, :]
        if more:
            dq_last, keep_last, got_last = refs[-4:-1]
            rows, wide = dq_last.shape[0], out.shape[1]
            parts_last = [dq_last[...]] + [
                (keep_last[k].astype(F32) + got_last[k].astype(F32)).astype(BF) for k in range(2)
            ]
            for k in range(3 * dim // wide):
                part, at = parts_last[k * wide // dim], k * wide % dim
                out[2 * m + n + k * rows : 2 * m + n + (k + 1) * rows, :] = part[:, at : at + wide]
    else:
        kvs, (keep, send, dq) = refs[:-3], refs[-3:]
        m = sum(kv.shape[0] for kv in kvs)
        parts = [keep.at[0], keep.at[1], send.at[0], send.at[1]]
    index = lax.broadcasted_iota(jnp.int32, (m, 1), 0)
    ok = spots(index, block, s[ME]) < limit_of(s, widths, last)
    for p in pairs or range(dim // 128):
        at, av = slice(p * 128, (p + 1) * 128), slice(dim + p * 128, dim + (p + 1) * 128)
        to = slice((p - pairs[0]) * 128, (p - pairs[0] + 1) * 128) if pairs else at
        k, v = rows_of(kvs, at), rows_of(kvs, av)
        q2, do2 = two_heads(q[:, at]), two_heads(do[first : first + n, at])
        raw = mm_nt(k, q2) * (HEAD_DIM**-0.5)
        scores = jnp.where(ok, raw, MASKED)
        expo = jnp.exp(scores - jnp.max(scores, axis=0, keepdims=True))
        probs = expo * (1.0 / jnp.sum(expo, axis=0, keepdims=True))
        dv = mm(probs.astype(BF), do2).astype(BF)
        dp = mm_nt(v, do2)
        inner = jnp.sum(probs * dp, axis=0, keepdims=True)
        ds = (probs * (dp - inner) * (HEAD_DIM**-0.5)).astype(BF)
        dk = mm(ds, q2).astype(BF)
        dq[:, to] = one_pair(mm_tn(ds, k)).astype(BF)
        for ref, part in zip(parts, (dk[: m // 2], dv[: m // 2], dk[m // 2 :], dv[m // 2 :])):
            ref[:, to] = part


def attention_bwd(s, q, kvs, do, first, last, block, pairs, more=()):
    n, dim = q.shape
    m = sum(kv.shape[0] for kv in kvs)
    return call(
        functools.partial(att_bwd_kernel, last=last, block=block, first=first, pairs=pairs, more=len(more)),
        "attention_bwd", 12,
        [shaped((2 * m + n + (len(more) and 3 * dim // len(pairs)), 128 * len(pairs)))] if pairs else [shaped((2, m // 2, dim)), shaped((2, m // 2, dim)), shaped((n, dim))],
        [], s, q, do, *kvs, *more, micros=4, bounds=True,
    )


def fold_kernel(s, widths, keep, got, keep_out, send_out):
    block = keep_out.shape[1]
    for k in range(2):
        total = (keep[k].astype(F32) + got[k].astype(F32)).astype(BF)
        keep_out[k] = total[:block]
        send_out[k] = total[block:]


def fold(s, keep, got):
    part = shaped((2, keep.shape[1] // 2, keep.shape[2]))
    return call(fold_kernel, "fold", 4, [part, part], [], s, keep, got, micros=0.5)


def stack_kernel(s, widths, *refs, count):
    at = 0
    for ref in refs[:count]:
        refs[-1][at : at + ref.shape[0], :] = ref[...]
        at += ref.shape[0]


def stack(s, *parts, there=()):
    shape = (sum(part.shape[0] for part in parts), parts[0].shape[1])
    kernel = functools.partial(stack_kernel, count=len(parts))
    return call(kernel, "stack", 8, [shaped(shape)], [], s, *parts, *there, micros=0.5, streamed=len(there))[0]


def cut_kernel(s, widths, a, b, *refs):
    first, second, both = refs[-3:]
    rows = first.shape[0]
    first[...] = a[:rows, :]
    second[...] = b[rows:, :]
    both[: 2 * rows, :] = b[...]
    both[2 * rows :, :] = a[...]


def cut(s, a, b, there):
    rows, dim = a.shape
    part = shaped((rows // 2, dim))
    return call(
        cut_kernel, "cut", 6, [part, part, shaped((2 * rows, dim))], [], s, a, b, *there, micros=0.3, streamed=len(there)
    )


def collect_kernel(s, widths, *refs):
    count = (len(refs) - 1) // 2
    at = 0
    for k, ref in enumerate(refs[:-1]):
        rows = refs[k % count].shape[0]
        refs[-1][at : at + rows, :] = ref[:rows, :]
        at += rows


def collect(s, own, others):
    shape = (2 * sum(part.shape[0] for part in own), own[0].shape[1])
    return call(collect_kernel, "collect", 6, [shaped(shape)], [], s, *own, *others, micros=0.5)[0]


def add_kernel(s, widths, keep, got, out, *, first):
    out[...] = (keep[...].astype(F32) + got[first : first + keep.shape[0], :].astype(F32)).astype(BF)


def add(s, keep, got, first):
    kernel = functools.partial(add_kernel, first=first)
    return call(kernel, "add", 4, [shaped(keep.shape)], [], s, keep, got, micros=0.5)[0]


def sorted_images(s, out, own, back, last):
    first = s[CHIP] == 0
    out[0] = jnp.where(first, own, back)
    out[1] = jnp.where(first, back, own)
    out[2] = last


def assemble_kernel(s, widths, mix0, mix1, mix2, loss, mix, losses):
    block = mix0.shape[0]
    sorted_images(s, mix, mix0[...], mix1[:block, :], mix2[...])
    first = s[CHIP] == 0
    own = loss[0:1, :block]
    back = sum(mix1[block : block + 8, k * block : (k + 1) * block].astype(F32) for k in range(3))[0:1]
    losses[0:1, :] = jnp.where(first, own, back)
    losses[1:2, :] = jnp.where(first, back, own)
    losses[2:3, :] = loss[0:1, 2 * block :]


def assemble(s, mix, loss):
    block, dim = mix[0].shape
    return call(
        assemble_kernel, "assemble", 8, [in_hbm((3, block, dim)), in_hbm((3, block), F32)], [],
        s, *mix, loss, micros=1,
    )


def assemble_dx_kernel(s, widths, dx0, pack, dx2, dx):
    block = dx0.shape[0]
    first = pack.shape[0] - 2 * block
    back = jnp.concatenate([pack[first : first + block, :], pack[first + block :, :]], axis=1)
    sorted_images(s, dx, dx0[...], back.astype(F32), dx2[...])


def assemble_dx(s, *dx):
    block, dim = dx[0].shape
    return call(assemble_dx_kernel, "assemble_dx", 8, [in_hbm((3, block, dim), F32)], [], s, *dx, micros=1)[0]


def halve_kernel(s, widths, keep, got, keep_out, send_out, *, at, first):
    rows = keep_out.shape[0]
    for out, side in ((keep_out, s[SIDES + at]), (send_out, 1 - s[SIDES + at])):
        here = keep[pl.ds(pl.multiple_of(side * rows, 16), rows), :].astype(F32)
        out[...] = (here + got[pl.ds(pl.multiple_of(first + side * rows, 16), rows), :].astype(F32)).astype(BF)


def halve(s, keep, got, at, first):
    part = shaped((keep.shape[0] // 2, keep.shape[1]))
    return call(functools.partial(halve_kernel, at=at, first=first), "halve", 8, [part, part], [], s, keep, got, micros=0.7)


def gelu_pair(x):
    z = jnp.abs(x) * (0.5**0.5)
    t = 1.0 / (1.0 + 0.3275911 * z)
    expo = jnp.exp(-0.5 * x * x)
    poly = t * (0.254829592 + t * (-0.284496736 + t * (1.421413741 + t * (-1.453152027 + t * 1.061405429))))
    tail = 0.5 * poly * expo
    cdf = jnp.where(x < 0.0, tail, 1.0 - tail)
    return x * cdf, cdf + x * (expo * 0.3989422804014327)


def mlp_tiles(side, h2, bup, wup, wdown, enc, act_ref, slope, tile):
    wide = slope.shape[1]
    for k in range(0, wide, tile):
        here, there = slice(k, k + tile), pl.ds(pl.multiple_of(side * wide + k, 128), tile)
        act, rate = gelu_pair(mm(h2[...], wup[:, there]) + bup[there].reshape(1, tile))
        act = act.astype(BF)
        act_ref[:, here] = act
        slope[:, here] = rate.astype(BF)
        enc[...] += mm(act, wdown[there, :])


def mlp_first_kernel(
    s, widths, got, att_main, att_last, h1, bout, gain, shift, bup, bdown, wout, wup, wdown, patches, mid, h2, enc, slope,
    send, x_own, sems, *, tile,
):
    dim = got.shape[1]
    half, wide = dim // 2, slope.shape[1]
    rows = att_main.shape[0]
    side = 1 - s[CORE]
    stream = Stream(sems, (patches.at[s[CHIP]], x_own.at[0]), (patches.at[2], x_own.at[1]))
    branch = mm(jnp.concatenate([att_main[...], att_last[...]], axis=0), wout[...])
    stream.wait(2)
    x = jnp.concatenate([x_own[0], got[...], x_own[1]], axis=0).astype(F32)
    middle = x + branch + line(bout)
    mid[...] = middle
    xhat, _ = norm_stats(middle)
    h2[...] = (xhat * line(gain) + line(shift)).astype(BF)
    enc[...] = middle + line(bdown)
    send[:, wide : wide + half] = side_of(h2, side, half)
    send[:rows, wide + half : wide + dim] = side_of(att_main, side, half)
    send[rows:, wide + half : wide + dim] = side_of(att_last, side, half)
    send[:, wide + dim :] = h1[...]
    mlp_tiles(side, h2, bup, wup, wdown, enc, send, slope, tile)


def mlp_second_kernel(s, widths, h2, enc_in, att_main, att_last, bup, wup, wdown, enc, slope, mine, *, tile):
    half, wide = h2.shape[1] // 2, slope.shape[1]
    rows = att_main.shape[0]
    enc[...] = enc_in[...]
    mine[:, wide : wide + half] = side_of(h2, s[CORE], half)
    mine[:rows, wide + half :] = side_of(att_main, s[CORE], half)
    mine[rows:, wide + half :] = side_of(att_last, s[CORE], half)
    mlp_tiles(s[CORE], h2, bup, wup, wdown, enc, mine, slope, tile)


def mlp_first(s, patches, got, att_main, att_last, h1, bout, gain, shift, bup, bdown, wout, wup, wdown):
    images, block, dim = patches.shape
    n, wide = images * block, wup.shape[1] // 2
    return call(
        functools.partial(mlp_first_kernel, tile=512), "mlp_first", 8,
        [
            shaped((n, dim), F32), shaped((n, dim)), shaped((n, dim), F32), shaped((n, wide)),
            shaped((n, wide + dim + dim // 2)),
        ],
        [pltpu.VMEM((2, block, dim), BF), pltpu.SemaphoreType.DMA((2,))],
        s, got, att_main, att_last, h1, bout, gain, shift, bup, bdown, wout, wup, wdown, patches, micros=6, streamed=1,
    )


def mlp_second(s, h2, enc, att_main, att_last, bup, wup, wdown):
    n, dim = h2.shape
    wide = wup.shape[1] // 2
    return call(
        functools.partial(mlp_second_kernel, tile=512), "mlp_second", 8,
        [shaped((n, dim), F32), shaped((n, wide)), shaped((n, wide + dim))], [],
        s, h2, enc, att_main, att_last, bup, wup, wdown, micros=5,
    )


def quant_kernel(s, widths, enc, cot_got, *refs, tile, scale):
    pieces, cot = refs[:-14], refs[-14]
    mix_own, mix_back, mix_last, loss, denc, dmlp, score, dweight, late, cot_own, mixes, losses, sems = refs[-13:]
    n, dim = enc.shape
    block = n // 3
    chunks, place = [], 0
    for piece in pieces:
        for first in range(0, piece.shape[0], tile):
            size = min(tile, piece.shape[0] - first)
            chunks.append((piece, slice(first, first + size), slice(place, place + size)))
            place += size + -size % 128
    stream = Stream(sems, (cot.at[s[CHIP]], cot_own.at[0]), (cot.at[2], cot_own.at[1]))
    low = enc[...].astype(BF)
    peak = None
    for piece, rows, cols in chunks:
        part = mm_nt(low, piece[rows, :]) * scale
        score[:, cols] = part
        top = jnp.max(part, axis=1, keepdims=True)
        peak = top if peak is None else jnp.maximum(peak, top)
    total = jnp.zeros_like(peak)
    late[...] = jnp.zeros_like(late)
    for piece, rows, cols in chunks:
        e = jnp.exp(score[:, cols] - peak)
        score[:, cols] = e
        total = total + jnp.sum(e, axis=1, keepdims=True)
        late[...] += mm(e.astype(BF), piece[rows, :])
    inv = 1.0 / total
    mix = late[...] * inv
    low = mix.astype(BF)
    mixes[: 2 * block, :] = low[: 2 * block]
    mixes[2 * block + 16 :, :] = low[2 * block :]
    index = lax.broadcasted_iota(jnp.int32, (n, 1), 0)
    spot = spots(index & (2 * block - 1), block, s[ME])
    ok = spot < jnp.where(index < 2 * block, limit_of(s, widths, False), limit_of(s, widths, True))
    diff = enc[...] - mix
    lost = jnp.where(ok, jnp.mean(diff * diff, axis=1, keepdims=True), 0.0)
    lost = jnp.transpose(jnp.broadcast_to(lost, (n, 128)))[0:8, :]
    losses[...] = lost
    back = lost[:, block : 2 * block]
    high = back.astype(BF)
    rest = back - high.astype(F32)
    below = 2 * block
    mixes[below : below + 16, :] = jnp.zeros((16, dim), BF)
    mixes[below : below + 8, :block] = high
    mixes[below : below + 8, block : 2 * block] = rest.astype(BF)
    mixes[below : below + 8, 2 * block : 3 * block] = (rest - rest.astype(BF).astype(F32)).astype(BF)
    spans = ((mix_own, 0, block), (mix_back, block, 2 * block + 16), (mix_last, 2 * block + 16, 3 * block + 16))
    outs = [pltpu.make_async_copy(mixes.at[a:b, :], out, sems.at[2 + k]) for k, (out, a, b) in enumerate(spans)]
    outs.append(pltpu.make_async_copy(losses, loss, sems.at[5]))
    for out in outs:
        out.start()
    pull = jnp.where(ok, (2.0 * COMMIT / dim) * diff, 0.0)
    denc[...] = pull
    stream.wait(2)
    cots = jnp.concatenate([cot_own[0], cot_got[...], cot_own[1]], axis=0).astype(F32)
    dmix = (cots - pull).astype(BF)
    inner = jnp.zeros_like(peak)
    for piece, rows, cols in chunks:
        d = mm_nt(dmix, piece[rows, :])
        dweight[:, cols] = d
        inner = inner + jnp.sum(score[:, cols] * d, axis=1, keepdims=True)
    inner = inner * inv
    inv = inv * scale
    for piece, rows, cols in chunks:
        dcode = (score[:, cols] * inv * (dweight[:, cols] - inner)).astype(BF)
        denc[...] += mm(dcode, piece[rows, :])
    dmlp[...] = denc[...].astype(BF)
    for out in outs:
        out.wait()


def quantizer(s, enc, cot, cot_got, pieces, tile=512):
    n, dim = enc.shape
    block = n // 3
    count = sum(-(-piece.shape[0] // tile) for piece in pieces)
    wide = count * tile
    return call(
        functools.partial(quant_kernel, tile=tile, scale=dim**-0.5), "quantizer", 21,
        [in_hbm((block, dim)), in_hbm((block + 16, dim)), in_hbm((block, dim))]
        + [in_hbm((8, n), F32), shaped((n, dim), F32), shaped((n, dim))],
        [
            pltpu.VMEM((n, wide), F32), pltpu.VMEM((n, wide), F32), pltpu.VMEM((n, dim), F32),
            pltpu.VMEM((2, block, dim), BF), pltpu.VMEM((n + 16, dim), BF), pltpu.VMEM((8, n), F32),
            pltpu.SemaphoreType.DMA((6,)),
        ],
        s, enc, cot_got, *pieces, cot, micros=14, streamed=1, by_hand=range(4), bounds=True,
    )


def quantizer_plain(s, enc, cots, book):
    n, dim = enc.shape
    block = n // 3
    index = jnp.arange(n)
    ok = spots(index & (2 * block - 1), block, lax.axis_index("seq")) < jnp.where(index < 2 * block, GRID_H * pick(s, lax.axis_index("seq") // 2, 0), GRID_H * s[2])
    scale = dim**-0.5
    scores = mm_nt(enc.astype(BF), book) * scale
    peak = jnp.max(scores, axis=-1, keepdims=True)
    log_total = peak + jnp.log(jnp.sum(jnp.exp(scores - peak), axis=-1, keepdims=True))
    weights = jnp.exp(scores - log_total)
    mix = mm(weights.astype(BF), book)
    diff = enc - mix
    loss = jnp.where(ok, jnp.mean(diff * diff, axis=-1), 0.0)
    pull = jnp.where(ok[:, None], 2.0 * COMMIT / dim * diff, 0.0)
    dmix = (cots.astype(F32) - pull).astype(BF)
    dweights = mm_nt(dmix, book)
    inner = jnp.sum(weights * dweights, axis=-1, keepdims=True)
    dcode = (weights * (dweights - inner) * scale).astype(BF)
    denc = mm(dcode, book) + pull
    low = mix.astype(BF)
    loss = jnp.broadcast_to(loss[None, :], (8, n))
    parts, rest = [], loss[:, block : 2 * block]
    for _ in range(3):
        parts.append(rest.astype(BF))
        rest = rest - parts[-1].astype(F32)
    parts = jnp.pad(jnp.concatenate(parts, axis=1), ((0, 8), (0, dim - 3 * block)))
    back = jnp.concatenate([low[block : 2 * block], parts])
    return low[:block], back, low[2 * block :], loss, denc, denc.astype(BF)


def mlp_bwd_kernel(
    s, widths, dmlp, denc, mid, gain, slope0, slope1, wdown, wup, wout, dp0, dp1, dbranch, dmid_ref, datt, rows, bup, acc,
    *, tile,
):
    hidden, wide = wup.shape[1], slope0.shape[1]
    for t in range(0, hidden, tile):
        span, half, here = slice(t, t + tile), t // wide, slice(t % wide, t % wide + tile)
        slope = jnp.where(s[CORE] == half, slope1[:, here], slope0[:, here]).astype(F32)
        dpre = (mm_nt(dmlp[...], wdown[span, :]) * slope).astype(BF)
        (dp0, dp1)[half][:, here] = dpre
        bup[:, span] = jnp.sum(dpre.astype(F32), axis=0, keepdims=True)
        part = mm_nt(dpre, wup[:, span])
        if t == 0:
            acc[...] = part
        else:
            acc[...] += part
    dy = acc[...]
    xhat, inv = norm_stats(mid[...])
    dmid = denc[...] + norm_back(xhat, inv, line(gain), dy)
    dmid_ref[...] = dmid
    low = dmid.astype(BF)
    dbranch[...] = low
    datt[...] = mm_nt(low, wout[...]).astype(BF)
    rows[0:1, :] = jnp.sum(dy * xhat, axis=0, keepdims=True)
    rows[1:2, :] = jnp.sum(dy, axis=0, keepdims=True)
    rows[2:3, :] = jnp.sum(low.astype(F32), axis=0, keepdims=True)
    rows[3:4, :] = jnp.sum(dmlp[...].astype(F32), axis=0, keepdims=True)


def mlp_bwd(s, dmlp, denc, mid, gain, slopes, wdown, wup, wout):
    n, dim = denc.shape
    hidden, tile = wup.shape[1], 512
    return call(
        functools.partial(mlp_bwd_kernel, tile=tile), "mlp_bwd", 8,
        [
            shaped((n, hidden // 2)), shaped((n, hidden // 2)), shaped((n, dim)), shaped((n, dim), F32),
            shaped((n, dim)), shaped((4, dim), F32), shaped((1, hidden), F32),
        ],
        [pltpu.VMEM((n, dim), F32)],
        s, dmlp, denc, mid, gain, *slopes, wdown, wup, wout, micros=9,
    )


TINY_UP, TINY_QKV = 32, 16


def labels(steps, index, part):
    return [[part if step == "y" else parity(index & step[1]) for step in order] for order in steps]


def place(s, first, steps, keep, send, index, part, rows, value):
    sides = labels(steps, index, part)
    slots = [functools.reduce(lambda x, y: 2 * x + y, side[1:], 0) for side in sides]
    here = sides[0][0] + (sides[1][0] - sides[0][0]) * s[CORE]
    slot = slots[0] + (slots[1] - slots[0]) * s[CORE]

    @pl.when(s[first] == here)
    def _():
        keep[slot, rows, :] = value

    @pl.when(s[first] != here)
    def _():
        send[slot, rows, :] = value


def quotient(index, size):
    return ((index.astype(F32) + 0.5) * (1.0 / size)).astype(jnp.int32)


def tiny_rows(rows, shards, half):
    dim = rows.shape[1]
    part = dim // shards
    shard = lax.broadcasted_iota(jnp.int32, (shards, dim), 0)
    of = quotient(lax.broadcasted_iota(jnp.int32, (shards, dim), 1), part)
    local = lax.broadcasted_iota(jnp.int32, (dim, 1), 0)
    local = local - quotient(local, part) * part
    lane = lax.broadcasted_iota(jnp.int32, (dim, half), 1)
    total = jnp.zeros((shards, half), F32)
    for k in range(4):
        spread = jnp.where(of == shard, jnp.broadcast_to(rows[k : k + 1, :], (shards, dim)), 0.0)
        total = total + mm(spread.astype(BF), (lane == local + k * part).astype(F32).astype(BF))
    return total


def grad_down_kernel(s, widths, dm, act0, act1, keep, send, *, shards, steps):
    n, half = act0.shape[0], keep.shape[2]
    rows = dm.shape[1] // shards // 2
    width = keep.shape[1] // rows * half
    full = (mm_tn(dm[:n, :], act0[:, :width]) + mm_tn(dm[n:, :], act1[:, :width])).astype(BF)
    for j in range(2 * shards):
        for k in range(width // half):
            value = full[j * rows : (j + 1) * rows, k * half : (k + 1) * half]
            place(s, SIDES, steps, keep, send, j // 2, j % 2, slice(k * rows, (k + 1) * rows), value)


def grad_down(s, dm, act0, act1, shards, steps):
    dim = dm.shape[1]
    half = dim // 2
    part = shaped((shards, dim // shards // 2 * ((act0.shape[1] - dim) // half), half))
    return call(
        functools.partial(grad_down_kernel, shards=shards, steps=steps), "grad_down", 10, [part, part], [],
        s, dm, act0, act1, micros=4,
    )


def grad_up_kernel(s, widths, a0, a1, *refs, shards, steps):
    d0, d1, (four, bup, keep, send) = refs[:3], refs[3:6], refs[6:]
    size, half = keep.shape[1], keep.shape[2]
    wide = d0[0].shape[1]
    hidden = 2 * wide
    first = hidden // 2
    cols = hidden // shards
    rows = 2 * half // shards
    per = shards // 4
    tiny = tiny_rows(four[...], shards, half)
    at = lax.broadcasted_iota(jnp.int32, (2 * size - half - rows, half), 0)

    def put(index, part, at, value):
        place(s, SIDES + 4, steps, keep, send, index, part, slice(at, at + value.shape[0]), value)

    h = slice(first + half, first + 2 * half)
    out = (mm_tn(d0[2][...], a0[:, h]) + mm_tn(d1[2][...], a1[:, h])).astype(BF)
    h = slice(first, first + half)
    for k in range(0, shards, per):
        side, first_col = k * cols // wide, k * cols % wide
        span = slice(first_col, first_col + per * cols)
        full = (mm_tn(a0[:, h], d0[side][:, span]) + mm_tn(a1[:, h], d1[side][:, span])).astype(BF)
        for j in range(per):
            put(k + j, 0, 0, full[:size, j * cols : (j + 1) * cols])
            put(k + j, 1, 0, full[size:, j * cols : (j + 1) * cols])
            put(k + j, 1, half - size, out[(k + j) * rows : (k + j + 1) * rows])
            both = jnp.where(at == 0, tiny[k + j : k + j + 1], 0.0)
            both = both + jnp.where(at == 1, bup[:, (k + j) * cols : (k + j + 1) * cols], 0.0)
            put(k + j, 1, half - size + rows, both.astype(BF))


def grad_up(s, mine, got, dp0, dp1, four, bup, shards, steps):
    half = got.shape[1] - mine.shape[1]
    dim = 2 * half
    part = shaped((shards, (half + dim // shards + TINY_UP) // 2, half))
    return call(
        functools.partial(grad_up_kernel, shards=shards, steps=steps), "grad_up", 10,
        [part, part], [], s, mine, got, *dp0, *dp1, four, bup, micros=5,
    )


def got_rows(owns):
    return owns[0].shape[0] // 5


def last_of(ref, step, n, block, dim):
    wide = ref.shape[1]
    blocks = [
        ref[5 * n + k * block : 5 * n + (k + 1) * block, :] for k in range(step * dim // wide, (step + 1) * dim // wide)
    ]
    return jnp.concatenate(blocks, axis=1)


def d_of(owns, gots, step, n):
    if step == 0:
        return jnp.concatenate([own[4 * n : 5 * n, :] for own in owns], axis=1)
    mine, theirs = slice((step - 1) * n, step * n), slice((step + 1) * n, (step + 2) * n)
    return jnp.concatenate(
        [(own[mine, :].astype(F32) + got[theirs, :].astype(F32)).astype(BF) for own, got in zip(owns, gots)], axis=1
    )


def grad_qkv_kernel(
    s, widths, *refs, shards, steps
):
    groups = (len(refs) - 4) // 2
    owns, gots = refs[:groups], refs[groups : 2 * groups]
    h_own, other, keep, send = refs[-4:]
    n, half = got_rows(owns), h_own.shape[1]
    block = n // 2
    dim = 2 * half
    h = slice(other.shape[1] - half, other.shape[1])
    size = 3 * dim // shards // 2

    def put(k, at, value):
        place(s, SIDES + 8, steps, keep, send, k // 2, k % 2, slice(at, at + value.shape[0]), value)

    for step in range(3):
        d_own, d_got = d_of(owns, gots, step, n), d_of(gots, owns, step, n)
        full = mm_tn(d_own, h_own[:n, :]) + mm_tn(d_got, other[:n, h])
        last_own, last_got = (last_of(refs[1], step, n, block, dim) for refs in (owns, gots))
        full = full + mm_tn(last_own, h_own[n:, :]) + mm_tn(last_got, other[n:, h])
        full = full.astype(BF)
        first = step * dim
        for k in range(first // size, (first + dim + size - 1) // size):
            lo, hi = max(first, k * size), min(first + dim, (k + 1) * size)
            put(k, lo - k * size, full[lo - first : hi - first])


def grad_qkv(s, owns, gots, h_own, other, shards, steps):
    half = h_own.shape[1]
    part = shaped((shards, 3 * half // shards, half))
    return call(
        functools.partial(grad_qkv_kernel, shards=shards, steps=steps), "grad_qkv", 12, [part, part], [],
        s, *owns, *gots, h_own, other, micros=4,
    )


def grad_vec_kernel(s, widths, norms, sums, keep, send, *, shards, steps):
    half = keep.shape[2]
    tiny = tiny_rows(jnp.concatenate([norms[...], sums[0:1, :], sums[2:3, :]], axis=0), shards, half)
    at = lax.broadcasted_iota(jnp.int32, (TINY_QKV, half), 0)
    for k in range(2 * shards):
        value = jnp.where(at == 0, tiny[k // 2 : k // 2 + 1], 0.0).astype(BF)
        place(s, SIDES + 8, steps, keep, send, k // 2, k % 2, slice(None), value)


def grad_vec(s, norms, sums, shards, steps):
    part = shaped((shards, TINY_QKV, norms.shape[1] // 2))
    return call(
        functools.partial(grad_vec_kernel, shards=shards, steps=steps), "grad_vec", 8, [part, part], [],
        s, norms, sums, micros=1,
    )


def qkv_bwd_kernel(
    s, widths, *refs
):
    groups = (len(refs) - 13) // 2
    owns, gots = refs[:groups], refs[groups : 2 * groups]
    x_got, gain, dmid, w, patches, dx0, dx1, dx2, norms, sums, acc, x_own, sems = refs[-13:]
    block, dim = x_got.shape
    n = 2 * block
    spans = [slice(k * dim, (k + 1) * dim) for k in range(3)]
    stream = Stream(sems, (patches.at[s[CHIP]], x_own.at[0]), (patches.at[2], x_own.at[1]))
    for k, cols in enumerate(spans):
        d = jnp.concatenate([d_of(owns, gots, k, n), last_of(owns[1], k, n, block, dim)], axis=0)
        sums[k : k + 1, :] = jnp.sum(d.astype(F32), axis=0, keepdims=True)
        part = mm_nt(d, w[:, cols])
        if k == 0:
            acc[...] = part
        else:
            acc[...] += part
    dy = acc[...]
    stream.wait(2)
    x = jnp.concatenate([x_own[0], x_got[...], x_own[1]], axis=0).astype(F32)
    xhat, inv = norm_stats(x)
    dx = dmid[...] + norm_back(xhat, inv, line(gain), dy)
    dx0[...] = dx[:block]
    for k in range(2):
        dx1[k * block : (k + 1) * block, :] = dx[block:n, k * dim // 2 : (k + 1) * dim // 2].astype(BF)
    dx2[...] = dx[n:]
    norms[0:1, :] = jnp.sum(dy * xhat, axis=0, keepdims=True)
    norms[1:2, :] = jnp.sum(dy, axis=0, keepdims=True)


def qkv_bwd(s, owns, gots, patches, x_got, gain, dmid, w):
    images, block, dim = patches.shape
    return call(
        qkv_bwd_kernel, "qkv_bwd", 9,
        [
            in_hbm((block, dim), F32), shaped((2 * block, dim // 2)), in_hbm((block, dim), F32),
            shaped((2, dim), F32), shaped((3, dim), F32),
        ],
        [
            pltpu.VMEM((images * block, dim), F32), pltpu.VMEM((2, block, dim), BF),
            pltpu.SemaphoreType.DMA((2,)),
        ],
        s, *owns, *gots, x_got, gain, dmid, w, patches, micros=4, streamed=1,
    )


def finish_kernel(s, widths, both, both_got, up, out, qkv, wdown, *vectors, rows_up, rows_qkv, size, parts):
    def sorted_of(value, other):
        cut = value.shape[0] // 2
        mine = [value[:cut].astype(F32), value[cut:].astype(F32)]
        theirs = [other[:cut].astype(F32), other[cut:].astype(F32)]
        second = s[CHIP] > 0
        pairs = [[jnp.where(second, v[1], v[0]), jnp.where(second, v[0], v[1])] for v in (mine, theirs)]
        swap_cores = s[CORE] > 0
        return [
            [jnp.where(swap_cores, b, a) for a, b in zip(*pairs)],
            [jnp.where(swap_cores, a, b) for a, b in zip(*pairs)],
        ]

    cores = sorted_of(both, both_got)
    rows = [jnp.concatenate([first[:rows_up], second[:rows_up]], axis=0) for first, second in cores]
    half = up.shape[0] // 2
    wide = out.shape[0]
    up[:half, :] = rows[0][:half]
    up[half:, :] = rows[1][:half]
    out[...] = jnp.concatenate([r[half : half + wide] for r in rows], axis=1)
    pieces = [jnp.concatenate([f[rows_up : rows_up + size], g[rows_up : rows_up + size]], axis=0) for f, g in cores]
    qkv[...] = jnp.concatenate(pieces, axis=1)
    two = rows[0][half + wide : half + wide + 8] + rows[1][half + wide : half + wide + 8]
    one = cores[0][0][rows_up + size : rows_up + size + 8] + cores[1][0][rows_up + size : rows_up + size + 8]
    for ref, (source, row, at) in zip(vectors, parts):
        ref[...] = (one, two)[source][row : row + 1, at : at + ref.shape[0]].reshape(ref.shape[0])
    first = rows_up + rows_qkv
    blocks = out.shape[0] // 2
    count = (both.shape[0] // 2 - first) // blocks
    for c, pair in enumerate(cores):
        for y, part in enumerate(pair):
            for k in range(count):
                at = (c * count + k) * half
                wdown[y * blocks : (y + 1) * blocks, at : at + half] = part[first + k * blocks : first + (k + 1) * blocks]


def finish(s, both, both_got, rows_up, rows_qkv, dim, hidden, shards):
    part, wide = dim // shards, hidden // shards
    size = 3 * dim // shards // 2
    parts = [(0, 0, k * part) for k in range(4)]
    parts += [(1, 0, 2 * part), (1, 0, 0), (1, 0, part), (1, 1, 0), (1, 0, 3 * part)]
    widths = [part] * 7 + [wide, part]
    return call(
        functools.partial(finish_kernel, rows_up=rows_up, rows_qkv=rows_qkv, size=size, parts=parts), "finish", 20,
        [in_hbm((dim, wide), F32), in_hbm((part, dim), F32), in_hbm((3 * part, dim), F32), in_hbm((part, hidden), F32)]
        + [in_hbm((width,), F32) for width in widths],
        [], s, both, both_got, micros=3,
    )


def hop(value, step0, step1):
    seq, img = lax.axis_size("seq"), lax.axis_size("img")
    pairs = []
    for s in range(seq):
        step = step1 if s % 2 else step0
        for i in range(img):
            to = (s ^ 2, i) if step == "y" else (s, i ^ (step if isinstance(step, int) else step[0]))
            pairs.append((s * img + i, to[0] * img + to[1]))
    return lax.ppermute(value, ("seq", "img"), pairs)


def plus(kept, got):
    return (kept.astype(F32) + got.astype(F32)).astype(BF)


class Sum:
    def __init__(self, s, chain, steps, keep, send):
        self.s, self.base, self.steps, self.at = s, chain * len(steps[0]), steps, 0
        self.keep, self.send = (part.reshape(-1, part.shape[-1]) for part in (keep, send))

    def go(self):
        self.got, self.first = hop(self.send, self.steps[0][self.at], self.steps[1][self.at]), 0
        self.at += 1

    def halve(self):
        if self.keep.shape[0] % 32 == 0:
            self.keep, self.send = halve(self.s, self.keep, self.got, self.base + self.at, self.first)
            return
        total = plus(self.keep, self.got[self.first : self.first + self.keep.shape[0]]).reshape(2, -1, self.keep.shape[1])
        side = sides_here(self.steps)[self.at]
        self.keep, self.send = pick(total, side, 0), pick(total, 1 - side, 0)

    def step(self):
        self.halve()
        self.go()

    def steps_left(self, most):
        while len(self.steps[0]) - self.at > most:
            self.step()

    def last(self):
        if self.keep.shape[0] % 16 == 0:
            return add(self.s, self.keep, self.got, self.first)
        return plus(self.keep, self.got[self.first : self.first + self.keep.shape[0]])


def go_together(s, a, b):
    if [order[a.at] for order in a.steps] != [order[b.at] for order in b.steps]:
        a.go()
        b.go()
        return
    rows = a.send.shape[0]
    both = stack(s, a.send, b.send) if rows % 16 == 0 else jnp.concatenate([a.send, b.send])
    got = hop(both, a.steps[0][a.at], a.steps[1][a.at])
    for chain, first in ((a, 0), (b, rows)):
        chain.got, chain.first = got, first
        chain.at += 1


def finish_plain(core, chip, both, both_got, rows_up, rows_qkv, dim, hidden, shards):
    part, wide, half = dim // shards, hidden // shards, dim // 2
    size = 3 * dim // shards // 2

    def sorted_of(value, other):
        pairs = []
        for v in (value, other):
            a, b = jnp.split(v.astype(F32), 2)
            pairs.append([jnp.where(chip == 0, a, b), jnp.where(chip == 0, b, a)])
        mine, theirs = pairs
        first = [jnp.where(core == 0, a, b) for a, b in zip(mine, theirs)]
        return [first, [jnp.where(core == 0, b, a) for a, b in zip(mine, theirs)]]

    cores = sorted_of(both, both_got)
    rows = [jnp.concatenate([f[:rows_up], g[:rows_up]]) for f, g in cores]
    up = jnp.concatenate([r[:wide].T for r in rows])
    out = jnp.concatenate([r[wide : wide + part] for r in rows], axis=1)
    pieces = [jnp.concatenate([f[rows_up : rows_up + size], g[rows_up : rows_up + size]]) for f, g in cores]
    two = sum(r[wide + part :] for r in rows).reshape(-1)
    one = sum(f[rows_up + size : rows_up + rows_qkv] for f, _ in cores).reshape(-1)
    downs = [[f[rows_up + rows_qkv :].reshape(-1, part // 2, half) for f in pair] for pair in cores]
    downs = [jnp.concatenate([f.transpose(1, 0, 2).reshape(part // 2, -1) for f in pair]) for pair in downs]
    down = jnp.concatenate(downs, axis=1)
    first = [one[k * part : (k + 1) * part] for k in range(4)]
    second = [two[k * part : (k + 1) * part] for k in (2, 0, 1)]
    last = [two[4 * part : 4 * part + wide], two[3 * part : 4 * part]]
    return [up, out, jnp.concatenate(pieces, axis=1), down, *first, *second, *last]


class Book:
    def __init__(self, s, codebook):
        n_img = lax.axis_size("img")
        bits = [1 << k for k in range(n_img.bit_length() - 1)]
        masks = [1, 2, 6] if n_img == 8 else bits
        self.orders = list(zip(masks[1:], [1, "y", *masks[3:]]))
        self.ends = ((1, masks[1]), ("y", masks[2]))
        self.s, self.value = s, codebook

    def stack(self, *parts, there=()):
        return stack(self.s, *parts, there=there) if sum(part.size for part in parts) < 1 << 21 else jnp.concatenate(parts)

    def start(self):
        self.got = hop(self.value, *self.orders.pop(0))

    def double(self):
        self.value = self.stack(self.value, self.got)

    def spread(self):
        self.beside, self.across = hop(self.value, *self.ends[0]), hop(self.value, *self.ends[1])
        self.other = [swap(self.value, "seq", 1)]

    def corner(self, there):
        if self.value.size < 1 << 21:
            *parts, self.sides = cut(self.s, self.across, self.beside, (there, self.other[0]))
        else:
            half = self.value.shape[0] // 2
            parts = self.across[:half], self.beside[half:]
            self.sides = jnp.concatenate([self.beside, self.across])
        self.corners = hop(parts[0], *self.ends[0]), hop(parts[1], *self.ends[1])
        self.other.append(swap(self.sides, "seq", 1))

    def finish(self):
        rest = self.stack(*self.corners, there=(self.other[1],))
        return [self.value, self.sides, rest, *self.other, swap(rest, "seq", 1)]


def shards(
    patches,
    widths,
    ln1_gain,
    ln1_bias,
    w_qkv,
    b_query,
    b_value,
    w_out,
    b_out,
    ln2_gain,
    ln2_bias,
    w_up,
    b_up,
    w_down,
    b_down,
    codebook,
    cotangent,
):
    images, block, dim = patches.shape
    hidden = w_up.shape[1]
    n_img = lax.axis_size("img")
    me = lax.axis_index("seq")
    chip, core = me // 2, me % 2
    half, main = dim // 2, 2 * block
    fits = codebook.shape[0] * n_img * lax.axis_size("seq") <= 4096
    aligned = n_img == 8 and dim // n_img // 2 % 16 == 0
    steps_down, steps_up, steps_qkv = plans(n_img)
    s = widths

    Order.token = jnp.zeros((8, 128), F32)
    book = Book(s, codebook)
    book.start()
    x_got = swap(pick(patches, 1 - chip, 0), "seq", 2)
    kv_last, h_last = kv_last_fwd(s, patches, ln1_gain, ln1_bias, b_value, w_qkv)
    kv_y = swap(kv_last, "seq", 2)
    while book.orders:
        book.double()
        book.start()
    q_main, q_last, *kvs, h_mine, h_send = qkv_fwd(s, patches, x_got, h_last, ln1_gain, ln1_bias, b_query, b_value, w_qkv)
    kvs.append(kv_last)
    kvs_other = [swap(kv, "seq", 1) for kv in kvs]
    book.double()
    book.spread()
    kvs_main = kvs[:2] + kvs_other[:2]
    att_main = attention_fwd(s, q_main, kvs_main, False, block)
    cot_got = swap(pick(cotangent, 1 - chip, 0), "seq", 2)
    kvs_last = [kvs[2], kv_y, kvs_other[2], swap(kv_y, "seq", 1)]
    att_last = attention_fwd(s, q_last, kvs_last, True, block)
    mid, h2, enc, slope0, send = mlp_first(
        s, patches, x_got, att_main, att_last, h_send, b_out, ln2_gain, ln2_bias, b_up, b_down, w_out, w_up,
        w_down,
    )
    got = swap(send, "seq", 1)
    book.corner(cot_got)
    enc, slope1, mine = mlp_second(s, h2, enc, att_main, att_last, b_up, w_up, w_down)
    pieces = book.finish()
    if fits:
        mix0, mix1, mix2, loss, denc, dmlp = quantizer(s, enc, cotangent, cot_got, pieces)
    else:
        cots = jnp.concatenate([pick(cotangent, chip, 0), cot_got, cotangent[2]])
        mix0, mix1, mix2, loss, denc, dmlp = quantizer_plain(s, enc, cots, jnp.concatenate(pieces))
    mix1 = swap(mix1, "seq", 2)

    def split(full, steps):
        rows, cols = full.shape[-2:]
        full = full.reshape([2] * len(steps[0]) + [rows // 2, cols])
        side = sides_here(steps)[0]
        return pick(full, side, 0), pick(full, 1 - side, 0)

    def lines_of(count, *vectors):
        rows = jnp.concatenate([v.reshape(n_img, -1) for v in vectors], axis=1).astype(BF)
        return jnp.pad(rows, ((0, 0), (0, count * half - rows.shape[1]))).reshape(n_img, count, half)

    dmlp_got = swap(dmlp, "seq", 1)
    both = jnp.concatenate([mine, got[:, : mine.shape[1]]])
    if aligned:
        dmlp_both = stack(s, dmlp, dmlp_got, there=(got,))
        keep, send = grad_down(s, dmlp_both, mine, got, n_img, steps_down)
    else:
        full = mm_tn(jnp.concatenate([dmlp, dmlp_got]), both[:, : hidden // 2]).astype(BF)
        full = full.reshape(n_img, 2, dim // n_img // 2, -1, half).transpose(0, 1, 3, 2, 4)
        keep, send = split(full.reshape(n_img, -1, half), steps_down)
    down = Sum(s, 0, steps_down, keep, send)
    down.go()
    *dp, dmid, datt, rows_two, sum_bup = mlp_bwd(s, dmlp, denc, mid, ln2_gain, (slope0, slope1), w_down, w_up, w_out)
    dp_got = [swap(part, "seq", 1) for part in dp]
    quantized, token_loss = assemble(s, (mix0, mix1, mix2), loss)
    keep_last, send_last, dq_last = attention_bwd(s, q_last, kvs_last, datt, main, True, block, ())
    got_last = swap(send_last, "seq", 1)
    keep_last, send_last = fold(s, keep_last, got_last)
    down.step()
    got_last = swap(send_last, "seq", 2)
    if aligned:
        keep, send = grad_up(s, mine, got, dp, dp_got, rows_two, sum_bup, n_img, steps_up)
    else:
        dps = jnp.concatenate([jnp.concatenate(dp, axis=1), jnp.concatenate(dp_got, axis=1)])
        up = mm_tn(both[:, hidden // 2 : hidden // 2 + half], dps[:, :hidden]).astype(BF)
        up = up.reshape(half, n_img, -1).transpose(1, 2, 0)
        out = mm_tn(dps[:, hidden:], both[:, hidden // 2 + half :]).astype(BF).reshape(n_img, -1, half)
        tiny = lines_of(TINY_UP, rows_two[0], rows_two[1], rows_two[2], rows_two[3], sum_bup[0])
        keep, send = split(jnp.concatenate([up, out, tiny], axis=1), steps_up)
    up = Sum(s, 1, steps_up, keep, send)
    up.go()
    d_main, d_got = [], []
    for pairs, more in (((0, 1), ()), ((2, 3), (dq_last, keep_last, got_last)), ((4, 5), ())):
        d_main += attention_bwd(s, q_main, kvs_main, datt, 0, False, block, pairs, more)
        d_got.append(swap(d_main[-1], "seq", 1))
        if len(d_main) == 2:
            down.step()
    if aligned:
        keep, send = grad_qkv(s, d_main, d_got, h_mine, got, n_img, steps_qkv)
    else:
        n = main

        def assembled(owns, gots):
            rows = [jnp.concatenate([own[4 * n : 5 * n] for own in owns], axis=1)]
            for k in (0, 1):
                mine, theirs = slice(k * n, (k + 1) * n), slice((k + 2) * n, (k + 3) * n)
                rows.append(jnp.concatenate([plus(own[mine], got[theirs]) for own, got in zip(owns, gots)], axis=1))
            last = owns[1][5 * n :].reshape(-1, block, owns[1].shape[1])
            return [jnp.concatenate(rows, axis=1), jnp.concatenate(list(last), axis=1)]

        d = jnp.concatenate(assembled(d_main, d_got) + assembled(d_got, d_main))
        h = jnp.concatenate([h_mine, got[:, -half:]])
        keep, send = split(mm_tn(d, h).astype(BF).reshape(n_img, -1, half), steps_qkv)
    qkv = Sum(s, 2, steps_qkv, keep, send)
    qkv.go()
    dx0, dx1, dx2, norms, sums = qkv_bwd(s, d_main, d_got, patches, x_got, ln1_gain, dmid, w_qkv)
    if aligned:
        keep, send = grad_vec(s, norms, sums, n_img, steps_qkv)
    else:
        tiny = lines_of(TINY_QKV, norms[0], norms[1], sums[0], sums[2])
        keep, send = split(jnp.concatenate([tiny, tiny], axis=1), steps_qkv)
    vec = Sum(s, 2, steps_qkv, keep, send)
    vec.go()
    up.step()
    down.step()
    def step_qkv():
        qkv.halve()
        vec.halve()
        go_together(s, qkv, vec)

    for _ in range(len(steps_qkv[0]) - 4):
        down.step()
        up.step()
        step_qkv()
    step_qkv()
    up.step()
    sum_down = down.last()
    down_other = swap(sum_down, "seq", 2)
    step_qkv()
    step_qkv()
    parts = (qkv.last(), vec.last())
    sum_qkv = stack(s, *parts, there=(down_other,)) if aligned else jnp.concatenate(parts)
    qkv_other = swap(stack(s, sum_qkv, dx1) if aligned else jnp.concatenate([sum_qkv, dx1]), "seq", 2)
    up.steps_left(0)
    sum_up = up.last()
    up_other = swap(sum_up, "seq", 2)
    own, others = (sum_up, sum_qkv, sum_down), (up_other, qkv_other, down_other)
    if aligned:
        both = collect(s, own, others)
    else:
        both = jnp.concatenate([*own, *[b[: a.shape[0]] for a, b in zip(own, others)]])
    both_got = swap(both, "seq", 1)
    grad_input = assemble_dx(s, dx0, qkv_other, dx2)
    done = (both, both_got, sum_up.shape[0], sum_qkv.shape[0], dim, hidden, n_img)
    weights = finish(s, *done) if aligned else finish_plain(core, chip, *done)
    g_up, g_out, g_qkv, g_down, g_gain1, g_shift1, g_bq, g_bv, g_bout, g_gain2, g_shift2, g_bup, g_bdown = weights

    return (
        quantized,
        token_loss,
        grad_input,
        g_gain1,
        g_shift1,
        g_qkv.T,
        g_bq,
        g_bv,
        g_out.T,
        g_bout,
        g_gain2,
        g_shift2,
        g_up,
        g_bup,
        g_down.T,
        g_bdown,
    )


def solution(mesh):
    return jax.shard_map(
        shards,
        mesh=mesh,
        in_specs=(
            P("img", "seq", None),
            P("img"),
            P(),
            P(),
            P(),
            P(),
            P(),
            P(),
            P(),
            P(),
            P(),
            P(),
            P(),
            P(),
            P(),
            P(("seq", "img"), None),
            P("img", "seq", None),
        ),
        out_specs=(
            P("img", "seq", None),
            P("img", "seq"),
            P("img", "seq", None),
            P("img"),
            P("img"),
            P(None, "img"),
            P("img"),
            P("img"),
            P(None, "img"),
            P("img"),
            P("img"),
            P("img"),
            P(None, "img"),
            P("img"),
            P(None, "img"),
            P("img"),
        ),
        check_vma=False,
    )
```
